32 devices in a mesh: rep: 8 (over z, core), shard: 4 (over y, x).
Axes of the slice: x: 2, y: 2, z: 4, core: 2. Of those that a mesh axis runs over, the one named last changes fastest.
Arguments:
- tokens: bfloat16 [8192, 2048], P(('rep', 'shard')), may hold values from -6 to 6
- segments: int32 [8192], P(('rep', 'shard')), may hold values from 0 to 3, as said below
- query_w: bfloat16 [2048, 2048], P('shard'), may hold values from -0.125 to 0.125
- key_w: bfloat16 [2048, 512], P('shard'), may hold values from -0.125 to 0.125
- value_w: bfloat16 [2048, 512], P('shard'), may hold values from -0.125 to 0.125
- proj_w: bfloat16 [2048, 2048], P('shard'), may hold values from -1.5 to 1.5
- attn_gain: float32 [2048], replicated, may hold values from 0.1 to 1.9
- gate_w: bfloat16 [2048, 8192], P('shard'), may hold values from -0.125 to 0.125
- up_w: bfloat16 [2048, 8192], P('shard'), may hold values from -0.125 to 0.125
- down_w: bfloat16 [8192, 2048], P('shard'), may hold values from -0.0625 to 0.0625
- mlp_gain: float32 [2048], replicated, may hold values from 0.1 to 1.9
- cotangent: bfloat16 [8192, 2048], P(('rep', 'shard')), may hold values from -6 to 6
Outputs:
- result: float32 [8192, 2048], P(('rep', 'shard'))
- grad_tokens: float32 [8192, 2048], P(('rep', 'shard'))
- grad_query: float32 [2048, 2048], P('shard')
- grad_key: float32 [2048, 512], P('shard')
- grad_value: float32 [2048, 512], P('shard')
- grad_proj: float32 [2048, 2048], P('shard')
- grad_attn_gain: float32 [2048], P('shard')
- grad_gate: float32 [2048, 8192], P('shard')
- grad_up: float32 [2048, 8192], P('shard')
- grad_down: float32 [8192, 2048], P('shard')
- grad_mlp_gain: float32 [2048], P('shard')
The draws below stay inside these ranges and needn't reach their ends.
Inputs may be any that keep to these rules, and one draw needn't show every extreme that they name: `segments`: each sequence of 1024 tokens (the rows of one index of rep) has segment numbers that start at 0 and never fall, and holds four documents; its second document begins within the sequence's first 256 tokens and ends within its last 256.
All inputs are finite; a program needn't handle non-finite values.
Results may differ from the reference program's by a relative error of at most 0.02.
Values may be sent and summed in bfloat16 or wider, within the bound.
A program may use at most 576 MiB of HBM per device.

```python
import math
import jax
import jax.numpy as jnp
from jax import lax

D = 2048
HEADS = 32
KV_HEADS = 8
HEAD = 64
FF = 8192
TOK_DEV = 256
KV_WIDTH = 512
LEN = 1024
TOKENS = 8192


def draw_segments(key, part):
    key = jax.random.fold_in(key, 11)
    groups = TOKENS // LEN
    key_one, key_two, key_three = jax.random.split(key, 3)
    first = jax.random.randint(key_one, (groups, 1), 1, TOK_DEV)
    last = LEN - jax.random.randint(key_two, (groups, 1), 2, TOK_DEV)
    extra = last + jax.random.randint(key_three, (groups, 1), jnp.ones_like(last), LEN - last)
    index = jnp.arange(LEN, dtype=jnp.int32)[None, :]
    seg_ids = (index >= first).astype(jnp.int32) + (index >= last).astype(jnp.int32) + (index >= extra).astype(jnp.int32)
    return seg_ids.reshape(TOKENS)


def block_scale(key, shape, cuts, least, top_value):
    level, own = 1.0, jax.random.fold_in(key, 6)
    for axis_at, shards_of in cuts:
        steps = jnp.exp(jax.random.uniform(jax.random.fold_in(own, axis_at), (shards_of,), jnp.float32, least / len(cuts), top_value / len(cuts)))
        level = level * jnp.repeat(steps, shape[axis_at] // shards_of).reshape([-1 if axis == axis_at else 1 for axis in range(len(shape))])
    return level


def gaussian(stream_key, shape, spread, reach, pieces=(), held_as=jnp.bfloat16):
    drawn = jax.random.normal(stream_key, shape, jnp.float32) * spread
    if len(pieces) > 0:
        drawn = block_scale(stream_key, shape, pieces, -0.22, 0.18) * drawn
    return jnp.clip(drawn, min=-reach, max=reach).astype(held_as)


def setup_inputs(seed: int = 0) -> dict:
    key_list = jax.random.split(jax.random.key(seed), 13)
    return {
        "tokens": gaussian(key_list[0], (TOKENS, D), 1.0, 6.0, ((0, 32),)),
        "segments": draw_segments(jax.random.fold_in(key_list[12], 71), 0),
        "query_w": gaussian(key_list[2], (D, D), D ** -0.5, 0.125, ((0, 4),)),
        "key_w": gaussian(key_list[3], (D, KV_WIDTH), D ** -0.5, 0.125, ((0, 4),)),
        "value_w": gaussian(key_list[4], (D, KV_WIDTH), D ** -0.5, 0.125, ((0, 4),)),
        "proj_w": gaussian(key_list[5], (D, D), 16 ** -0.5, 1.5, ((0, 4),)),
        "attn_gain": jnp.clip(1.0 + 0.18 * jax.random.normal(key_list[6], (D,), jnp.float32), 0.1, 1.9),
        "gate_w": gaussian(key_list[7], (D, FF), D ** -0.5, 0.125, ((0, 4),)),
        "up_w": gaussian(key_list[8], (D, FF), D ** -0.5, 0.125, ((0, 4),)),
        "down_w": gaussian(key_list[9], (FF, D), FF ** -0.5, 0.0625, ((0, 4),)),
        "mlp_gain": jnp.clip(1.0 + 0.18 * jax.random.normal(key_list[10], (D,), jnp.float32), 0.1, 1.9),
        "cotangent": gaussian(key_list[11], (TOKENS, D), 1.0, 6.0, ((0, 32),)),
    }


epsilon = 1e-05
rope_base = 500000.0
highest = lax.Precision.HIGHEST

@jax.custom_vjp
def low(v):
    return lax.optimization_barrier(v.astype(jnp.bfloat16)).astype(jnp.float32)

@jax.custom_vjp
def low_back(v):
    return v

def low_keep(v):
    return (low(v), None)

def low_pass(kept, grad):
    return (grad,)

def back_keep(v):
    return (v, None)

def back_low(kept, grad):
    return (low(grad),)
low.defvjp(low_keep, low_pass)
low_back.defvjp(back_keep, back_low)

def matmul_f(left, right):
    return jnp.dot(left, right, precision=highest, preferred_element_type=jnp.float32)

def normalize(values, gain_vec):
    inv_rms = lax.rsqrt(lax.optimization_barrier(jnp.mean(values * values, axis=-1, keepdims=True)) + epsilon)
    return values * inv_rms * gain_vec

def doc_positions(seg_ids):
    index = jnp.arange(seg_ids.shape[0], dtype=jnp.int32)
    fresh = (index == 0) | (seg_ids != jnp.roll(seg_ids, 1))
    begins = lax.cummax(jnp.where(fresh, index, jnp.zeros_like(index)), axis=0)
    return index - begins

def rope_tables(positions):
    freqs = rope_base ** (-(jnp.arange(HEAD // 2, dtype=jnp.float32) * (2.0 / HEAD)))
    angles = positions.astype(jnp.float32)[:, None] * freqs[None, :]
    return (jnp.cos(angles)[:, None, :], jnp.sin(angles)[:, None, :])

def rotate(values, cos_table, sin_table):
    row_count = values.shape[0]
    shaped = values.reshape(row_count, -1, HEAD)
    first_half = shaped[..., :HEAD // 2]
    second_half = shaped[..., HEAD // 2:]
    turned = jnp.concatenate([first_half * cos_table - second_half * sin_table, second_half * cos_table + first_half * sin_table], axis=-1)
    return turned.reshape(row_count, -1)

def block_forward(inputs, seg_ids, query_w, key_w, value_w, proj_w, attn_gain, gate_w, up_w, down_w, mlp_gain):
    length = inputs.shape[0]
    group = HEADS // KV_HEADS
    scale_factor = 1.0 / math.sqrt(HEAD)
    cos_table, sin_table = rope_tables(doc_positions(seg_ids))
    normed = low(normalize(inputs, attn_gain))
    queries = low(rotate(low_back(matmul_f(normed, query_w)), cos_table, sin_table))
    keys = low(rotate(low_back(matmul_f(normed, key_w)), cos_table, sin_table))
    values = low(low_back(matmul_f(normed, value_w)))
    query_heads = queries.reshape(length, KV_HEADS, group, HEAD).transpose(1, 2, 0, 3)
    key_heads = keys.reshape(length, KV_HEADS, HEAD).transpose(1, 0, 2)
    value_heads = values.reshape(length, KV_HEADS, HEAD).transpose(1, 0, 2)
    index = jnp.arange(length, dtype=jnp.int32)
    allowed = (seg_ids[:, None] == seg_ids[None, :]) & (index[None, :] <= index[:, None])

    def head_block(operands):
        query_h, key_h, value_h = operands
        scores = low_back(jnp.einsum('gqd,kd->gqk', query_h, key_h, precision=highest) * scale_factor)
        scores = jnp.where(allowed[None], scores, -1e+30)
        top = lax.optimization_barrier(jnp.max(scores, axis=-1, keepdims=True))
        expo = jnp.exp(scores - top)
        probs = expo / lax.optimization_barrier(jnp.sum(expo, axis=-1, keepdims=True))
        return jnp.einsum('gqk,kd->gqd', low(probs), value_h, precision=highest)
    mixed = lax.map(jax.checkpoint(head_block), (query_heads, key_heads, value_heads))
    mixed = low(low_back(mixed.transpose(2, 0, 1, 3).reshape(length, HEADS * HEAD)))
    hidden = inputs + low_back(matmul_f(mixed, proj_w))
    normed_mlp = low(normalize(hidden, mlp_gain))
    gate_val = low_back(matmul_f(normed_mlp, gate_w))
    up_val = low_back(matmul_f(normed_mlp, up_w))
    activ = low(jax.nn.silu(gate_val) * up_val)
    return hidden + matmul_f(activ, down_w)

def reference(tokens, segments, query_w, key_w, value_w, proj_w, attn_gain, gate_w, up_w, down_w, mlp_gain, cotangent):
    params = tuple((item.astype(jnp.float32) for item in (query_w, key_w, value_w, proj_w, attn_gain, gate_w, up_w, down_w, mlp_gain)))
    groups = TOKENS // LEN
    inputs = tokens.astype(jnp.float32).reshape(groups, LEN, D)
    seg_all = segments.reshape(groups, LEN)
    cot_all = cotangent.astype(jnp.float32).reshape(groups, LEN, D)

    def one_sequence(running, seq_item):
        seq_x, seq_seg, seq_cot = seq_item

        def forward(x_in, *weights_in):
            return block_forward(x_in, seq_seg, *weights_in)
        outcome, pullback = jax.vjp(forward, seq_x, *params)
        gradients = pullback(seq_cot)
        return (tuple((acc + new for acc, new in zip(running, gradients[1:]))), (outcome, gradients[0]))
    start_sums = tuple((jnp.zeros(item.shape, jnp.float32) for item in params))
    sums, (outcomes, input_grads) = lax.scan(one_sequence, start_sums, (inputs, seg_all, cot_all))
    return (outcomes.reshape(TOKENS, D), input_grads.reshape(TOKENS, D), sums[0], sums[1], sums[2], sums[3], sums[4], sums[5], sums[6], sums[7], sums[8])
```

```python
import functools
import math

import jax
import jax.numpy as jnp
from jax import lax
from jax.experimental import pallas as pl
from jax.experimental.pallas import tpu as pltpu
from jax.sharding import PartitionSpec as P

HEADS = 32
KV_HEADS = 8
HEAD = 64
GROUP = HEADS // KV_HEADS
SCALE = 1.0 / math.sqrt(HEAD)
TILE = 256
NEG = -1e30
MIB = 1024 * 1024

epsilon = 1e-05
rope_base = 500000.0
F32 = jnp.float32
BF16 = jnp.bfloat16


def dot(left, right, dims):
    return lax.dot_general(left, right, (dims, ((), ())), preferred_element_type=F32)


NN = ((1,), (0,))
NT = ((1,), (1,))
TN = ((0,), (0,))
TT = ((0,), (1,))


MESH = pl.DeviceIdType.MESH


def place():
    return lax.axis_index("rep"), lax.axis_index("shard")


def remote(src, dst, sends, recvs, index, rep, shard):
    return pltpu.make_async_remote_copy(
        src_ref=src,
        dst_ref=dst,
        send_sem=sends.at[index],
        recv_sem=recvs.at[index],
        device_id=(rep, shard),
        device_id_type=MESH,
    )


def greet(partners):
    barrier = pltpu.get_barrier_semaphore()
    for partner in partners:
        pl.semaphore_signal(barrier, inc=1, device_id=partner, device_id_type=MESH)
    pl.semaphore_wait(barrier, len(partners))


def plane_partners(rep, me, shards):
    return [(rep, me ^ step) for step in range(1, shards)]


class Spread:
    def __init__(self, shards, own, full, columns, sends, recvs, local_sem):
        rep, me = place()
        quarter = rep % 4
        count = own.shape[0]
        part = count // 4
        own_rows = pl.ds(pl.multiple_of(quarter * part, part), part)

        def at(shard, which):
            return full.at[pl.ds(pl.multiple_of(shard * count + which * part, part), part), :]

        def piece(shard):
            return own.at[own_rows, :] if columns is None else own.at[own_rows, columns(shard)]

        self.first, self.core, self.layer, self.last = [], [], [], []
        n = shards - 1
        for i in range(n):
            peer = me ^ (i + 1)
            self.first.append(remote(piece(peer), at(me, quarter), sends, recvs, i, rep, peer))
            mine = at(peer, quarter)
            self.core.append(remote(mine, mine, sends, recvs, n + i, rep ^ 1, me))
            self.layer.append(remote(mine, mine, sends, recvs, 2 * n + i, rep ^ 2, me))
            theirs = at(peer, quarter ^ 2)
            self.last.append(remote(theirs, theirs, sends, recvs, 3 * n + i, rep ^ 1, me))
        kept = own if columns is None else own.at[:, columns(me)]
        self.kept = pltpu.make_async_copy(
            kept, full.at[pl.ds(pl.multiple_of(me * count, count), count), :], local_sem
        )

    def start(self):
        for copy in self.first:
            copy.start()
        self.kept.start()

    def hand_on(self):
        for i, copy in enumerate(self.first):
            copy.wait_recv()
            self.layer[i].start()
            self.core[i].start()

    def hand_on_last(self):
        for i, copy in enumerate(self.layer):
            copy.wait_recv()
            self.last[i].start()

    def finish(self):
        for copy in self.core + self.last:
            copy.wait_recv()
        for copy in self.first + self.core + self.layer + self.last:
            copy.wait_send()
        self.kept.wait()

    @staticmethod
    def semaphores(shards):
        n = 4 * (shards - 1)
        return [
            pltpu.SemaphoreType.DMA((n,)),
            pltpu.SemaphoreType.DMA((n,)),
            pltpu.SemaphoreType.DMA,
        ]


class Gather:
    def __init__(self, shards, own, full, sends, recvs, local_sem=None):
        rep, me = place()
        count = own.shape[0]
        half = count // 2

        def at(shard, start, size):
            return full.at[pl.ds(pl.multiple_of(shard * count + start, half), size), :]

        self.direct, self.passed, self.kept = [], [], None
        if shards == 4:
            for i, (step, start) in enumerate(((1, 0), (2, half), (1, half), (2, 0))):
                self.direct.append(
                    remote(
                        own.at[pl.ds(start, half), :], at(me, start, half),
                        sends, recvs, i, rep, me ^ step,
                    )
                )
            for i, (step, start) in enumerate(((1, 0), (2, half))):
                came = at(me ^ step, start, half)
                self.passed.append(remote(came, came, sends, recvs, 4 + i, rep, me ^ step ^ 3))
        else:
            for i in range(shards - 1):
                self.direct.append(
                    remote(own, at(me, 0, count), sends, recvs, i, rep, me ^ (i + 1))
                )
        if local_sem is not None:
            self.kept = pltpu.make_async_copy(own, at(me, 0, count), local_sem)

    def start(self):
        for copy in self.direct:
            copy.start()
        if self.kept is not None:
            self.kept.start()

    def hand_on(self):
        for i, copy in enumerate(self.passed):
            self.direct[i].wait_recv()
            copy.start()

    def finish(self):
        for copy in self.direct[len(self.passed) :] + self.passed:
            copy.wait_recv()
        for copy in self.direct + self.passed:
            copy.wait_send()
        if self.kept is not None:
            self.kept.wait()

    @staticmethod
    def semaphores(shards):
        n = max(6, shards - 1)
        return [
            pltpu.SemaphoreType.DMA((n,)),
            pltpu.SemaphoreType.DMA((n,)),
            pltpu.SemaphoreType.DMA,
        ]


def column_block(part):
    return lambda shard: pl.ds(pl.multiple_of(shard * part, part), part)


def pair_partners(rep, me):
    return [(rep ^ 1, me), (rep ^ 2, me)]


ANY = pl.BlockSpec(memory_space=pl.ANY)
IN_VMEM = pl.BlockSpec(memory_space=pltpu.VMEM)


def first_kernel(shards, part, tokens, seg, qkv, tokens_all, seg_all, qkv_m, *sems):
    rep, me = place()
    greet(plane_partners(rep, me, shards) + pair_partners(rep, me))
    weight = Spread(shards, qkv, qkv_m, column_block(part), *sems[:3])
    rows = Gather(shards, tokens, tokens_all, *sems[3:6])
    seg_send, seg_recv, seg_local = sems[6:]
    segs = [
        remote(seg, seg_all.at[me], seg_send, seg_recv, i, rep, me ^ (i + 1))
        for i in range(shards - 1)
    ]
    weight.start()
    for copy in segs:
        copy.start()
    rows.start()
    own_seg = pltpu.make_async_copy(seg, seg_all.at[me], seg_local)
    own_seg.start()
    weight.hand_on()
    rows.hand_on()
    weight.hand_on_last()
    weight.finish()
    rows.finish()
    for copy in segs:
        copy.wait()
    own_seg.wait()


def first(tokens, seg, qkv_w, shards):
    rows, width = tokens.shape
    part = qkv_w.shape[1] // shards
    n = shards - 1
    return pl.pallas_call(
        functools.partial(first_kernel, shards, part),
        in_specs=[ANY] * 3,
        out_specs=[ANY] * 3,
        out_shape=[
            jax.ShapeDtypeStruct((shards * rows, width), tokens.dtype),
            jax.ShapeDtypeStruct((shards,) + seg.shape, seg.dtype),
            jax.ShapeDtypeStruct((shards * qkv_w.shape[0], part), qkv_w.dtype),
        ],
        scratch_shapes=Spread.semaphores(shards)
        + Gather.semaphores(shards)
        + [pltpu.SemaphoreType.DMA((n,)), pltpu.SemaphoreType.DMA((n,)), pltpu.SemaphoreType.DMA],
        compiler_params=pltpu.CompilerParams(
            collective_id=0, has_side_effects=True, vmem_limit_bytes=40 * MIB
        ),
        name="first",
    )(tokens, seg, qkv_w)


def inverse_rms(values):
    return lax.rsqrt(jnp.mean(values * values, axis=-1, keepdims=True) + epsilon)


def doc_positions(seg_ids):
    index = jnp.arange(seg_ids.shape[0], dtype=jnp.int32)
    fresh = (index == 0) | (seg_ids != jnp.roll(seg_ids, 1))
    begins = lax.cummax(jnp.where(fresh, index, jnp.zeros_like(index)), axis=0)
    return index - begins


def rope_tables(positions):
    freqs = rope_base ** (-(jnp.arange(HEAD // 2, dtype=F32) * (2.0 / HEAD)))
    angles = freqs[:, None] * positions.astype(F32)[None, :]
    return (jnp.cos(angles), jnp.sin(angles))


def rotate(values, cos_t, sin_t):
    shaped = values.reshape(-1, 2, HEAD // 2, values.shape[1])
    first, second = shaped[:, 0], shaped[:, 1]
    turned = jnp.stack(
        [first * cos_t - second * sin_t, second * cos_t + first * sin_t], axis=1
    )
    return turned.reshape(values.shape)


def side_by_side(ref, start):
    return jnp.concatenate(
        [ref[h * HEAD : (h + 1) * HEAD, pl.ds(start, TILE)] for h in range(GROUP)], axis=1
    )


def block_bias(seg_col_ref, seg_row_ref, key_at, query_at):
    same = seg_col_ref[pl.ds(key_at, TILE), :] == seg_row_ref[:, pl.ds(query_at, TILE)]
    key_index = key_at + lax.broadcasted_iota(jnp.int32, (TILE, TILE), 0)
    query_index = query_at + lax.broadcasted_iota(jnp.int32, (TILE, TILE), 1)
    bias = jnp.where(same & (key_index <= query_index), 0.0, NEG).astype(F32)
    return jnp.concatenate([bias] * GROUP, axis=1)


def attend_kernel(
    shards, ffn_part, seg_col, seg_row, q_ref, k_ref, v_ref, cot, proj_w, gate_w, up_w,
    out_ref, lse_ref, cot_all, proj_m, gate_m, up_m, *sems,
):
    block = pl.program_id(1)
    at = pl.program_id(0) * pl.num_programs(1) + block
    steps = pl.num_programs(0) * pl.num_programs(1)
    rep, me = place()
    gate = Spread(shards, gate_w, gate_m, column_block(ffn_part), *sems[:3])
    up = Spread(shards, up_w, up_m, column_block(ffn_part), *sems[3:6])
    proj = Spread(shards, proj_w, proj_m, None, *sems[6:9])
    cots = Gather(shards, cot, cot_all, *sems[9:12])

    @pl.when(at == 0)
    def _():
        greet(plane_partners(rep, me, shards) + pair_partners(rep, me))
        proj.start()
        gate.start()
        up.start()
        cots.start()

    query_at = pl.multiple_of(block * TILE, TILE)
    queries = side_by_side(q_ref, query_at)
    wide = GROUP * TILE

    def step(c, carry):
        top, total, acc = carry
        key_at = pl.multiple_of(c * TILE, TILE)
        scores = dot(k_ref[0, pl.ds(key_at, TILE), :], queries, NN)
        scores = scores + block_bias(seg_col, seg_row, key_at, query_at)
        new_top = jnp.maximum(top, jnp.max(scores, axis=0, keepdims=True))
        expo = jnp.exp(scores - new_top)
        fade = jnp.exp(top - new_top)
        total = total * fade + jnp.sum(expo, axis=0, keepdims=True)
        acc = acc * fade + dot(v_ref[:, pl.ds(key_at, TILE)], expo.astype(BF16), NN)
        return new_top, total, acc

    start = (
        jnp.full((1, wide), NEG, F32),
        jnp.zeros((1, wide), F32),
        jnp.zeros((HEAD, wide), F32),
    )
    carry = step(block, start)
    top, total, acc = lax.fori_loop(0, block, step, carry)
    mixed = (acc / total).astype(BF16)
    lse = top + jnp.log(total)
    for h in range(GROUP):
        out_ref[h * HEAD : (h + 1) * HEAD, :] = mixed[:, h * TILE : (h + 1) * TILE]
        lse_ref[0, h : h + 1, :] = lse[:, h * TILE : (h + 1) * TILE]

    @pl.when(at == steps // 2)
    def _():
        proj.hand_on()

    @pl.when(at == steps - 1)
    def _():
        gate.hand_on()
        proj.hand_on_last()
        up.hand_on()
        cots.hand_on()
        gate.hand_on_last()
        up.hand_on_last()
        for transfer in (proj, gate, up, cots):
            transfer.finish()


def attend(q_t, k, v_t, seg, cot, proj_w, gate_w, up_w, shards):
    kv_heads, length, _ = k.shape
    blocks = length // TILE
    rows = GROUP * HEAD
    width = cot.shape[1]
    part = gate_w.shape[1] // shards
    return pl.pallas_call(
        functools.partial(attend_kernel, shards, part),
        grid=(kv_heads, blocks),
        in_specs=[
            pl.BlockSpec((length, 1), lambda g, n: (0, 0)),
            pl.BlockSpec((1, length), lambda g, n: (0, 0)),
            pl.BlockSpec((rows, length), lambda g, n: (g, 0)),
            pl.BlockSpec((1, length, HEAD), lambda g, n: (g, 0, 0)),
            pl.BlockSpec((HEAD, length), lambda g, n: (g, 0)),
        ]
        + [ANY] * 4,
        out_specs=[
            pl.BlockSpec((rows, TILE), lambda g, n: (g, n)),
            pl.BlockSpec((1, GROUP, TILE), lambda g, n: (g, 0, n)),
        ]
        + [ANY] * 4,
        out_shape=[
            jax.ShapeDtypeStruct(q_t.shape, BF16),
            jax.ShapeDtypeStruct((kv_heads, GROUP, length), F32),
            jax.ShapeDtypeStruct((length, width), BF16),
            jax.ShapeDtypeStruct((shards * proj_w.shape[0], width), BF16),
            jax.ShapeDtypeStruct((width, part), BF16),
            jax.ShapeDtypeStruct((width, part), BF16),
        ],
        scratch_shapes=3 * Spread.semaphores(shards) + Gather.semaphores(shards),
        compiler_params=pltpu.CompilerParams(
            collective_id=1, has_side_effects=True, vmem_limit_bytes=40 * MIB
        ),
        name="attend",
    )(seg[:, None], seg[None, :], q_t, k, v_t, cot, proj_w, gate_w, up_w)


def hidden_kernel(
    shards, mixed_t, proj_m, tokens, gain, hidden_ref, rms_ref, normed_all,
    mixed_own, normed, mix_send, mix_recv, gather_send, gather_recv, local_sem,
):
    rep, me = place()
    part, _ = mixed_t.shape
    count = tokens.shape[0]
    greet(plane_partners(rep, me, shards))

    def columns(shard):
        return mixed_t.at[:, pl.ds(pl.multiple_of(shard * count, count), count)]

    copies = [
        remote(columns(me ^ (i + 1)), mixed_own.at[i], mix_send, mix_recv, i, rep, me ^ (i + 1))
        for i in range(shards - 1)
    ]
    for copy in copies:
        copy.start()

    def product(block, shard):
        rows = proj_m[pl.ds(pl.multiple_of(shard * part, part), part), :]
        return dot(block, rows, TN)

    hidden_ref[...] = tokens[...].astype(F32) + product(
        mixed_t[:, pl.ds(pl.multiple_of(me * count, count), count)], me
    )
    for i, copy in enumerate(copies):
        copy.wait_recv()
        hidden_ref[...] += product(mixed_own[i], me ^ (i + 1))
    hidden = hidden_ref[...]
    rms = lax.rsqrt(jnp.mean(hidden * hidden, axis=-1, keepdims=True) + epsilon)
    rms_ref[...] = rms
    normed[...] = (hidden * rms * gain[...]).astype(BF16)
    gather = Gather(shards, normed, normed_all, gather_send, gather_recv, local_sem)
    gather.start()
    for copy in copies:
        copy.wait_send()
    gather.hand_on()
    gather.finish()


def hidden_layer(mixed_t, proj_m, tokens, gain, shards):
    part, length = mixed_t.shape
    count, width = tokens.shape
    n = shards - 1
    return pl.pallas_call(
        functools.partial(hidden_kernel, shards),
        in_specs=[IN_VMEM] * 4,
        out_specs=[IN_VMEM, IN_VMEM, ANY],
        out_shape=[
            jax.ShapeDtypeStruct((count, width), F32),
            jax.ShapeDtypeStruct((count, 1), F32),
            jax.ShapeDtypeStruct((length, width), BF16),
        ],
        scratch_shapes=[
            pltpu.VMEM((n, part, count), BF16),
            pltpu.VMEM((count, width), BF16),
            pltpu.SemaphoreType.DMA((n,)),
            pltpu.SemaphoreType.DMA((n,)),
        ]
        + Gather.semaphores(shards),
        compiler_params=pltpu.CompilerParams(
            collective_id=2, has_side_effects=True, vmem_limit_bytes=40 * MIB
        ),
        name="hidden",
    )(mixed_t, proj_m, tokens, gain[None, :])


def ffn_kernel(x_ref, cot_ref, gate_w, up_w, down_w, activ_ref, dgate_ref, dup_ref):
    def rows_of(m, _):
        here = pl.ds(pl.multiple_of(m * 256, 256), 256)
        x = x_ref[here, :]
        gate = dot(x, gate_w[...], NN)
        up = dot(x, up_w[...], NN)
        grad_activ = dot(cot_ref[here, :], down_w[...], NT)
        sigm = jax.nn.sigmoid(gate)
        swish = gate * sigm
        activ_ref[here, :] = (swish * up).astype(BF16)
        dup_ref[here, :] = (grad_activ * swish).astype(BF16)
        dgate_ref[here, :] = (
            grad_activ * up * sigm * (1.0 + gate * (1.0 - sigm))
        ).astype(BF16)
        return 0

    lax.fori_loop(0, x_ref.shape[0] // 256, rows_of, 0)


def ffn(x, cot, gate_w, up_w, down_w):
    length, width = x.shape
    part = gate_w.shape[1]
    tile = 256
    whole = pl.BlockSpec((length, width), lambda n: (0, 0))
    out = pl.BlockSpec((length, tile), lambda n: (0, n))
    return pl.pallas_call(
        ffn_kernel,
        grid=(part // tile,),
        in_specs=[
            whole,
            whole,
            pl.BlockSpec((width, tile), lambda n: (0, n)),
            pl.BlockSpec((width, tile), lambda n: (0, n)),
            pl.BlockSpec((tile, width), lambda n: (n, 0)),
        ],
        out_specs=[out] * 3,
        out_shape=[jax.ShapeDtypeStruct((length, part), BF16)] * 3,
        compiler_params=pltpu.CompilerParams(vmem_limit_bytes=56 * MIB),
        cost_estimate=pl.CostEstimate(
            flops=6 * length * width * part,
            bytes_accessed=2 * (2 * length * width + 3 * width * part + 3 * length * part),
            transcendentals=length * part,
        ),
        name="ffn",
    )(x, cot, gate_w, up_w, down_w)


def split_rows(ref, index, size):
    return ref.at[pl.ds(pl.multiple_of(index * size, size), size), :]


class Plan:
    def __init__(self, shards, reps, length, width, ffn_part, q_part, kv_part):
        self.shards, self.reps, self.length, self.width = shards, reps, length, width
        self.ffn_part, self.q_part, self.kv_part = ffn_part, q_part, kv_part
        self.layers = reps // 2
        self.half = self.layers // 2
        self.rows = width // 2
        self.own = width // shards
        self.block = self.own // 2
        self.proj_half = q_part // 2
        self.proj_blocks = self.rows // self.proj_half
        counts = [
            width // TILE, ffn_part // TILE, ffn_part // TILE,
            width // TILE // self.proj_blocks, q_part // TILE, 1,
        ]
        self.starts = [sum(counts[:i]) for i in range(7)]
        self.chunks = self.starts[6]
        lag = 1
        self.lag = lag
        self.meet = 1 + lag * self.half
        self.spread = 1 + lag * (self.layers - 1)
        self.hand = self.spread + lag
        self.slots = self.chunks + self.hand + 1
        self.mine_ring = 2 + lag * (self.half - 1)
        self.sum_ring = lag + 2


KEPT, CAME = 0, 1


def backward_kernel(
    plan, activ, dgate, dup, x, cot_all, back_part, res_part, hidden, cot, tokens, proj_w,
    qkv_m, normed,
    mlp_rms, mlp_gain, attn_gain, seg_col, seg_row, cos_ref, sin_ref, lse_ref, q_ref, mixed_ref,
    k_ref, kt_ref, v_ref,
    f_down, f_gate, f_up, f_proj, f_q, f_kv, result_ref, tokens_out, gains_out,
    swapped, from_outer, from_middle, totals, back_land, res_land, norm_land, norm_part,
    left_a, left_b, right, proj_v, qkv_v, hidden_v, cot_v, tokens_v, row_sum, land_v,
    mine, theirs, swap_v, outer_v, middle_v, sums, total_v,
    grad_hidden, gh_own, gh_all, g_t, back_t, dk_acc, dv_acc,
    gain_part, gain_land, gain_sum, gain_reps,
    load_sem, right_sem, small_sem, swap_send, swap_recv, in_send, outer_recv, middle_recv,
    out_send, total_recv, total_store, cross_recv, cross_send, keep_sem, pass_send, pass_recv,
    back_send, back_recv, res_send, res_recv, norm_send, norm_recv,
    gather_send, gather_recv, gather_local, gain_send, gain_recv, rep_send, rep_recv,
):
    p = plan
    shards, reps, n = p.shards, p.reps, p.shards - 1
    rep, me = place()
    core, layer = rep % 2, rep // 2
    upper = layer >= p.half
    depth = jnp.where(upper, p.layers - 1 - layer, layer)
    inward = jnp.where(upper, rep - 2, rep + 2)
    outward = jnp.where(upper, rep + 2, rep - 2)
    is_middle = depth == p.half - 1
    count = cot.shape[0]
    down_at, gate_at, up_at, proj_at, q_at, kv_at, end_at = p.starts
    half_rows = p.ffn_part // 2

    greet(plane_partners(rep, me, shards) + [(rep ^ i, me) for i in range(1, reps)])

    def load(src, dst, i):
        return pltpu.make_async_copy(src, dst, load_sem.at[i])

    load_activ = load(activ, left_a.at[:, pl.ds(0, p.ffn_part)], 0)
    load_x = load(x, left_b, 1)
    load_normed = load(normed, left_a.at[:, pl.ds(0, p.width)], 2)
    load_proj = load(proj_w, proj_v, 3)
    load_qkv = load(qkv_m, qkv_v, 4)
    load_hidden = load(hidden, hidden_v, 5)
    load_cot = load(cot, cot_v, 6)
    load_tokens = load(tokens, tokens_v, 7)

    def load_right(t):
        slot = right.at[t % 2]

        def copies(action):
            def tile(ref, first):
                at = pl.ds(pl.multiple_of((t - first) * TILE, TILE), TILE)
                return pltpu.make_async_copy(ref.at[:, at], slot, right_sem.at[t % 2])

            @pl.when(t < gate_at)
            def _():
                action(tile(cot_all, down_at))

            @pl.when((t >= gate_at) & (t < up_at))
            def _():
                action(tile(dgate, gate_at))

            @pl.when((t >= up_at) & (t < proj_at))
            def _():
                action(tile(dup, up_at))

        return copies

    def scatter(part, land, sends, recvs):
        return [
            remote(split_rows(part, me ^ (i + 1), count), land.at[i], sends, recvs, i, rep, me ^ (i + 1))
            for i in range(n)
        ]

    back_rows = scatter(back_part, back_land, back_send, back_recv)
    res_rows = scatter(res_part, res_land, res_send, res_recv)
    norm_rows = scatter(norm_part, norm_land, norm_send, norm_recv)

    def fetch_rows(copies, part, land):
        for copy in copies:
            copy.wait_recv()
        pieces = [split_rows(part, me, count)] + [land.at[i] for i in range(n)]
        loads = [
            pltpu.make_async_copy(piece, land_v.at[i % 2], small_sem.at[i % 2])
            for i, piece in enumerate(pieces)
        ]
        loads[0].start()
        for i, piece in enumerate(loads):
            if i + 1 < len(loads):
                loads[i + 1].start()
            piece.wait()

            def strip(here, i=i):
                value = land_v[i % 2, here, :].astype(F32)
                row_sum[here, :] = value if i == 0 else row_sum[here, :] + value

            strips(strip)

    STRIP = 32

    def strips(body):
        def go(i, carry):
            body(pl.ds(pl.multiple_of(i * STRIP, STRIP), STRIP))
            return carry

        lax.fori_loop(0, count // STRIP, go, 0)

    def norm_strip(here, values, rms, gain, row):
        grad_in = row_sum[here, :]
        weighted = grad_in * gain
        inner = jnp.mean(weighted * values, axis=-1, keepdims=True)
        gain_part[row : row + 1, :] += jnp.sum(grad_in * values * rms, axis=0, keepdims=True)
        return rms * weighted - values * (rms * rms * rms) * inner

    gather = Gather(shards, gh_own, gh_all, gather_send, gather_recv, gather_local)

    def hidden_back():
        load_hidden.wait()
        load_cot.wait()
        fetch_rows(back_rows, back_part, back_land)
        gain_part[...] = jnp.zeros_like(gain_part)

        def strip(here):
            grad = cot_v[here, :].astype(F32) + norm_strip(
                here, hidden_v[here, :], mlp_rms[here, :], mlp_gain[...], 1
            )
            grad_hidden[here, :] = grad
            gh_own[here, :] = grad.astype(BF16)

        strips(strip)
        gather.start()

    def finish_result():
        fetch_rows(res_rows, res_part, res_land)

        def strip(here):
            result_ref[here, :] = hidden_v[here, :] + row_sum[here, :]

        strips(strip)

    def mixed_back():
        gather.finish()
        load_proj.wait()

        def go(i, carry):
            here = pl.ds(pl.multiple_of(i * TILE, TILE), TILE)
            g_t[:, here] = dot(proj_v[...], gh_all[here, :], NT).astype(BF16)
            return carry

        lax.fori_loop(0, p.length // TILE, go, 0)

    blocks = p.length // TILE
    rows = GROUP * HEAD
    wide = GROUP * TILE
    mid = HEAD // 2

    def attention_unit(unit):
        g, block = unit // blocks, unit % blocks
        query_at = pl.multiple_of(block * TILE, TILE)
        here_q = pl.ds(query_at, TILE)

        def beside(ref):
            return jnp.concatenate(
                [
                    ref[pl.ds(pl.multiple_of(g * rows + h * HEAD, HEAD), HEAD), here_q]
                    for h in range(GROUP)
                ],
                axis=1,
            )

        queries, grads, mixed = beside(q_ref), beside(g_t), beside(mixed_ref)
        lse = jnp.concatenate([lse_ref[g, h : h + 1, here_q] for h in range(GROUP)], axis=1)
        inner = jnp.sum(grads.astype(F32) * mixed.astype(F32), axis=0, keepdims=True)

        @pl.when(block == 0)
        def _():
            dk_acc[...] = jnp.zeros_like(dk_acc)
            dv_acc[...] = jnp.zeros_like(dv_acc)

        def step(c, acc):
            key_at = pl.multiple_of(c * TILE, TILE)
            here = pl.ds(key_at, TILE)
            scores = dot(k_ref[g, here, :], queries, NN)
            scores = scores + block_bias(seg_col, seg_row, key_at, query_at)
            probs = jnp.exp(scores - lse)
            grad_probs = dot(v_ref[g, here, :], grads, NN)
            grad_scores = (probs * (grad_probs - inner)).astype(BF16)
            dv_acc[:, here] += dot(grads, probs.astype(BF16), NT)
            dk_acc[:, here] += dot(queries, grad_scores, NT)
            key_rows = pl.ds(pl.multiple_of(g * HEAD, HEAD), HEAD)
            return acc + dot(kt_ref[key_rows, here], grad_scores, NN)

        acc = lax.fori_loop(0, block + 1, step, jnp.zeros((HEAD, wide), F32))
        cos, sin = cos_ref[:, here_q], sin_ref[:, here_q]
        for h in range(GROUP):
            grad = acc[:, h * TILE : (h + 1) * TILE] * SCALE
            first, second = grad[:mid], grad[mid:]
            at = pl.multiple_of(g * rows + h * HEAD, HEAD)
            back_t[pl.ds(at, mid), here_q] = (first * cos + second * sin).astype(BF16)
            back_t[pl.ds(at + mid, mid), here_q] = (second * cos - first * sin).astype(BF16)

        @pl.when(block == blocks - 1)
        def _():
            cos, sin = cos_ref[...], sin_ref[...]
            first, second = dk_acc[:mid, :], dk_acc[mid:, :]
            at = pl.multiple_of(p.q_part + g * HEAD, HEAD)
            back_t[pl.ds(at, mid), :] = (first * cos + second * sin).astype(BF16)
            back_t[pl.ds(at + mid, mid), :] = (second * cos - first * sin).astype(BF16)
            at = pl.multiple_of(p.q_part + p.kv_part + g * HEAD, HEAD)
            back_t[pl.ds(at, HEAD), :] = dv_acc[...].astype(BF16)

    def normed_back():
        load_qkv.wait()

        stores = [
            pltpu.make_async_copy(
                land_v.at[i % 2], norm_part.at[pl.ds(i * count, count), :], small_sem.at[i % 2]
            )
            for i in range(shards)
        ]
        for i, store in enumerate(stores):
            if i >= 2:
                stores[i - 2].wait()
            here = pl.ds(i * count, count)
            land_v[i % 2] = dot(back_t[:, here].T, qkv_v[...], NT).astype(BF16)
            store.start()
        for store in stores[-2:]:
            store.wait()
        for copy in norm_rows:
            copy.start()

    gain_cols = p.width // shards

    def gain_slice(shard):
        return pl.ds(pl.multiple_of(shard * gain_cols, gain_cols), gain_cols)

    gain_plane = [
        remote(
            gain_part.at[:, gain_slice(me ^ (i + 1))], gain_land.at[me],
            gain_send, gain_recv, i, rep, me ^ (i + 1),
        )
        for i in range(n)
    ]
    gain_all = [
        remote(gain_sum, gain_reps.at[rep], rep_send, rep_recv, i, rep ^ (i + 1), me)
        for i in range(reps - 1)
    ]

    def tokens_back():
        load_tokens.wait()
        fetch_rows(norm_rows, norm_part, norm_land)

        def strip(here):
            values = tokens_v[here, :].astype(F32)
            rms = lax.rsqrt(jnp.mean(values * values, axis=-1, keepdims=True) + epsilon)
            tokens_out[here, :] = grad_hidden[here, :] + norm_strip(
                here, values, rms, attn_gain[...], 0
            )

        strips(strip)
        gain_land[me] = gain_part[:, gain_slice(me)]
        for copy in gain_plane:
            copy.start()

    def gains_plane():
        for copy in gain_plane:
            copy.wait_recv()
        total = gain_land[0]
        for s in range(1, shards):
            total = total + gain_land[s]
        gain_sum[...] = total
        gain_reps[rep] = total
        for copy in gain_all:
            copy.start()

    def gains_reps():
        for copy in gain_all:
            copy.wait_recv()
        total = gain_reps[0]
        for r in range(1, reps):
            total = total + gain_reps[r]
        gains_out[...] = total

    def swap(j):
        return remote(theirs.at[j % 2], swapped.at[j], swap_send, swap_recv, 0, rep ^ 1, me)

    def swap_copy(j):
        return pltpu.make_async_remote_copy(
            src_ref=theirs.at[j % 2], dst_ref=swapped.at[j],
            send_sem=swap_send.at[j % 2], recv_sem=swap_recv.at[j],
            device_id=(rep ^ 1, me), device_id_type=MESH,
        )

    def store_chunk(slot, other_slot, at, size, product, columns=TILE):
        here = pl.ds(pl.multiple_of(at, size), size)
        mine[slot, here, :columns] = product(core).astype(BF16)
        theirs[other_slot, here, :columns] = product(1 - core).astype(BF16)

    def make(t):
        slot, other = t % p.mine_ring, t % 2

        @pl.when(t >= 2)
        def _():
            swap_copy(t - 2).wait_send()

        @pl.when(t < proj_at)
        def _():
            load_right(t)(lambda copy: copy.wait())

        @pl.when(t + 1 < proj_at)
        def _():
            load_right(t + 1)(lambda copy: copy.start())

        @pl.when(t < gate_at)
        def _():
            size = min(TILE, half_rows)

            def go(i, carry):
                def product(which):
                    at = pl.multiple_of(which * half_rows + i * size, size)
                    return dot(left_a[:, pl.ds(at, size)], right[t % 2], TN)

                store_chunk(slot, other, i * size, size, product)
                return carry

            lax.fori_loop(0, half_rows // size, go, 0)

        def wide_chunk(left, factor, columns):
            def go(s, carry):
                def product(which):
                    at = pl.multiple_of(s * p.own + which * p.block, p.block)
                    return dot(left[:, pl.ds(at, p.block)], factor(), TN)

                store_chunk(slot, other, s * p.block, p.block, product, columns)
                return carry

            lax.fori_loop(0, shards, go, 0)

        @pl.when((t >= gate_at) & (t < proj_at))
        def _():
            wide_chunk(left_b, lambda: right[t % 2], TILE)

        @pl.when((t >= proj_at) & (t < q_at))
        def _():
            def go(i, carry):
                at = pl.multiple_of(((t - proj_at) * p.proj_blocks + i) * TILE, TILE)

                def product(which):
                    part = pl.ds(pl.multiple_of(which * p.proj_half, p.proj_half), p.proj_half)
                    return dot(mixed_ref[part, :], gh_all[:, pl.ds(at, TILE)], NN)

                store_chunk(slot, other, i * p.proj_half, p.proj_half, product)
                return carry

            lax.fori_loop(0, p.proj_blocks, go, 0)

        @pl.when((t >= q_at) & (t < kv_at))
        def _():
            at = pl.multiple_of((t - q_at) * TILE, TILE)
            right[t % 2] = back_t[pl.ds(at, TILE), :].T
            wide_chunk(left_a, lambda: right[t % 2], TILE)

        @pl.when(t == kv_at)
        def _():
            columns = 2 * p.kv_part
            right[t % 2, :, :columns] = back_t[p.q_part :, :].T
            wide_chunk(left_a, lambda: right[t % 2, :, :columns], columns)

        swap_copy(t).start()

    def inward_copies(j):
        common = dict(
            src_ref=sums.at[j % p.sum_ring], send_sem=in_send.at[j % p.sum_ring],
            device_id=(inward, me), device_id_type=MESH,
        )
        to_layer = pltpu.make_async_remote_copy(
            dst_ref=from_outer.at[j], recv_sem=outer_recv.at[j], **common
        )
        to_middle = pltpu.make_async_remote_copy(
            dst_ref=from_middle.at[j], recv_sem=middle_recv.at[j], **common
        )
        return to_layer, to_middle

    def outward_copy(src, j):
        return pltpu.make_async_remote_copy(
            src_ref=src, dst_ref=totals.at[j], send_sem=out_send.at[j % 2],
            recv_sem=total_recv.at[j], device_id=(outward, me), device_id_type=MESH,
        )

    def add_rows(body):
        def go(i, carry):
            body(pl.ds(pl.multiple_of(i * TILE, TILE), TILE))
            return carry

        lax.fori_loop(0, p.rows // TILE, go, 0)

    def send_inward(j):
        @pl.when((j >= 0) & (j < p.chunks))
        def _():
            swap_copy(j).wait_recv()
            first = pltpu.make_async_copy(swapped.at[j], swap_v, small_sem.at[2])
            second = pltpu.make_async_copy(from_outer.at[j], outer_v, small_sem.at[3])
            first.start()

            @pl.when(depth > 0)
            def _():
                inward_copies(j)[0].wait_recv()
                second.start()

            @pl.when(j >= p.sum_ring)
            def _():
                inward_copies(j - p.sum_ring)[0].wait_send()

            first.wait()
            ours = mine.at[j % p.mine_ring]
            total = sums.at[j % p.sum_ring]

            @pl.when(depth > 0)
            def _():
                second.wait()

                def add(here):
                    total[here, :] = (
                        ours[here, :].astype(F32)
                        + swap_v[here, :].astype(F32)
                        + outer_v[here, :].astype(F32)
                    ).astype(BF16)

                add_rows(add)

            @pl.when(depth == 0)
            def _():
                def add(here):
                    total[here, :] = (
                        ours[here, :].astype(F32) + swap_v[here, :].astype(F32)
                    ).astype(BF16)

                add_rows(add)

            to_layer, to_middle = inward_copies(j)

            @pl.when(is_middle)
            def _():
                to_middle.start()

            @pl.when(jnp.logical_not(is_middle))
            def _():
                to_layer.start()

    def store_total(j):
        return pltpu.make_async_copy(total_v.at[j % 2], totals.at[j], total_store.at[j % 2])

    def meet_in_middle(j):
        @pl.when(is_middle & (j >= 0) & (j < p.chunks))
        def _():
            inward_copies(j)[1].wait_recv()
            fetch = pltpu.make_async_copy(from_middle.at[j], middle_v, small_sem.at[4])
            fetch.start()

            if p.half > 1:

                @pl.when(j >= 2)
                def _():
                    outward_copy(total_v.at[j % 2], j - 2).wait_send()

            fetch.wait()
            out, held = total_v.at[j % 2], sums.at[j % p.sum_ring]

            def add(here):
                out[here, :] = (
                    held[here, :].astype(F32) + middle_v[here, :].astype(F32)
                ).astype(BF16)

            add_rows(add)
            if p.half > 1:
                outward_copy(out, j).start()
            store_total(j).start()
            store_total(j).wait()

    def send_outward(j):
        @pl.when(jnp.logical_not(is_middle) & (j >= 0) & (j < p.chunks))
        def _():
            outward_copy(totals.at[j], j).wait_recv()

            @pl.when(depth > 0)
            def _():
                @pl.when(j >= 2)
                def _():
                    outward_copy(totals.at[j], j - 2).wait_send()

                outward_copy(totals.at[j], j).start()

    def put_down(blocks_of, sem):
        for src, dst in blocks_of:
            pltpu.make_async_copy(src, dst, keep_sem.at[sem]).start()
            remote_pass(src, dst, sem).start()

    def remote_pass(src, dst, sem):
        return pltpu.make_async_remote_copy(
            src_ref=src, dst_ref=dst, send_sem=pass_send.at[sem], recv_sem=pass_recv.at[sem],
            device_id=(rep ^ 1, me), device_id_type=MESH,
        )

    def window(full, shard, part, tile, columns=TILE):
        at = pl.multiple_of(shard * part + tile * columns, columns)
        return full.at[pl.ds(pl.multiple_of(core * p.block, p.block), p.block), pl.ds(at, columns)]

    WIDE = (
        (gate_at, up_at, f_gate, p.ffn_part, 1, TILE),
        (up_at, proj_at, f_up, p.ffn_part, 2, TILE),
        (q_at, kv_at, f_q, p.q_part, 4, TILE),
        (kv_at, end_at, f_kv, 2 * p.kv_part, 5, 2 * p.kv_part),
    )

    def spread_total(j):
        @pl.when((j >= 0) & (j < gate_at))
        def _():
            at = pl.ds(pl.multiple_of(j * TILE, TILE), TILE)
            here = pl.ds(pl.multiple_of(core * half_rows, half_rows), half_rows)
            put_down([(totals.at[j, pl.ds(0, half_rows), :], f_down.at[here, at])], 0)

        @pl.when((j >= proj_at) & (j < q_at))
        def _():
            here = pl.ds(pl.multiple_of(core * p.proj_half, p.proj_half), p.proj_half)
            pairs = []
            for i in range(p.proj_blocks):
                at = pl.multiple_of(((j - proj_at) * p.proj_blocks + i) * TILE, TILE)
                src = totals.at[j, pl.ds(i * p.proj_half, p.proj_half), :]
                pairs.append((src, f_proj.at[here, pl.ds(at, TILE)]))
            put_down(pairs, 3)

        for first, last, full, part, sem, columns in WIDE:

            @pl.when((j >= first) & (j < last))
            def _():
                def block(shard):
                    at = pl.ds(pl.multiple_of(shard * p.block, p.block), p.block)
                    return totals.at[j, at, pl.ds(0, columns)]

                place_here = window(full, me, part, j - first, columns)
                for i in range(n):
                    pltpu.make_async_remote_copy(
                        src_ref=block(me ^ (i + 1)), dst_ref=place_here,
                        send_sem=cross_send.at[sem], recv_sem=cross_recv.at[j],
                        device_id=(rep, me ^ (i + 1)), device_id_type=MESH,
                    ).start()
                put_down([(block(me), place_here)], sem)

    def pass_on(j):
        for first, last, full, part, sem, columns in WIDE:

            @pl.when((j >= first) & (j < last))
            def _():
                came = totals.at[j, pl.ds(0, n * p.block), pl.ds(0, columns)]
                pltpu.make_async_copy(came, came, cross_recv.at[j]).wait()
                for i in range(n):
                    here = window(full, me ^ (i + 1), part, j - first, columns)
                    remote_pass(here, here, sem).start()

    load_activ.start()
    load_right(0)(lambda copy: copy.start())
    for copy in back_rows:
        copy.start()
    for copy in (load_x, load_hidden, load_cot, load_proj, load_qkv, load_tokens):
        copy.start()
    load_activ.wait()

    units = (p.length // TILE) * (p.kv_part // HEAD)
    rows_slot, pass_slot, mixed_slot = 4, 6, 8
    unit_slot = mixed_slot + 1
    per_slot = 2
    last_unit_slot = unit_slot + (units + per_slot - 1) // per_slot
    result_slot = last_unit_slot
    norm_slot = last_unit_slot
    tokens_slot = norm_slot + 5
    gain_slot = tokens_slot + 1
    rep_slot = gain_slot + 1
    assert proj_at > mixed_slot and q_at > norm_slot and rep_slot < p.slots

    def slot(t, carry):
        send_inward(t - 1 - p.lag * depth)
        meet_in_middle(t - p.meet)
        send_outward(t - p.spread + p.lag * depth)
        spread_total(t - p.spread)
        pass_on(t - p.hand)

        @pl.when(t == gate_at)
        def _():
            load_x.wait()
            load_normed.start()

        @pl.when(t == q_at)
        def _():
            load_normed.wait()

        @pl.when(t < p.chunks)
        def _():
            make(t)

        def at(when, action):
            @pl.when(t == when)
            def _():
                action()

        at(rows_slot, hidden_back)
        at(pass_slot, gather.hand_on)
        at(mixed_slot, mixed_back)

        @pl.when((t >= unit_slot) & (t < last_unit_slot))
        def _():
            def go(i, c):
                attention_unit((t - unit_slot) * per_slot + i)
                return c

            lax.fori_loop(0, per_slot, go, 0)

        def start_result():
            for copy in res_rows:
                copy.start()

        at(unit_slot, start_result)
        at(result_slot, finish_result)
        at(norm_slot, normed_back)
        at(tokens_slot, tokens_back)
        at(gain_slot, gains_plane)
        at(rep_slot, gains_reps)
        return carry

    lax.fori_loop(0, p.slots, slot, 0)

    for j in range(max(0, p.chunks - 2), p.chunks):
        swap_copy(j).wait_send()
    for j in range(max(0, p.chunks - p.sum_ring), p.chunks):
        inward_copies(j)[0].wait_send()
    if p.half > 1:

        @pl.when(depth > 0)
        def _():
            for j in range(max(0, p.chunks - 2), p.chunks):
                outward_copy(total_v.at[j % 2], j).wait_send()

    for copies in (back_rows, res_rows, norm_rows, gain_plane, gain_all):
        for copy in copies:
            copy.wait_send()

    def settle(ref, sem):
        pltpu.make_async_copy(ref, ref, sem).wait()

    for sem, full in ((0, f_down), (3, f_proj)):
        part = full.at[pl.ds(0, full.shape[0] // 2), :]
        settle(part, keep_sem.at[sem])
        settle(part, pass_send.at[sem])
        settle(part, pass_recv.at[sem])
    for _, _, full, part, sem, _ in WIDE:
        here = full.at[pl.ds(0, p.block), :]
        settle(here, pass_send.at[sem])
        settle(here, pass_recv.at[sem])
        settle(full.at[pl.ds(0, p.block), pl.ds(0, part)], keep_sem.at[sem])
        settle(full.at[pl.ds(0, p.block), pl.ds(0, n * part)], cross_send.at[sem])


def backward(
    shards, reps, activ, dgate, dup, x, cot_all, back_part, res_part, hidden, cot, tokens, proj_w,
    qkv_m, normed, mlp_rms, mlp_gain, attn_gain, seg, cos_t, sin_t, lse, q_t, mixed_t, k, k_t, v,
):
    length, width = x.shape
    count = cot.shape[0]
    ffn_part = activ.shape[1]
    q_part, kv_part = q_t.shape[0], k_t.shape[0]
    n = shards - 1
    p = Plan(shards, reps, length, width, ffn_part, q_part, kv_part)
    shape = jax.ShapeDtypeStruct
    own = width // shards
    chunk = (p.rows, TILE)
    dma = pltpu.SemaphoreType.DMA
    lefts = max(ffn_part, width)
    return pl.pallas_call(
        functools.partial(backward_kernel, p),
        in_specs=[ANY] * 13 + [IN_VMEM] * 13,
        out_specs=[ANY] * 6 + [IN_VMEM] * 3 + [ANY] * 8,
        out_shape=[
            shape((ffn_part, width), BF16),
            shape((own, shards * ffn_part), BF16),
            shape((own, shards * ffn_part), BF16),
            shape((q_part, width), BF16),
            shape((own, shards * q_part), BF16),
            shape((own, shards * 2 * kv_part), BF16),
            shape((count, width), F32),
            shape((count, width), F32),
            shape((8, width // shards), F32),
        ]
        + [shape((p.chunks,) + chunk, BF16)] * 4
        + [shape((n, count, width), BF16)] * 3
        + [shape((length, width), BF16)],
        scratch_shapes=[
            pltpu.VMEM((length, lefts), BF16),
            pltpu.VMEM((length, width), BF16),
            pltpu.VMEM((2, length, TILE), BF16),
            pltpu.VMEM(proj_w.shape, BF16),
            pltpu.VMEM(qkv_m.shape, BF16),
            pltpu.VMEM((count, width), F32),
            pltpu.VMEM((count, width), BF16),
            pltpu.VMEM((count, width), BF16),
            pltpu.VMEM((count, width), F32),
            pltpu.VMEM((2, count, width), BF16),
            pltpu.VMEM((p.mine_ring,) + chunk, BF16),
            pltpu.VMEM((2,) + chunk, BF16),
            pltpu.VMEM(chunk, BF16),
            pltpu.VMEM(chunk, BF16),
            pltpu.VMEM(chunk, BF16),
            pltpu.VMEM((p.sum_ring,) + chunk, BF16),
            pltpu.VMEM((2,) + chunk, BF16),
            pltpu.VMEM((count, width), F32),
            pltpu.VMEM((count, width), BF16),
            pltpu.VMEM((length, width), BF16),
            pltpu.VMEM((q_part, length), BF16),
            pltpu.VMEM((q_part + 2 * kv_part, length), BF16),
            pltpu.VMEM((HEAD, length), F32),
            pltpu.VMEM((HEAD, length), F32),
            pltpu.VMEM((8, width), F32),
            pltpu.VMEM((shards, 8, own), F32),
            pltpu.VMEM((8, own), F32),
            pltpu.VMEM((reps, 8, own), F32),
            dma((8,)), dma((2,)), dma((5,)), dma((2,)), dma((p.chunks,)), dma((p.sum_ring,)),
            dma((p.chunks,)), dma((p.chunks,)), dma((2,)), dma((p.chunks,)), dma((2,)),
            dma((p.chunks,)), dma((6,)), dma((6,)), dma((6,)), dma((6,)),
            dma((n,)), dma((n,)), dma((n,)), dma((n,)), dma((n,)), dma((n,)),
        ]
        + Gather.semaphores(shards)
        + [dma((n,)), dma((n,)), dma((reps - 1,)), dma((reps - 1,))],
        compiler_params=pltpu.CompilerParams(
            collective_id=3, has_side_effects=True, vmem_limit_bytes=62 * MIB
        ),
        name="backward",
    )(
        activ, dgate, dup, x, cot_all, back_part, res_part, hidden, cot, tokens, proj_w,
        qkv_m, normed, mlp_rms, mlp_gain[None, :], attn_gain[None, :], seg[:, None], seg[None, :],
        cos_t, sin_t, lse, q_t, mixed_t, k, k_t, v,
    )[:9]


def local(
    tokens, segments, query_w, key_w, value_w, proj_w, attn_gain,
    gate_w, up_w, down_w, mlp_gain, cotangent,
):
    shards = lax.axis_size("shard")
    reps = lax.axis_size("rep")
    tok_count, width = tokens.shape
    kv_part = key_w.shape[1] // shards
    q_part = query_w.shape[1] // shards
    length = tok_count * shards

    qkv_w = jnp.concatenate(
        [
            w[:, s * (w.shape[1] // shards) : (s + 1) * (w.shape[1] // shards)]
            for s in range(shards)
            for w in (query_w, key_w, value_w)
        ],
        axis=1,
    )
    tokens_all, seg, qkv_m = first(tokens, segments[None, :], qkv_w, shards)
    seg = seg.reshape(length)

    cos_t, sin_t = rope_tables(doc_positions(seg))
    inputs_all = tokens_all.astype(F32)
    normed = (inputs_all * inverse_rms(inputs_all) * attn_gain).astype(BF16)
    qkv_t = dot(qkv_m, normed, TT)
    q_t = (rotate(qkv_t[:q_part], cos_t, sin_t).astype(BF16).astype(F32) * SCALE).astype(BF16)
    k_t = rotate(qkv_t[q_part : q_part + kv_part], cos_t, sin_t).astype(BF16)
    v_t = qkv_t[q_part + kv_part :].astype(BF16)
    k = k_t.reshape(-1, HEAD, length).transpose(0, 2, 1)
    v = v_t.reshape(-1, HEAD, length).transpose(0, 2, 1)
    mixed_t, lse, cot_all, proj_m, gate_m, up_m = attend(
        q_t, k, v_t, seg, cotangent, proj_w, gate_w, up_w, shards
    )
    hidden, mlp_rms, normed_mlp = hidden_layer(mixed_t, proj_m, tokens, mlp_gain, shards)

    activ, dgate, dup = ffn(normed_mlp, cot_all, gate_m, up_m, down_w)
    back_part = (dot(dgate, gate_m, NT) + dot(dup, up_m, NT)).astype(BF16)
    res_part = dot(activ, down_w, NN).astype(BF16)
    down, gate, up, proj, query, kv, result, grad_tokens, gains = backward(
        shards, reps, activ, dgate, dup, normed_mlp, cot_all, back_part, res_part, hidden,
        cotangent, tokens, proj_w, qkv_m, normed, mlp_rms, mlp_gain, attn_gain, seg,
        cos_t, sin_t, lse, q_t, mixed_t, k, k_t, v,
    )

    def every_other(first):
        parts = [
            kv[:, (2 * s + first) * kv_part : (2 * s + first + 1) * kv_part] for s in range(shards)
        ]
        return jnp.concatenate(parts, axis=1).astype(F32)

    return (
        result, grad_tokens, query.astype(F32), every_other(0), every_other(1), proj.astype(F32),
        gains[0], gate.astype(F32), up.astype(F32), down.astype(F32), gains[1],
    )


def solution(mesh):
    rows = P(("rep", "shard"), None)
    held = P("shard", None)
    in_specs = (
        rows, P(("rep", "shard")), held, held, held, held, P(), held, held, held, P(), rows,
    )
    out_specs = (
        rows, rows, held, held, held, held, P("shard"), held, held, held, P("shard"),
    )
    return jax.shard_map(local, mesh=mesh, in_specs=in_specs, out_specs=out_specs, check_vma=False)
```

```python
import functools
import math

import jax
import jax.numpy as jnp
from jax import lax
from jax.experimental import pallas as pl
from jax.experimental.pallas import tpu as pltpu
from jax.sharding import PartitionSpec as P

HEADS = 32
KV_HEADS = 8
HEAD = 64
GROUP = HEADS // KV_HEADS
SCALE = 1.0 / math.sqrt(HEAD)
TILE = 256
NEG = -1e30
MIB = 1024 * 1024

epsilon = 1e-05
rope_base = 500000.0
F32 = jnp.float32
BF16 = jnp.bfloat16


def dot(left, right, dims):
    return lax.dot_general(left, right, (dims, ((), ())), preferred_element_type=F32)


NN = ((1,), (0,))
NT = ((1,), (1,))
TN = ((0,), (0,))
TT = ((0,), (1,))


MESH = pl.DeviceIdType.MESH


def place():
    return lax.axis_index("rep"), lax.axis_index("shard")


def remote(src, dst, sends, recvs, index, rep, shard):
    return pltpu.make_async_remote_copy(
        src_ref=src,
        dst_ref=dst,
        send_sem=sends.at[index],
        recv_sem=recvs.at[index],
        device_id=(rep, shard),
        device_id_type=MESH,
    )


def greet(partners):
    barrier = pltpu.get_barrier_semaphore()
    for partner in partners:
        pl.semaphore_signal(barrier, inc=1, device_id=partner, device_id_type=MESH)
    pl.semaphore_wait(barrier, len(partners))


def plane_partners(rep, me, shards):
    return [(rep, me ^ step) for step in range(1, shards)]


class Spread:
    def __init__(self, shards, own, full, columns, sends, recvs, held=None, held_sem=None):
        rep, me = place()
        quarter = rep % 4
        count = own.shape[0]
        part = count // 4
        own_rows = pl.ds(pl.multiple_of(quarter * part, part), part)

        def at(shard, which):
            return full.at[pl.ds(pl.multiple_of(shard * count + which * part, part), part), :]

        def piece(shard):
            return own.at[own_rows, :] if columns is None else own.at[own_rows, columns(shard)]

        self.first, self.core, self.layer, self.last = [], [], [], []
        n = shards - 1
        for i in range(n):
            peer = me ^ (i + 1)
            self.first.append(remote(piece(peer), at(me, quarter), sends, recvs, i, rep, peer))
            mine = at(peer, quarter)
            self.core.append(remote(mine, mine, sends, recvs, n + i, rep ^ 1, me))
            self.layer.append(remote(mine, mine, sends, recvs, 2 * n + i, rep ^ 2, me))
            theirs = at(peer, quarter ^ 2)
            self.last.append(remote(theirs, theirs, sends, recvs, 3 * n + i, rep ^ 1, me))
        self.take = self.keep = None
        if held is not None:
            kept = full.at[pl.ds(pl.multiple_of(me * count, count), count), :]
            self.take = pltpu.make_async_copy(own.at[:, columns(me)], held, held_sem.at[0])
            self.keep = pltpu.make_async_copy(held, kept, held_sem.at[1])

    def start(self):
        for copy in self.first:
            copy.start()
        if self.take is not None:
            self.take.start()

    def hand_on(self):
        if self.take is not None:
            self.take.wait()
            self.keep.start()
        for i, copy in enumerate(self.first):
            copy.wait_recv()
            self.layer[i].start()
            self.core[i].start()

    def hand_on_last(self):
        for i, copy in enumerate(self.layer):
            copy.wait_recv()
            self.last[i].start()

    def finish(self):
        for copy in self.core + self.last:
            copy.wait_recv()
        for copy in self.first + self.core + self.layer + self.last:
            copy.wait_send()
        if self.keep is not None:
            self.keep.wait()

    @staticmethod
    def semaphores(shards):
        n = 4 * (shards - 1)
        return [pltpu.SemaphoreType.DMA((n,)), pltpu.SemaphoreType.DMA((n,))]


class Gather:
    def __init__(self, shards, own, full, sends, recvs, local_sem=None):
        rep, me = place()
        count = own.shape[0]
        half = count // 2

        def at(shard, start, size):
            return full.at[pl.ds(pl.multiple_of(shard * count + start, half), size), :]

        self.direct, self.passed, self.kept = [], [], None
        if shards == 4:
            for i, (step, start) in enumerate(((1, 0), (2, half), (1, half), (2, 0))):
                self.direct.append(
                    remote(
                        own.at[pl.ds(start, half), :], at(me, start, half),
                        sends, recvs, i, rep, me ^ step,
                    )
                )
            for i, (step, start) in enumerate(((1, 0), (2, half))):
                came = at(me ^ step, start, half)
                self.passed.append(remote(came, came, sends, recvs, 4 + i, rep, me ^ step ^ 3))
        else:
            for i in range(shards - 1):
                self.direct.append(
                    remote(own, at(me, 0, count), sends, recvs, i, rep, me ^ (i + 1))
                )
        if local_sem is not None:
            self.kept = pltpu.make_async_copy(own, at(me, 0, count), local_sem)

    def start(self):
        for copy in self.direct:
            copy.start()
        if self.kept is not None:
            self.kept.start()

    def hand_on(self):
        for i, copy in enumerate(self.passed):
            self.direct[i].wait_recv()
            copy.start()

    def finish(self):
        for copy in self.direct[len(self.passed) :] + self.passed:
            copy.wait_recv()
        for copy in self.direct + self.passed:
            copy.wait_send()
        if self.kept is not None:
            self.kept.wait()

    @staticmethod
    def semaphores(shards):
        n = max(6, shards - 1)
        return [
            pltpu.SemaphoreType.DMA((n,)),
            pltpu.SemaphoreType.DMA((n,)),
            pltpu.SemaphoreType.DMA,
        ]


def split_rows(ref, index, size):
    return ref.at[pl.ds(pl.multiple_of(index * size, size), size), :]


def column_block(part):
    return lambda shard: pl.ds(pl.multiple_of(shard * part, part), part)


def pair_partners(rep, me):
    return [(rep ^ 1, me), (rep ^ 2, me)]


ANY = pl.BlockSpec(memory_space=pl.ANY)
IN_VMEM = pl.BlockSpec(memory_space=pltpu.VMEM)


def first_kernel(shards, parts, tokens, seg, *refs):
    rep, me = place()
    count = len(parts)
    weights, (tokens_all, seg_all, qkv_m, tokens_v) = refs[:count], refs[count : count + 4]
    held, held_sem, sems = refs[count + 4 : 2 * count + 4], refs[2 * count + 4], refs[2 * count + 5 :]
    take = pltpu.make_async_copy(tokens, tokens_v, held_sem.at[count, 0])
    take.start()
    greet(plane_partners(rep, me, shards) + pair_partners(rep, me))
    at, spreads = 0, []
    for weight, part, i in zip(weights, parts, range(count)):
        full = qkv_m.at[:, pl.ds(at, part)]
        spreads.append(
            Spread(
                shards, weight, full, column_block(part), *sems[2 * i : 2 * i + 2],
                held[i], held_sem.at[i],
            )
        )
        at += part
    sems = sems[2 * count :]
    rows = Gather(shards, tokens_v, tokens_all, *sems[:3])
    seg_send, seg_recv, seg_local = sems[3:]
    segs = [
        remote(seg, seg_all.at[me], seg_send, seg_recv, i, rep, me ^ (i + 1))
        for i in range(shards - 1)
    ]
    for spread in spreads:
        spread.start()
    for copy in segs:
        copy.start()
    take.wait()
    rows.start()
    own_seg = pltpu.make_async_copy(seg, seg_all.at[me], seg_local)
    own_seg.start()
    for spread in spreads:
        spread.hand_on()
    rows.hand_on()
    for spread in spreads:
        spread.hand_on_last()
    for spread in spreads:
        spread.finish()
    rows.finish()
    for copy in segs:
        copy.wait()
    own_seg.wait()


def first(tokens, seg, weights, shards):
    rows, width = tokens.shape
    parts = [w.shape[1] // shards for w in weights]
    n = shards - 1
    return pl.pallas_call(
        functools.partial(first_kernel, shards, parts),
        in_specs=[ANY] * (2 + len(weights)),
        out_specs=[ANY] * 3,
        out_shape=[
            jax.ShapeDtypeStruct((shards * rows, width), tokens.dtype),
            jax.ShapeDtypeStruct((shards,) + seg.shape, seg.dtype),
            jax.ShapeDtypeStruct((width, sum(parts)), BF16),
        ],
        scratch_shapes=[pltpu.VMEM(tokens.shape, BF16)]
        + [pltpu.VMEM((w.shape[0], part), BF16) for w, part in zip(weights, parts)]
        + [pltpu.SemaphoreType.DMA((len(weights) + 1, 2))]
        + len(weights) * Spread.semaphores(shards)
        + Gather.semaphores(shards)
        + [pltpu.SemaphoreType.DMA((n,)), pltpu.SemaphoreType.DMA((n,)), pltpu.SemaphoreType.DMA],
        compiler_params=pltpu.CompilerParams(
            collective_id=0, has_side_effects=True, vmem_limit_bytes=40 * MIB
        ),
        name="first",
    )(tokens, seg, *weights)


def doc_positions(seg_ids):
    index = jnp.arange(seg_ids.shape[0], dtype=jnp.int32)
    fresh = (index == 0) | (seg_ids != jnp.roll(seg_ids, 1))
    begins = lax.cummax(jnp.where(fresh, index, jnp.zeros_like(index)), axis=0)
    return index - begins


def rope_tables(positions):
    freqs = rope_base ** (-(jnp.arange(HEAD // 2, dtype=F32) * (2.0 / HEAD)))
    angles = freqs[:, None] * positions.astype(F32)[None, :]
    return (jnp.cos(angles), jnp.sin(angles))


def side_by_side(ref, group, here):
    rows = GROUP * HEAD
    return jnp.concatenate(
        [
            ref[pl.ds(pl.multiple_of(group * rows + h * HEAD, HEAD), HEAD), here]
            for h in range(GROUP)
        ],
        axis=1,
    )


def block_bias(seg_col_ref, seg_row_ref, key_at, query_at):
    same = seg_col_ref[pl.ds(key_at, TILE), :] == seg_row_ref[:, pl.ds(query_at, TILE)]
    key_index = key_at + lax.broadcasted_iota(jnp.int32, (TILE, TILE), 0)
    query_index = query_at + lax.broadcasted_iota(jnp.int32, (TILE, TILE), 1)
    bias = jnp.where(same & (key_index <= query_index), 0.0, NEG).astype(F32)
    return jnp.concatenate([bias] * GROUP, axis=1)


def attend_kernel(
    shards, ffn_part, early, tokens, qkv_m, cot, proj_w, gate_w, up_w, gain, seg_col, seg_row,
    cos_ref, sin_ref,
    normed_out, cot_all, proj_m, gate_m, up_m, q_ref, k_ref, kt_ref, v_ref, out_ref, lse_ref,
    tokens_v, normed_v, qkv_v, turned_v, vt_ref, cot_v, load_sem, store_sem, qkv_sem, *sems,
):
    rep, me = place()
    length, width = tokens.shape
    kv_heads = k_ref.shape[0]
    q_part, kv_part = q_ref.shape[0], kt_ref.shape[0]
    blocks = length // TILE

    def first_tiles(shard):
        return pl.ds(pl.multiple_of(shard * ffn_part, ffn_part), early)

    proj = Spread(shards, proj_w, proj_m, None, *sems[:2])
    gate = Spread(shards, gate_w, gate_m, first_tiles, *sems[2:4])
    up = Spread(shards, up_w, up_m, first_tiles, *sems[4:6])
    cots = Gather(shards, cot_v, cot_all, *sems[6:9])

    def block_rows(i):
        return pl.ds(pl.multiple_of(i * TILE, TILE), TILE)

    def load(i):
        return pltpu.make_async_copy(tokens.at[block_rows(i), :], tokens_v.at[i % 2], load_sem.at[i % 2])

    def store(i):
        return pltpu.make_async_copy(
            normed_v.at[i % 2], normed_out.at[block_rows(i), :], store_sem.at[i % 2]
        )

    weights = pltpu.make_async_copy(qkv_m, qkv_v, qkv_sem.at[0])
    take = pltpu.make_async_copy(cot, cot_v, qkv_sem.at[1])
    take.start()
    weights.start()
    load(0).start()
    greet(plane_partners(rep, me, shards) + pair_partners(rep, me))
    proj.start()
    gate.start()
    up.start()
    take.wait()
    cots.start()
    weights.wait()

    def turn_weights(i, carry):
        turned_v[:, block_rows(i)] = qkv_v[block_rows(i), :].T
        return carry

    lax.fori_loop(0, width // TILE, turn_weights, 0)

    half = HEAD // 2

    def project(i, carry):
        here = block_rows(i)

        @pl.when(i + 1 < blocks)
        def _():
            load(i + 1).start()

        load(i).wait()

        @pl.when(i >= 2)
        def _():
            store(i - 2).wait()

        values = tokens_v[i % 2].astype(F32)
        rms = lax.rsqrt(jnp.mean(values * values, axis=-1, keepdims=True) + epsilon)
        normed_v[i % 2] = (values * rms * gain[...]).astype(BF16)
        store(i).start()
        heads = dot(turned_v[...], normed_v[i % 2], NT)
        cos, sin = cos_ref[:, here], sin_ref[:, here]

        def turned(at):
            first, second = heads[at : at + half], heads[at + half : at + HEAD]
            return (
                (first * cos - second * sin).astype(BF16),
                (second * cos + first * sin).astype(BF16),
            )

        for at in range(0, q_part, HEAD):
            first, second = turned(at)
            q_ref[at : at + half, here] = (first.astype(F32) * SCALE).astype(BF16)
            q_ref[at + half : at + HEAD, here] = (second.astype(F32) * SCALE).astype(BF16)
        for g in range(kv_heads):
            at = g * HEAD
            first, second = turned(q_part + at)
            kt_ref[at : at + half, here] = first
            kt_ref[at + half : at + HEAD, here] = second
            vt_ref[at : at + HEAD, here] = heads[
                q_part + kv_part + at : q_part + kv_part + at + HEAD
            ].astype(BF16)
            k_ref[g, here, :] = kt_ref[at : at + HEAD, here].T
            v_ref[g, here, :] = vt_ref[at : at + HEAD, here].T
        return carry

    lax.fori_loop(0, blocks, project, 0)
    for i in range(max(0, blocks - 2), blocks):
        store(i).wait()
    proj.hand_on()
    gate.hand_on()
    wide = GROUP * TILE

    def unit(at, carry_out):
        g, block = at // blocks, at % blocks
        query_at = pl.multiple_of(block * TILE, TILE)
        here = pl.ds(query_at, TILE)
        queries = side_by_side(q_ref, g, here)
        value_rows = pl.ds(pl.multiple_of(g * HEAD, HEAD), HEAD)

        def step(c, carry):
            top, total, acc = carry
            key_at = pl.multiple_of(c * TILE, TILE)
            keys = pl.ds(key_at, TILE)
            scores = dot(k_ref[g, keys, :], queries, NN)
            scores = scores + block_bias(seg_col, seg_row, key_at, query_at)
            new_top = jnp.maximum(top, jnp.max(scores, axis=0, keepdims=True))
            expo = jnp.exp(scores - new_top)
            fade = jnp.exp(top - new_top)
            total = total * fade + jnp.sum(expo, axis=0, keepdims=True)
            acc = acc * fade + dot(vt_ref[value_rows, keys], expo.astype(BF16), NN)
            return new_top, total, acc

        start = (
            jnp.full((1, wide), NEG, F32),
            jnp.zeros((1, wide), F32),
            jnp.zeros((HEAD, wide), F32),
        )
        top, total, acc = lax.fori_loop(0, block, step, step(block, start))
        mixed = (acc / total).astype(BF16)
        lse = top + jnp.log(total)
        for h in range(GROUP):
            at_row = pl.multiple_of(g * GROUP * HEAD + h * HEAD, HEAD)
            out_ref[pl.ds(at_row, HEAD), here] = mixed[:, h * TILE : (h + 1) * TILE]
            lse_ref[g, h : h + 1, here] = lse[:, h * TILE : (h + 1) * TILE]
        return carry_out

    units = kv_heads * blocks
    lax.fori_loop(0, units // 2, unit, 0)
    up.hand_on()
    proj.hand_on_last()
    gate.hand_on_last()
    lax.fori_loop(units // 2, units, unit, 0)
    up.hand_on_last()
    cots.hand_on()
    for transfer in (proj, gate, up, cots):
        transfer.finish()


def attend(
    tokens_all, qkv_m, cot, proj_w, gate_w, up_w, gain, seg, cos_t, sin_t, q_part, kv_part,
    early, shards,
):
    length, width = tokens_all.shape
    kv_heads = kv_part // HEAD
    part = gate_w.shape[1] // shards
    shape = jax.ShapeDtypeStruct
    dma = pltpu.SemaphoreType.DMA
    return pl.pallas_call(
        functools.partial(attend_kernel, shards, part, early),
        in_specs=[ANY] * 6 + [IN_VMEM] * 5,
        out_specs=[ANY] * 5 + [IN_VMEM] * 6,
        out_shape=[
            shape((length, width), BF16),
            shape((length, width), BF16),
            shape((shards * proj_w.shape[0], width), BF16),
            shape((width, early), BF16),
            shape((width, early), BF16),
            shape((q_part, length), BF16),
            shape((kv_heads, length, HEAD), BF16),
            shape((kv_part, length), BF16),
            shape((kv_heads, length, HEAD), BF16),
            shape((q_part, length), BF16),
            shape((kv_heads, GROUP, length), F32),
        ],
        scratch_shapes=[
            pltpu.VMEM((2, TILE, width), BF16),
            pltpu.VMEM((2, TILE, width), BF16),
            pltpu.VMEM(qkv_m.shape, BF16),
            pltpu.VMEM(qkv_m.shape[::-1], BF16),
            pltpu.VMEM((kv_part, length), BF16),
            pltpu.VMEM(cot.shape, BF16),
            dma((2,)), dma((2,)), dma((2,)),
        ]
        + 3 * Spread.semaphores(shards)
        + Gather.semaphores(shards),
        compiler_params=pltpu.CompilerParams(
            collective_id=1, has_side_effects=True, vmem_limit_bytes=48 * MIB
        ),
        name="attend",
    )(
        tokens_all, qkv_m, cot, proj_w, gate_w, up_w, gain[None, :], seg[:, None], seg[None, :],
        cos_t, sin_t,
    )


def hidden_kernel(
    shards, mixed_t, proj_m, proj_w, tokens, gain, hidden_ref, rms_ref, normed_all,
    proj_v, mixed_own, normed, proj_sem, mix_send, mix_recv, gather_send, gather_recv, local_sem,
):
    rep, me = place()
    part, _ = mixed_t.shape
    count = tokens.shape[0]
    rows = [
        pltpu.make_async_copy(
            split_rows(proj_m, me ^ i, part) if i else proj_w,
            split_rows(proj_v, me ^ i, part),
            proj_sem.at[i],
        )
        for i in range(shards)
    ]
    for copy in rows:
        copy.start()
    greet(plane_partners(rep, me, shards))

    def columns(shard):
        return mixed_t.at[:, pl.ds(pl.multiple_of(shard * count, count), count)]

    copies = [
        remote(columns(me ^ (i + 1)), mixed_own.at[i], mix_send, mix_recv, i, rep, me ^ (i + 1))
        for i in range(shards - 1)
    ]
    for copy in copies:
        copy.start()

    def product(block, i):
        rows[i].wait()
        return dot(block, split_rows(proj_v, me ^ i, part)[...], TN)

    hidden_ref[...] = tokens[...].astype(F32) + product(
        mixed_t[:, pl.ds(pl.multiple_of(me * count, count), count)], 0
    )
    for i, copy in enumerate(copies):
        copy.wait_recv()
        hidden_ref[...] += product(mixed_own[i], i + 1)
    hidden = hidden_ref[...]
    rms = lax.rsqrt(jnp.mean(hidden * hidden, axis=-1, keepdims=True) + epsilon)
    rms_ref[...] = rms
    normed[...] = (hidden * rms * gain[...]).astype(BF16)
    gather = Gather(shards, normed, normed_all, gather_send, gather_recv, local_sem)
    gather.start()
    for copy in copies:
        copy.wait_send()
    gather.hand_on()
    gather.finish()


def hidden_layer(mixed_t, proj_m, proj_w, tokens, gain, shards):
    part, length = mixed_t.shape
    count, width = tokens.shape
    n = shards - 1
    return pl.pallas_call(
        functools.partial(hidden_kernel, shards),
        in_specs=[IN_VMEM, ANY, ANY, IN_VMEM, IN_VMEM],
        out_specs=[IN_VMEM, IN_VMEM, ANY],
        out_shape=[
            jax.ShapeDtypeStruct((count, width), F32),
            jax.ShapeDtypeStruct((count, 1), F32),
            jax.ShapeDtypeStruct((length, width), BF16),
        ],
        scratch_shapes=[
            pltpu.VMEM(proj_m.shape, BF16),
            pltpu.VMEM((n, part, count), BF16),
            pltpu.VMEM((count, width), BF16),
            pltpu.SemaphoreType.DMA((shards,)),
            pltpu.SemaphoreType.DMA((n,)),
            pltpu.SemaphoreType.DMA((n,)),
        ]
        + Gather.semaphores(shards),
        compiler_params=pltpu.CompilerParams(
            collective_id=2, has_side_effects=True, vmem_limit_bytes=40 * MIB
        ),
        name="hidden",
    )(mixed_t, proj_m, proj_w, tokens, gain[None, :])


class Plan:
    def __init__(self, shards, reps, length, width, ffn_part, q_part, kv_part):
        self.shards, self.reps, self.length, self.width = shards, reps, length, width
        self.ffn_part, self.q_part, self.kv_part = ffn_part, q_part, kv_part
        self.layers = reps // 2
        self.half = self.layers // 2
        self.rows = width // 2
        self.own = width // shards
        self.block = self.own // 2
        self.proj_half = q_part // 2
        self.proj_blocks = self.rows // self.proj_half
        self.tiles = ffn_part // TILE
        self.out_tiles = width // TILE
        per_slot = 4
        self.back_slot = self.tiles
        self.send_slot = self.back_slot + self.out_tiles // per_slot - 1
        self.rows_slot = self.send_slot + 4
        self.pass_slot = self.rows_slot + 2
        self.mixed_slot = self.rows_slot + 4
        self.unit_slot = self.mixed_slot + 1
        self.per_slot = per_slot
        self.units = (length // TILE) * (kv_part // HEAD)
        self.norm_slot = self.unit_slot + self.units // 2
        self.tokens_slot = self.norm_slot + 5
        self.gain_slot = self.tokens_slot + 1
        self.rep_slot = self.gain_slot + 1
        proj = width // TILE // self.proj_blocks
        self.ffn_end = 3 * self.tiles
        self.proj_at = max(self.ffn_end, self.norm_slot)
        self.q_at = max(self.proj_at + proj, self.norm_slot + 1)
        assert self.q_at == self.proj_at + proj
        self.kv_at = self.q_at + q_part // TILE
        self.chunks = self.kv_at + 1
        self.res_slot = max(self.ffn_end + 1, self.norm_slot + 1)
        self.result_slot = self.res_slot + self.out_tiles // 2 + 3
        lag = 3 if self.layers <= 4 else 1
        self.lag = lag
        self.meet = 1 + lag * self.half
        self.spread = 1 + lag * (self.layers - 1)
        self.hand = self.spread + lag
        self.slots = max(self.chunks + self.hand, self.rep_slot, self.result_slot) + 1
        self.mine_ring = 2 + lag * (self.half - 1)
        self.sum_ring = lag + 2


def backward_kernel(
    plan, early, x, cot_all, gate_w, up_w, gate_e, up_e, down_w, hidden, tokens, proj_w, qkv_m,
    normed,
    mlp_rms, mlp_gain, attn_gain, seg_col, seg_row, cos_ref, sin_ref, lse_ref, q_ref, mixed_ref,
    k_ref, kt_ref, v_ref,
    f_down, f_gate, f_up, f_proj, f_q, f_kv, result_ref, tokens_out, gains_out,
    swapped, from_outer, from_middle, totals, back_land, res_land, norm_land, norm_part,
    gate_m, up_m, activ, dgate, dup, back_part, res_part,
    left_a, left_b, right, gate_v, up_v, down_v, back_v, tile_v, both, proj_v, qkv_v, hidden_v,
    row_sum, land_v,
    mine, theirs, swap_v, outer_v, middle_v, sums, total_v,
    grad_hidden, gh_own, g_t, back_t, dk_acc, dv_acc,
    gain_part, gain_land, gain_sum, gain_reps,
    load_sem, right_sem, small_sem, swap_send, swap_recv, in_send, outer_recv, middle_recv,
    out_send, total_recv, total_store, cross_recv, cross_send, pass_send, pass_recv,
    back_send, back_recv, res_send, res_recv, norm_send, norm_recv,
    gather_send, gather_recv, gather_local, gain_send, gain_recv, rep_send, rep_recv,
    tile_send, tile_recv, tile_pass, tile_passed, down_sem, back_sem, tile_sem,
):
    p = plan
    shards, reps, n = p.shards, p.reps, p.shards - 1
    rep, me = place()
    core, layer = rep % 2, rep // 2
    upper = layer >= p.half
    depth = jnp.where(upper, p.layers - 1 - layer, layer)
    inward = jnp.where(upper, rep - 2, rep + 2)
    outward = jnp.where(upper, rep + 2, rep - 2)
    is_middle = depth == p.half - 1
    count = tokens.shape[0]
    ffn_end, proj_at, q_at, kv_at, end_at = p.ffn_end, p.proj_at, p.q_at, p.kv_at, p.chunks
    gh_all = both.at[:, pl.ds(0, p.width)]

    def columns(index, size=TILE):
        return pl.ds(pl.multiple_of(index * size, size), size)

    def load(src, dst, i):
        return pltpu.make_async_copy(src, dst, load_sem.at[i])

    load_cot = load(cot_all, left_a, 0)
    load_x = load(x, left_b, 1)
    load_normed = load(normed, left_a, 2)
    load_proj = load(proj_w, proj_v, 3)
    load_qkv = load(qkv_m, qkv_v, 4)
    load_hidden = load(hidden, hidden_v, 5)
    load_activ = load(activ, left_b.at[:, pl.ds(0, p.ffn_part)], 6)
    load_tokens = load(tokens, gh_own, 7)
    first_tile = early // TILE

    def tile_bytes(tile, sem):
        piece = gate_m.at[pl.ds(0, 2 * n * p.block), pl.ds(0, TILE)]
        return pltpu.make_async_copy(piece, piece, sem.at[tile])

    def send_tile(tile):
        rows = columns(core, p.block)
        into = pl.ds(pl.multiple_of(me * p.own + core * p.block, p.block), p.block)
        for weight, full in ((gate_w, gate_m), (up_w, up_m)):
            for i in range(n):
                peer = me ^ (i + 1)
                at = pl.ds(pl.multiple_of(peer * p.ffn_part + tile * TILE, TILE), TILE)
                pltpu.make_async_remote_copy(
                    src_ref=weight.at[rows, at], dst_ref=full.at[into, columns(tile)],
                    send_sem=tile_send.at[tile], recv_sem=tile_recv.at[tile],
                    device_id=(rep, peer), device_id_type=MESH,
                ).start()

    def pass_tile(tile):
        tile_bytes(tile, tile_recv).wait()
        for full in (gate_m, up_m):
            for i in range(n):
                peer = me ^ (i + 1)
                at = pl.ds(pl.multiple_of(peer * p.own + core * p.block, p.block), p.block)
                piece = full.at[at, columns(tile)]
                pltpu.make_async_remote_copy(
                    src_ref=piece, dst_ref=piece,
                    send_sem=tile_pass.at[tile], recv_sem=tile_passed.at[tile],
                    device_id=(rep ^ 1, me), device_id_type=MESH,
                ).start()

    def load_down(tile):
        return pltpu.make_async_copy(down_w.at[columns(tile), :], down_v, down_sem.at[0])

    def load_tile(tile):
        @pl.when(tile >= first_tile)
        def _():
            tile_bytes(tile, tile_passed).wait()

        own_at = pl.ds(pl.multiple_of(me * p.ffn_part + tile * TILE, TILE), TILE)
        held_rows = [pl.ds(pl.multiple_of((me ^ i) * p.own, p.own), p.own) for i in range(shards)]
        for i, (weight, tiles, full, held) in enumerate(
            ((gate_w, gate_e, gate_m, gate_v), (up_w, up_e, up_m, up_v))
        ):
            sem = down_sem.at[i + 1]
            pltpu.make_async_copy(weight.at[:, own_at], held.at[held_rows[0], :], sem).start()
            for rows in held_rows[1:]:

                @pl.when(tile < first_tile)
                def _(rows=rows, tiles=tiles, held=held, sem=sem):
                    src = tiles.at[rows, columns(tile)]
                    pltpu.make_async_copy(src, held.at[rows, :], sem).start()

                @pl.when(tile >= first_tile)
                def _(rows=rows, full=full, held=held, sem=sem):
                    src = full.at[rows, columns(tile)]
                    pltpu.make_async_copy(src, held.at[rows, :], sem).start()

        load_down(tile).start()

    def store_tile(tile):
        dup_columns = pl.ds(pl.multiple_of(p.ffn_part + tile * TILE, TILE), TILE)
        return [
            pltpu.make_async_copy(src, dst.at[:, columns(tile)], tile_sem.at[i])
            for i, (src, dst) in enumerate(
                (
                    (tile_v.at[tile % 2], activ),
                    (both.at[:, columns(tile)], dgate),
                    (both.at[:, dup_columns], dup),
                )
            )
        ]

    def stored(tile):
        for copy in store_tile(tile):
            copy.wait()

    def ffn_tile(tile):
        for i, held in enumerate((gate_v, up_v)):
            pltpu.make_async_copy(held, held, down_sem.at[i + 1]).wait()
        load_down(tile).wait()
        dup_columns = pl.ds(pl.multiple_of(p.ffn_part + tile * TILE, TILE), TILE)

        def go(i, carry):
            here = columns(i)
            rows = left_b[here, :]
            gate = dot(rows, gate_v[...], NN)
            up = dot(rows, up_v[...], NN)
            grad_activ = dot(left_a[here, :], down_v[...], NT)
            sigm = jax.nn.sigmoid(gate)
            swish = gate * sigm
            tile_v[tile % 2, here, :] = (swish * up).astype(BF16)
            both[here, columns(tile)] = (
                grad_activ * up * sigm * (1.0 + gate * (1.0 - sigm))
            ).astype(BF16)
            both[here, dup_columns] = (grad_activ * swish).astype(BF16)
            return carry

        lax.fori_loop(0, p.length // TILE, go, 0)

        @pl.when(tile >= 2)
        def _():
            stored(tile - 1)

        for copy in store_tile(tile):
            copy.start()

        @pl.when(tile == 0)
        def _():
            stored(0)

        @pl.when(tile + 1 < p.tiles)
        def _():
            load_tile(tile + 1)

    def load_back(tile):
        slot = tile % 2
        per_shard = p.own // TILE
        for i, (weight, tiles, full) in enumerate(
            ((gate_w, gate_e, gate_m), (up_w, up_e, up_m))
        ):
            sem, at = back_sem.at[slot, i], i * p.ffn_part

            @pl.when(tile // per_shard == me)
            def _(weight=weight, sem=sem, at=at):
                src = weight.at[columns(tile - me * per_shard), columns(me, p.ffn_part)]
                pltpu.make_async_copy(src, back_v.at[slot, :, pl.ds(at, p.ffn_part)], sem).start()

            @pl.when(tile // per_shard != me)
            def _(tiles=tiles, full=full, sem=sem, at=at):
                into = back_v.at[slot, :, pl.ds(at, early)]
                pltpu.make_async_copy(tiles.at[columns(tile), :], into, sem).start()
                rest = p.ffn_part - early
                into = back_v.at[slot, :, pl.ds(at + early, rest)]
                src = full.at[columns(tile), pl.ds(early, rest)]
                pltpu.make_async_copy(src, into, sem).start()

    def wait_back(tile):
        slot = tile % 2
        for i in range(2):
            half = back_v.at[slot, :, pl.ds(i * p.ffn_part, p.ffn_part)]
            pltpu.make_async_copy(half, half, back_sem.at[slot, i]).wait()

    def back_tiles(first):
        def store(tile):
            return pltpu.make_async_copy(
                tile_v.at[tile % 2], back_part.at[:, columns(tile)], tile_sem.at[tile % 2]
            )

        @pl.when(first == 0)
        def _():
            stored(p.tiles - 1)
            load_back(0)

        def tile_go(k, carry):
            tile = first + k
            wait_back(tile)

            @pl.when(tile + 1 < p.out_tiles)
            def _():
                load_back(tile + 1)

            @pl.when(k >= 2)
            def _():
                store(tile - 2).wait()

            def go(i, c):
                here = columns(i)
                tile_v[tile % 2, here, :] = dot(both[here, :], back_v[tile % 2], NT).astype(BF16)
                return c

            lax.fori_loop(0, p.length // TILE, go, 0)
            store(tile).start()
            return carry

        lax.fori_loop(0, p.per_slot, tile_go, 0)
        for k in range(max(0, p.per_slot - 2), p.per_slot):
            store(first + k).wait()

    def load_res(tile):
        def copies(action):
            for i, held in enumerate((gate_v, up_v)):

                @pl.when(tile % 2 == i)
                def _(i=i, held=held):
                    action(
                        pltpu.make_async_copy(
                            down_w.at[:, columns(tile)], held.at[pl.ds(0, p.ffn_part), :], back_sem.at[i, 0]
                        )
                    )

        return copies

    def res_tiles(first):
        def store(tile):
            return pltpu.make_async_copy(
                tile_v.at[tile % 2], res_part.at[:, columns(tile)], tile_sem.at[tile % 2]
            )

        for k, held in enumerate((gate_v, up_v)):
            tile = first + k
            load_res(tile)(lambda copy: copy.wait())

            @pl.when(tile + 1 < p.out_tiles)
            def _(tile=tile):
                load_res(tile + 1)(lambda copy: copy.start())

            def go(i, c, k=k, held=held):
                here = columns(i)
                tile_v[k, here, :] = dot(
                    left_b[here, : p.ffn_part], held[: p.ffn_part, :], NN
                ).astype(BF16)
                return c

            lax.fori_loop(0, p.length // TILE, go, 0)
            store(tile).start()
        store(first).wait()
        store(first + 1).wait()

    def load_right(t):
        slot = right.at[t % 2]
        tile, kind = t // 3, t % 3

        def copies(action):
            for i, ref in enumerate((activ, dgate, dup)):

                @pl.when((t < ffn_end) & (kind == i))
                def _(ref=ref):
                    action(
                        pltpu.make_async_copy(
                            ref.at[:, columns(tile)], slot, right_sem.at[t % 2]
                        )
                    )

        return copies

    def scatter(part, land, sends, recvs):
        return [
            remote(split_rows(part, me ^ (i + 1), count), land.at[i], sends, recvs, i, rep, me ^ (i + 1))
            for i in range(n)
        ]

    back_rows = scatter(back_part, back_land, back_send, back_recv)
    res_rows = scatter(res_part, res_land, res_send, res_recv)
    norm_rows = scatter(norm_part, norm_land, norm_send, norm_recv)

    def fetch_rows(copies, part, land):
        for copy in copies:
            copy.wait_recv()
        pieces = [split_rows(part, me, count)] + [land.at[i] for i in range(n)]
        loads = [
            pltpu.make_async_copy(piece, land_v.at[i % 2], small_sem.at[i % 2])
            for i, piece in enumerate(pieces)
        ]
        loads[0].start()
        for i, piece in enumerate(loads):
            if i + 1 < len(loads):
                loads[i + 1].start()
            piece.wait()

            def strip(here, i=i):
                value = land_v[i % 2, here, :].astype(F32)
                row_sum[here, :] = value if i == 0 else row_sum[here, :] + value

            strips(strip)

    STRIP = 32

    def strips(body):
        def go(i, carry):
            body(pl.ds(pl.multiple_of(i * STRIP, STRIP), STRIP))
            return carry

        lax.fori_loop(0, count // STRIP, go, 0)

    def norm_strip(here, values, rms, gain, row):
        grad_in = row_sum[here, :]
        weighted = grad_in * gain
        inner = jnp.mean(weighted * values, axis=-1, keepdims=True)
        gain_part[row : row + 1, :] += jnp.sum(grad_in * values * rms, axis=0, keepdims=True)
        return rms * weighted - values * (rms * rms * rms) * inner

    gather = Gather(shards, gh_own, gh_all, gather_send, gather_recv, gather_local)

    def hidden_back():
        load_hidden.wait()
        fetch_rows(back_rows, back_part, back_land)
        gain_part[...] = jnp.zeros_like(gain_part)

        def strip(here):
            own = pl.ds(pl.multiple_of(me * count, count) + here.start, STRIP)
            grad = left_a[own, :].astype(F32) + norm_strip(
                here, hidden_v[here, :], mlp_rms[here, :], mlp_gain[...], 1
            )
            grad_hidden[here, :] = grad
            gh_own[here, :] = grad.astype(BF16)

        strips(strip)
        gather.start()

    def finish_result():
        fetch_rows(res_rows, res_part, res_land)

        def strip(here):
            row_sum[here, :] = hidden_v[here, :] + row_sum[here, :]

        strips(strip)
        store_result = pltpu.make_async_copy(row_sum, result_ref, small_sem.at[0])
        store_result.start()
        store_result.wait()

    def mixed_back():
        gather.finish()
        load_proj.wait()

        def go(i, carry):
            here = pl.ds(pl.multiple_of(i * TILE, TILE), TILE)
            g_t[:, here] = dot(proj_v[...], both[here, : p.width], NT).astype(BF16)
            return carry

        lax.fori_loop(0, p.length // TILE, go, 0)

    blocks = p.length // TILE
    rows = GROUP * HEAD
    wide = GROUP * TILE
    mid = HEAD // 2

    def attention_unit(unit):
        g, block = unit // blocks, unit % blocks
        query_at = pl.multiple_of(block * TILE, TILE)
        here_q = pl.ds(query_at, TILE)

        queries = side_by_side(q_ref, g, here_q)
        grads = side_by_side(g_t, g, here_q)
        mixed = side_by_side(mixed_ref, g, here_q)
        lse = jnp.concatenate([lse_ref[g, h : h + 1, here_q] for h in range(GROUP)], axis=1)
        inner = jnp.sum(grads.astype(F32) * mixed.astype(F32), axis=0, keepdims=True)

        @pl.when(block == 0)
        def _():
            dk_acc[...] = jnp.zeros_like(dk_acc)
            dv_acc[...] = jnp.zeros_like(dv_acc)

        def step(c, acc):
            key_at = pl.multiple_of(c * TILE, TILE)
            here = pl.ds(key_at, TILE)
            scores = dot(k_ref[g, here, :], queries, NN)
            scores = scores + block_bias(seg_col, seg_row, key_at, query_at)
            probs = jnp.exp(scores - lse)
            grad_probs = dot(v_ref[g, here, :], grads, NN)
            grad_scores = (probs * (grad_probs - inner)).astype(BF16)
            dv_acc[:, here] += dot(grads, probs.astype(BF16), NT)
            dk_acc[:, here] += dot(queries, grad_scores, NT)
            key_rows = pl.ds(pl.multiple_of(g * HEAD, HEAD), HEAD)
            return acc + dot(kt_ref[key_rows, here], grad_scores, NN)

        acc = lax.fori_loop(0, block + 1, step, jnp.zeros((HEAD, wide), F32))
        cos, sin = cos_ref[:, here_q], sin_ref[:, here_q]
        for h in range(GROUP):
            grad = acc[:, h * TILE : (h + 1) * TILE] * SCALE
            first, second = grad[:mid], grad[mid:]
            at = pl.multiple_of(g * rows + h * HEAD, HEAD)
            back_t[pl.ds(at, mid), here_q] = (first * cos + second * sin).astype(BF16)
            back_t[pl.ds(at + mid, mid), here_q] = (second * cos - first * sin).astype(BF16)

        @pl.when(block == blocks - 1)
        def _():
            cos, sin = cos_ref[...], sin_ref[...]
            first, second = dk_acc[:mid, :], dk_acc[mid:, :]
            at = pl.multiple_of(p.q_part + g * HEAD, HEAD)
            back_t[pl.ds(at, mid), :] = (first * cos + second * sin).astype(BF16)
            back_t[pl.ds(at + mid, mid), :] = (second * cos - first * sin).astype(BF16)
            at = pl.multiple_of(p.q_part + p.kv_part + g * HEAD, HEAD)
            back_t[pl.ds(at, HEAD), :] = dv_acc[...].astype(BF16)

    def normed_back():
        load_qkv.wait()

        stores = [
            pltpu.make_async_copy(
                land_v.at[i % 2], norm_part.at[pl.ds(i * count, count), :], small_sem.at[i % 2]
            )
            for i in range(shards)
        ]
        for i, store in enumerate(stores):
            if i >= 2:
                stores[i - 2].wait()
            here = pl.ds(i * count, count)
            land_v[i % 2] = dot(back_t[:, here].T, qkv_v[...], NT).astype(BF16)
            store.start()
        for store in stores[-2:]:
            store.wait()
        for copy in norm_rows:
            copy.start()

    gain_cols = p.width // shards

    def gain_slice(shard):
        return pl.ds(pl.multiple_of(shard * gain_cols, gain_cols), gain_cols)

    gain_plane = [
        remote(
            gain_part.at[:, gain_slice(me ^ (i + 1))], gain_land.at[me],
            gain_send, gain_recv, i, rep, me ^ (i + 1),
        )
        for i in range(n)
    ]
    gain_all = [
        remote(gain_sum, gain_reps.at[rep], rep_send, rep_recv, i, rep ^ (i + 1), me)
        for i in range(reps - 1)
    ]

    def tokens_back():
        load_tokens.start()
        load_tokens.wait()
        fetch_rows(norm_rows, norm_part, norm_land)

        def strip(here):
            values = gh_own[here, :].astype(F32)
            rms = lax.rsqrt(jnp.mean(values * values, axis=-1, keepdims=True) + epsilon)
            grad_hidden[here, :] += norm_strip(here, values, rms, attn_gain[...], 0)

        strips(strip)
        store_tokens = pltpu.make_async_copy(grad_hidden, tokens_out, small_sem.at[0])
        store_tokens.start()
        store_tokens.wait()
        gain_land[me] = gain_part[:, gain_slice(me)]
        for copy in gain_plane:
            copy.start()

    def gains_plane():
        for copy in gain_plane:
            copy.wait_recv()
        total = gain_land[0]
        for s in range(1, shards):
            total = total + gain_land[s]
        gain_sum[...] = total
        gain_reps[rep] = total
        for copy in gain_all:
            copy.start()

    def gains_reps():
        for copy in gain_all:
            copy.wait_recv()
        total = gain_reps[0]
        for r in range(1, reps):
            total = total + gain_reps[r]
        gains_out[...] = total

    def swap_copy(j):
        return pltpu.make_async_remote_copy(
            src_ref=theirs.at[j % 2], dst_ref=swapped.at[j],
            send_sem=swap_send.at[j % 2], recv_sem=swap_recv.at[j],
            device_id=(rep ^ 1, me), device_id_type=MESH,
        )

    def store_chunk(slot, other_slot, at, size, product, columns=TILE):
        here = pl.ds(pl.multiple_of(at, size), size)
        mine[slot, here, :columns] = product(core).astype(BF16)
        theirs[other_slot, here, :columns] = product(1 - core).astype(BF16)

    def make(t):
        slot, other = t % p.mine_ring, t % 2

        @pl.when(t >= 2)
        def _():
            swap_copy(t - 2).wait_send()

        @pl.when(t == 0)
        def _():
            load_right(0)(lambda copy: copy.start())

        load_right(t)(lambda copy: copy.wait())

        @pl.when(t + 1 < ffn_end)
        def _():
            load_right(t + 1)(lambda copy: copy.start())

        @pl.when((t < ffn_end) & (t % 3 == 0))
        def _():
            left = right[t % 2].T

            def go(i, carry):
                def product(which):
                    at = pl.multiple_of(which * p.rows + i * TILE, TILE)
                    return dot(left, left_a[:, pl.ds(at, TILE)], NN)

                store_chunk(slot, other, i * TILE, TILE, product)
                return carry

            lax.fori_loop(0, p.rows // TILE, go, 0)

        def wide_chunk(left, factor, columns):
            def go(s, carry):
                def product(which):
                    at = pl.multiple_of(s * p.own + which * p.block, p.block)
                    return dot(factor, left[:, pl.ds(at, p.block)], NN).T

                store_chunk(slot, other, s * p.block, p.block, product, columns)
                return carry

            lax.fori_loop(0, shards, go, 0)

        @pl.when((t < ffn_end) & (t % 3 > 0))
        def _():
            wide_chunk(left_b, right[t % 2].T, TILE)

        @pl.when((t >= proj_at) & (t < q_at))
        def _():
            def go(i, carry):
                at = columns((t - proj_at) * p.proj_blocks + i)

                def product(which):
                    part = columns(which, p.proj_half)
                    return dot(mixed_ref[part, :], both[:, at], NN)

                store_chunk(slot, other, i * p.proj_half, p.proj_half, product)
                return carry

            lax.fori_loop(0, p.proj_blocks, go, 0)

        @pl.when((t >= q_at) & (t < kv_at))
        def _():
            wide_chunk(left_a, back_t[columns(t - q_at), :], TILE)

        @pl.when(t == kv_at)
        def _():
            wide_chunk(left_a, back_t[p.q_part :, :], 2 * p.kv_part)

        swap_copy(t).start()

    def inward_copies(j):
        common = dict(
            src_ref=sums.at[j % p.sum_ring], send_sem=in_send.at[j % p.sum_ring],
            device_id=(inward, me), device_id_type=MESH,
        )
        to_layer = pltpu.make_async_remote_copy(
            dst_ref=from_outer.at[j], recv_sem=outer_recv.at[j], **common
        )
        to_middle = pltpu.make_async_remote_copy(
            dst_ref=from_middle.at[j], recv_sem=middle_recv.at[j], **common
        )
        return to_layer, to_middle

    def total_places(j, action):
        @pl.when(is_chunk(j, 0))
        def _():
            action(
                [
                    (
                        i * TILE, TILE, TILE,
                        f_down.at[
                            columns(j // 3),
                            pl.ds(pl.multiple_of(core * p.rows + i * TILE, TILE), TILE),
                        ],
                    )
                    for i in range(p.rows // TILE)
                ]
            )

        @pl.when((j >= proj_at) & (j < q_at))
        def _():
            action(
                [
                    (
                        i * p.proj_half, p.proj_half, TILE,
                        f_proj.at[
                            columns(core, p.proj_half),
                            columns((j - proj_at) * p.proj_blocks + i),
                        ],
                    )
                    for i in range(p.proj_blocks)
                ]
            )

        for when, full, part, tile, sem, wide_by in wide_kinds(j):

            @pl.when(when)
            def _(full=full, part=part, tile=tile, wide_by=wide_by):
                blocks = []
                for i in range(shards):
                    at = pl.multiple_of((me ^ i) * p.block, p.block)
                    place_there = totals.at[j, pl.ds(at, p.block), pl.ds(0, wide_by)]
                    if i == 0:
                        place_there = window(full, me, part, tile, wide_by)
                    blocks.append((at, p.block, wide_by, place_there))
                action(blocks)

    def chunk_bytes(j, sem):
        @pl.when(j == kv_at)
        def _():
            whole = totals.at[0, :, pl.ds(0, 2 * p.kv_part)]
            pltpu.make_async_copy(whole, whole, sem).wait()

        @pl.when(j != kv_at)
        def _():
            whole = totals.at[0]
            pltpu.make_async_copy(whole, whole, sem).wait()

    def send_total(src, dst, j):
        return pltpu.make_async_remote_copy(
            src_ref=src, dst_ref=dst, send_sem=out_send.at[j % 2],
            recv_sem=total_recv.at[j], device_id=(outward, me), device_id_type=MESH,
        )

    def add_rows(body):
        def go(i, carry):
            body(pl.ds(pl.multiple_of(i * TILE, TILE), TILE))
            return carry

        lax.fori_loop(0, p.rows // TILE, go, 0)

    def load_swapped(j):
        return pltpu.make_async_copy(swapped.at[j], swap_v, small_sem.at[2])

    def load_outer(j):
        return pltpu.make_async_copy(from_outer.at[j], outer_v, small_sem.at[3])

    def load_middle(j):
        return pltpu.make_async_copy(from_middle.at[j], middle_v, small_sem.at[4])

    def valid(j):
        return (j >= 0) & (j < p.chunks)

    def take_inward(j):
        @pl.when(valid(j))
        def _():
            swap_copy(j).wait_recv()
            load_swapped(j).start()

            @pl.when(depth > 0)
            def _():
                inward_copies(j)[0].wait_recv()
                load_outer(j).start()

    def send_inward(j):
        @pl.when(valid(j))
        def _():
            @pl.when(j >= p.sum_ring)
            def _():
                inward_copies(j - p.sum_ring)[0].wait_send()

            load_swapped(j).wait()
            ours = mine.at[j % p.mine_ring]
            total = sums.at[j % p.sum_ring]

            @pl.when(depth > 0)
            def _():
                load_outer(j).wait()

                def add(here):
                    total[here, :] = (
                        ours[here, :].astype(F32)
                        + swap_v[here, :].astype(F32)
                        + outer_v[here, :].astype(F32)
                    ).astype(BF16)

                add_rows(add)

            @pl.when(depth == 0)
            def _():
                def add(here):
                    total[here, :] = (
                        ours[here, :].astype(F32) + swap_v[here, :].astype(F32)
                    ).astype(BF16)

                add_rows(add)

            to_layer, to_middle = inward_copies(j)

            @pl.when(is_middle)
            def _():
                to_middle.start()

            @pl.when(jnp.logical_not(is_middle))
            def _():
                to_layer.start()

    def take_middle(j):
        @pl.when(is_middle & valid(j))
        def _():
            inward_copies(j)[1].wait_recv()
            load_middle(j).start()

        @pl.when(is_middle & valid(j - 1))
        def _():
            chunk_bytes(j - 1, total_store.at[0])

    def meet_in_middle(j):
        @pl.when(is_middle & valid(j))
        def _():
            if p.half > 1:

                @pl.when(j >= 2)
                def _():
                    chunk_bytes(j - 2, out_send.at[j % 2])

            load_middle(j).wait()
            out, held = total_v.at[j % 2], sums.at[j % p.sum_ring]

            def add(here):
                out[here, :] = (
                    held[here, :].astype(F32) + middle_v[here, :].astype(F32)
                ).astype(BF16)

            add_rows(add)

            def put(blocks):
                for at, size, wide_by, dst in blocks:
                    src = out.at[pl.ds(at, size), pl.ds(0, wide_by)]
                    if p.half > 1:
                        send_total(src, dst, j).start()
                    pltpu.make_async_copy(src, dst, total_store.at[0]).start()

            total_places(j, put)

    def send_outward(j):
        @pl.when(jnp.logical_not(is_middle) & valid(j))
        def _():
            chunk_bytes(j, total_recv.at[j])

            if p.half > 2:

                @pl.when(depth > 0)
                def _():
                    @pl.when(j >= 2)
                    def _():
                        chunk_bytes(j - 2, out_send.at[j % 2])

                    def put(blocks):
                        for _, _, _, dst in blocks:
                            send_total(dst, dst, j).start()

                    total_places(j, put)

    def remote_pass(src, dst, sem):
        return pltpu.make_async_remote_copy(
            src_ref=src, dst_ref=dst, send_sem=pass_send.at[sem], recv_sem=pass_recv.at[sem],
            device_id=(rep ^ 1, me), device_id_type=MESH,
        )

    def window(full, shard, part, tile, columns=TILE):
        at = pl.multiple_of(shard * part + tile * columns, columns)
        return full.at[pl.ds(pl.multiple_of(core * p.block, p.block), p.block), pl.ds(at, columns)]

    def is_chunk(j, kind):
        return (j >= 0) & (j < ffn_end) & (j % 3 == kind)

    def wide_kinds(j):
        return (
            (is_chunk(j, 1), f_gate, p.ffn_part, j // 3, 1, TILE),
            (is_chunk(j, 2), f_up, p.ffn_part, j // 3, 2, TILE),
            ((j >= q_at) & (j < kv_at), f_q, p.q_part, j - q_at, 4, TILE),
            (j == kv_at, f_kv, 2 * p.kv_part, 0, 5, 2 * p.kv_part),
        )

    def spread_total(j):
        for kind, sem in ((is_chunk(j, 0), 0), ((j >= proj_at) & (j < q_at), 3)):

            @pl.when(kind)
            def _(sem=sem):
                def put(blocks):
                    for _, _, _, dst in blocks:
                        remote_pass(dst, dst, sem).start()

                total_places(j, put)

        for when, full, part, tile, sem, wide_by in wide_kinds(j):

            @pl.when(when)
            def _(full=full, part=part, tile=tile, sem=sem, wide_by=wide_by):
                place_here = window(full, me, part, tile, wide_by)
                for i in range(n):
                    at = columns(me ^ (i + 1), p.block)
                    pltpu.make_async_remote_copy(
                        src_ref=totals.at[j, at, pl.ds(0, wide_by)], dst_ref=place_here,
                        send_sem=cross_send.at[sem], recv_sem=cross_recv.at[j],
                        device_id=(rep, me ^ (i + 1)), device_id_type=MESH,
                    ).start()
                remote_pass(place_here, place_here, sem).start()

    def pass_on(j):
        for when, full, part, tile, sem, wide_by in wide_kinds(j):

            @pl.when(when)
            def _(full=full, part=part, tile=tile, sem=sem, wide_by=wide_by):
                came = totals.at[j, pl.ds(0, n * p.block), pl.ds(0, wide_by)]
                pltpu.make_async_copy(came, came, cross_recv.at[j]).wait()
                for i in range(n):
                    here = window(full, me ^ (i + 1), part, tile, wide_by)
                    remote_pass(here, here, sem).start()

    for copy in (load_x, load_cot):
        copy.start()
    load_tile(0)
    greet(plane_partners(rep, me, shards) + [(rep ^ i, me) for i in range(1, reps)])
    ahead = 3
    for tile in range(first_tile, min(first_tile + ahead, p.tiles)):
        send_tile(tile)
    for copy in (load_hidden, load_proj, load_qkv):
        copy.start()
    for copy in (load_x, load_cot):
        copy.wait()

    def slot(t, carry):
        take_inward(t - 1 - p.lag * depth)
        take_middle(t - p.meet)
        send_outward(t - p.spread + p.lag * depth)
        spread_total(t - p.spread)
        pass_on(t - p.hand)

        @pl.when(t + first_tile + ahead < p.tiles)
        def _():
            send_tile(t + first_tile + ahead)

        @pl.when(t < p.tiles)
        def _():
            ffn_tile(t)

        @pl.when((t >= p.back_slot) & (t <= p.send_slot))
        def _():
            back_tiles((t - p.back_slot) * p.per_slot)

        @pl.when(t == ffn_end)
        def _():
            load_normed.start()
            load_activ.start()

        @pl.when(t == q_at)
        def _():
            load_normed.wait()

        @pl.when(t < p.chunks)
        def _():
            make(t)

        def at(when, action):
            @pl.when(t == when)
            def _():
                action()

        def start_rows(copies):
            for copy in copies:
                copy.start()

        @pl.when((t + 2 >= first_tile) & (t + 2 < p.tiles))
        def _():
            pass_tile(t + 2)

        send_inward(t - 1 - p.lag * depth)
        meet_in_middle(t - p.meet)
        at(p.send_slot, lambda: start_rows(back_rows))
        at(p.rows_slot, hidden_back)
        at(p.pass_slot, gather.hand_on)
        at(p.mixed_slot, mixed_back)

        @pl.when((t >= p.unit_slot) & (t < p.norm_slot))
        def _():
            def go(i, c):
                attention_unit((t - p.unit_slot) * 2 + i)
                return c

            lax.fori_loop(0, 2, go, 0)

        at(p.norm_slot, normed_back)
        at(p.tokens_slot, tokens_back)
        at(p.gain_slot, gains_plane)
        at(p.rep_slot, gains_reps)

        @pl.when((t >= p.res_slot) & (t < p.res_slot + p.out_tiles // 2))
        def _():
            @pl.when(t == p.res_slot)
            def _():
                load_activ.wait()
                load_res(0)(lambda copy: copy.start())

            res_tiles((t - p.res_slot) * 2)

        at(p.res_slot + p.out_tiles // 2 - 1, lambda: start_rows(res_rows))
        at(p.result_slot, finish_result)
        return carry

    lax.fori_loop(0, p.slots, slot, 0)

    for j in range(max(0, p.chunks - 2), p.chunks):
        swap_copy(j).wait_send()
    for j in range(max(0, p.chunks - p.sum_ring), p.chunks):
        inward_copies(j)[0].wait_send()
    if p.half > 1:

        @pl.when(depth > 0)
        def _():
            for j in range(max(0, p.chunks - 2), p.chunks):
                chunk_bytes(j, out_send.at[j % 2])

    for copies in (back_rows, res_rows, norm_rows, gain_plane, gain_all):
        for copy in copies:
            copy.wait_send()

    def settle(ref, sem):
        pltpu.make_async_copy(ref, ref, sem).wait()

    for tile in range(first_tile, p.tiles):
        tile_bytes(tile, tile_send).wait()
        tile_bytes(tile, tile_pass).wait()
    for sem, part in (
        (0, f_down.at[:, pl.ds(0, p.rows)]),
        (3, f_proj.at[pl.ds(0, p.proj_half), :]),
    ):
        settle(part, pass_send.at[sem])
        settle(part, pass_recv.at[sem])
    for _, full, part, _, sem, _ in wide_kinds(0):
        here = full.at[pl.ds(0, p.block), :]
        settle(here, pass_send.at[sem])
        settle(here, pass_recv.at[sem])
        settle(full.at[pl.ds(0, p.block), pl.ds(0, n * part)], cross_send.at[sem])


def backward(
    shards, reps, x, cot_all, gate_w, up_w, gate_e, up_e, down_w, hidden, tokens, proj_w,
    qkv_m, normed, mlp_rms, mlp_gain, attn_gain, seg, cos_t, sin_t, lse, q_t, mixed_t, k, k_t, v,
):
    length, width = x.shape
    count = tokens.shape[0]
    ffn_part = down_w.shape[0]
    q_part, kv_part = q_t.shape[0], k_t.shape[0]
    n = shards - 1
    p = Plan(shards, reps, length, width, ffn_part, q_part, kv_part)
    shape = jax.ShapeDtypeStruct
    own = width // shards
    chunk = (p.rows, TILE)
    dma = pltpu.SemaphoreType.DMA
    return pl.pallas_call(
        functools.partial(backward_kernel, p, gate_e.shape[1]),
        in_specs=[ANY] * 12 + [IN_VMEM] * 13,
        out_specs=[ANY] * 8 + [IN_VMEM] + [ANY] * 15,
        out_shape=[
            shape((ffn_part, width), BF16),
            shape((own, shards * ffn_part), BF16),
            shape((own, shards * ffn_part), BF16),
            shape((q_part, width), BF16),
            shape((own, shards * q_part), BF16),
            shape((own, shards * 2 * kv_part), BF16),
            shape((count, width), F32),
            shape((count, width), F32),
            shape((8, width // shards), F32),
        ]
        + [shape((p.chunks,) + chunk, BF16)] * 4
        + [shape((n, count, width), BF16)] * 3
        + [shape((length, width), BF16)]
        + [shape((width, ffn_part), BF16)] * 2
        + [shape((length, ffn_part), BF16)] * 3
        + [shape((length, width), BF16)] * 2,
        scratch_shapes=[
            pltpu.VMEM((length, width), BF16),
            pltpu.VMEM((length, width), BF16),
            pltpu.VMEM((2, length, TILE), BF16),
            pltpu.VMEM((width, TILE), BF16),
            pltpu.VMEM((width, TILE), BF16),
            pltpu.VMEM((TILE, width), BF16),
            pltpu.VMEM((2, TILE, 2 * ffn_part), BF16),
            pltpu.VMEM((2, length, TILE), BF16),
            pltpu.VMEM((length, 2 * ffn_part), BF16),
            pltpu.VMEM(proj_w.shape, BF16),
            pltpu.VMEM(qkv_m.shape, BF16),
            pltpu.VMEM((count, width), F32),
            pltpu.VMEM((count, width), F32),
            pltpu.VMEM((2, count, width), BF16),
            pltpu.VMEM((p.mine_ring,) + chunk, BF16),
            pltpu.VMEM((2,) + chunk, BF16),
            pltpu.VMEM(chunk, BF16),
            pltpu.VMEM(chunk, BF16),
            pltpu.VMEM(chunk, BF16),
            pltpu.VMEM((p.sum_ring,) + chunk, BF16),
            pltpu.VMEM((2,) + chunk, BF16),
            pltpu.VMEM((count, width), F32),
            pltpu.VMEM((count, width), BF16),
            pltpu.VMEM((q_part, length), BF16),
            pltpu.VMEM((q_part + 2 * kv_part, length), BF16),
            pltpu.VMEM((HEAD, length), F32),
            pltpu.VMEM((HEAD, length), F32),
            pltpu.VMEM((8, width), F32),
            pltpu.VMEM((shards, 8, own), F32),
            pltpu.VMEM((8, own), F32),
            pltpu.VMEM((reps, 8, own), F32),
            dma((12,)), dma((2,)), dma((5,)), dma((2,)), dma((p.chunks,)), dma((p.sum_ring,)),
            dma((p.chunks,)), dma((p.chunks,)), dma((2,)), dma((p.chunks,)), dma((2,)),
            dma((p.chunks,)), dma((6,)), dma((6,)), dma((6,)),
            dma((n,)), dma((n,)), dma((n,)), dma((n,)), dma((n,)), dma((n,)),
        ]
        + Gather.semaphores(shards)
        + [dma((n,)), dma((n,)), dma((reps - 1,)), dma((reps - 1,))]
        + [dma((p.tiles,))] * 4
        + [dma((3,)), dma((2, 2)), dma((3,))],
        compiler_params=pltpu.CompilerParams(
            collective_id=3, has_side_effects=True, vmem_limit_bytes=63 * MIB + MIB // 2
        ),
        name="backward",
    )(
        x, cot_all, gate_w, up_w, gate_e, up_e, down_w, hidden, tokens, proj_w,
        qkv_m, normed, mlp_rms, mlp_gain[None, :], attn_gain[None, :], seg[:, None], seg[None, :],
        cos_t, sin_t, lse, q_t, mixed_t, k, k_t, v,
    )[:9]


def local(
    tokens, segments, query_w, key_w, value_w, proj_w, attn_gain,
    gate_w, up_w, down_w, mlp_gain, cotangent,
):
    shards = lax.axis_size("shard")
    reps = lax.axis_size("rep")
    tok_count, width = tokens.shape
    kv_part = key_w.shape[1] // shards
    q_part = query_w.shape[1] // shards
    length = tok_count * shards

    if kv_part % 128:
        kv_w = jnp.concatenate(
            [
                w[:, s * kv_part : (s + 1) * kv_part]
                for s in range(shards)
                for w in (key_w, value_w)
            ],
            axis=1,
        )
        weights = (query_w, kv_w)
    else:
        weights = (query_w, key_w, value_w)
    tokens_all, seg, qkv_m = first(tokens, segments[None, :], weights, shards)
    seg = seg.reshape(length)
    cos_t, sin_t = rope_tables(doc_positions(seg))
    early = min(2 * TILE, down_w.shape[0] // 2)
    normed, cot_all, proj_m, gate_e, up_e, q_t, k, k_t, v, mixed_t, lse = attend(
        tokens_all, qkv_m, cotangent, proj_w, gate_w, up_w, attn_gain, seg, cos_t, sin_t,
        q_part, kv_part, early, shards,
    )
    hidden, mlp_rms, normed_mlp = hidden_layer(mixed_t, proj_m, proj_w, tokens, mlp_gain, shards)
    down, gate, up, proj, query, kv, result, grad_tokens, gains = backward(
        shards, reps, normed_mlp, cot_all, gate_w, up_w, gate_e, up_e, down_w, hidden, tokens,
        proj_w, qkv_m, normed, mlp_rms, mlp_gain, attn_gain, seg, cos_t, sin_t, lse, q_t,
        mixed_t, k, k_t, v,
    )

    def every_other(first):
        parts = [
            kv[:, (2 * s + first) * kv_part : (2 * s + first + 1) * kv_part] for s in range(shards)
        ]
        return jnp.concatenate(parts, axis=1).astype(F32)

    return (
        result, grad_tokens, query.astype(F32), every_other(0), every_other(1), proj.astype(F32),
        gains[0], gate.astype(F32), up.astype(F32), down.astype(F32), gains[1],
    )


def solution(mesh):
    rows = P(("rep", "shard"), None)
    held = P("shard", None)
    in_specs = (
        rows, P(("rep", "shard")), held, held, held, held, P(), held, held, held, P(), rows,
    )
    out_specs = (
        rows, rows, held, held, held, held, P("shard"), held, held, held, P("shard"),
    )
    return jax.shard_map(local, mesh=mesh, in_specs=in_specs, out_specs=out_specs, check_vma=False)
```

```python
import functools
import math

import jax
import jax.numpy as jnp
from jax import lax
from jax.experimental import pallas as pl
from jax.experimental.pallas import tpu as pltpu
from jax.sharding import PartitionSpec as P

HEADS = 32
KV_HEADS = 8
HEAD = 64
GROUP = HEADS // KV_HEADS
SCALE = 1.0 / math.sqrt(HEAD)
TILE = 256
NEG = -1e30
MIB = 1024 * 1024
FULL = 63 * MIB + MIB // 2

epsilon = 1e-05
rope_base = 500000.0
F32 = jnp.float32
BF16 = jnp.bfloat16


def dot(left, right, dims):
    return lax.dot_general(left, right, (dims, ((), ())), preferred_element_type=F32)


NN = ((1,), (0,))
NT = ((1,), (1,))
TN = ((0,), (0,))
TT = ((0,), (1,))


MESH = pl.DeviceIdType.MESH


def place():
    return lax.axis_index("rep"), lax.axis_index("shard")


def remote(src, dst, sends, recvs, index, rep, shard):
    return pltpu.make_async_remote_copy(
        src_ref=src,
        dst_ref=dst,
        send_sem=sends.at[index],
        recv_sem=recvs.at[index],
        device_id=(rep, shard),
        device_id_type=MESH,
    )


def greet(partners):
    barrier = pltpu.get_barrier_semaphore()
    for partner in partners:
        pl.semaphore_signal(barrier, inc=1, device_id=partner, device_id_type=MESH)
    pl.semaphore_wait(barrier, len(partners))


def plane_partners(rep, me, shards):
    return [(rep, me ^ step) for step in range(1, shards)]


class Spread:
    def __init__(self, shards, own, full, columns, sends, recvs, held=None, held_sem=None):
        rep, me = place()
        quarter = rep % 4
        count = own.shape[0]
        part = count // 4
        own_rows = pl.ds(pl.multiple_of(quarter * part, part), part)

        def at(shard, which):
            return full.at[pl.ds(pl.multiple_of(shard * count + which * part, part), part), :]

        def piece(shard):
            return own.at[own_rows, :] if columns is None else own.at[own_rows, columns(shard)]

        self.first, self.core, self.layer, self.last = [], [], [], []
        n = shards - 1
        for i in range(n):
            peer = me ^ (i + 1)
            self.first.append(remote(piece(peer), at(me, quarter), sends, recvs, i, rep, peer))
            mine = at(peer, quarter)
            self.core.append(remote(mine, mine, sends, recvs, n + i, rep ^ 1, me))
            self.layer.append(remote(mine, mine, sends, recvs, 2 * n + i, rep ^ 2, me))
            theirs = at(peer, quarter ^ 2)
            self.last.append(remote(theirs, theirs, sends, recvs, 3 * n + i, rep ^ 1, me))
        self.take = self.keep = None
        if held is not None:
            kept = full.at[pl.ds(pl.multiple_of(me * count, count), count), :]
            self.take = pltpu.make_async_copy(own.at[:, columns(me)], held, held_sem.at[0])
            self.keep = pltpu.make_async_copy(held, kept, held_sem.at[1])

    def start(self):
        for copy in self.first:
            copy.start()
        if self.take is not None:
            self.take.start()

    def hand_on(self):
        if self.take is not None:
            self.take.wait()
            self.keep.start()
        for i, copy in enumerate(self.first):
            copy.wait_recv()
            self.layer[i].start()
            self.core[i].start()

    def hand_on_last(self):
        for i, copy in enumerate(self.layer):
            copy.wait_recv()
            self.last[i].start()

    def finish(self):
        for copy in self.core + self.last:
            copy.wait_recv()
        for copy in self.first + self.core + self.layer + self.last:
            copy.wait_send()
        if self.keep is not None:
            self.keep.wait()

    @staticmethod
    def semaphores(shards):
        n = 4 * (shards - 1)
        return [pltpu.SemaphoreType.DMA((n,)), pltpu.SemaphoreType.DMA((n,))]


class Gather:
    def __init__(self, shards, own, full, sends, recvs, local_sem=None):
        rep, me = place()
        count = own.shape[0]
        half = count // 2

        def at(shard, start, size):
            return full.at[pl.ds(pl.multiple_of(shard * count + start, half), size), :]

        self.direct, self.passed, self.kept = [], [], None
        if shards == 4:
            for i, (step, start) in enumerate(((1, 0), (2, half), (1, half), (2, 0))):
                self.direct.append(
                    remote(
                        own.at[pl.ds(start, half), :], at(me, start, half),
                        sends, recvs, i, rep, me ^ step,
                    )
                )
            for i, (step, start) in enumerate(((1, 0), (2, half))):
                came = at(me ^ step, start, half)
                self.passed.append(remote(came, came, sends, recvs, 4 + i, rep, me ^ step ^ 3))
        else:
            for i in range(shards - 1):
                self.direct.append(
                    remote(own, at(me, 0, count), sends, recvs, i, rep, me ^ (i + 1))
                )
        if local_sem is not None:
            self.kept = pltpu.make_async_copy(own, at(me, 0, count), local_sem)

    def start(self):
        for copy in self.direct:
            copy.start()
        if self.kept is not None:
            self.kept.start()

    def hand_on(self):
        for i, copy in enumerate(self.passed):
            self.direct[i].wait_recv()
            copy.start()

    def finish(self):
        for copy in self.direct[len(self.passed) :] + self.passed:
            copy.wait_recv()
        for copy in self.direct + self.passed:
            copy.wait_send()
        if self.kept is not None:
            self.kept.wait()

    @staticmethod
    def semaphores(shards):
        n = max(6, shards - 1)
        return [
            pltpu.SemaphoreType.DMA((n,)),
            pltpu.SemaphoreType.DMA((n,)),
            pltpu.SemaphoreType.DMA,
        ]


def split_rows(ref, index, size):
    return ref.at[pl.ds(pl.multiple_of(index * size, size), size), :]


def column_block(part):
    return lambda shard: pl.ds(pl.multiple_of(shard * part, part), part)


def pair_partners(rep, me):
    return [(rep ^ 1, me), (rep ^ 2, me)]


ANY = pl.BlockSpec(memory_space=pl.ANY)
IN_VMEM = pl.BlockSpec(memory_space=pltpu.VMEM)


def first_kernel(shards, parts, tokens, seg, *refs):
    rep, me = place()
    count = len(parts)
    weights, (tokens_all, seg_all, qkv_m, tokens_v) = refs[:count], refs[count : count + 4]
    held, held_sem, sems = refs[count + 4 : 2 * count + 4], refs[2 * count + 4], refs[2 * count + 5 :]
    take = pltpu.make_async_copy(tokens, tokens_v, held_sem.at[count, 0])
    take.start()
    greet(plane_partners(rep, me, shards) + pair_partners(rep, me))
    at, spreads = 0, []
    for weight, part, i in zip(weights, parts, range(count)):
        full = qkv_m.at[:, pl.ds(at, part)]
        spreads.append(
            Spread(
                shards, weight, full, column_block(part), *sems[2 * i : 2 * i + 2],
                held[i], held_sem.at[i],
            )
        )
        at += part
    sems = sems[2 * count :]
    rows = Gather(shards, tokens_v, tokens_all, *sems[:3])
    seg_send, seg_recv, seg_local = sems[3:]
    segs = [
        remote(seg, seg_all.at[me], seg_send, seg_recv, i, rep, me ^ (i + 1))
        for i in range(shards - 1)
    ]
    for spread in spreads:
        spread.start()
    for copy in segs:
        copy.start()
    take.wait()
    rows.start()
    own_seg = pltpu.make_async_copy(seg, seg_all.at[me], seg_local)
    own_seg.start()
    for spread in spreads:
        spread.hand_on()
    rows.hand_on()
    for spread in spreads:
        spread.hand_on_last()
    for spread in spreads:
        spread.finish()
    rows.finish()
    for copy in segs:
        copy.wait()
    own_seg.wait()


def first(tokens, seg, weights, shards):
    rows, width = tokens.shape
    parts = [w.shape[1] // shards for w in weights]
    n = shards - 1
    return pl.pallas_call(
        functools.partial(first_kernel, shards, parts),
        in_specs=[ANY] * (2 + len(weights)),
        out_specs=[ANY] * 3,
        out_shape=[
            jax.ShapeDtypeStruct((shards * rows, width), tokens.dtype),
            jax.ShapeDtypeStruct((shards,) + seg.shape, seg.dtype),
            jax.ShapeDtypeStruct((width, sum(parts)), BF16),
        ],
        scratch_shapes=[pltpu.VMEM(tokens.shape, BF16)]
        + [pltpu.VMEM((w.shape[0], part), BF16) for w, part in zip(weights, parts)]
        + [pltpu.SemaphoreType.DMA((len(weights) + 1, 2))]
        + len(weights) * Spread.semaphores(shards)
        + Gather.semaphores(shards)
        + [pltpu.SemaphoreType.DMA((n,)), pltpu.SemaphoreType.DMA((n,)), pltpu.SemaphoreType.DMA],
        compiler_params=pltpu.CompilerParams(
            collective_id=0, has_side_effects=True, vmem_limit_bytes=FULL
        ),
        name="first",
    )(tokens, seg, *weights)


def doc_positions(seg_ids):
    index = jnp.arange(seg_ids.shape[0], dtype=jnp.int32)
    fresh = (index == 0) | (seg_ids != jnp.roll(seg_ids, 1))
    begins = lax.cummax(jnp.where(fresh, index, jnp.zeros_like(index)), axis=0)
    return index - begins


def rope_tables(positions):
    freqs = rope_base ** (-(jnp.arange(HEAD // 2, dtype=F32) * (2.0 / HEAD)))
    angles = freqs[:, None] * positions.astype(F32)[None, :]
    return (jnp.cos(angles), jnp.sin(angles))


def side_by_side(ref, group, here):
    rows = GROUP * HEAD
    return jnp.concatenate(
        [
            ref[pl.ds(pl.multiple_of(group * rows + h * HEAD, HEAD), HEAD), here]
            for h in range(GROUP)
        ],
        axis=1,
    )


def block_bias(seg_col_ref, seg_row_ref, key_at, query_at):
    same = seg_col_ref[pl.ds(key_at, TILE), :] == seg_row_ref[:, pl.ds(query_at, TILE)]
    key_index = key_at + lax.broadcasted_iota(jnp.int32, (TILE, TILE), 0)
    query_index = query_at + lax.broadcasted_iota(jnp.int32, (TILE, TILE), 1)
    bias = jnp.where(same & (key_index <= query_index), 0.0, NEG).astype(F32)
    return jnp.concatenate([bias] * GROUP, axis=1)


def attend_kernel(
    shards, ffn_part, early, tokens, qkv_m, cot, proj_w, gate_w, up_w, gain, seg_col, seg_row,
    cos_ref, sin_ref,
    normed_out, cot_all, proj_m, gate_m, up_m, q_ref, k_ref, kt_ref, v_ref, out_ref, lse_ref,
    tokens_v, normed_v, qkv_v, turned_v, vt_ref, cot_v, load_sem, store_sem, qkv_sem, *sems,
):
    rep, me = place()
    length, width = tokens.shape
    kv_heads = k_ref.shape[0]
    q_part, kv_part = q_ref.shape[0], kt_ref.shape[0]
    blocks = length // TILE

    def first_tiles(shard):
        return pl.ds(pl.multiple_of(shard * ffn_part, ffn_part), early)

    proj = Spread(shards, proj_w, proj_m, None, *sems[:2])
    gate = Spread(shards, gate_w, gate_m, first_tiles, *sems[2:4])
    up = Spread(shards, up_w, up_m, first_tiles, *sems[4:6])
    cots = Gather(shards, cot_v, cot_all, *sems[6:9])

    def block_rows(i):
        return pl.ds(pl.multiple_of(i * TILE, TILE), TILE)

    def load(i):
        return pltpu.make_async_copy(tokens.at[block_rows(i), :], tokens_v.at[i % 2], load_sem.at[i % 2])

    def store(i):
        return pltpu.make_async_copy(
            normed_v.at[i % 2], normed_out.at[block_rows(i), :], store_sem.at[i % 2]
        )

    weights = pltpu.make_async_copy(qkv_m, qkv_v, qkv_sem.at[0])
    take = pltpu.make_async_copy(cot, cot_v, qkv_sem.at[1])
    take.start()
    weights.start()
    load(0).start()
    greet(plane_partners(rep, me, shards) + pair_partners(rep, me))
    proj.start()
    gate.start()
    up.start()
    take.wait()
    cots.start()
    weights.wait()

    def turn_weights(i, carry):
        turned_v[:, block_rows(i)] = qkv_v[block_rows(i), :].T
        return carry

    lax.fori_loop(0, width // TILE, turn_weights, 0)

    half = HEAD // 2

    def project(i, carry):
        here = block_rows(i)

        @pl.when(i + 1 < blocks)
        def _():
            load(i + 1).start()

        load(i).wait()

        @pl.when(i >= 2)
        def _():
            store(i - 2).wait()

        values = tokens_v[i % 2].astype(F32)
        rms = lax.rsqrt(jnp.mean(values * values, axis=-1, keepdims=True) + epsilon)
        normed_v[i % 2] = (values * rms * gain[...]).astype(BF16)
        store(i).start()
        heads = dot(turned_v[...], normed_v[i % 2], NT)
        cos, sin = cos_ref[:, here], sin_ref[:, here]

        def turned(at):
            first, second = heads[at : at + half], heads[at + half : at + HEAD]
            return (
                (first * cos - second * sin).astype(BF16),
                (second * cos + first * sin).astype(BF16),
            )

        for at in range(0, q_part, HEAD):
            first, second = turned(at)
            q_ref[at : at + half, here] = (first.astype(F32) * SCALE).astype(BF16)
            q_ref[at + half : at + HEAD, here] = (second.astype(F32) * SCALE).astype(BF16)
        for g in range(kv_heads):
            at = g * HEAD
            first, second = turned(q_part + at)
            kt_ref[at : at + half, here] = first
            kt_ref[at + half : at + HEAD, here] = second
            vt_ref[at : at + HEAD, here] = heads[
                q_part + kv_part + at : q_part + kv_part + at + HEAD
            ].astype(BF16)
            k_ref[g, here, :] = kt_ref[at : at + HEAD, here].T
            v_ref[g, here, :] = vt_ref[at : at + HEAD, here].T
        return carry

    lax.fori_loop(0, blocks, project, 0)
    for i in range(max(0, blocks - 2), blocks):
        store(i).wait()
    proj.hand_on()
    gate.hand_on()
    wide = GROUP * TILE

    def unit(at, carry_out):
        g, block = at // blocks, at % blocks
        query_at = pl.multiple_of(block * TILE, TILE)
        here = pl.ds(query_at, TILE)
        queries = side_by_side(q_ref, g, here)
        value_rows = pl.ds(pl.multiple_of(g * HEAD, HEAD), HEAD)

        def step(c, carry):
            top, total, acc = carry
            key_at = pl.multiple_of(c * TILE, TILE)
            keys = pl.ds(key_at, TILE)
            scores = dot(k_ref[g, keys, :], queries, NN)
            scores = scores + block_bias(seg_col, seg_row, key_at, query_at)
            new_top = jnp.maximum(top, jnp.max(scores, axis=0, keepdims=True))
            expo = jnp.exp(scores - new_top)
            fade = jnp.exp(top - new_top)
            total = total * fade + jnp.sum(expo, axis=0, keepdims=True)
            acc = acc * fade + dot(vt_ref[value_rows, keys], expo.astype(BF16), NN)
            return new_top, total, acc

        start = (
            jnp.full((1, wide), NEG, F32),
            jnp.zeros((1, wide), F32),
            jnp.zeros((HEAD, wide), F32),
        )
        top, total, acc = lax.fori_loop(0, block, step, step(block, start))
        mixed = (acc / total).astype(BF16)
        lse = top + jnp.log(total)
        for h in range(GROUP):
            at_row = pl.multiple_of(g * GROUP * HEAD + h * HEAD, HEAD)
            out_ref[pl.ds(at_row, HEAD), here] = mixed[:, h * TILE : (h + 1) * TILE]
            lse_ref[g, h : h + 1, here] = lse[:, h * TILE : (h + 1) * TILE]
        return carry_out

    units = kv_heads * blocks
    lax.fori_loop(0, units // 2, unit, 0)
    up.hand_on()
    proj.hand_on_last()
    gate.hand_on_last()
    lax.fori_loop(units // 2, units, unit, 0)
    up.hand_on_last()
    cots.hand_on()
    for transfer in (proj, gate, up, cots):
        transfer.finish()


def attend(
    tokens_all, qkv_m, cot, proj_w, gate_w, up_w, gain, seg, cos_t, sin_t, q_part, kv_part,
    early, shards,
):
    length, width = tokens_all.shape
    kv_heads = kv_part // HEAD
    part = gate_w.shape[1] // shards
    shape = jax.ShapeDtypeStruct
    dma = pltpu.SemaphoreType.DMA
    return pl.pallas_call(
        functools.partial(attend_kernel, shards, part, early),
        in_specs=[ANY] * 6 + [IN_VMEM] * 5,
        out_specs=[ANY] * 5 + [IN_VMEM] * 6,
        out_shape=[
            shape((length, width), BF16),
            shape((length, width), BF16),
            shape((shards * proj_w.shape[0], width), BF16),
            shape((width, early), BF16),
            shape((width, early), BF16),
            shape((q_part, length), BF16),
            shape((kv_heads, length, HEAD), BF16),
            shape((kv_part, length), BF16),
            shape((kv_heads, length, HEAD), BF16),
            shape((q_part, length), BF16),
            shape((kv_heads, GROUP, length), F32),
        ],
        scratch_shapes=[
            pltpu.VMEM((2, TILE, width), BF16),
            pltpu.VMEM((2, TILE, width), BF16),
            pltpu.VMEM(qkv_m.shape, BF16),
            pltpu.VMEM(qkv_m.shape[::-1], BF16),
            pltpu.VMEM((kv_part, length), BF16),
            pltpu.VMEM(cot.shape, BF16),
            dma((2,)), dma((2,)), dma((2,)),
        ]
        + 3 * Spread.semaphores(shards)
        + Gather.semaphores(shards),
        compiler_params=pltpu.CompilerParams(
            collective_id=1, has_side_effects=True, vmem_limit_bytes=FULL
        ),
        name="attend",
    )(
        tokens_all, qkv_m, cot, proj_w, gate_w, up_w, gain[None, :], seg[:, None], seg[None, :],
        cos_t, sin_t,
    )


def hidden_kernel(
    shards, mixed_t, proj_m, proj_w, cot_all, down_w, tokens, gain, hidden_ref, rms_ref, normed_all,
    grad_activ, proj_v, mixed_own, normed, cot_v, down_v, out_v, cot_sem, out_sem, proj_sem, mix_send, mix_recv, gather_send, gather_recv, local_sem,
):
    rep, me = place()
    part, _ = mixed_t.shape
    count = tokens.shape[0]
    rows = [
        pltpu.make_async_copy(
            split_rows(proj_m, me ^ i, part) if i else proj_w,
            split_rows(proj_v, me ^ i, part),
            proj_sem.at[i],
        )
        for i in range(shards)
    ]
    for copy in rows:
        copy.start()
    early = [
        pltpu.make_async_copy(cot_all, cot_v, cot_sem.at[0]),
        pltpu.make_async_copy(down_w, down_v, cot_sem.at[1]),
    ]
    for copy in early:
        copy.start()
    greet(plane_partners(rep, me, shards))

    def columns(shard):
        return mixed_t.at[:, pl.ds(pl.multiple_of(shard * count, count), count)]

    copies = [
        remote(columns(me ^ (i + 1)), mixed_own.at[i], mix_send, mix_recv, i, rep, me ^ (i + 1))
        for i in range(shards - 1)
    ]
    for copy in copies:
        copy.start()

    def product(block, i):
        rows[i].wait()
        return dot(block, split_rows(proj_v, me ^ i, part)[...], TN)

    hidden_ref[...] = tokens[...].astype(F32) + product(
        mixed_t[:, pl.ds(pl.multiple_of(me * count, count), count)], 0
    )
    for i, copy in enumerate(copies):
        copy.wait_recv()
        hidden_ref[...] += product(mixed_own[i], i + 1)
    hidden = hidden_ref[...]
    rms = lax.rsqrt(jnp.mean(hidden * hidden, axis=-1, keepdims=True) + epsilon)
    rms_ref[...] = rms
    normed[...] = (hidden * rms * gain[...]).astype(BF16)
    gather = Gather(shards, normed, normed_all, gather_send, gather_recv, local_sem)
    gather.start()
    for copy in copies:
        copy.wait_send()
    for copy in early:
        copy.wait()

    steps = down_w.shape[0] // TILE

    def store(i):
        at = pl.ds(pl.multiple_of(i * TILE, TILE), TILE)
        return pltpu.make_async_copy(out_v.at[i % 2], grad_activ.at[:, at], out_sem.at[i % 2])

    def step(i, carry):
        @pl.when(i >= 2)
        def _():
            store(i - 2).wait()

        units = down_v[pl.ds(pl.multiple_of(i * TILE, TILE), TILE), :]
        out_v[i % 2] = dot(cot_v[...], units, NT).astype(BF16)
        store(i).start()
        return carry

    lax.fori_loop(0, steps // 2, step, 0)
    gather.hand_on()
    lax.fori_loop(steps // 2, steps, step, 0)
    for i in range(max(0, steps - 2), steps):
        store(i).wait()
    gather.finish()


def hidden_layer(mixed_t, proj_m, proj_w, cot_all, down_w, tokens, gain, shards):
    part, length = mixed_t.shape
    count, width = tokens.shape
    n = shards - 1
    return pl.pallas_call(
        functools.partial(hidden_kernel, shards),
        in_specs=[IN_VMEM, ANY, ANY, ANY, ANY, IN_VMEM, IN_VMEM],
        out_specs=[IN_VMEM, IN_VMEM, ANY, ANY],
        out_shape=[
            jax.ShapeDtypeStruct((count, width), F32),
            jax.ShapeDtypeStruct((count, 1), F32),
            jax.ShapeDtypeStruct((length, width), BF16),
            jax.ShapeDtypeStruct((length, down_w.shape[0]), BF16),
        ],
        scratch_shapes=[
            pltpu.VMEM(proj_m.shape, BF16),
            pltpu.VMEM((n, part, count), BF16),
            pltpu.VMEM((count, width), BF16),
            pltpu.VMEM(cot_all.shape, BF16),
            pltpu.VMEM(down_w.shape, BF16),
            pltpu.VMEM((2, length, TILE), BF16),
            pltpu.SemaphoreType.DMA((2,)),
            pltpu.SemaphoreType.DMA((2,)),
            pltpu.SemaphoreType.DMA((shards,)),
            pltpu.SemaphoreType.DMA((n,)),
            pltpu.SemaphoreType.DMA((n,)),
        ]
        + Gather.semaphores(shards),
        compiler_params=pltpu.CompilerParams(
            collective_id=2, has_side_effects=True, vmem_limit_bytes=FULL
        ),
        name="hidden",
    )(mixed_t, proj_m, proj_w, cot_all, down_w, tokens, gain[None, :])


class Plan:
    def __init__(self, shards, reps, length, width, ffn_part, q_part, kv_part):
        self.shards, self.reps, self.length, self.width = shards, reps, length, width
        self.ffn_part, self.q_part, self.kv_part = ffn_part, q_part, kv_part
        self.layers = reps // 2
        self.half = self.layers // 2
        self.rows = width // 2
        self.own = width // shards
        self.block = self.own // 2
        self.proj_half = q_part // 2
        self.proj_blocks = self.rows // self.proj_half
        self.tiles = ffn_part // TILE
        self.out_tiles = width // TILE
        per_slot = 3
        self.back_slot = self.tiles
        self.send_slot = self.back_slot + -(-self.out_tiles // per_slot) - 1
        self.rows_slot = self.send_slot + 5
        self.pass_slot = self.rows_slot + 2
        self.mixed_slot = self.rows_slot + 4
        self.unit_slot = self.mixed_slot + 1
        self.per_slot = per_slot
        self.units = (length // TILE) * (kv_part // HEAD)
        self.norm_slot = self.unit_slot + self.units // 2
        self.tokens_slot = self.norm_slot + 5
        self.ffn_end = 3 * self.tiles
        self.q_at = max(self.ffn_end, self.norm_slot)
        self.kv_at = self.q_at + q_part // TILE
        self.proj_at = self.kv_at + 1
        self.chunks = self.proj_at + width // TILE // self.proj_blocks
        self.res_slot = max(self.ffn_end + 1, self.norm_slot + 1)
        self.res_send_slot = max(self.res_slot + self.out_tiles // 2 - 1, self.tokens_slot + 1)
        self.result_slot = self.res_send_slot + 8
        lag = 2 if self.layers == 4 else 1
        skips = [self.send_slot + 1] if self.layers == 4 else []
        more = [self.send_slot + 3] if skips else []
        self.skips = {hop: skips if hop == 1 else skips + more for hop in range(1, self.half + 1)}
        self.lag = lag
        self.most = lag + len(skips)
        self.arrive = 1 + self.most * (self.layers - 1)
        self.spread_slot = self.pass_slot
        self.hand = 6
        self.gain_slot = self.tokens_slot + 2
        self.rep_slot = max(self.chunks + self.arrive, self.gain_slot + 1)
        self.slots = max(self.chunks + self.arrive + self.hand, self.rep_slot, self.result_slot) + 1
        assert self.spread_slot + self.chunks // 2 < self.slots - self.hand
        self.mine_ring = 2 + self.most * (self.half - 1)
        self.sum_ring = self.most + 2

    def hop_chunk(self, t, hop):
        skips = self.skips.get(hop, [])
        chunk = t - 1 - self.lag * hop
        for skip in skips:
            chunk = chunk - (t >= skip).astype(jnp.int32)
        for skip in skips:
            chunk = jnp.where(t == skip, -1, chunk)
        return chunk


def backward_kernel(
    plan, early, x, cot_all, grad_activ, gate_w, up_w, gate_e, up_e, down_w, hidden, tokens, proj_w, qkv_m,
    normed,
    mlp_rms, mlp_gain, attn_gain, seg_col, seg_row, cos_ref, sin_ref, lse_ref, q_ref, mixed_ref,
    k_ref, kt_ref, v_ref,
    f_down, f_gate, f_up, f_proj, f_q, f_kv, result_ref, tokens_out, gains_out,
    swapped, from_outer, from_middle, totals, back_land, res_land, norm_land, norm_part,
    gate_m, up_m, activ, dgate, dup, back_part, res_part,
    left_a, left_b, right, gate_v, up_v, grad_v, back_v, tile_v, both, proj_v, qkv_v, hidden_v,
    row_sum, land_v,
    mine, theirs, swap_v, outer_v, middle_v, sums, total_v,
    grad_hidden, gh_own, g_t, back_t, dk_acc, dv_acc,
    gain_part, gain_land, gain_sum, gain_reps,
    load_sem, right_sem, small_sem, swap_send, swap_recv, in_send, outer_recv, middle_recv,
    out_send, total_recv, total_store, cross_recv, cross_send, pass_send, pass_recv,
    back_send, back_recv, res_send, res_recv, norm_send, norm_recv,
    gather_send, gather_recv, gather_local, gain_send, gain_recv, rep_send, rep_recv,
    tile_send, tile_recv, tile_pass, tile_passed, down_sem, back_sem, tile_sem,
):
    p = plan
    shards, reps, n = p.shards, p.reps, p.shards - 1
    rep, me = place()
    core, layer = rep % 2, rep // 2
    upper = layer >= p.half
    depth = jnp.where(upper, p.layers - 1 - layer, layer)
    inward = jnp.where(upper, rep - 2, rep + 2)
    outward = jnp.where(upper, rep + 2, rep - 2)
    is_middle = depth == p.half - 1
    count = tokens.shape[0]
    ffn_end, proj_at, q_at, kv_at, end_at = p.ffn_end, p.proj_at, p.q_at, p.kv_at, p.chunks
    gh_all = both.at[:, pl.ds(0, p.width)]

    def columns(index, size=TILE):
        return pl.ds(pl.multiple_of(index * size, size), size)

    def load(src, dst, i):
        return pltpu.make_async_copy(src, dst, load_sem.at[i])

    load_cot = load(cot_all, left_a, 0)
    load_x = load(x, left_b, 1)
    load_normed = load(normed, left_a, 2)
    load_proj = load(proj_w, proj_v, 3)
    load_qkv = load(qkv_m, qkv_v, 4)
    load_hidden = load(hidden, hidden_v, 5)
    load_activ = load(activ, left_b.at[:, pl.ds(0, p.ffn_part)], 6)
    load_tokens = load(tokens, gh_own, 7)
    first_tile = early // TILE
    assert first_tile >= 2 or p.tiles < 3

    def tile_bytes(tile, sem):
        piece = gate_m.at[pl.ds(0, 2 * n * p.block), pl.ds(0, TILE)]
        return pltpu.make_async_copy(piece, piece, sem.at[tile])

    def send_tile(tile):
        rows = columns(core, p.block)
        into = pl.ds(pl.multiple_of(me * p.own + core * p.block, p.block), p.block)
        for weight, full in ((gate_w, gate_m), (up_w, up_m)):
            for i in range(n):
                peer = me ^ (i + 1)
                at = pl.ds(pl.multiple_of(peer * p.ffn_part + tile * TILE, TILE), TILE)
                pltpu.make_async_remote_copy(
                    src_ref=weight.at[rows, at], dst_ref=full.at[into, columns(tile)],
                    send_sem=tile_send.at[tile], recv_sem=tile_recv.at[tile],
                    device_id=(rep, peer), device_id_type=MESH,
                ).start()

    def pass_tile(tile):
        tile_bytes(tile, tile_recv).wait()
        for full in (gate_m, up_m):
            for i in range(n):
                peer = me ^ (i + 1)
                at = pl.ds(pl.multiple_of(peer * p.own + core * p.block, p.block), p.block)
                piece = full.at[at, columns(tile)]
                pltpu.make_async_remote_copy(
                    src_ref=piece, dst_ref=piece,
                    send_sem=tile_pass.at[tile], recv_sem=tile_passed.at[tile],
                    device_id=(rep ^ 1, me), device_id_type=MESH,
                ).start()

    def load_grad(tile):
        return pltpu.make_async_copy(grad_activ.at[:, columns(tile)], grad_v, down_sem.at[0])

    def load_tile(tile):
        @pl.when(tile >= first_tile)
        def _():
            tile_bytes(tile, tile_passed).wait()

        own_at = pl.ds(pl.multiple_of(me * p.ffn_part + tile * TILE, TILE), TILE)
        held_rows = [pl.ds(pl.multiple_of((me ^ i) * p.own, p.own), p.own) for i in range(shards)]
        for i, (weight, tiles, full, held) in enumerate(
            ((gate_w, gate_e, gate_m, gate_v), (up_w, up_e, up_m, up_v))
        ):
            sem = down_sem.at[i + 1]
            pltpu.make_async_copy(weight.at[:, own_at], held.at[held_rows[0], :], sem).start()
            for rows in held_rows[1:]:

                @pl.when(tile < first_tile)
                def _(rows=rows, tiles=tiles, held=held, sem=sem):
                    src = tiles.at[rows, columns(tile)]
                    pltpu.make_async_copy(src, held.at[rows, :], sem).start()

                @pl.when(tile >= first_tile)
                def _(rows=rows, full=full, held=held, sem=sem):
                    src = full.at[rows, columns(tile)]
                    pltpu.make_async_copy(src, held.at[rows, :], sem).start()

        load_grad(tile).start()

    def store_tile(tile):
        dup_columns = pl.ds(pl.multiple_of(p.ffn_part + tile * TILE, TILE), TILE)
        return [
            pltpu.make_async_copy(src, dst.at[:, columns(tile)], tile_sem.at[i])
            for i, (src, dst) in enumerate(
                (
                    (tile_v.at[tile % 2], activ),
                    (both.at[:, columns(tile)], dgate),
                    (both.at[:, dup_columns], dup),
                )
            )
        ]

    def stored(tile):
        for copy in store_tile(tile):
            copy.wait()

    def ffn_tile(tile):
        for i, held in enumerate((gate_v, up_v)):
            pltpu.make_async_copy(held, held, down_sem.at[i + 1]).wait()
        load_grad(tile).wait()
        dup_columns = pl.ds(pl.multiple_of(p.ffn_part + tile * TILE, TILE), TILE)

        def go(i, carry):
            here = columns(i)
            rows = left_b[here, :]
            gate = dot(rows, gate_v[...], NN)
            up = dot(rows, up_v[...], NN)
            grad = grad_v[here, :].astype(F32)
            sigm = jax.nn.sigmoid(gate)
            swish = gate * sigm
            tile_v[tile % 2, here, :] = (swish * up).astype(BF16)
            both[here, columns(tile)] = (
                grad * up * sigm * (1.0 + gate * (1.0 - sigm))
            ).astype(BF16)
            both[here, dup_columns] = (grad * swish).astype(BF16)
            return carry

        lax.fori_loop(0, p.length // TILE, go, 0)

        @pl.when(tile >= 2)
        def _():
            stored(tile - 1)

        for copy in store_tile(tile):
            copy.start()

        @pl.when(tile == 0)
        def _():
            stored(0)

        @pl.when(tile + 1 < p.tiles)
        def _():
            load_tile(tile + 1)

    def load_back(tile):
        slot = tile % 2
        per_shard = p.own // TILE
        for i, (weight, tiles, full) in enumerate(
            ((gate_w, gate_e, gate_m), (up_w, up_e, up_m))
        ):
            sem, at = back_sem.at[slot, i], i * p.ffn_part

            @pl.when(tile // per_shard == me)
            def _(weight=weight, sem=sem, at=at):
                src = weight.at[columns(tile - me * per_shard), columns(me, p.ffn_part)]
                pltpu.make_async_copy(src, back_v.at[slot, :, pl.ds(at, p.ffn_part)], sem).start()

            @pl.when(tile // per_shard != me)
            def _(tiles=tiles, full=full, sem=sem, at=at):
                into = back_v.at[slot, :, pl.ds(at, early)]
                pltpu.make_async_copy(tiles.at[columns(tile), :], into, sem).start()
                rest = p.ffn_part - early
                into = back_v.at[slot, :, pl.ds(at + early, rest)]
                src = full.at[columns(tile), pl.ds(early, rest)]
                pltpu.make_async_copy(src, into, sem).start()

    def wait_back(tile):
        slot = tile % 2
        for i in range(2):
            half = back_v.at[slot, :, pl.ds(i * p.ffn_part, p.ffn_part)]
            pltpu.make_async_copy(half, half, back_sem.at[slot, i]).wait()

    def back_tiles(first):
        def store(tile):
            return pltpu.make_async_copy(
                tile_v.at[tile % 2], back_part.at[:, columns(tile)], tile_sem.at[tile % 2]
            )

        @pl.when(first == 0)
        def _():
            stored(p.tiles - 1)
            load_back(0)

        def tile_go(k, carry):
            tile = first + k
            wait_back(tile)

            @pl.when(tile + 1 < p.out_tiles)
            def _():
                load_back(tile + 1)

            @pl.when(k >= 2)
            def _():
                store(tile - 2).wait()

            def go(i, c):
                here = columns(i)
                tile_v[tile % 2, here, :] = dot(both[here, :], back_v[tile % 2], NT).astype(BF16)
                return c

            lax.fori_loop(0, p.length // TILE, go, 0)
            store(tile).start()
            return carry

        size = jnp.minimum(p.per_slot, p.out_tiles - first)
        lax.fori_loop(0, size, tile_go, 0)
        store(first + size - 2).wait()
        store(first + size - 1).wait()

    def load_res(tile):
        def copies(action):
            for i, held in enumerate((gate_v, up_v)):

                @pl.when(tile % 2 == i)
                def _(i=i, held=held):
                    action(
                        pltpu.make_async_copy(
                            down_w.at[:, columns(tile)], held.at[pl.ds(0, p.ffn_part), :], back_sem.at[i, 0]
                        )
                    )

        return copies

    def res_tiles(first):
        def store(tile):
            return pltpu.make_async_copy(
                tile_v.at[tile % 2], res_part.at[:, columns(tile)], tile_sem.at[tile % 2]
            )

        for k, held in enumerate((gate_v, up_v)):
            tile = first + k
            load_res(tile)(lambda copy: copy.wait())

            @pl.when(tile + 1 < p.out_tiles)
            def _(tile=tile):
                load_res(tile + 1)(lambda copy: copy.start())

            def go(i, c, k=k, held=held):
                here = columns(i)
                tile_v[k, here, :] = dot(
                    left_b[here, : p.ffn_part], held[: p.ffn_part, :], NN
                ).astype(BF16)
                return c

            lax.fori_loop(0, p.length // TILE, go, 0)
            store(tile).start()
        store(first).wait()
        store(first + 1).wait()

    def load_right(t):
        slot = right.at[t % 2]
        tile, kind = t // 3, t % 3

        def copies(action):
            for i, ref in enumerate((activ, dgate, dup)):

                @pl.when((t < ffn_end) & (kind == i))
                def _(ref=ref):
                    action(
                        pltpu.make_async_copy(
                            ref.at[:, columns(tile)], slot, right_sem.at[t % 2]
                        )
                    )

        return copies

    def scatter(part, land, sends, recvs):
        return [
            remote(split_rows(part, me ^ (i + 1), count), land.at[i], sends, recvs, i, rep, me ^ (i + 1))
            for i in range(n)
        ]

    back_rows = scatter(back_part, back_land, back_send, back_recv)
    res_rows = scatter(res_part, res_land, res_send, res_recv)
    norm_rows = scatter(norm_part, norm_land, norm_send, norm_recv)

    def fetch_rows(copies, part, land):
        for copy in copies:
            copy.wait_recv()
        pieces = [split_rows(part, me, count)] + [land.at[i] for i in range(n)]
        loads = [
            pltpu.make_async_copy(piece, land_v.at[i % 2], small_sem.at[i % 2])
            for i, piece in enumerate(pieces)
        ]
        loads[0].start()
        for i, piece in enumerate(loads):
            if i + 1 < len(loads):
                loads[i + 1].start()
            piece.wait()

            def strip(here, i=i):
                value = land_v[i % 2, here, :].astype(F32)
                row_sum[here, :] = value if i == 0 else row_sum[here, :] + value

            strips(strip)

    STRIP = 32

    def strips(body):
        def go(i, carry):
            body(pl.ds(pl.multiple_of(i * STRIP, STRIP), STRIP))
            return carry

        lax.fori_loop(0, count // STRIP, go, 0)

    def norm_strip(here, values, rms, gain, row):
        grad_in = row_sum[here, :]
        weighted = grad_in * gain
        inner = jnp.mean(weighted * values, axis=-1, keepdims=True)
        gain_part[row : row + 1, :] += jnp.sum(grad_in * values * rms, axis=0, keepdims=True)
        return rms * weighted - values * (rms * rms * rms) * inner

    gather = Gather(shards, gh_own, gh_all, gather_send, gather_recv, gather_local)

    def hidden_back():
        load_hidden.wait()
        fetch_rows(back_rows, back_part, back_land)
        gain_part[...] = jnp.zeros_like(gain_part)

        def strip(here):
            own = pl.ds(pl.multiple_of(me * count, count) + here.start, STRIP)
            grad = left_a[own, :].astype(F32) + norm_strip(
                here, hidden_v[here, :], mlp_rms[here, :], mlp_gain[...], 1
            )
            grad_hidden[here, :] = grad
            gh_own[here, :] = grad.astype(BF16)

        strips(strip)
        gather.start()

    def finish_result():
        fetch_rows(res_rows, res_part, res_land)

        def strip(here):
            row_sum[here, :] = hidden_v[here, :] + row_sum[here, :]

        strips(strip)
        store_result = pltpu.make_async_copy(row_sum, result_ref, small_sem.at[0])
        store_result.start()
        store_result.wait()

    def mixed_back():
        gather.finish()
        load_proj.wait()

        def go(i, carry):
            here = pl.ds(pl.multiple_of(i * TILE, TILE), TILE)
            g_t[:, here] = dot(proj_v[...], both[here, : p.width], NT).astype(BF16)
            return carry

        lax.fori_loop(0, p.length // TILE, go, 0)

    blocks = p.length // TILE
    rows = GROUP * HEAD
    wide = GROUP * TILE
    mid = HEAD // 2

    def attention_unit(unit):
        g, block = unit // blocks, unit % blocks
        query_at = pl.multiple_of(block * TILE, TILE)
        here_q = pl.ds(query_at, TILE)

        queries = side_by_side(q_ref, g, here_q)
        grads = side_by_side(g_t, g, here_q)
        mixed = side_by_side(mixed_ref, g, here_q)
        lse = jnp.concatenate([lse_ref[g, h : h + 1, here_q] for h in range(GROUP)], axis=1)
        inner = jnp.sum(grads.astype(F32) * mixed.astype(F32), axis=0, keepdims=True)

        @pl.when(block == 0)
        def _():
            dk_acc[...] = jnp.zeros_like(dk_acc)
            dv_acc[...] = jnp.zeros_like(dv_acc)

        def step(c, acc):
            key_at = pl.multiple_of(c * TILE, TILE)
            here = pl.ds(key_at, TILE)
            scores = dot(k_ref[g, here, :], queries, NN)
            scores = scores + block_bias(seg_col, seg_row, key_at, query_at)
            probs = jnp.exp(scores - lse)
            grad_probs = dot(v_ref[g, here, :], grads, NN)
            grad_scores = (probs * (grad_probs - inner)).astype(BF16)
            dv_acc[:, here] += dot(grads, probs.astype(BF16), NT)
            dk_acc[:, here] += dot(queries, grad_scores, NT)
            key_rows = pl.ds(pl.multiple_of(g * HEAD, HEAD), HEAD)
            return acc + dot(kt_ref[key_rows, here], grad_scores, NN)

        acc = lax.fori_loop(0, block + 1, step, jnp.zeros((HEAD, wide), F32))
        cos, sin = cos_ref[:, here_q], sin_ref[:, here_q]
        for h in range(GROUP):
            grad = acc[:, h * TILE : (h + 1) * TILE] * SCALE
            first, second = grad[:mid], grad[mid:]
            at = pl.multiple_of(g * rows + h * HEAD, HEAD)
            back_t[pl.ds(at, mid), here_q] = (first * cos + second * sin).astype(BF16)
            back_t[pl.ds(at + mid, mid), here_q] = (second * cos - first * sin).astype(BF16)

        @pl.when(block == blocks - 1)
        def _():
            cos, sin = cos_ref[...], sin_ref[...]
            first, second = dk_acc[:mid, :], dk_acc[mid:, :]
            at = pl.multiple_of(p.q_part + g * HEAD, HEAD)
            back_t[pl.ds(at, mid), :] = (first * cos + second * sin).astype(BF16)
            back_t[pl.ds(at + mid, mid), :] = (second * cos - first * sin).astype(BF16)
            at = pl.multiple_of(p.q_part + p.kv_part + g * HEAD, HEAD)
            back_t[pl.ds(at, HEAD), :] = dv_acc[...].astype(BF16)

    def normed_back():
        load_qkv.wait()

        stores = [
            pltpu.make_async_copy(
                land_v.at[i % 2], norm_part.at[pl.ds(i * count, count), :], small_sem.at[i % 2]
            )
            for i in range(shards)
        ]
        for i, store in enumerate(stores):
            if i >= 2:
                stores[i - 2].wait()
            here = pl.ds(i * count, count)
            land_v[i % 2] = dot(back_t[:, here].T, qkv_v[...], NT).astype(BF16)
            store.start()
        for store in stores[-2:]:
            store.wait()
        for copy in norm_rows:
            copy.start()

    gain_cols = p.width // shards

    def gain_slice(shard):
        return pl.ds(pl.multiple_of(shard * gain_cols, gain_cols), gain_cols)

    gain_plane = [
        remote(
            gain_part.at[:, gain_slice(me ^ (i + 1))], gain_land.at[me],
            gain_send, gain_recv, i, rep, me ^ (i + 1),
        )
        for i in range(n)
    ]
    gain_all = [
        remote(gain_sum, gain_reps.at[rep], rep_send, rep_recv, i, rep ^ (i + 1), me)
        for i in range(reps - 1)
    ]

    def tokens_back():
        load_tokens.start()
        load_tokens.wait()
        fetch_rows(norm_rows, norm_part, norm_land)

        def strip(here):
            values = gh_own[here, :].astype(F32)
            rms = lax.rsqrt(jnp.mean(values * values, axis=-1, keepdims=True) + epsilon)
            grad_hidden[here, :] += norm_strip(here, values, rms, attn_gain[...], 0)

        strips(strip)
        store_tokens = pltpu.make_async_copy(grad_hidden, tokens_out, small_sem.at[0])
        store_tokens.start()
        store_tokens.wait()
        gain_land[me] = gain_part[:, gain_slice(me)]
        for copy in gain_plane:
            copy.start()

    def gains_plane():
        for copy in gain_plane:
            copy.wait_recv()
        total = gain_land[0]
        for s in range(1, shards):
            total = total + gain_land[s]
        gain_sum[...] = total
        gain_reps[rep] = total
        for copy in gain_all:
            copy.start()

    def gains_reps():
        for copy in gain_all:
            copy.wait_recv()
        total = gain_reps[0]
        for r in range(1, reps):
            total = total + gain_reps[r]
        gains_out[...] = total

    def swap_copy(j):
        return pltpu.make_async_remote_copy(
            src_ref=theirs.at[j % 2], dst_ref=swapped.at[j],
            send_sem=swap_send.at[j % 2], recv_sem=swap_recv.at[j],
            device_id=(rep ^ 1, me), device_id_type=MESH,
        )

    def store_chunk(slot, other_slot, at, size, product, columns=TILE):
        here = pl.ds(pl.multiple_of(at, size), size)
        mine[slot, here, :columns] = product(core).astype(BF16)
        theirs[other_slot, here, :columns] = product(1 - core).astype(BF16)

    def make(t):
        slot, other = t % p.mine_ring, t % 2

        @pl.when(t >= 2)
        def _():
            swap_copy(t - 2).wait_send()

        @pl.when(t == 0)
        def _():
            load_right(0)(lambda copy: copy.start())

        load_right(t)(lambda copy: copy.wait())

        @pl.when(t + 1 < ffn_end)
        def _():
            load_right(t + 1)(lambda copy: copy.start())

        @pl.when((t < ffn_end) & (t % 3 == 0))
        def _():
            left = right[t % 2].T

            def go(i, carry):
                def product(which):
                    at = pl.multiple_of(which * p.rows + i * TILE, TILE)
                    return dot(left, left_a[:, pl.ds(at, TILE)], NN)

                store_chunk(slot, other, i * TILE, TILE, product)
                return carry

            lax.fori_loop(0, p.rows // TILE, go, 0)

        def wide_chunk(left, factor, columns):
            def go(s, carry):
                def product(which):
                    at = pl.multiple_of(s * p.own + which * p.block, p.block)
                    return dot(factor, left[:, pl.ds(at, p.block)], NN).T

                store_chunk(slot, other, s * p.block, p.block, product, columns)
                return carry

            lax.fori_loop(0, shards, go, 0)

        @pl.when((t < ffn_end) & (t % 3 > 0))
        def _():
            wide_chunk(left_b, right[t % 2].T, TILE)

        @pl.when((t >= proj_at) & (t < end_at))
        def _():
            def go(i, carry):
                at = columns((t - proj_at) * p.proj_blocks + i)

                def product(which):
                    part = columns(which, p.proj_half)
                    return dot(mixed_ref[part, :], both[:, at], NN)

                store_chunk(slot, other, i * p.proj_half, p.proj_half, product)
                return carry

            lax.fori_loop(0, p.proj_blocks, go, 0)

        @pl.when((t >= q_at) & (t < kv_at))
        def _():
            wide_chunk(left_a, back_t[columns(t - q_at), :], TILE)

        @pl.when(t == kv_at)
        def _():
            wide_chunk(left_a, back_t[p.q_part :, :], 2 * p.kv_part)

        swap_copy(t).start()

    def inward_copies(j):
        common = dict(
            src_ref=sums.at[j % p.sum_ring], send_sem=in_send.at[j % p.sum_ring],
            device_id=(inward, me), device_id_type=MESH,
        )
        to_layer = pltpu.make_async_remote_copy(
            dst_ref=from_outer.at[j], recv_sem=outer_recv.at[j], **common
        )
        to_middle = pltpu.make_async_remote_copy(
            dst_ref=from_middle.at[j], recv_sem=middle_recv.at[j], **common
        )
        return to_layer, to_middle

    def total_places(j, action):
        @pl.when(is_chunk(j, 0))
        def _():
            action(
                [
                    (
                        i * TILE, TILE, TILE,
                        f_down.at[
                            columns(j // 3),
                            pl.ds(pl.multiple_of(core * p.rows + i * TILE, TILE), TILE),
                        ],
                    )
                    for i in range(p.rows // TILE)
                ]
            )

        @pl.when((j >= proj_at) & (j < end_at))
        def _():
            action(
                [
                    (
                        i * p.proj_half, p.proj_half, TILE,
                        f_proj.at[
                            columns(core, p.proj_half),
                            columns((j - proj_at) * p.proj_blocks + i),
                        ],
                    )
                    for i in range(p.proj_blocks)
                ]
            )

        for when, full, part, tile, sem, wide_by in wide_kinds(j):

            @pl.when(when)
            def _(full=full, part=part, tile=tile, wide_by=wide_by):
                blocks = []
                for i in range(shards):
                    at = pl.multiple_of((me ^ i) * p.block, p.block)
                    place_there = totals.at[j, pl.ds(at, p.block), pl.ds(0, wide_by)]
                    if i == 0:
                        place_there = window(full, me, part, tile, wide_by)
                    blocks.append((at, p.block, wide_by, place_there))
                action(blocks)

    def chunk_bytes(j, sem):
        @pl.when(j == kv_at)
        def _():
            whole = totals.at[0, :, pl.ds(0, 2 * p.kv_part)]
            pltpu.make_async_copy(whole, whole, sem).wait()

        @pl.when(j != kv_at)
        def _():
            whole = totals.at[0]
            pltpu.make_async_copy(whole, whole, sem).wait()

    def send_total(src, dst, j):
        return pltpu.make_async_remote_copy(
            src_ref=src, dst_ref=dst, send_sem=out_send.at[j % 2],
            recv_sem=total_recv.at[j], device_id=(outward, me), device_id_type=MESH,
        )

    def add_rows(body):
        def go(i, carry):
            body(pl.ds(pl.multiple_of(i * TILE, TILE), TILE))
            return carry

        lax.fori_loop(0, p.rows // TILE, go, 0)

    def load_swapped(j):
        return pltpu.make_async_copy(swapped.at[j], swap_v, small_sem.at[2])

    def load_outer(j):
        return pltpu.make_async_copy(from_outer.at[j], outer_v, small_sem.at[3])

    def load_middle(j):
        return pltpu.make_async_copy(from_middle.at[j], middle_v, small_sem.at[4])

    def valid(j):
        return (j >= 0) & (j < p.chunks)

    def take_inward(j):
        @pl.when(valid(j))
        def _():
            swap_copy(j).wait_recv()
            load_swapped(j).start()

            @pl.when(depth > 0)
            def _():
                inward_copies(j)[0].wait_recv()
                load_outer(j).start()

    def send_inward(j):
        @pl.when(valid(j))
        def _():
            @pl.when(j >= p.sum_ring)
            def _():
                inward_copies(j - p.sum_ring)[0].wait_send()

            load_swapped(j).wait()
            ours = mine.at[j % p.mine_ring]
            total = sums.at[j % p.sum_ring]

            @pl.when(depth > 0)
            def _():
                load_outer(j).wait()

                def add(here):
                    total[here, :] = (
                        ours[here, :].astype(F32)
                        + swap_v[here, :].astype(F32)
                        + outer_v[here, :].astype(F32)
                    ).astype(BF16)

                add_rows(add)

            @pl.when(depth == 0)
            def _():
                def add(here):
                    total[here, :] = (
                        ours[here, :].astype(F32) + swap_v[here, :].astype(F32)
                    ).astype(BF16)

                add_rows(add)

            to_layer, to_middle = inward_copies(j)

            @pl.when(is_middle)
            def _():
                to_middle.start()

            @pl.when(jnp.logical_not(is_middle))
            def _():
                to_layer.start()

    def take_middle(j):
        @pl.when(is_middle & valid(j))
        def _():
            inward_copies(j)[1].wait_recv()
            load_middle(j).start()

    def meet_in_middle(j):
        @pl.when(is_middle & valid(j))
        def _():
            @pl.when(j >= 1)
            def _():
                chunk_bytes(j - 1, total_store.at[0])

            if p.half > 1:

                @pl.when(j >= 2)
                def _():
                    chunk_bytes(j - 2, out_send.at[j % 2])

            load_middle(j).wait()
            out, held = total_v.at[j % 2], sums.at[j % p.sum_ring]

            def add(here):
                out[here, :] = (
                    held[here, :].astype(F32) + middle_v[here, :].astype(F32)
                ).astype(BF16)

            add_rows(add)

            def put(blocks):
                for at, size, wide_by, dst in blocks:
                    src = out.at[pl.ds(at, size), pl.ds(0, wide_by)]
                    if p.half > 1:
                        send_total(src, dst, j).start()
                    pltpu.make_async_copy(src, dst, total_store.at[0]).start()

            total_places(j, put)

    def last_store(t):
        @pl.when(is_middle & (t == p.chunks + p.arrive - 1))
        def _():
            chunk_bytes(p.chunks - 1, total_store.at[0])

    def send_outward(j):
        @pl.when(jnp.logical_not(is_middle) & valid(j))
        def _():
            chunk_bytes(j, total_recv.at[j])

            if p.half > 2:

                @pl.when(depth > 0)
                def _():
                    @pl.when(j >= 2)
                    def _():
                        chunk_bytes(j - 2, out_send.at[j % 2])

                    def put(blocks):
                        for _, _, _, dst in blocks:
                            send_total(dst, dst, j).start()

                    total_places(j, put)

    def remote_pass(src, dst, sem):
        return pltpu.make_async_remote_copy(
            src_ref=src, dst_ref=dst, send_sem=pass_send.at[sem], recv_sem=pass_recv.at[sem],
            device_id=(rep ^ 1, me), device_id_type=MESH,
        )

    def window(full, shard, part, tile, columns=TILE):
        at = pl.multiple_of(shard * part + tile * columns, columns)
        return full.at[pl.ds(pl.multiple_of(core * p.block, p.block), p.block), pl.ds(at, columns)]

    def is_chunk(j, kind):
        return (j >= 0) & (j < ffn_end) & (j % 3 == kind)

    def wide_kinds(j):
        return (
            (is_chunk(j, 1), f_gate, p.ffn_part, j // 3, 1, TILE),
            (is_chunk(j, 2), f_up, p.ffn_part, j // 3, 2, TILE),
            ((j >= q_at) & (j < kv_at), f_q, p.q_part, j - q_at, 4, TILE),
            (j == kv_at, f_kv, 2 * p.kv_part, 0, 5, 2 * p.kv_part),
        )

    def spread_total(j):
        for kind, sem in ((is_chunk(j, 0), 0), ((j >= proj_at) & (j < end_at), 3)):

            @pl.when(kind)
            def _(sem=sem):
                def put(blocks):
                    for _, _, _, dst in blocks:
                        remote_pass(dst, dst, sem).start()

                total_places(j, put)

        for when, full, part, tile, sem, wide_by in wide_kinds(j):

            @pl.when(when)
            def _(full=full, part=part, tile=tile, sem=sem, wide_by=wide_by):
                place_here = window(full, me, part, tile, wide_by)
                for i in range(n):
                    at = columns(me ^ (i + 1), p.block)
                    pltpu.make_async_remote_copy(
                        src_ref=totals.at[j, at, pl.ds(0, wide_by)], dst_ref=place_here,
                        send_sem=cross_send.at[sem], recv_sem=cross_recv.at[j],
                        device_id=(rep, me ^ (i + 1)), device_id_type=MESH,
                    ).start()
                remote_pass(place_here, place_here, sem).start()

    def pass_on(j):
        for when, full, part, tile, sem, wide_by in wide_kinds(j):

            @pl.when(when)
            def _(full=full, part=part, tile=tile, sem=sem, wide_by=wide_by):
                came = totals.at[j, pl.ds(0, n * p.block), pl.ds(0, wide_by)]
                pltpu.make_async_copy(came, came, cross_recv.at[j]).wait()
                for i in range(n):
                    here = window(full, me ^ (i + 1), part, tile, wide_by)
                    remote_pass(here, here, sem).start()

    for copy in (load_x, load_cot):
        copy.start()
    load_tile(0)
    greet(plane_partners(rep, me, shards) + [(rep ^ i, me) for i in range(1, reps)])
    ahead = 3
    for tile in range(first_tile, min(first_tile + ahead, p.tiles)):
        send_tile(tile)
    for copy in (load_hidden, load_proj, load_qkv):
        copy.start()
    for copy in (load_x, load_cot):
        copy.wait()

    def slot(t, carry):
        inner = t - 1
        for hop in range(1, p.half):
            inner = jnp.where(depth == hop, p.hop_chunk(t, hop), inner)
        met = p.hop_chunk(t, p.half)
        take_inward(inner)
        take_middle(met)
        send_inward(inner)
        meet_in_middle(met)
        send_outward(t - p.arrive + p.most * depth)

        def spread_until(u):
            ready = jnp.minimum(u - p.arrive + 1, p.chunks)
            return jnp.maximum(jnp.minimum(ready, 2 * (u - p.spread_slot + 1)), 0)

        def over(action, u):
            def go(j, c):
                action(j)
                return c

            lax.fori_loop(spread_until(u - 1), spread_until(u), go, 0)

        last_store(t)
        over(spread_total, t)
        over(pass_on, t - p.hand)

        @pl.when(t + first_tile + ahead < p.tiles)
        def _():
            send_tile(t + first_tile + ahead)

        @pl.when((t > 0) & (t + 1 >= first_tile) & (t + 1 < p.tiles))
        def _():
            pass_tile(t + 1)

        @pl.when(t < p.tiles)
        def _():
            ffn_tile(t)

        @pl.when((t >= p.back_slot) & (t <= p.send_slot))
        def _():
            back_tiles((t - p.back_slot) * p.per_slot)

        @pl.when(t == ffn_end)
        def _():
            load_normed.start()
            load_activ.start()

        @pl.when(t == q_at)
        def _():
            load_normed.wait()

        def at(when, action):
            @pl.when(t == when)
            def _():
                action()

        def start_rows(copies):
            for copy in copies:
                copy.start()

        at(p.send_slot, lambda: start_rows(back_rows))
        at(p.rows_slot, hidden_back)
        at(p.pass_slot, gather.hand_on)
        at(p.mixed_slot, mixed_back)

        @pl.when((t >= p.unit_slot) & (t < p.norm_slot))
        def _():
            def go(i, c):
                attention_unit((t - p.unit_slot) * 2 + i)
                return c

            lax.fori_loop(0, 2, go, 0)

        at(p.norm_slot, normed_back)

        @pl.when(t < p.chunks)
        def _():
            make(t)

        at(p.tokens_slot, tokens_back)
        at(p.gain_slot, gains_plane)
        at(p.rep_slot, gains_reps)

        @pl.when((t >= p.res_slot) & (t < p.res_slot + p.out_tiles // 2))
        def _():
            @pl.when(t == p.res_slot)
            def _():
                load_activ.wait()
                load_res(0)(lambda copy: copy.start())

            res_tiles((t - p.res_slot) * 2)

        at(p.res_send_slot, lambda: start_rows(res_rows))
        at(p.result_slot, finish_result)
        return carry

    lax.fori_loop(0, p.slots, slot, 0)

    for j in range(max(0, p.chunks - 2), p.chunks):
        swap_copy(j).wait_send()
    for j in range(max(0, p.chunks - p.sum_ring), p.chunks):
        inward_copies(j)[0].wait_send()
    if p.half > 1:

        @pl.when(depth > 0)
        def _():
            for j in range(max(0, p.chunks - 2), p.chunks):
                chunk_bytes(j, out_send.at[j % 2])

    for copies in (back_rows, res_rows, norm_rows, gain_plane, gain_all):
        for copy in copies:
            copy.wait_send()

    def settle(ref, sem):
        pltpu.make_async_copy(ref, ref, sem).wait()

    for tile in range(first_tile, p.tiles):
        tile_bytes(tile, tile_send).wait()
        tile_bytes(tile, tile_pass).wait()
    for sem, part in (
        (0, f_down.at[:, pl.ds(0, p.rows)]),
        (3, f_proj.at[pl.ds(0, p.proj_half), :]),
    ):
        settle(part, pass_send.at[sem])
        settle(part, pass_recv.at[sem])
    for _, full, part, _, sem, _ in wide_kinds(0):
        here = full.at[pl.ds(0, p.block), :]
        settle(here, pass_send.at[sem])
        settle(here, pass_recv.at[sem])
        settle(full.at[pl.ds(0, p.block), pl.ds(0, n * part)], cross_send.at[sem])


def backward(
    shards, reps, x, cot_all, grad_activ, gate_w, up_w, gate_e, up_e, down_w, hidden, tokens, proj_w,
    qkv_m, normed, mlp_rms, mlp_gain, attn_gain, seg, cos_t, sin_t, lse, q_t, mixed_t, k, k_t, v,
):
    length, width = x.shape
    count = tokens.shape[0]
    ffn_part = down_w.shape[0]
    q_part, kv_part = q_t.shape[0], k_t.shape[0]
    n = shards - 1
    p = Plan(shards, reps, length, width, ffn_part, q_part, kv_part)
    shape = jax.ShapeDtypeStruct
    own = width // shards
    chunk = (p.rows, TILE)
    dma = pltpu.SemaphoreType.DMA
    return pl.pallas_call(
        functools.partial(backward_kernel, p, gate_e.shape[1]),
        in_specs=[ANY] * 13 + [IN_VMEM] * 13,
        out_specs=[ANY] * 8 + [IN_VMEM] + [ANY] * 15,
        out_shape=[
            shape((ffn_part, width), BF16),
            shape((own, shards * ffn_part), BF16),
            shape((own, shards * ffn_part), BF16),
            shape((q_part, width), BF16),
            shape((own, shards * q_part), BF16),
            shape((own, shards * 2 * kv_part), BF16),
            shape((count, width), F32),
            shape((count, width), F32),
            shape((8, width // shards), F32),
        ]
        + [shape((p.chunks,) + chunk, BF16)] * 4
        + [shape((n, count, width), BF16)] * 3
        + [shape((length, width), BF16)]
        + [shape((width, ffn_part), BF16)] * 2
        + [shape((length, ffn_part), BF16)] * 3
        + [shape((length, width), BF16)] * 2,
        scratch_shapes=[
            pltpu.VMEM((length, width), BF16),
            pltpu.VMEM((length, width), BF16),
            pltpu.VMEM((2, length, TILE), BF16),
            pltpu.VMEM((width, TILE), BF16),
            pltpu.VMEM((width, TILE), BF16),
            pltpu.VMEM((length, TILE), BF16),
            pltpu.VMEM((2, TILE, 2 * ffn_part), BF16),
            pltpu.VMEM((2, length, TILE), BF16),
            pltpu.VMEM((length, 2 * ffn_part), BF16),
            pltpu.VMEM(proj_w.shape, BF16),
            pltpu.VMEM(qkv_m.shape, BF16),
            pltpu.VMEM((count, width), F32),
            pltpu.VMEM((count, width), F32),
            pltpu.VMEM((2, count, width), BF16),
            pltpu.VMEM((p.mine_ring,) + chunk, BF16),
            pltpu.VMEM((2,) + chunk, BF16),
            pltpu.VMEM(chunk, BF16),
            pltpu.VMEM(chunk, BF16),
            pltpu.VMEM(chunk, BF16),
            pltpu.VMEM((p.sum_ring,) + chunk, BF16),
            pltpu.VMEM((2,) + chunk, BF16),
            pltpu.VMEM((count, width), F32),
            pltpu.VMEM((count, width), BF16),
            pltpu.VMEM((q_part, length), BF16),
            pltpu.VMEM((q_part + 2 * kv_part, length), BF16),
            pltpu.VMEM((HEAD, length), F32),
            pltpu.VMEM((HEAD, length), F32),
            pltpu.VMEM((8, width), F32),
            pltpu.VMEM((shards, 8, own), F32),
            pltpu.VMEM((8, own), F32),
            pltpu.VMEM((reps, 8, own), F32),
            dma((12,)), dma((2,)), dma((5,)), dma((2,)), dma((p.chunks,)), dma((p.sum_ring,)),
            dma((p.chunks,)), dma((p.chunks,)), dma((2,)), dma((p.chunks,)), dma((2,)),
            dma((p.chunks,)), dma((6,)), dma((6,)), dma((6,)),
            dma((n,)), dma((n,)), dma((n,)), dma((n,)), dma((n,)), dma((n,)),
        ]
        + Gather.semaphores(shards)
        + [dma((n,)), dma((n,)), dma((reps - 1,)), dma((reps - 1,))]
        + [dma((p.tiles,))] * 4
        + [dma((3,)), dma((2, 2)), dma((3,))],
        compiler_params=pltpu.CompilerParams(
            collective_id=3, has_side_effects=True, vmem_limit_bytes=FULL
        ),
        name="backward",
    )(
        x, cot_all, grad_activ, gate_w, up_w, gate_e, up_e, down_w, hidden, tokens, proj_w,
        qkv_m, normed, mlp_rms, mlp_gain[None, :], attn_gain[None, :], seg[:, None], seg[None, :],
        cos_t, sin_t, lse, q_t, mixed_t, k, k_t, v,
    )[:9]


def widen_kernel(count, rows, columns, *refs):
    srcs, dsts = refs[:count], refs[count : 2 * count]
    narrow, wide, in_sem, out_sem = refs[2 * count :]
    depth = narrow.shape[0]
    loads, stores = [], []
    for src, dst in zip(srcs, dsts):
        for r in range(src.shape[0] // rows):
            for c in range(src.shape[1] // columns):
                at = (pl.ds(r * rows, rows), pl.ds(c * columns, columns))
                slot = len(loads) % depth
                direct = src.dtype == dst.dtype
                into = wide.at[slot] if direct else narrow.at[slot]
                loads.append(pltpu.make_async_copy(src.at[at], into, in_sem.at[slot]))
                stores.append(
                    (pltpu.make_async_copy(wide.at[slot], dst.at[at], out_sem.at[slot]), direct)
                )
    total = len(loads)
    ahead = depth - 1

    def load(i):
        if stores[i][1] and i >= depth:
            stores[i - depth][0].wait()
        loads[i].start()

    for i in range(min(ahead, total)):
        load(i)
    for i in range(total):
        slot = i % depth
        store, direct = stores[i]
        loads[i].wait()
        if not direct:
            if i >= depth:
                stores[i - depth][0].wait()
            for strip in range(0, rows, 64):
                wide[slot, pl.ds(strip, 64), :] = narrow[slot, pl.ds(strip, 64), :].astype(F32)
        store.start()
        if i + ahead < total:
            load(i + ahead)
    for i in range(max(0, total - depth), total):
        stores[i][0].wait()


def widen(arrays):
    rows, columns, depth = 256, 2048, 4
    rows = min([rows] + [a.shape[0] for a in arrays])
    shapes = [jax.ShapeDtypeStruct(a.shape, F32) for a in arrays]
    return pl.pallas_call(
        functools.partial(widen_kernel, len(arrays), rows, columns),
        in_specs=[ANY] * len(arrays),
        out_specs=[ANY] * len(arrays),
        out_shape=shapes,
        scratch_shapes=[
            pltpu.VMEM((depth, rows, columns), BF16),
            pltpu.VMEM((depth, rows, columns), F32),
            pltpu.SemaphoreType.DMA((depth,)),
            pltpu.SemaphoreType.DMA((depth,)),
        ],
        compiler_params=pltpu.CompilerParams(vmem_limit_bytes=FULL),
        name="widen",
    )(*arrays)


def local(
    tokens, segments, query_w, key_w, value_w, proj_w, attn_gain,
    gate_w, up_w, down_w, mlp_gain, cotangent,
):
    shards = lax.axis_size("shard")
    reps = lax.axis_size("rep")
    tok_count, width = tokens.shape
    kv_part = key_w.shape[1] // shards
    q_part = query_w.shape[1] // shards
    length = tok_count * shards

    if kv_part % 128:
        kv_w = jnp.concatenate(
            [
                w[:, s * kv_part : (s + 1) * kv_part]
                for s in range(shards)
                for w in (key_w, value_w)
            ],
            axis=1,
        )
        weights = (query_w, kv_w)
    else:
        weights = (query_w, key_w, value_w)
    tokens_all, seg, qkv_m = first(tokens, segments[None, :], weights, shards)
    seg = seg.reshape(length)
    cos_t, sin_t = rope_tables(doc_positions(seg))
    early = min(2 * TILE, down_w.shape[0] // 2)
    normed, cot_all, proj_m, gate_e, up_e, q_t, k, k_t, v, mixed_t, lse = attend(
        tokens_all, qkv_m, cotangent, proj_w, gate_w, up_w, attn_gain, seg, cos_t, sin_t,
        q_part, kv_part, early, shards,
    )
    hidden, mlp_rms, normed_mlp, grad_activ = hidden_layer(
        mixed_t, proj_m, proj_w, cot_all, down_w, tokens, mlp_gain, shards
    )
    down, gate, up, proj, query, kv, result, grad_tokens, gains = backward(
        shards, reps, normed_mlp, cot_all, grad_activ, gate_w, up_w, gate_e, up_e, down_w, hidden, tokens,
        proj_w, qkv_m, normed, mlp_rms, mlp_gain, attn_gain, seg, cos_t, sin_t, lse, q_t,
        mixed_t, k, k_t, v,
    )

    def every_other(first):
        parts = [
            kv[:, (2 * s + first) * kv_part : (2 * s + first + 1) * kv_part] for s in range(shards)
        ]
        return jnp.concatenate(parts, axis=1).astype(F32)

    gate, up, down, query, proj, result, grad_tokens = widen(
        [gate, up, down, query, proj, result, grad_tokens]
    )
    return (
        result, grad_tokens, query, every_other(0), every_other(1), proj, gains[0], gate, up, down,
        gains[1],
    )


def solution(mesh):
    rows = P(("rep", "shard"), None)
    held = P("shard", None)
    in_specs = (
        rows, P(("rep", "shard")), held, held, held, held, P(), held, held, held, P(), rows,
    )
    out_specs = (
        rows, rows, held, held, held, held, P("shard"), held, held, held, P("shard"),
    )
    return jax.shard_map(local, mesh=mesh, in_specs=in_specs, out_specs=out_specs, check_vma=False)
```

```python
import functools
import math

import jax
import jax.numpy as jnp
from jax import lax
from jax.experimental import pallas as pl
from jax.experimental.pallas import tpu as pltpu
from jax.sharding import PartitionSpec as P

HEADS = 32
KV_HEADS = 8
HEAD = 64
GROUP = HEADS // KV_HEADS
SCALE = 1.0 / math.sqrt(HEAD)
TILE = 256
ROWS = 512
NEG = -1e30
MIB = 1024 * 1024
FULL = 63 * MIB + MIB // 2

epsilon = 1e-05
rope_base = 500000.0
F32 = jnp.float32
BF16 = jnp.bfloat16


def dot(left, right, dims):
    return lax.dot_general(left, right, (dims, ((), ())), preferred_element_type=F32)


NN = ((1,), (0,))
NT = ((1,), (1,))
TN = ((0,), (0,))
TT = ((0,), (1,))


MESH = pl.DeviceIdType.MESH


def place():
    return lax.axis_index("rep"), lax.axis_index("shard")


def remote(src, dst, sends, recvs, index, rep, shard):
    return pltpu.make_async_remote_copy(
        src_ref=src,
        dst_ref=dst,
        send_sem=sends.at[index],
        recv_sem=recvs.at[index],
        device_id=(rep, shard),
        device_id_type=MESH,
    )


def greet(partners):
    barrier = pltpu.get_barrier_semaphore()
    for partner in partners:
        pl.semaphore_signal(barrier, inc=1, device_id=partner, device_id_type=MESH)
    pl.semaphore_wait(barrier, len(partners))


def plane_partners(rep, me, shards):
    return [(rep, me ^ step) for step in range(1, shards)]


class Spread:
    def __init__(self, shards, own, full, columns, sends, recvs, held=None, held_sem=None):
        rep, me = place()
        quarter = rep % 4
        count = own.shape[0]
        part = count // 4
        own_rows = pl.ds(pl.multiple_of(quarter * part, part), part)

        def at(shard, which):
            return full.at[pl.ds(pl.multiple_of(shard * count + which * part, part), part), :]

        def piece(shard):
            return own.at[own_rows, :] if columns is None else own.at[own_rows, columns(shard)]

        self.first, self.core, self.layer, self.last = [], [], [], []
        n = shards - 1
        for i in range(n):
            peer = me ^ (i + 1)
            self.first.append(remote(piece(peer), at(me, quarter), sends, recvs, i, rep, peer))
            mine = at(peer, quarter)
            self.core.append(remote(mine, mine, sends, recvs, n + i, rep ^ 1, me))
            self.layer.append(remote(mine, mine, sends, recvs, 2 * n + i, rep ^ 2, me))
            theirs = at(peer, quarter ^ 2)
            self.last.append(remote(theirs, theirs, sends, recvs, 3 * n + i, rep ^ 1, me))
        self.take = self.keep = None
        if held is not None:
            kept = full.at[pl.ds(pl.multiple_of(me * count, count), count), :]
            self.take = pltpu.make_async_copy(own.at[:, columns(me)], held, held_sem.at[0])
            self.keep = pltpu.make_async_copy(held, kept, held_sem.at[1])

    def start(self):
        for copy in self.first:
            copy.start()
        if self.take is not None:
            self.take.start()

    def hand_on(self):
        if self.take is not None:
            self.take.wait()
            self.keep.start()
        for i, copy in enumerate(self.first):
            copy.wait_recv()
            self.layer[i].start()
            self.core[i].start()

    def hand_on_last(self):
        for i, copy in enumerate(self.layer):
            copy.wait_recv()
            self.last[i].start()

    def finish(self):
        for copy in self.core + self.last:
            copy.wait_recv()
        for copy in self.first + self.core + self.layer + self.last:
            copy.wait_send()
        if self.keep is not None:
            self.keep.wait()

    @staticmethod
    def semaphores(shards):
        n = 4 * (shards - 1)
        return [pltpu.SemaphoreType.DMA((n,)), pltpu.SemaphoreType.DMA((n,))]


class Gather:
    def __init__(self, shards, own, full, sends, recvs, local_sem=None):
        rep, me = place()
        count = own.shape[0]
        half = count // 2

        def at(shard, start, size):
            return full.at[pl.ds(pl.multiple_of(shard * count + start, half), size), :]

        self.direct, self.passed, self.kept = [], [], None
        if shards == 4:
            for i, (step, start) in enumerate(((1, 0), (2, half), (1, half), (2, 0))):
                self.direct.append(
                    remote(
                        own.at[pl.ds(start, half), :], at(me, start, half),
                        sends, recvs, i, rep, me ^ step,
                    )
                )
            for i, (step, start) in enumerate(((1, 0), (2, half))):
                came = at(me ^ step, start, half)
                self.passed.append(remote(came, came, sends, recvs, 4 + i, rep, me ^ step ^ 3))
        else:
            for i in range(shards - 1):
                self.direct.append(
                    remote(own, at(me, 0, count), sends, recvs, i, rep, me ^ (i + 1))
                )
        if local_sem is not None:
            self.kept = pltpu.make_async_copy(own, at(me, 0, count), local_sem)

    def start(self):
        for copy in self.direct:
            copy.start()
        if self.kept is not None:
            self.kept.start()

    def hand_on(self):
        for i, copy in enumerate(self.passed):
            self.direct[i].wait_recv()
            copy.start()

    def finish(self):
        for copy in self.direct[len(self.passed) :] + self.passed:
            copy.wait_recv()
        for copy in self.direct + self.passed:
            copy.wait_send()
        if self.kept is not None:
            self.kept.wait()

    @staticmethod
    def semaphores(shards):
        n = max(6, shards - 1)
        return [
            pltpu.SemaphoreType.DMA((n,)),
            pltpu.SemaphoreType.DMA((n,)),
            pltpu.SemaphoreType.DMA,
        ]


def split_rows(ref, index, size):
    return ref.at[pl.ds(pl.multiple_of(index * size, size), size), :]


def column_block(part):
    return lambda shard: pl.ds(pl.multiple_of(shard * part, part), part)


def pair_partners(rep, me):
    return [(rep ^ 1, me), (rep ^ 2, me)]


ANY = pl.BlockSpec(memory_space=pl.ANY)
IN_VMEM = pl.BlockSpec(memory_space=pltpu.VMEM)


def first_kernel(shards, parts, tokens, seg, *refs):
    rep, me = place()
    count = len(parts)
    weights, (tokens_all, seg_all, qkv_m, tokens_v) = refs[:count], refs[count : count + 4]
    held, held_sem, sems = refs[count + 4 : 2 * count + 4], refs[2 * count + 4], refs[2 * count + 5 :]
    take = pltpu.make_async_copy(tokens, tokens_v, held_sem.at[count, 0])
    take.start()
    greet(plane_partners(rep, me, shards) + pair_partners(rep, me))
    at, spreads = 0, []
    for weight, part, i in zip(weights, parts, range(count)):
        full = qkv_m.at[:, pl.ds(at, part)]
        spreads.append(
            Spread(
                shards, weight, full, column_block(part), *sems[2 * i : 2 * i + 2],
                held[i], held_sem.at[i],
            )
        )
        at += part
    sems = sems[2 * count :]
    rows = Gather(shards, tokens_v, tokens_all, *sems[:3])
    seg_send, seg_recv, seg_local = sems[3:]
    segs = [
        remote(seg, seg_all.at[me], seg_send, seg_recv, i, rep, me ^ (i + 1))
        for i in range(shards - 1)
    ]
    for spread in spreads:
        spread.start()
    for copy in segs:
        copy.start()
    take.wait()
    rows.start()
    own_seg = pltpu.make_async_copy(seg, seg_all.at[me], seg_local)
    own_seg.start()
    for spread in spreads:
        spread.hand_on()
    rows.hand_on()
    for spread in spreads:
        spread.hand_on_last()
    for spread in spreads:
        spread.finish()
    rows.finish()
    for copy in segs:
        copy.wait()
    own_seg.wait()


def first(tokens, seg, weights, shards):
    rows, width = tokens.shape
    parts = [w.shape[1] // shards for w in weights]
    n = shards - 1
    return pl.pallas_call(
        functools.partial(first_kernel, shards, parts),
        in_specs=[ANY] * (2 + len(weights)),
        out_specs=[ANY] * 3,
        out_shape=[
            jax.ShapeDtypeStruct((shards * rows, width), tokens.dtype),
            jax.ShapeDtypeStruct((shards,) + seg.shape, seg.dtype),
            jax.ShapeDtypeStruct((width, sum(parts)), BF16),
        ],
        scratch_shapes=[pltpu.VMEM(tokens.shape, BF16)]
        + [pltpu.VMEM((w.shape[0], part), BF16) for w, part in zip(weights, parts)]
        + [pltpu.SemaphoreType.DMA((len(weights) + 1, 2))]
        + len(weights) * Spread.semaphores(shards)
        + Gather.semaphores(shards)
        + [pltpu.SemaphoreType.DMA((n,)), pltpu.SemaphoreType.DMA((n,)), pltpu.SemaphoreType.DMA],
        compiler_params=pltpu.CompilerParams(
            collective_id=0, has_side_effects=True, vmem_limit_bytes=FULL
        ),
        name="first",
    )(tokens, seg, *weights)


def doc_positions(seg_ids):
    index = jnp.arange(seg_ids.shape[0], dtype=jnp.int32)
    fresh = (index == 0) | (seg_ids != jnp.roll(seg_ids, 1))
    begins = lax.cummax(jnp.where(fresh, index, jnp.zeros_like(index)), axis=0)
    return index - begins


def rope_tables(positions):
    freqs = rope_base ** (-(jnp.arange(HEAD // 2, dtype=F32) * (2.0 / HEAD)))
    angles = freqs[:, None] * positions.astype(F32)[None, :]
    return (jnp.cos(angles), jnp.sin(angles))


def side_by_side(ref, group, here):
    rows = GROUP * HEAD
    return jnp.concatenate(
        [
            ref[pl.ds(pl.multiple_of(group * rows + h * HEAD, HEAD), HEAD), here]
            for h in range(GROUP)
        ],
        axis=1,
    )


def block_bias(seg_col_ref, seg_row_ref, key_at, query_at):
    same = seg_col_ref[pl.ds(key_at, TILE), :] == seg_row_ref[:, pl.ds(query_at, TILE)]
    key_index = key_at + lax.broadcasted_iota(jnp.int32, (TILE, TILE), 0)
    query_index = query_at + lax.broadcasted_iota(jnp.int32, (TILE, TILE), 1)
    bias = jnp.where(same & (key_index <= query_index), 0.0, NEG).astype(F32)
    return jnp.concatenate([bias] * GROUP, axis=1)


def attend_kernel(
    shards, ffn_part, early, tokens, qkv_m, cot, proj_w, gate_w, up_w, gain, seg_col, seg_row,
    cos_ref, sin_ref,
    normed_out, cot_all, proj_m, gate_m, up_m, q_ref, k_ref, kt_ref, v_ref, out_ref, lse_ref,
    tokens_v, normed_v, qkv_v, turned_v, vt_ref, cot_v, load_sem, store_sem, qkv_sem, *sems,
):
    rep, me = place()
    length, width = tokens.shape
    kv_heads = k_ref.shape[0]
    q_part, kv_part = q_ref.shape[0], kt_ref.shape[0]
    blocks = length // TILE

    def first_tiles(shard):
        return pl.ds(pl.multiple_of(shard * ffn_part, ffn_part), early)

    halves = (pl.ds(0, width // 2), pl.ds(width // 2, width // 2))
    projs = [
        Spread(shards, proj_w.at[:, part], proj_m.at[:, part], None, *sems[2 * i : 2 * i + 2])
        for i, part in enumerate(halves)
    ]
    gate = Spread(shards, gate_w, gate_m, first_tiles, *sems[4:6])
    up = Spread(shards, up_w, up_m, first_tiles, *sems[6:8])
    cots = Gather(shards, cot_v, cot_all, *sems[8:11])

    def block_rows(i):
        return pl.ds(pl.multiple_of(i * TILE, TILE), TILE)

    def load(i):
        return pltpu.make_async_copy(tokens.at[block_rows(i), :], tokens_v.at[i % 2], load_sem.at[i % 2])

    def store(i):
        return pltpu.make_async_copy(
            normed_v.at[i % 2], normed_out.at[block_rows(i), :], store_sem.at[i % 2]
        )

    weights = pltpu.make_async_copy(qkv_m, qkv_v, qkv_sem.at[0])
    take = pltpu.make_async_copy(cot, cot_v, qkv_sem.at[1])
    take.start()
    weights.start()
    load(0).start()
    greet(plane_partners(rep, me, shards) + pair_partners(rep, me))
    for proj in projs:
        proj.start()
    gate.start()
    up.start()
    take.wait()
    cots.start()
    weights.wait()

    def turn_weights(i, carry):
        turned_v[:, block_rows(i)] = qkv_v[block_rows(i), :].T
        return carry

    lax.fori_loop(0, width // TILE, turn_weights, 0)

    half = HEAD // 2

    def project(i, carry):
        here = block_rows(i)

        @pl.when(i + 1 < blocks)
        def _():
            load(i + 1).start()

        load(i).wait()

        @pl.when(i >= 2)
        def _():
            store(i - 2).wait()

        values = tokens_v[i % 2].astype(F32)
        rms = lax.rsqrt(jnp.mean(values * values, axis=-1, keepdims=True) + epsilon)
        normed_v[i % 2] = (values * rms * gain[...]).astype(BF16)
        store(i).start()
        heads = dot(turned_v[...], normed_v[i % 2], NT)
        cos, sin = cos_ref[:, here], sin_ref[:, here]

        def turned(at):
            first, second = heads[at : at + half], heads[at + half : at + HEAD]
            return (
                (first * cos - second * sin).astype(BF16),
                (second * cos + first * sin).astype(BF16),
            )

        for at in range(0, q_part, HEAD):
            first, second = turned(at)
            q_ref[at : at + half, here] = (first.astype(F32) * SCALE).astype(BF16)
            q_ref[at + half : at + HEAD, here] = (second.astype(F32) * SCALE).astype(BF16)
        for g in range(kv_heads):
            at = g * HEAD
            first, second = turned(q_part + at)
            kt_ref[at : at + half, here] = first
            kt_ref[at + half : at + HEAD, here] = second
            vt_ref[at : at + HEAD, here] = heads[
                q_part + kv_part + at : q_part + kv_part + at + HEAD
            ].astype(BF16)
            k_ref[g, here, :] = kt_ref[at : at + HEAD, here].T
            v_ref[g, here, :] = vt_ref[at : at + HEAD, here].T
        return carry

    lax.fori_loop(0, blocks, project, 0)
    for i in range(max(0, blocks - 2), blocks):
        store(i).wait()
    for proj in projs:
        proj.hand_on()
    wide = GROUP * TILE

    def unit(at, carry_out):
        g, block = at // blocks, at % blocks
        query_at = pl.multiple_of(block * TILE, TILE)
        here = pl.ds(query_at, TILE)
        queries = side_by_side(q_ref, g, here)
        value_rows = pl.ds(pl.multiple_of(g * HEAD, HEAD), HEAD)

        def step(c, carry):
            top, total, acc = carry
            key_at = pl.multiple_of(c * TILE, TILE)
            keys = pl.ds(key_at, TILE)
            scores = dot(k_ref[g, keys, :], queries, NN)
            scores = scores + block_bias(seg_col, seg_row, key_at, query_at)
            new_top = jnp.maximum(top, jnp.max(scores, axis=0, keepdims=True))
            expo = jnp.exp(scores - new_top)
            fade = jnp.exp(top - new_top)
            total = total * fade + jnp.sum(expo, axis=0, keepdims=True)
            acc = acc * fade + dot(vt_ref[value_rows, keys], expo.astype(BF16), NN)
            return new_top, total, acc

        start = (
            jnp.full((1, wide), NEG, F32),
            jnp.zeros((1, wide), F32),
            jnp.zeros((HEAD, wide), F32),
        )
        top, total, acc = lax.fori_loop(0, block, step, step(block, start))
        mixed = (acc / total).astype(BF16)
        lse = top + jnp.log(total)
        for h in range(GROUP):
            at_row = pl.multiple_of(g * GROUP * HEAD + h * HEAD, HEAD)
            out_ref[pl.ds(at_row, HEAD), here] = mixed[:, h * TILE : (h + 1) * TILE]
            lse_ref[g, h : h + 1, here] = lse[:, h * TILE : (h + 1) * TILE]
        return carry_out

    units = kv_heads * blocks
    lax.fori_loop(0, units // 2, unit, 0)
    gate.hand_on()
    up.hand_on()
    lax.fori_loop(units // 2, units, unit, 0)
    for proj in projs:
        proj.hand_on_last()
    cots.hand_on()
    gate.hand_on_last()
    up.hand_on_last()
    for transfer in (*projs, gate, up, cots):
        transfer.finish()


def attend(
    tokens_all, qkv_m, cot, proj_w, gate_w, up_w, gain, seg, cos_t, sin_t, q_part, kv_part,
    early, shards,
):
    length, width = tokens_all.shape
    kv_heads = kv_part // HEAD
    part = gate_w.shape[1] // shards
    shape = jax.ShapeDtypeStruct
    dma = pltpu.SemaphoreType.DMA
    return pl.pallas_call(
        functools.partial(attend_kernel, shards, part, early),
        in_specs=[ANY] * 6 + [IN_VMEM] * 5,
        out_specs=[ANY] * 5 + [IN_VMEM] * 6,
        out_shape=[
            shape((length, width), BF16),
            shape((length, width), BF16),
            shape((shards * proj_w.shape[0], width), BF16),
            shape((width, early), BF16),
            shape((width, early), BF16),
            shape((q_part, length), BF16),
            shape((kv_heads, length, HEAD), BF16),
            shape((kv_part, length), BF16),
            shape((kv_heads, length, HEAD), BF16),
            shape((q_part, length), BF16),
            shape((kv_heads, GROUP, length), F32),
        ],
        scratch_shapes=[
            pltpu.VMEM((2, TILE, width), BF16),
            pltpu.VMEM((2, TILE, width), BF16),
            pltpu.VMEM(qkv_m.shape, BF16),
            pltpu.VMEM(qkv_m.shape[::-1], BF16),
            pltpu.VMEM((kv_part, length), BF16),
            pltpu.VMEM(cot.shape, BF16),
            dma((2,)), dma((2,)), dma((2,)),
        ]
        + 4 * Spread.semaphores(shards)
        + Gather.semaphores(shards),
        compiler_params=pltpu.CompilerParams(
            collective_id=1, has_side_effects=True, vmem_limit_bytes=FULL
        ),
        name="attend",
    )(
        tokens_all, qkv_m, cot, proj_w, gate_w, up_w, gain[None, :], seg[:, None], seg[None, :],
        cos_t, sin_t,
    )


def hidden_kernel(
    shards, mixed_t, proj_m, proj_w, cot_all, down_w, tokens, gain, hidden_ref, rms_ref, normed_all,
    grad_activ, proj_v, mixed_own, normed, cot_v, down_v, out_v, cot_sem, out_sem, proj_sem, mix_send, mix_recv, gather_send, gather_recv, local_sem,
):
    rep, me = place()
    part, _ = mixed_t.shape
    count = tokens.shape[0]
    rows = [
        pltpu.make_async_copy(
            split_rows(proj_m, me ^ i, part) if i else proj_w,
            split_rows(proj_v, me ^ i, part),
            proj_sem.at[i],
        )
        for i in range(shards)
    ]
    for copy in rows:
        copy.start()
    early = [
        pltpu.make_async_copy(cot_all, cot_v, cot_sem.at[0]),
        pltpu.make_async_copy(down_w, down_v, cot_sem.at[1]),
    ]
    for copy in early:
        copy.start()
    greet(plane_partners(rep, me, shards))

    def columns(shard):
        return mixed_t.at[:, pl.ds(pl.multiple_of(shard * count, count), count)]

    copies = [
        remote(columns(me ^ (i + 1)), mixed_own.at[i], mix_send, mix_recv, i, rep, me ^ (i + 1))
        for i in range(shards - 1)
    ]
    for copy in copies:
        copy.start()

    def product(block, i):
        rows[i].wait()
        return dot(block, split_rows(proj_v, me ^ i, part)[...], TN)

    hidden_ref[...] = tokens[...].astype(F32) + product(
        mixed_t[:, pl.ds(pl.multiple_of(me * count, count), count)], 0
    )
    for i, copy in enumerate(copies):
        copy.wait_recv()
        hidden_ref[...] += product(mixed_own[i], i + 1)
    hidden = hidden_ref[...]
    rms = lax.rsqrt(jnp.mean(hidden * hidden, axis=-1, keepdims=True) + epsilon)
    rms_ref[...] = rms
    normed[...] = (hidden * rms * gain[...]).astype(BF16)
    gather = Gather(shards, normed, normed_all, gather_send, gather_recv, local_sem)
    gather.start()
    for copy in copies:
        copy.wait_send()
    for copy in early:
        copy.wait()

    steps = down_w.shape[0] // TILE

    def store(i):
        at = pl.ds(pl.multiple_of(i * TILE, TILE), TILE)
        return pltpu.make_async_copy(out_v.at[i % 2], grad_activ.at[:, at], out_sem.at[i % 2])

    def step(i, carry):
        @pl.when(i >= 2)
        def _():
            store(i - 2).wait()

        units = down_v[pl.ds(pl.multiple_of(i * TILE, TILE), TILE), :]
        out_v[i % 2] = dot(cot_v[...], units, NT).astype(BF16)
        store(i).start()
        return carry

    lax.fori_loop(0, steps // 2, step, 0)
    gather.hand_on()
    lax.fori_loop(steps // 2, steps, step, 0)
    for i in range(max(0, steps - 2), steps):
        store(i).wait()
    gather.finish()


def hidden_layer(mixed_t, proj_m, proj_w, cot_all, down_w, tokens, gain, shards):
    part, length = mixed_t.shape
    count, width = tokens.shape
    n = shards - 1
    return pl.pallas_call(
        functools.partial(hidden_kernel, shards),
        in_specs=[IN_VMEM, ANY, ANY, ANY, ANY, IN_VMEM, IN_VMEM],
        out_specs=[IN_VMEM, IN_VMEM, ANY, ANY],
        out_shape=[
            jax.ShapeDtypeStruct((count, width), F32),
            jax.ShapeDtypeStruct((count, 1), F32),
            jax.ShapeDtypeStruct((length, width), BF16),
            jax.ShapeDtypeStruct((length, down_w.shape[0]), BF16),
        ],
        scratch_shapes=[
            pltpu.VMEM(proj_m.shape, BF16),
            pltpu.VMEM((n, part, count), BF16),
            pltpu.VMEM((count, width), BF16),
            pltpu.VMEM(cot_all.shape, BF16),
            pltpu.VMEM(down_w.shape, BF16),
            pltpu.VMEM((2, length, TILE), BF16),
            pltpu.SemaphoreType.DMA((2,)),
            pltpu.SemaphoreType.DMA((2,)),
            pltpu.SemaphoreType.DMA((shards,)),
            pltpu.SemaphoreType.DMA((n,)),
            pltpu.SemaphoreType.DMA((n,)),
        ]
        + Gather.semaphores(shards),
        compiler_params=pltpu.CompilerParams(
            collective_id=2, has_side_effects=True, vmem_limit_bytes=FULL
        ),
        name="hidden",
    )(mixed_t, proj_m, proj_w, cot_all, down_w, tokens, gain[None, :])


class Plan:
    def __init__(self, shards, reps, length, width, ffn_part, q_part, kv_part):
        self.shards, self.reps, self.length, self.width = shards, reps, length, width
        self.ffn_part, self.q_part, self.kv_part = ffn_part, q_part, kv_part
        self.layers = reps // 2
        self.half = self.layers // 2
        self.rows = width // 2
        self.own = width // shards
        self.block = self.own // 2
        self.proj_half = q_part // 2
        self.proj_blocks = self.rows // self.proj_half
        self.tiles = ffn_part // TILE
        self.out_tiles = width // TILE
        per_slot = 2
        self.back_slot = self.tiles
        self.send_slot = self.back_slot + -(-self.out_tiles // per_slot) - 1
        self.rows_slot = self.send_slot + 4
        self.pass_slot = self.rows_slot + 1
        self.mixed_slot = self.rows_slot + 3
        self.unit_slot = self.mixed_slot + 1
        self.per_slot = per_slot
        self.units = (length // TILE) * (kv_part // HEAD)
        self.norm_slot = self.unit_slot + self.units // 2
        self.ffn_end = 3 * self.tiles
        self.q_at = max(self.ffn_end, self.norm_slot)
        self.kv_at = self.q_at + q_part // TILE
        self.proj_at = self.kv_at + 1
        self.chunks = self.proj_at + width // TILE // self.proj_blocks
        self.tokens_slot = max(self.norm_slot + 7, self.chunks + self.half + 1)
        self.early_res = length <= 1024
        if self.early_res:
            self.res_slot = self.send_slot + 1
            self.res_send_slot = max(self.mixed_slot + 1, self.res_slot + self.out_tiles // 2)
            self.result_slot = self.res_send_slot + 5
            assert self.result_slot < self.norm_slot + 4
        else:
            self.res_slot = max(self.ffn_end + 1, self.norm_slot + 1)
            self.res_send_slot = max(self.res_slot + self.out_tiles // 2 - 1, self.tokens_slot + 1)
            self.result_slot = self.res_send_slot + 6
        self.arrive = self.layers + 2
        self.spread_slot = self.mixed_slot + 1
        self.spread_first = max(0, self.send_slot - self.arrive)
        self.hand = 6
        self.gain_slot = self.tokens_slot + 2
        self.rep_slot = max(self.chunks + self.arrive, self.gain_slot + 1)
        self.slots = max(self.chunks + self.arrive + self.hand, self.rep_slot, self.result_slot) + 1
        assert self.spread_slot + self.chunks // 2 < self.slots - self.hand
        self.mine_ring = self.half + 1
        self.sum_ring = 3


def backward_kernel(
    plan, early, x, cot_all, grad_activ, gate_w, up_w, gate_e, up_e, down_w, hidden, tokens, proj_w, qkv_m,
    normed,
    mlp_rms, mlp_gain, attn_gain, seg_col, seg_row, cos_ref, sin_ref, lse_ref, q_ref, mixed_ref,
    k_ref, kt_ref, v_ref,
    f_down, f_gate, f_up, f_proj, f_q, f_kv, result_ref, tokens_out, gains_out,
    swapped, from_outer, from_middle, totals, back_land, res_land, norm_land, norm_part,
    gate_m, up_m, activ, dgate, dup, back_part, res_part,
    left_a, left_b, right, gate_v, up_v, grad_v, back_v, tile_v, both, proj_v, qkv_v, hidden_v,
    row_sum, land_v,
    mine, theirs, swap_v, outer_v, middle_v, sums, total_v,
    grad_hidden, gh_own, g_t, back_t, dk_acc, dv_acc, activ_v,
    gain_part, gain_land, gain_sum, gain_reps,
    load_sem, right_sem, small_sem, swap_send, swap_recv, in_send, outer_recv, middle_recv,
    out_send, total_recv, total_store, cross_recv, cross_send, pass_send, pass_recv,
    back_send, back_recv, res_send, res_recv, norm_send, norm_recv,
    gather_send, gather_recv, gather_local, gain_send, gain_recv, rep_send, rep_recv,
    tile_send, tile_recv, tile_pass, tile_passed, down_sem, back_sem, tile_sem,
):
    p = plan
    shards, reps, n = p.shards, p.reps, p.shards - 1
    rep, me = place()
    core, layer = rep % 2, rep // 2
    upper = layer >= p.half
    depth = jnp.where(upper, p.layers - 1 - layer, layer)
    inward = jnp.where(upper, rep - 2, rep + 2)
    outward = jnp.where(upper, rep + 2, rep - 2)
    is_middle = depth == p.half - 1
    count = tokens.shape[0]
    ffn_end, proj_at, q_at, kv_at, end_at = p.ffn_end, p.proj_at, p.q_at, p.kv_at, p.chunks
    gh_all = both.at[:, pl.ds(0, p.width)]

    def columns(index, size=TILE):
        return pl.ds(pl.multiple_of(index * size, size), size)

    def load(src, dst, i):
        return pltpu.make_async_copy(src, dst, load_sem.at[i])

    load_cot = load(cot_all, left_a, 0)
    load_x = load(x, left_b, 1)
    load_normed = load(normed, left_a, 2)
    load_proj = load(proj_w, proj_v, 3)
    load_qkv = load(qkv_m, qkv_v, 4)
    load_hidden = load(hidden, hidden_v, 5)
    load_activ = load(activ, left_b.at[:, pl.ds(0, p.ffn_part)], 6)
    load_tokens = load(tokens, gh_own, 7)
    first_tile = early // TILE
    assert first_tile >= 2 or p.tiles < 3

    def tile_bytes(tile, sem):
        piece = gate_m.at[pl.ds(0, 2 * n * p.block), pl.ds(0, TILE)]
        return pltpu.make_async_copy(piece, piece, sem.at[tile])

    def send_tile(tile):
        rows = columns(core, p.block)
        into = pl.ds(pl.multiple_of(me * p.own + core * p.block, p.block), p.block)
        for weight, full in ((gate_w, gate_m), (up_w, up_m)):
            for i in range(n):
                peer = me ^ (i + 1)
                at = pl.ds(pl.multiple_of(peer * p.ffn_part + tile * TILE, TILE), TILE)
                pltpu.make_async_remote_copy(
                    src_ref=weight.at[rows, at], dst_ref=full.at[into, columns(tile)],
                    send_sem=tile_send.at[tile], recv_sem=tile_recv.at[tile],
                    device_id=(rep, peer), device_id_type=MESH,
                ).start()

    def pass_tile(tile):
        tile_bytes(tile, tile_recv).wait()
        for full in (gate_m, up_m):
            for i in range(n):
                peer = me ^ (i + 1)
                at = pl.ds(pl.multiple_of(peer * p.own + core * p.block, p.block), p.block)
                piece = full.at[at, columns(tile)]
                pltpu.make_async_remote_copy(
                    src_ref=piece, dst_ref=piece,
                    send_sem=tile_pass.at[tile], recv_sem=tile_passed.at[tile],
                    device_id=(rep ^ 1, me), device_id_type=MESH,
                ).start()

    def load_grad(tile):
        return pltpu.make_async_copy(grad_activ.at[:, columns(tile)], grad_v, down_sem.at[0])

    def load_tile(tile):
        @pl.when(tile >= first_tile)
        def _():
            tile_bytes(tile, tile_passed).wait()

        own_at = pl.ds(pl.multiple_of(me * p.ffn_part + tile * TILE, TILE), TILE)
        held_rows = [pl.ds(pl.multiple_of((me ^ i) * p.own, p.own), p.own) for i in range(shards)]
        for i, (weight, tiles, full, held) in enumerate(
            ((gate_w, gate_e, gate_m, gate_v), (up_w, up_e, up_m, up_v))
        ):
            sem = down_sem.at[i + 1]
            pltpu.make_async_copy(weight.at[:, own_at], held.at[held_rows[0], :], sem).start()
            for rows in held_rows[1:]:

                @pl.when(tile < first_tile)
                def _(rows=rows, tiles=tiles, held=held, sem=sem):
                    src = tiles.at[rows, columns(tile)]
                    pltpu.make_async_copy(src, held.at[rows, :], sem).start()

                @pl.when(tile >= first_tile)
                def _(rows=rows, full=full, held=held, sem=sem):
                    src = full.at[rows, columns(tile)]
                    pltpu.make_async_copy(src, held.at[rows, :], sem).start()

        load_grad(tile).start()

    def units_of(tile):
        return activ_v.at[:, columns(tile)] if p.early_res else tile_v.at[tile % 2]

    def store_tile(tile):
        dup_columns = pl.ds(pl.multiple_of(p.ffn_part + tile * TILE, TILE), TILE)
        return [
            pltpu.make_async_copy(src, dst.at[:, columns(tile)], tile_sem.at[i])
            for i, (src, dst) in enumerate(
                (
                    (units_of(tile), activ),
                    (both.at[:, columns(tile)], dgate),
                    (both.at[:, dup_columns], dup),
                )
            )
        ]

    def stored(tile):
        for copy in store_tile(tile):
            copy.wait()

    def ffn_tile(tile):
        for i, held in enumerate((gate_v, up_v)):
            pltpu.make_async_copy(held, held, down_sem.at[i + 1]).wait()
        load_grad(tile).wait()
        dup_columns = pl.ds(pl.multiple_of(p.ffn_part + tile * TILE, TILE), TILE)

        def go(i, carry):
            here = columns(i, ROWS)
            rows = left_b[here, :]
            gate = dot(rows, gate_v[...], NN)
            up = dot(rows, up_v[...], NN)
            grad = grad_v[here, :].astype(F32)
            sigm = jax.nn.sigmoid(gate)
            swish = gate * sigm
            units_of(tile)[here, :] = (swish * up).astype(BF16)
            both[here, columns(tile)] = (
                grad * up * sigm * (1.0 + gate * (1.0 - sigm))
            ).astype(BF16)
            both[here, dup_columns] = (grad * swish).astype(BF16)
            return carry

        lax.fori_loop(0, p.length // ROWS, go, 0)

        @pl.when(tile >= 2)
        def _():
            stored(tile - 1)

        for copy in store_tile(tile):
            copy.start()

        @pl.when(tile == 0)
        def _():
            stored(0)

        @pl.when(tile + 1 < p.tiles)
        def _():
            load_tile(tile + 1)

        @pl.when(tile + 1 == p.tiles)
        def _():
            load_back(0)

    def load_back(tile):
        slot = tile % 2
        per_shard = p.own // TILE
        for i, (weight, tiles, full) in enumerate(
            ((gate_w, gate_e, gate_m), (up_w, up_e, up_m))
        ):
            sem, at = back_sem.at[slot, i], i * p.ffn_part

            @pl.when(tile // per_shard == me)
            def _(weight=weight, sem=sem, at=at):
                src = weight.at[columns(tile - me * per_shard), columns(me, p.ffn_part)]
                pltpu.make_async_copy(src, back_v.at[slot, :, pl.ds(at, p.ffn_part)], sem).start()

            @pl.when(tile // per_shard != me)
            def _(tiles=tiles, full=full, sem=sem, at=at):
                into = back_v.at[slot, :, pl.ds(at, early)]
                pltpu.make_async_copy(tiles.at[columns(tile), :], into, sem).start()
                rest = p.ffn_part - early
                into = back_v.at[slot, :, pl.ds(at + early, rest)]
                src = full.at[columns(tile), pl.ds(early, rest)]
                pltpu.make_async_copy(src, into, sem).start()

    def wait_back(tile):
        slot = tile % 2
        for i in range(2):
            half = back_v.at[slot, :, pl.ds(i * p.ffn_part, p.ffn_part)]
            pltpu.make_async_copy(half, half, back_sem.at[slot, i]).wait()

    def back_tiles(first):
        def store(tile):
            return pltpu.make_async_copy(
                tile_v.at[tile % 2], back_part.at[:, columns(tile)], tile_sem.at[tile % 2]
            )

        @pl.when(first == 0)
        def _():
            stored(p.tiles - 1)

        def tile_go(k, carry):
            tile = first + k
            wait_back(tile)

            @pl.when(tile + 1 < p.out_tiles)
            def _():
                load_back(tile + 1)

            @pl.when(k >= 2)
            def _():
                store(tile - 2).wait()

            def go(i, c):
                here = columns(i, ROWS)
                tile_v[tile % 2, here, :] = dot(both[here, :], back_v[tile % 2], NT).astype(BF16)
                return c

            lax.fori_loop(0, p.length // ROWS, go, 0)
            store(tile).start()
            return carry

        size = jnp.minimum(p.per_slot, p.out_tiles - first)
        lax.fori_loop(0, size, tile_go, 0)
        store(first + size - 2).wait()
        store(first + size - 1).wait()

    def load_res(tile):
        def copies(action):
            for i, held in enumerate((gate_v, up_v)):

                @pl.when(tile % 2 == i)
                def _(i=i, held=held):
                    action(
                        pltpu.make_async_copy(
                            down_w.at[:, columns(tile)], held.at[pl.ds(0, p.ffn_part), :], back_sem.at[i, 0]
                        )
                    )

        return copies

    def res_tiles(first):
        hidden_units = activ_v if p.early_res else left_b

        def store(tile):
            return pltpu.make_async_copy(
                tile_v.at[tile % 2], res_part.at[:, columns(tile)], tile_sem.at[tile % 2]
            )

        for k, held in enumerate((gate_v, up_v)):
            tile = first + k
            load_res(tile)(lambda copy: copy.wait())

            @pl.when(tile + 1 < p.out_tiles)
            def _(tile=tile):
                load_res(tile + 1)(lambda copy: copy.start())

            def go(i, c, k=k, held=held):
                here = columns(i, ROWS)
                tile_v[k, here, :] = dot(
                    hidden_units[here, : p.ffn_part], held[: p.ffn_part, :], NN
                ).astype(BF16)
                return c

            lax.fori_loop(0, p.length // ROWS, go, 0)
            store(tile).start()
        store(first).wait()
        store(first + 1).wait()

    def load_right(t):
        slot = right.at[t % 2]
        tile, kind = t // 3, t % 3

        def copies(action):
            for i, ref in enumerate((activ, dgate, dup)):

                @pl.when((t < ffn_end) & (kind == i))
                def _(ref=ref):
                    action(
                        pltpu.make_async_copy(
                            ref.at[:, columns(tile)], slot, right_sem.at[t % 2]
                        )
                    )

        return copies

    side = p.width // 2
    left_half, right_half = pl.ds(0, side), pl.ds(side, side)

    def rows_of(shard):
        return pl.ds(pl.multiple_of(shard * count, count), count)

    class Scatter:
        def __init__(self, part, land, sends, recvs):
            self.part, self.land = part, land
            self.second = []
            if shards != 4:
                self.first = [
                    remote(split_rows(part, me ^ (i + 1), count), land.at[i], sends, recvs, i, rep, me ^ (i + 1))
                    for i in range(n)
                ]
                return
            order = (
                (3, left_half, 0, right_half, 1),
                (3, right_half, 1, right_half, 2),
                (1, left_half, 0, left_half, 1),
                (2, right_half, 1, left_half, 2),
            )
            self.first = [
                remote(
                    part.at[rows_of(me ^ block), cols], land.at[into, :, into_cols],
                    sends, recvs, i, rep, me ^ to,
                )
                for i, (block, cols, into, into_cols, to) in enumerate(order)
            ]
            self.second = [
                remote(gh_own.at[:, cols], land.at[2, :, cols], sends, recvs, 4 + i, rep, me ^ to)
                for i, (cols, to) in enumerate(((left_half, 2), (right_half, 1)))
            ]

        def start(self):
            for copy in self.first:
                copy.start()

        def hand_on(self):
            if not self.second:
                return
            for copy in self.first[:2]:
                copy.wait_recv()
            loads = [
                (self.part.at[rows_of(me ^ 2), left_half], 0, left_half),
                (self.part.at[rows_of(me ^ 1), right_half], 0, right_half),
                (self.land.at[0, :, right_half], 1, left_half),
                (self.land.at[1, :, right_half], 1, right_half),
            ]
            for src, slot, cols in loads:
                pltpu.make_async_copy(src, land_v.at[slot, :, cols], small_sem.at[slot]).start()
            for slot in range(2):
                pltpu.make_async_copy(land_v.at[slot], land_v.at[slot], small_sem.at[slot]).wait()

            def strip(here):
                gh_own[here, :] = (
                    land_v[0, here, :].astype(F32) + land_v[1, here, :].astype(F32)
                ).astype(BF16)

            strips(strip)
            for copy in self.second:
                copy.start()

        def fetch(self):
            for copy in self.first[2 if self.second else 0 :] + self.second:
                copy.wait_recv()
            for copy in self.second:
                copy.wait_send()
            pieces = [[(split_rows(self.part, me, count), pl.ds(0, p.width))]]
            if self.second:
                pieces.append(
                    [
                        (self.land.at[0, :, left_half], left_half),
                        (self.land.at[1, :, left_half], right_half),
                    ]
                )
                pieces.append([(self.land.at[2], pl.ds(0, p.width))])
            else:
                pieces += [[(self.land.at[i], pl.ds(0, p.width))] for i in range(n)]

            def load(i):
                for src, cols in pieces[i]:
                    pltpu.make_async_copy(
                        src, land_v.at[i % 2, :, cols], small_sem.at[i % 2]
                    ).start()

            load(0)
            for i in range(len(pieces)):
                if i + 1 < len(pieces):
                    load(i + 1)
                held = land_v.at[i % 2]
                pltpu.make_async_copy(held, held, small_sem.at[i % 2]).wait()

                def strip(here, i=i):
                    value = land_v[i % 2, here, :].astype(F32)
                    row_sum[here, :] = value if i == 0 else row_sum[here, :] + value

                strips(strip)

        def settle(self):
            for copy in self.first:
                copy.wait_send()

    back_rows = Scatter(back_part, back_land, back_send, back_recv)
    res_rows = Scatter(res_part, res_land, res_send, res_recv)
    norm_rows = Scatter(norm_part, norm_land, norm_send, norm_recv)

    STRIP = 32

    def strips(body):
        def go(i, carry):
            body(pl.ds(pl.multiple_of(i * STRIP, STRIP), STRIP))
            return carry

        lax.fori_loop(0, count // STRIP, go, 0)

    def norm_strip(here, values, rms, gain, row):
        grad_in = row_sum[here, :]
        weighted = grad_in * gain
        inner = jnp.mean(weighted * values, axis=-1, keepdims=True)
        gain_part[row : row + 1, :] += jnp.sum(grad_in * values * rms, axis=0, keepdims=True)
        return rms * weighted - values * (rms * rms * rms) * inner

    gather = Gather(shards, gh_own, gh_all, gather_send, gather_recv, gather_local)

    def hidden_back():
        load_hidden.wait()
        back_rows.fetch()
        gain_part[...] = jnp.zeros_like(gain_part)

        def strip(here):
            own = pl.ds(pl.multiple_of(me * count, count) + here.start, STRIP)
            grad = left_a[own, :].astype(F32) + norm_strip(
                here, hidden_v[here, :], mlp_rms[here, :], mlp_gain[...], 1
            )
            grad_hidden[here, :] = grad
            gh_own[here, :] = grad.astype(BF16)

        strips(strip)
        gather.start()

    def finish_result():
        res_rows.fetch()

        def strip(here):
            row_sum[here, :] = hidden_v[here, :] + row_sum[here, :]

        strips(strip)
        store_result = pltpu.make_async_copy(row_sum, result_ref, small_sem.at[0])
        store_result.start()
        store_result.wait()

    def mixed_back():
        gather.finish()
        load_proj.wait()

        def go(i, carry):
            here = pl.ds(pl.multiple_of(i * TILE, TILE), TILE)
            g_t[:, here] = dot(proj_v[...], both[here, : p.width], NT).astype(BF16)
            return carry

        lax.fori_loop(0, p.length // TILE, go, 0)

    blocks = p.length // TILE
    rows = GROUP * HEAD
    wide = GROUP * TILE
    mid = HEAD // 2

    def attention_unit(unit):
        g, block = unit // blocks, unit % blocks
        query_at = pl.multiple_of(block * TILE, TILE)
        here_q = pl.ds(query_at, TILE)

        queries = side_by_side(q_ref, g, here_q)
        grads = side_by_side(g_t, g, here_q)
        mixed = side_by_side(mixed_ref, g, here_q)
        lse = jnp.concatenate([lse_ref[g, h : h + 1, here_q] for h in range(GROUP)], axis=1)
        inner = jnp.sum(grads.astype(F32) * mixed.astype(F32), axis=0, keepdims=True)

        @pl.when(block == 0)
        def _():
            dk_acc[...] = jnp.zeros_like(dk_acc)
            dv_acc[...] = jnp.zeros_like(dv_acc)

        def step(c, acc):
            key_at = pl.multiple_of(c * TILE, TILE)
            here = pl.ds(key_at, TILE)
            scores = dot(k_ref[g, here, :], queries, NN)
            scores = scores + block_bias(seg_col, seg_row, key_at, query_at)
            probs = jnp.exp(scores - lse)
            grad_probs = dot(v_ref[g, here, :], grads, NN)
            grad_scores = (probs * (grad_probs - inner)).astype(BF16)
            dv_acc[:, here] += dot(grads, probs.astype(BF16), NT)
            dk_acc[:, here] += dot(queries, grad_scores, NT)
            key_rows = pl.ds(pl.multiple_of(g * HEAD, HEAD), HEAD)
            return acc + dot(kt_ref[key_rows, here], grad_scores, NN)

        acc = lax.fori_loop(0, block + 1, step, jnp.zeros((HEAD, wide), F32))
        cos, sin = cos_ref[:, here_q], sin_ref[:, here_q]
        for h in range(GROUP):
            grad = acc[:, h * TILE : (h + 1) * TILE] * SCALE
            first, second = grad[:mid], grad[mid:]
            at = pl.multiple_of(g * rows + h * HEAD, HEAD)
            back_t[pl.ds(at, mid), here_q] = (first * cos + second * sin).astype(BF16)
            back_t[pl.ds(at + mid, mid), here_q] = (second * cos - first * sin).astype(BF16)

        @pl.when(block == blocks - 1)
        def _():
            cos, sin = cos_ref[...], sin_ref[...]
            first, second = dk_acc[:mid, :], dk_acc[mid:, :]
            at = pl.multiple_of(p.q_part + g * HEAD, HEAD)
            back_t[pl.ds(at, mid), :] = (first * cos + second * sin).astype(BF16)
            back_t[pl.ds(at + mid, mid), :] = (second * cos - first * sin).astype(BF16)
            at = pl.multiple_of(p.q_part + p.kv_part + g * HEAD, HEAD)
            back_t[pl.ds(at, HEAD), :] = dv_acc[...].astype(BF16)

    def normed_back():
        load_qkv.wait()

        stores = [
            pltpu.make_async_copy(
                land_v.at[i % 2], norm_part.at[pl.ds(i * count, count), :], small_sem.at[i % 2]
            )
            for i in range(shards)
        ]
        for i, store in enumerate(stores):
            if i >= 2:
                stores[i - 2].wait()
            here = pl.ds(i * count, count)
            land_v[i % 2] = dot(back_t[:, here].T, qkv_v[...], NT).astype(BF16)
            store.start()
        for store in stores[-2:]:
            store.wait()
        norm_rows.start()

    gain_cols = p.width // shards

    def gain_slice(shard):
        return pl.ds(pl.multiple_of(shard * gain_cols, gain_cols), gain_cols)

    gain_plane = [
        remote(
            gain_part.at[:, gain_slice(me ^ (i + 1))], gain_land.at[me],
            gain_send, gain_recv, i, rep, me ^ (i + 1),
        )
        for i in range(n)
    ]
    gain_all = [
        remote(gain_sum, gain_reps.at[rep], rep_send, rep_recv, i, rep ^ (i + 1), me)
        for i in range(reps - 1)
    ]

    def tokens_back():
        norm_rows.fetch()
        load_tokens.start()
        load_tokens.wait()

        def strip(here):
            values = gh_own[here, :].astype(F32)
            rms = lax.rsqrt(jnp.mean(values * values, axis=-1, keepdims=True) + epsilon)
            grad_hidden[here, :] += norm_strip(here, values, rms, attn_gain[...], 0)

        strips(strip)
        store_tokens = pltpu.make_async_copy(grad_hidden, tokens_out, small_sem.at[0])
        store_tokens.start()
        store_tokens.wait()
        gain_land[me] = gain_part[:, gain_slice(me)]
        for copy in gain_plane:
            copy.start()

    def gains_plane():
        for copy in gain_plane:
            copy.wait_recv()
        total = gain_land[0]
        for s in range(1, shards):
            total = total + gain_land[s]
        gain_sum[...] = total
        gain_reps[rep] = total
        for copy in gain_all:
            copy.start()

    def gains_reps():
        for copy in gain_all:
            copy.wait_recv()
        total = gain_reps[0]
        for r in range(1, reps):
            total = total + gain_reps[r]
        gains_out[...] = total

    def swap_copy(j):
        return pltpu.make_async_remote_copy(
            src_ref=theirs.at[j % 2], dst_ref=swapped.at[j],
            send_sem=swap_send.at[j % 2], recv_sem=swap_recv.at[j],
            device_id=(rep ^ 1, me), device_id_type=MESH,
        )

    def store_chunk(slot, other_slot, at, size, product, columns=TILE):
        here = pl.ds(pl.multiple_of(at, size), size)
        mine[slot, here, :columns] = product(core).astype(BF16)
        theirs[other_slot, here, :columns] = product(1 - core).astype(BF16)

    def make(t):
        slot, other = t % p.mine_ring, t % 2

        @pl.when(t >= 2)
        def _():
            swap_copy(t - 2).wait_send()

        @pl.when(t == 0)
        def _():
            load_right(0)(lambda copy: copy.start())

        load_right(t)(lambda copy: copy.wait())

        @pl.when(t + 1 < ffn_end)
        def _():
            load_right(t + 1)(lambda copy: copy.start())

        @pl.when((t < ffn_end) & (t % 3 == 0))
        def _():
            left = right[t % 2].T

            def product(which):
                return dot(left, left_a[:, columns(which, p.rows)], NN).astype(BF16)

            ours, others = product(core), product(1 - core)
            for at in range(0, p.rows, TILE):
                mine[slot, at : at + TILE, :] = ours[:, at : at + TILE]
                theirs[other, at : at + TILE, :] = others[:, at : at + TILE]

        def wide_chunk(left, factor, columns):
            def go(s, carry):
                def product(which):
                    at = pl.multiple_of(s * p.own + which * p.block, p.block)
                    return dot(factor, left[:, pl.ds(at, p.block)], NN).T

                store_chunk(slot, other, s * p.block, p.block, product, columns)
                return carry

            lax.fori_loop(0, shards, go, 0)

        @pl.when((t < ffn_end) & (t % 3 > 0))
        def _():
            wide_chunk(left_b, right[t % 2].T, TILE)

        @pl.when((t >= proj_at) & (t < end_at))
        def _():
            def go(i, carry):
                at = columns((t - proj_at) * p.proj_blocks + i)

                def product(which):
                    part = columns(which, p.proj_half)
                    return dot(mixed_ref[part, :], both[:, at], NN)

                store_chunk(slot, other, i * p.proj_half, p.proj_half, product)
                return carry

            lax.fori_loop(0, p.proj_blocks, go, 0)

        @pl.when((t >= q_at) & (t < kv_at))
        def _():
            wide_chunk(left_a, back_t[columns(t - q_at), :], TILE)

        @pl.when(t == kv_at)
        def _():
            wide_chunk(left_a, back_t[p.q_part :, :], 2 * p.kv_part)

        swap_copy(t).start()

    def inward_copies(j):
        common = dict(
            src_ref=sums.at[j % p.sum_ring], send_sem=in_send.at[j % p.sum_ring],
            device_id=(inward, me), device_id_type=MESH,
        )
        to_layer = pltpu.make_async_remote_copy(
            dst_ref=from_outer.at[j], recv_sem=outer_recv.at[j], **common
        )
        to_middle = pltpu.make_async_remote_copy(
            dst_ref=from_middle.at[j], recv_sem=middle_recv.at[j], **common
        )
        return to_layer, to_middle

    def total_places(j, action):
        @pl.when(is_chunk(j, 0))
        def _():
            action(
                [
                    (
                        i * TILE, TILE, TILE,
                        f_down.at[
                            columns(j // 3),
                            pl.ds(pl.multiple_of(core * p.rows + i * TILE, TILE), TILE),
                        ],
                    )
                    for i in range(p.rows // TILE)
                ]
            )

        @pl.when((j >= proj_at) & (j < end_at))
        def _():
            action(
                [
                    (
                        i * p.proj_half, p.proj_half, TILE,
                        f_proj.at[
                            columns(core, p.proj_half),
                            columns((j - proj_at) * p.proj_blocks + i),
                        ],
                    )
                    for i in range(p.proj_blocks)
                ]
            )

        for when, full, part, tile, sem, wide_by in wide_kinds(j):

            @pl.when(when)
            def _(full=full, part=part, tile=tile, wide_by=wide_by):
                blocks = []
                for i in range(shards):
                    at = pl.multiple_of((me ^ i) * p.block, p.block)
                    place_there = totals.at[j, pl.ds(at, p.block), pl.ds(0, wide_by)]
                    if i == 0:
                        place_there = window(full, me, part, tile, wide_by)
                    blocks.append((at, p.block, wide_by, place_there))
                action(blocks)

    def chunk_bytes(j, sem):
        @pl.when(j == kv_at)
        def _():
            whole = totals.at[0, :, pl.ds(0, 2 * p.kv_part)]
            pltpu.make_async_copy(whole, whole, sem).wait()

        @pl.when(j != kv_at)
        def _():
            whole = totals.at[0]
            pltpu.make_async_copy(whole, whole, sem).wait()

    def send_total(src, dst, j):
        return pltpu.make_async_remote_copy(
            src_ref=src, dst_ref=dst, send_sem=out_send.at[j % 2],
            recv_sem=total_recv.at[j], device_id=(outward, me), device_id_type=MESH,
        )

    def add_rows(body):
        def go(i, carry):
            body(pl.ds(pl.multiple_of(i * TILE, TILE), TILE))
            return carry

        lax.fori_loop(0, p.rows // TILE, go, 0)

    def load_swapped(j):
        return pltpu.make_async_copy(swapped.at[j], swap_v, small_sem.at[2])

    def load_outer(j):
        return pltpu.make_async_copy(from_outer.at[j], outer_v, small_sem.at[3])

    def load_middle(j):
        return pltpu.make_async_copy(from_middle.at[j], middle_v, small_sem.at[4])

    def valid(j):
        return (j >= 0) & (j < p.chunks)

    def take_inward(j):
        @pl.when(valid(j))
        def _():
            swap_copy(j).wait_recv()
            load_swapped(j).start()

            @pl.when(depth > 0)
            def _():
                inward_copies(j)[0].wait_recv()
                load_outer(j).start()

    def send_inward(j):
        @pl.when(valid(j))
        def _():
            @pl.when(j >= p.sum_ring)
            def _():
                inward_copies(j - p.sum_ring)[0].wait_send()

            load_swapped(j).wait()
            ours = mine.at[j % p.mine_ring]
            total = sums.at[j % p.sum_ring]

            @pl.when(depth > 0)
            def _():
                load_outer(j).wait()

                def add(here):
                    total[here, :] = (
                        ours[here, :].astype(F32)
                        + swap_v[here, :].astype(F32)
                        + outer_v[here, :].astype(F32)
                    ).astype(BF16)

                add_rows(add)

            @pl.when(depth == 0)
            def _():
                def add(here):
                    total[here, :] = (
                        ours[here, :].astype(F32) + swap_v[here, :].astype(F32)
                    ).astype(BF16)

                add_rows(add)

            to_layer, to_middle = inward_copies(j)

            @pl.when(is_middle)
            def _():
                to_middle.start()

            @pl.when(jnp.logical_not(is_middle))
            def _():
                to_layer.start()

    def take_middle(j):
        @pl.when(is_middle & valid(j))
        def _():
            inward_copies(j)[1].wait_recv()
            load_middle(j).start()

    def meet_in_middle(j):
        @pl.when(is_middle & valid(j))
        def _():
            @pl.when(j >= 1)
            def _():
                chunk_bytes(j - 1, total_store.at[0])

            if p.half > 1:

                @pl.when(j >= 2)
                def _():
                    chunk_bytes(j - 2, out_send.at[j % 2])

            load_middle(j).wait()
            out, held = total_v.at[j % 2], sums.at[j % p.sum_ring]

            def add(here):
                out[here, :] = (
                    held[here, :].astype(F32) + middle_v[here, :].astype(F32)
                ).astype(BF16)

            add_rows(add)

            def put(blocks):
                for at, size, wide_by, dst in blocks:
                    src = out.at[pl.ds(at, size), pl.ds(0, wide_by)]
                    if p.half > 1:
                        send_total(src, dst, j).start()
                    pltpu.make_async_copy(src, dst, total_store.at[0]).start()

            total_places(j, put)

    def last_store(t):
        @pl.when(is_middle & (t == p.chunks + p.arrive - 1))
        def _():
            chunk_bytes(p.chunks - 1, total_store.at[0])

    def send_outward(j):
        @pl.when(jnp.logical_not(is_middle) & valid(j))
        def _():
            chunk_bytes(j, total_recv.at[j])

            if p.half > 2:

                @pl.when(depth > 0)
                def _():
                    @pl.when(j >= 2)
                    def _():
                        chunk_bytes(j - 2, out_send.at[j % 2])

                    def put(blocks):
                        for _, _, _, dst in blocks:
                            send_total(dst, dst, j).start()

                    total_places(j, put)

    def remote_pass(src, dst, sem):
        return pltpu.make_async_remote_copy(
            src_ref=src, dst_ref=dst, send_sem=pass_send.at[sem], recv_sem=pass_recv.at[sem],
            device_id=(rep ^ 1, me), device_id_type=MESH,
        )

    def window(full, shard, part, tile, columns=TILE):
        at = pl.multiple_of(shard * part + tile * columns, columns)
        return full.at[pl.ds(pl.multiple_of(core * p.block, p.block), p.block), pl.ds(at, columns)]

    def is_chunk(j, kind):
        return (j >= 0) & (j < ffn_end) & (j % 3 == kind)

    def wide_kinds(j):
        return (
            (is_chunk(j, 1), f_gate, p.ffn_part, j // 3, 1, TILE),
            (is_chunk(j, 2), f_up, p.ffn_part, j // 3, 2, TILE),
            ((j >= q_at) & (j < kv_at), f_q, p.q_part, j - q_at, 4, TILE),
            (j == kv_at, f_kv, 2 * p.kv_part, 0, 5, 2 * p.kv_part),
        )

    def spread_total(j):
        for kind, sem in ((is_chunk(j, 0), 0), ((j >= proj_at) & (j < end_at), 3)):

            @pl.when(kind)
            def _(sem=sem):
                def put(blocks):
                    for _, _, _, dst in blocks:
                        remote_pass(dst, dst, sem).start()

                total_places(j, put)

        for when, full, part, tile, sem, wide_by in wide_kinds(j):

            @pl.when(when)
            def _(full=full, part=part, tile=tile, sem=sem, wide_by=wide_by):
                place_here = window(full, me, part, tile, wide_by)
                for i in range(n):
                    at = columns(me ^ (i + 1), p.block)
                    pltpu.make_async_remote_copy(
                        src_ref=totals.at[j, at, pl.ds(0, wide_by)], dst_ref=place_here,
                        send_sem=cross_send.at[sem], recv_sem=cross_recv.at[j],
                        device_id=(rep, me ^ (i + 1)), device_id_type=MESH,
                    ).start()
                remote_pass(place_here, place_here, sem).start()

    def pass_on(j):
        for when, full, part, tile, sem, wide_by in wide_kinds(j):

            @pl.when(when)
            def _(full=full, part=part, tile=tile, sem=sem, wide_by=wide_by):
                came = totals.at[j, pl.ds(0, n * p.block), pl.ds(0, wide_by)]
                pltpu.make_async_copy(came, came, cross_recv.at[j]).wait()
                for i in range(n):
                    here = window(full, me ^ (i + 1), part, tile, wide_by)
                    remote_pass(here, here, sem).start()

    for copy in (load_x, load_cot):
        copy.start()
    load_tile(0)
    greet(plane_partners(rep, me, shards) + [(rep ^ i, me) for i in range(1, reps)])
    ahead = 3
    for tile in range(first_tile, min(first_tile + ahead, p.tiles)):
        send_tile(tile)
    for copy in (load_hidden, load_proj, load_qkv):
        copy.start()
    for copy in (load_x, load_cot):
        copy.wait()

    def slot(t, carry):
        inner = t - 1 - depth
        met = t - 1 - p.half
        take_inward(inner)
        send_inward(inner)
        send_outward(t - p.arrive + depth)

        def spread_until(u):
            ready = jnp.minimum(u - p.arrive + 1, p.chunks)
            later = p.spread_first + 2 * jnp.maximum(u - p.spread_slot + 1, 0)
            most = jnp.where(u < p.send_slot, p.chunks, later)
            return jnp.maximum(jnp.minimum(ready, most), 0)

        def over(action, u):
            def go(j, c):
                action(j)
                return c

            lax.fori_loop(spread_until(u - 1), spread_until(u), go, 0)

        last_store(t)
        over(spread_total, t)
        over(pass_on, t - p.hand)

        @pl.when(t + first_tile + ahead < p.tiles)
        def _():
            send_tile(t + first_tile + ahead)

        @pl.when((t > 0) & (t + 1 >= first_tile) & (t + 1 < p.tiles))
        def _():
            pass_tile(t + 1)

        @pl.when(t < p.tiles)
        def _():
            ffn_tile(t)

        @pl.when((t >= p.back_slot) & (t <= p.send_slot))
        def _():
            back_tiles((t - p.back_slot) * p.per_slot)

        @pl.when(t == ffn_end)
        def _():
            load_normed.start()
            if not p.early_res:
                load_activ.start()

        @pl.when(t == q_at)
        def _():
            load_normed.wait()

        def at(when, action):
            @pl.when(t == when)
            def _():
                action()

        take_middle(met)
        meet_in_middle(met)
        at(p.send_slot, back_rows.start)
        at(p.send_slot + 2, back_rows.hand_on)
        at(p.rows_slot, hidden_back)
        at(p.pass_slot, gather.hand_on)
        at(p.mixed_slot, mixed_back)

        @pl.when((t >= p.unit_slot) & (t < p.norm_slot))
        def _():
            def go(i, c):
                attention_unit((t - p.unit_slot) * 2 + i)
                return c

            lax.fori_loop(0, 2, go, 0)

        at(p.norm_slot, normed_back)
        at(p.norm_slot + 4, norm_rows.hand_on)

        @pl.when(t < p.chunks)
        def _():
            make(t)

        at(p.tokens_slot, tokens_back)
        at(p.gain_slot, gains_plane)
        at(p.rep_slot, gains_reps)

        @pl.when((t >= p.res_slot) & (t < p.res_slot + p.out_tiles // 2))
        def _():
            @pl.when(t == p.res_slot)
            def _():
                if not p.early_res:
                    load_activ.wait()
                load_res(0)(lambda copy: copy.start())

            res_tiles((t - p.res_slot) * 2)

        at(p.res_send_slot, res_rows.start)
        at(p.res_send_slot + 3, res_rows.hand_on)
        at(p.result_slot, finish_result)
        return carry

    lax.fori_loop(0, p.slots, slot, 0)

    for j in range(max(0, p.chunks - 2), p.chunks):
        swap_copy(j).wait_send()
    for j in range(max(0, p.chunks - p.sum_ring), p.chunks):
        inward_copies(j)[0].wait_send()
    if p.half > 1:

        @pl.when(depth > 0)
        def _():
            for j in range(max(0, p.chunks - 2), p.chunks):
                chunk_bytes(j, out_send.at[j % 2])

    for rows in (back_rows, res_rows, norm_rows):
        rows.settle()
    for copies in (gain_plane, gain_all):
        for copy in copies:
            copy.wait_send()

    def settle(ref, sem):
        pltpu.make_async_copy(ref, ref, sem).wait()

    for tile in range(first_tile, p.tiles):
        tile_bytes(tile, tile_send).wait()
        tile_bytes(tile, tile_pass).wait()
    for sem, part in (
        (0, f_down.at[:, pl.ds(0, p.rows)]),
        (3, f_proj.at[pl.ds(0, p.proj_half), :]),
    ):
        settle(part, pass_send.at[sem])
        settle(part, pass_recv.at[sem])
    for _, full, part, _, sem, _ in wide_kinds(0):
        here = full.at[pl.ds(0, p.block), :]
        settle(here, pass_send.at[sem])
        settle(here, pass_recv.at[sem])
        settle(full.at[pl.ds(0, p.block), pl.ds(0, n * part)], cross_send.at[sem])


def backward(
    shards, reps, x, cot_all, grad_activ, gate_w, up_w, gate_e, up_e, down_w, hidden, tokens, proj_w,
    qkv_m, normed, mlp_rms, mlp_gain, attn_gain, seg, cos_t, sin_t, lse, q_t, mixed_t, k, k_t, v,
):
    length, width = x.shape
    count = tokens.shape[0]
    ffn_part = down_w.shape[0]
    q_part, kv_part = q_t.shape[0], k_t.shape[0]
    n = shards - 1
    p = Plan(shards, reps, length, width, ffn_part, q_part, kv_part)
    shape = jax.ShapeDtypeStruct
    own = width // shards
    chunk = (p.rows, TILE)
    dma = pltpu.SemaphoreType.DMA
    return pl.pallas_call(
        functools.partial(backward_kernel, p, gate_e.shape[1]),
        in_specs=[ANY] * 13 + [IN_VMEM] * 13,
        out_specs=[ANY] * 8 + [IN_VMEM] + [ANY] * 15,
        out_shape=[
            shape((ffn_part, width), BF16),
            shape((own, shards * ffn_part), BF16),
            shape((own, shards * ffn_part), BF16),
            shape((q_part, width), BF16),
            shape((own, shards * q_part), BF16),
            shape((own, shards * 2 * kv_part), BF16),
            shape((count, width), F32),
            shape((count, width), F32),
            shape((8, width // shards), F32),
        ]
        + [shape((p.chunks,) + chunk, BF16)] * 4
        + [shape((n, count, width), BF16)] * 3
        + [shape((length, width), BF16)]
        + [shape((width, ffn_part), BF16)] * 2
        + [shape((length, ffn_part), BF16)] * 3
        + [shape((length, width), BF16)] * 2,
        scratch_shapes=[
            pltpu.VMEM((length, width), BF16),
            pltpu.VMEM((length, width), BF16),
            pltpu.VMEM((2, length, TILE), BF16),
            pltpu.VMEM((width, TILE), BF16),
            pltpu.VMEM((width, TILE), BF16),
            pltpu.VMEM((length, TILE), BF16),
            pltpu.VMEM((2, TILE, 2 * ffn_part), BF16),
            pltpu.VMEM((2, length, TILE), BF16),
            pltpu.VMEM((length, 2 * ffn_part), BF16),
            pltpu.VMEM(proj_w.shape, BF16),
            pltpu.VMEM(qkv_m.shape, BF16),
            pltpu.VMEM((count, width), F32),
            pltpu.VMEM((count, width), F32),
            pltpu.VMEM((2, count, width), BF16),
            pltpu.VMEM((p.mine_ring,) + chunk, BF16),
            pltpu.VMEM((2,) + chunk, BF16),
            pltpu.VMEM(chunk, BF16),
            pltpu.VMEM(chunk, BF16),
            pltpu.VMEM(chunk, BF16),
            pltpu.VMEM((p.sum_ring,) + chunk, BF16),
            pltpu.VMEM((2,) + chunk, BF16),
            pltpu.VMEM((count, width), F32),
            pltpu.VMEM((count, width), BF16),
            pltpu.VMEM((q_part, length), BF16),
            pltpu.VMEM((q_part + 2 * kv_part, length), BF16),
            pltpu.VMEM((HEAD, length), F32),
            pltpu.VMEM((HEAD, length), F32),
            pltpu.VMEM((length, ffn_part) if p.early_res else (16, 128), BF16),
            pltpu.VMEM((8, width), F32),
            pltpu.VMEM((shards, 8, own), F32),
            pltpu.VMEM((8, own), F32),
            pltpu.VMEM((reps, 8, own), F32),
            dma((12,)), dma((2,)), dma((5,)), dma((2,)), dma((p.chunks,)), dma((p.sum_ring,)),
            dma((p.chunks,)), dma((p.chunks,)), dma((2,)), dma((p.chunks,)), dma((2,)),
            dma((p.chunks,)), dma((6,)), dma((6,)), dma((6,)),
        ]
        + [dma((max(6, n),))] * 6
        + Gather.semaphores(shards)
        + [dma((n,)), dma((n,)), dma((reps - 1,)), dma((reps - 1,))]
        + [dma((p.tiles,))] * 4
        + [dma((3,)), dma((2, 2)), dma((3,))],
        compiler_params=pltpu.CompilerParams(
            collective_id=3, has_side_effects=True, vmem_limit_bytes=FULL
        ),
        name="backward",
    )(
        x, cot_all, grad_activ, gate_w, up_w, gate_e, up_e, down_w, hidden, tokens, proj_w,
        qkv_m, normed, mlp_rms, mlp_gain[None, :], attn_gain[None, :], seg[:, None], seg[None, :],
        cos_t, sin_t, lse, q_t, mixed_t, k, k_t, v,
    )[:9]


def widen_kernel(count, rows, columns, *refs):
    srcs, dsts = refs[:count], refs[count : 2 * count]
    narrow, wide, in_sem, out_sem = refs[2 * count :]
    depth = narrow.shape[0]
    loads, stores = [], []
    for src, dst in zip(srcs, dsts):
        for r in range(src.shape[0] // rows):
            for c in range(src.shape[1] // columns):
                at = (pl.ds(r * rows, rows), pl.ds(c * columns, columns))
                slot = len(loads) % depth
                direct = src.dtype == dst.dtype
                into = wide.at[slot] if direct else narrow.at[slot]
                loads.append(pltpu.make_async_copy(src.at[at], into, in_sem.at[slot]))
                stores.append(
                    (pltpu.make_async_copy(wide.at[slot], dst.at[at], out_sem.at[slot]), direct)
                )
    total = len(loads)
    ahead = depth - 1

    def load(i):
        if stores[i][1] and i >= depth:
            stores[i - depth][0].wait()
        loads[i].start()

    for i in range(min(ahead, total)):
        load(i)
    for i in range(total):
        slot = i % depth
        store, direct = stores[i]
        loads[i].wait()
        if not direct:
            if i >= depth:
                stores[i - depth][0].wait()
            for strip in range(0, rows, 64):
                wide[slot, pl.ds(strip, 64), :] = narrow[slot, pl.ds(strip, 64), :].astype(F32)
        store.start()
        if i + ahead < total:
            load(i + ahead)
    for i in range(max(0, total - depth), total):
        stores[i][0].wait()


def widen(arrays):
    rows, columns, depth = 256, 2048, 4
    rows = min([rows] + [a.shape[0] for a in arrays])
    shapes = [jax.ShapeDtypeStruct(a.shape, F32) for a in arrays]
    return pl.pallas_call(
        functools.partial(widen_kernel, len(arrays), rows, columns),
        in_specs=[ANY] * len(arrays),
        out_specs=[ANY] * len(arrays),
        out_shape=shapes,
        scratch_shapes=[
            pltpu.VMEM((depth, rows, columns), BF16),
            pltpu.VMEM((depth, rows, columns), F32),
            pltpu.SemaphoreType.DMA((depth,)),
            pltpu.SemaphoreType.DMA((depth,)),
        ],
        compiler_params=pltpu.CompilerParams(vmem_limit_bytes=FULL),
        name="widen",
    )(*arrays)


def local(
    tokens, segments, query_w, key_w, value_w, proj_w, attn_gain,
    gate_w, up_w, down_w, mlp_gain, cotangent,
):
    shards = lax.axis_size("shard")
    reps = lax.axis_size("rep")
    tok_count, width = tokens.shape
    kv_part = key_w.shape[1] // shards
    q_part = query_w.shape[1] // shards
    length = tok_count * shards

    if kv_part % 128:
        kv_w = jnp.concatenate(
            [
                w[:, s * kv_part : (s + 1) * kv_part]
                for s in range(shards)
                for w in (key_w, value_w)
            ],
            axis=1,
        )
        weights = (query_w, kv_w)
    else:
        weights = (query_w, key_w, value_w)
    tokens_all, seg, qkv_m = first(tokens, segments[None, :], weights, shards)
    seg = seg.reshape(length)
    cos_t, sin_t = rope_tables(doc_positions(seg))
    early = min(2 * TILE, down_w.shape[0] // 2)
    normed, cot_all, proj_m, gate_e, up_e, q_t, k, k_t, v, mixed_t, lse = attend(
        tokens_all, qkv_m, cotangent, proj_w, gate_w, up_w, attn_gain, seg, cos_t, sin_t,
        q_part, kv_part, early, shards,
    )
    hidden, mlp_rms, normed_mlp, grad_activ = hidden_layer(
        mixed_t, proj_m, proj_w, cot_all, down_w, tokens, mlp_gain, shards
    )
    down, gate, up, proj, query, kv, result, grad_tokens, gains = backward(
        shards, reps, normed_mlp, cot_all, grad_activ, gate_w, up_w, gate_e, up_e, down_w, hidden, tokens,
        proj_w, qkv_m, normed, mlp_rms, mlp_gain, attn_gain, seg, cos_t, sin_t, lse, q_t,
        mixed_t, k, k_t, v,
    )

    def every_other(first):
        parts = [
            kv[:, (2 * s + first) * kv_part : (2 * s + first + 1) * kv_part] for s in range(shards)
        ]
        return jnp.concatenate(parts, axis=1).astype(F32)

    gate, up, down, query, proj, result, grad_tokens = widen(
        [gate, up, down, query, proj, result, grad_tokens]
    )
    return (
        result, grad_tokens, query, every_other(0), every_other(1), proj, gains[0], gate, up, down,
        gains[1],
    )


def solution(mesh):
    rows = P(("rep", "shard"), None)
    held = P("shard", None)
    in_specs = (
        rows, P(("rep", "shard")), held, held, held, held, P(), held, held, held, P(), rows,
    )
    out_specs = (
        rows, rows, held, held, held, held, P("shard"), held, held, held, P("shard"),
    )
    return jax.shard_map(local, mesh=mesh, in_specs=in_specs, out_specs=out_specs, check_vma=False)
```

```python
import functools
import math

import jax
import jax.numpy as jnp
from jax import lax
from jax.experimental import pallas as pl
from jax.experimental.pallas import tpu as pltpu
from jax.sharding import PartitionSpec as P

HEADS = 32
KV_HEADS = 8
HEAD = 64
GROUP = HEADS // KV_HEADS
SCALE = 1.0 / math.sqrt(HEAD)
TILE = 256
ROWS = 512
NEG = -1e30
MIB = 1024 * 1024
FULL = 63 * MIB + MIB // 2

epsilon = 1e-05
rope_base = 500000.0
F32 = jnp.float32
BF16 = jnp.bfloat16


def dot(left, right, dims):
    return lax.dot_general(left, right, (dims, ((), ())), preferred_element_type=F32)


NN = ((1,), (0,))
NT = ((1,), (1,))
TN = ((0,), (0,))
TT = ((0,), (1,))


MESH = pl.DeviceIdType.MESH


def place():
    return lax.axis_index("rep"), lax.axis_index("shard")


def remote(src, dst, sends, recvs, index, rep, shard):
    return pltpu.make_async_remote_copy(
        src_ref=src,
        dst_ref=dst,
        send_sem=sends.at[index],
        recv_sem=recvs.at[index],
        device_id=(rep, shard),
        device_id_type=MESH,
    )


def greet(partners):
    barrier = pltpu.get_barrier_semaphore()
    for partner in partners:
        pl.semaphore_signal(barrier, inc=1, device_id=partner, device_id_type=MESH)
    pl.semaphore_wait(barrier, len(partners))


def plane_partners(rep, me, shards):
    return [(rep, me ^ step) for step in range(1, shards)]


class Spread:
    def __init__(self, shards, own, full, columns, sends, recvs, held=None, held_sem=None):
        rep, me = place()
        quarter = rep % 4
        count = own.shape[0]
        part = count // 4
        own_rows = pl.ds(pl.multiple_of(quarter * part, part), part)

        def at(shard, which):
            return full.at[pl.ds(pl.multiple_of(shard * count + which * part, part), part), :]

        def piece(shard):
            return own.at[own_rows, :] if columns is None else own.at[own_rows, columns(shard)]

        self.first, self.core, self.layer, self.last = [], [], [], []
        n = shards - 1
        for i in range(n):
            peer = me ^ (i + 1)
            self.first.append(remote(piece(peer), at(me, quarter), sends, recvs, i, rep, peer))
            mine = at(peer, quarter)
            self.core.append(remote(mine, mine, sends, recvs, n + i, rep ^ 1, me))
            self.layer.append(remote(mine, mine, sends, recvs, 2 * n + i, rep ^ 2, me))
            theirs = at(peer, quarter ^ 2)
            self.last.append(remote(theirs, theirs, sends, recvs, 3 * n + i, rep ^ 1, me))
        self.take = self.keep = None
        if held is not None:
            kept = full.at[pl.ds(pl.multiple_of(me * count, count), count), :]
            self.take = pltpu.make_async_copy(own.at[:, columns(me)], held, held_sem.at[0])
            self.keep = pltpu.make_async_copy(held, kept, held_sem.at[1])

    def start(self):
        for copy in self.first:
            copy.start()
        if self.take is not None:
            self.take.start()

    def hand_on(self):
        if self.take is not None:
            self.take.wait()
            self.keep.start()
        for i, copy in enumerate(self.first):
            copy.wait_recv()
            self.layer[i].start()
            self.core[i].start()

    def hand_on_last(self):
        for i, copy in enumerate(self.layer):
            copy.wait_recv()
            self.last[i].start()

    def finish(self):
        for copy in self.core + self.last:
            copy.wait_recv()
        for copy in self.first + self.core + self.layer + self.last:
            copy.wait_send()
        if self.keep is not None:
            self.keep.wait()

    @staticmethod
    def semaphores(shards):
        n = 4 * (shards - 1)
        return [pltpu.SemaphoreType.DMA((n,)), pltpu.SemaphoreType.DMA((n,))]


class Gather:
    def __init__(self, shards, own, full, sends, recvs, local_sem=None):
        rep, me = place()
        count = own.shape[0]
        half = count // 2

        def at(shard, start, size):
            return full.at[pl.ds(pl.multiple_of(shard * count + start, half), size), :]

        self.direct, self.passed, self.kept = [], [], None
        if shards == 4:
            for i, (step, start) in enumerate(((1, 0), (2, half), (1, half), (2, 0))):
                self.direct.append(
                    remote(
                        own.at[pl.ds(start, half), :], at(me, start, half),
                        sends, recvs, i, rep, me ^ step,
                    )
                )
            for i, (step, start) in enumerate(((1, 0), (2, half))):
                came = at(me ^ step, start, half)
                self.passed.append(remote(came, came, sends, recvs, 4 + i, rep, me ^ step ^ 3))
        else:
            for i in range(shards - 1):
                self.direct.append(
                    remote(own, at(me, 0, count), sends, recvs, i, rep, me ^ (i + 1))
                )
        if local_sem is not None:
            self.kept = pltpu.make_async_copy(own, at(me, 0, count), local_sem)

    def start(self):
        for copy in self.direct:
            copy.start()
        if self.kept is not None:
            self.kept.start()

    def hand_on(self):
        for i, copy in enumerate(self.passed):
            self.direct[i].wait_recv()
            copy.start()

    def finish(self):
        for copy in self.direct[len(self.passed) :] + self.passed:
            copy.wait_recv()
        for copy in self.direct + self.passed:
            copy.wait_send()
        if self.kept is not None:
            self.kept.wait()

    @staticmethod
    def semaphores(shards):
        n = max(6, shards - 1)
        return [
            pltpu.SemaphoreType.DMA((n,)),
            pltpu.SemaphoreType.DMA((n,)),
            pltpu.SemaphoreType.DMA,
        ]


def split_rows(ref, index, size):
    return ref.at[pl.ds(pl.multiple_of(index * size, size), size), :]


def column_block(part):
    return lambda shard: pl.ds(pl.multiple_of(shard * part, part), part)


def pair_partners(rep, me):
    return [(rep ^ 1, me), (rep ^ 2, me)]


ANY = pl.BlockSpec(memory_space=pl.ANY)
IN_VMEM = pl.BlockSpec(memory_space=pltpu.VMEM)


def rope_tables(seg_col, seg_row, freqs):
    length = seg_row.shape[1]
    begins = jnp.sum((seg_col < seg_row).astype(jnp.int32), axis=0, keepdims=True)
    positions = lax.broadcasted_iota(jnp.int32, (1, length), 1) - begins
    angles = freqs * positions.astype(F32)
    return (jnp.cos(angles), jnp.sin(angles))


def side_by_side(ref, group, here):
    rows = GROUP * HEAD
    return jnp.concatenate(
        [
            ref[pl.ds(pl.multiple_of(group * rows + h * HEAD, HEAD), HEAD), here]
            for h in range(GROUP)
        ],
        axis=1,
    )


def block_bias(seg_col_ref, seg_row_ref, key_at, query_at):
    same = seg_col_ref[pl.ds(key_at, TILE), :] == seg_row_ref[:, pl.ds(query_at, TILE)]
    key_index = key_at + lax.broadcasted_iota(jnp.int32, (TILE, TILE), 0)
    query_index = query_at + lax.broadcasted_iota(jnp.int32, (TILE, TILE), 1)
    bias = jnp.where(same & (key_index <= query_index), 0.0, NEG).astype(F32)
    return jnp.concatenate([bias] * GROUP, axis=1)


def attend_kernel(
    shards, ffn_part, early, parts, tokens, seg, cot, proj_w, gate_w, up_w, *refs,
):
    count = len(parts)
    weights, refs = refs[:count], refs[count:]
    (
        gain, freqs, normed_out, cot_all, proj_m, gate_m, up_m, qkv_m,
        q_ref, k_ref, kt_ref, v_ref, out_ref, lse_ref, cos_ref, sin_ref, seg_col, seg_row,
        tokens_v, normed_v, qkv_v, turned_v, vt_ref, cot_v, seg_v, store_sem, qkv_sem, own_sem,
        seg_send, seg_recv, *sems,
    ) = refs
    rep, me = place()
    length, width = tokens_v.shape
    kv_heads = k_ref.shape[0]
    q_part, kv_part = q_ref.shape[0], kt_ref.shape[0]
    blocks = length // TILE

    at, spreads, own = 0, [], []
    for i, (weight, part) in enumerate(zip(weights, parts)):
        full, rows = qkv_v.at[:, pl.ds(at, part)], weight.shape[0]
        spreads.append(
            Spread(shards, weight, full, column_block(part), *sems[2 * i : 2 * i + 2])
        )
        own.append(
            pltpu.make_async_copy(
                weight.at[:, column_block(part)(me)], split_rows(full, me, rows), own_sem.at[i]
            )
        )
        at += part
    sems = sems[2 * count :]
    rows = Gather(shards, tokens, tokens_v, *sems[:3])
    segs = [
        remote(seg, seg_v.at[me], seg_send, seg_recv, i, rep, me ^ (i + 1))
        for i in range(shards - 1)
    ]
    own.append(pltpu.make_async_copy(seg, seg_v.at[me], own_sem.at[count]))
    take = pltpu.make_async_copy(cot, cot_v, own_sem.at[count + 1])
    sems = sems[3:]

    def first_tiles(shard):
        return pl.ds(pl.multiple_of(shard * ffn_part, ffn_part), early)

    halves = (pl.ds(0, width // 2), pl.ds(width // 2, width // 2))
    projs = [
        Spread(shards, proj_w.at[:, part], proj_m.at[:, part], None, *sems[2 * i : 2 * i + 2])
        for i, part in enumerate(halves)
    ]
    gate = Spread(shards, gate_w, gate_m, first_tiles, *sems[4:6])
    up = Spread(shards, up_w, up_m, first_tiles, *sems[6:8])
    cots = Gather(shards, cot_v, cot_all, *sems[8:11])

    for copy in (*own, take):
        copy.start()
    greet(plane_partners(rep, me, shards) + pair_partners(rep, me))
    for spread in spreads:
        spread.start()
    for copy in segs:
        copy.start()
    rows.start()
    for spread in spreads:
        spread.hand_on()
    rows.hand_on()
    for transfer in (*projs, gate, up):
        transfer.start()
    take.wait()
    cots.start()
    for spread in spreads:
        spread.hand_on_last()

    for copy in segs:
        copy.wait()
    for copy in own:
        copy.wait()
    seg_row[...] = jnp.concatenate([seg_v[i] for i in range(shards)], axis=1)
    tall = jnp.broadcast_to(seg_row[...], (8, length)).astype(F32).T[:, :1]
    seg_col[...] = tall.astype(jnp.int32)
    cos_ref[...], sin_ref[...] = rope_tables(seg_col[...], seg_row[...], freqs[...])
    for spread in spreads:
        spread.finish()
    keep_qkv = pltpu.make_async_copy(qkv_v, qkv_m, qkv_sem)
    keep_qkv.start()

    def block_rows(i):
        return pl.ds(pl.multiple_of(i * TILE, TILE), TILE)

    def store(i):
        return pltpu.make_async_copy(
            normed_v.at[i % 2], normed_out.at[block_rows(i), :], store_sem.at[i % 2]
        )

    def turn_weights(i, carry):
        turned_v[:, block_rows(i)] = qkv_v[block_rows(i), :].T
        return carry

    lax.fori_loop(0, width // TILE, turn_weights, 0)
    rows.finish()
    half = HEAD // 2

    def project(i, carry):
        here = block_rows(i)

        @pl.when(i >= 2)
        def _():
            store(i - 2).wait()

        values = tokens_v[here, :].astype(F32)
        rms = lax.rsqrt(jnp.mean(values * values, axis=-1, keepdims=True) + epsilon)
        normed_v[i % 2] = (values * rms * gain[...]).astype(BF16)
        store(i).start()
        heads = dot(turned_v[...], normed_v[i % 2], NT)
        cos, sin = cos_ref[:, here], sin_ref[:, here]

        def turned(at):
            first, second = heads[at : at + half], heads[at + half : at + HEAD]
            return (
                (first * cos - second * sin).astype(BF16),
                (second * cos + first * sin).astype(BF16),
            )

        for at in range(0, q_part, HEAD):
            first, second = turned(at)
            q_ref[at : at + half, here] = (first.astype(F32) * SCALE).astype(BF16)
            q_ref[at + half : at + HEAD, here] = (second.astype(F32) * SCALE).astype(BF16)
        for g in range(kv_heads):
            at = g * HEAD
            first, second = turned(q_part + at)
            kt_ref[at : at + half, here] = first
            kt_ref[at + half : at + HEAD, here] = second
            vt_ref[at : at + HEAD, here] = heads[
                q_part + kv_part + at : q_part + kv_part + at + HEAD
            ].astype(BF16)
            k_ref[g, here, :] = kt_ref[at : at + HEAD, here].T
            v_ref[g, here, :] = vt_ref[at : at + HEAD, here].T
        return carry

    lax.fori_loop(0, blocks, project, 0)
    for i in range(max(0, blocks - 2), blocks):
        store(i).wait()
    wide = GROUP * TILE

    def unit(at, carry_out):
        g, block = at // blocks, at % blocks
        query_at = pl.multiple_of(block * TILE, TILE)
        here = pl.ds(query_at, TILE)
        queries = side_by_side(q_ref, g, here)
        value_rows = pl.ds(pl.multiple_of(g * HEAD, HEAD), HEAD)

        def step(c, carry):
            top, total, acc = carry
            key_at = pl.multiple_of(c * TILE, TILE)
            keys = pl.ds(key_at, TILE)
            scores = dot(k_ref[g, keys, :], queries, NN)
            scores = scores + block_bias(seg_col, seg_row, key_at, query_at)
            new_top = jnp.maximum(top, jnp.max(scores, axis=0, keepdims=True))
            expo = jnp.exp(scores - new_top)
            fade = jnp.exp(top - new_top)
            total = total * fade + jnp.sum(expo, axis=0, keepdims=True)
            acc = acc * fade + dot(vt_ref[value_rows, keys], expo.astype(BF16), NN)
            return new_top, total, acc

        start = (
            jnp.full((1, wide), NEG, F32),
            jnp.zeros((1, wide), F32),
            jnp.zeros((HEAD, wide), F32),
        )
        top, total, acc = lax.fori_loop(0, block, step, step(block, start))
        mixed = (acc / total).astype(BF16)
        lse = top + jnp.log(total)
        for h in range(GROUP):
            at_row = pl.multiple_of(g * GROUP * HEAD + h * HEAD, HEAD)
            out_ref[pl.ds(at_row, HEAD), here] = mixed[:, h * TILE : (h + 1) * TILE]
            lse_ref[g, h : h + 1, here] = lse[:, h * TILE : (h + 1) * TILE]
        return carry_out

    units = kv_heads * blocks
    lax.fori_loop(0, units // 2, unit, 0)
    for proj in projs:
        proj.hand_on()
    lax.fori_loop(units // 2, units, unit, 0)
    gate.hand_on()
    up.hand_on()
    for proj in projs:
        proj.hand_on_last()
    cots.hand_on()
    gate.hand_on_last()
    up.hand_on_last()
    for transfer in (*projs, gate, up, cots):
        transfer.finish()
    keep_qkv.wait()


def attend(
    tokens, seg, weights, cot, proj_w, gate_w, up_w, gain, q_part, kv_part, early, shards
):
    count, width = tokens.shape
    length = shards * count
    kv_heads = kv_part // HEAD
    ffn_part = gate_w.shape[1] // shards
    parts = [w.shape[1] // shards for w in weights]
    freqs = rope_base ** (-(jnp.arange(HEAD // 2, dtype=F32) * (2.0 / HEAD)))
    shape = jax.ShapeDtypeStruct
    dma = pltpu.SemaphoreType.DMA
    n = shards - 1
    return pl.pallas_call(
        functools.partial(attend_kernel, shards, ffn_part, early, parts),
        in_specs=[ANY] * (6 + len(weights)) + [IN_VMEM] * 2,
        out_specs=[ANY] * 6 + [IN_VMEM] * 10,
        out_shape=[
            shape((length, width), BF16),
            shape((length, width), BF16),
            shape((shards * proj_w.shape[0], width), BF16),
            shape((width, early), BF16),
            shape((width, early), BF16),
            shape((width, sum(parts)), BF16),
            shape((q_part, length), BF16),
            shape((kv_heads, length, HEAD), BF16),
            shape((kv_part, length), BF16),
            shape((kv_heads, length, HEAD), BF16),
            shape((q_part, length), BF16),
            shape((kv_heads, GROUP, length), F32),
            shape((HEAD // 2, length), F32),
            shape((HEAD // 2, length), F32),
            shape((length, 1), jnp.int32),
            shape((1, length), jnp.int32),
        ],
        scratch_shapes=[
            pltpu.VMEM((length, width), BF16),
            pltpu.VMEM((2, TILE, width), BF16),
            pltpu.VMEM((width, sum(parts)), BF16),
            pltpu.VMEM((sum(parts), width), BF16),
            pltpu.VMEM((kv_part, length), BF16),
            pltpu.VMEM(cot.shape, BF16),
            pltpu.VMEM((shards, 1, count), jnp.int32),
            dma((2,)), dma, dma((len(weights) + 2,)), dma((n,)), dma((n,)),
        ]
        + len(weights) * Spread.semaphores(shards)
        + Gather.semaphores(shards)
        + 4 * Spread.semaphores(shards)
        + Gather.semaphores(shards),
        compiler_params=pltpu.CompilerParams(
            collective_id=1, has_side_effects=True, vmem_limit_bytes=FULL
        ),
        name="attend",
    )(tokens, seg, cot, proj_w, gate_w, up_w, *weights, gain[None, :], freqs[:, None])


def hidden_kernel(
    shards, mixed_t, proj_m, proj_w, cot_all, down_w, tokens, gain, hidden_ref, rms_ref, normed_all,
    grad_activ, proj_v, mixed_own, normed, cot_v, down_v, out_v, cot_sem, out_sem, proj_sem, mix_send, mix_recv, gather_send, gather_recv, local_sem,
):
    rep, me = place()
    part, _ = mixed_t.shape
    count = tokens.shape[0]
    rows = [
        pltpu.make_async_copy(
            split_rows(proj_m, me ^ i, part) if i else proj_w,
            split_rows(proj_v, me ^ i, part),
            proj_sem.at[i],
        )
        for i in range(shards)
    ]
    for copy in rows:
        copy.start()
    early = [
        pltpu.make_async_copy(cot_all, cot_v, cot_sem.at[0]),
        pltpu.make_async_copy(down_w, down_v, cot_sem.at[1]),
    ]
    for copy in early:
        copy.start()
    greet(plane_partners(rep, me, shards))

    def columns(shard):
        return mixed_t.at[:, pl.ds(pl.multiple_of(shard * count, count), count)]

    copies = [
        remote(columns(me ^ (i + 1)), mixed_own.at[i], mix_send, mix_recv, i, rep, me ^ (i + 1))
        for i in range(shards - 1)
    ]
    for copy in copies:
        copy.start()

    def product(block, i):
        rows[i].wait()
        return dot(block, split_rows(proj_v, me ^ i, part)[...], TN)

    hidden_ref[...] = tokens[...].astype(F32) + product(
        mixed_t[:, pl.ds(pl.multiple_of(me * count, count), count)], 0
    )
    for i, copy in enumerate(copies):
        copy.wait_recv()
        hidden_ref[...] += product(mixed_own[i], i + 1)
    hidden = hidden_ref[...]
    rms = lax.rsqrt(jnp.mean(hidden * hidden, axis=-1, keepdims=True) + epsilon)
    rms_ref[...] = rms
    normed[...] = (hidden * rms * gain[...]).astype(BF16)
    gather = Gather(shards, normed, normed_all, gather_send, gather_recv, local_sem)
    gather.start()
    for copy in copies:
        copy.wait_send()
    for copy in early:
        copy.wait()

    steps = down_w.shape[0] // TILE

    def store(i):
        at = pl.ds(pl.multiple_of(i * TILE, TILE), TILE)
        return pltpu.make_async_copy(out_v.at[i % 2], grad_activ.at[:, at], out_sem.at[i % 2])

    def step(i, carry):
        @pl.when(i >= 2)
        def _():
            store(i - 2).wait()

        units = down_v[pl.ds(pl.multiple_of(i * TILE, TILE), TILE), :]
        out_v[i % 2] = dot(cot_v[...], units, NT).astype(BF16)
        store(i).start()
        return carry

    lax.fori_loop(0, steps // 2, step, 0)
    gather.hand_on()
    lax.fori_loop(steps // 2, steps, step, 0)
    for i in range(max(0, steps - 2), steps):
        store(i).wait()
    gather.finish()


def hidden_layer(mixed_t, proj_m, proj_w, cot_all, down_w, tokens, gain, shards):
    part, length = mixed_t.shape
    count, width = tokens.shape
    n = shards - 1
    return pl.pallas_call(
        functools.partial(hidden_kernel, shards),
        in_specs=[IN_VMEM, ANY, ANY, ANY, ANY, IN_VMEM, IN_VMEM],
        out_specs=[IN_VMEM, IN_VMEM, ANY, ANY],
        out_shape=[
            jax.ShapeDtypeStruct((count, width), F32),
            jax.ShapeDtypeStruct((count, 1), F32),
            jax.ShapeDtypeStruct((length, width), BF16),
            jax.ShapeDtypeStruct((length, down_w.shape[0]), BF16),
        ],
        scratch_shapes=[
            pltpu.VMEM(proj_m.shape, BF16),
            pltpu.VMEM((n, part, count), BF16),
            pltpu.VMEM((count, width), BF16),
            pltpu.VMEM(cot_all.shape, BF16),
            pltpu.VMEM(down_w.shape, BF16),
            pltpu.VMEM((2, length, TILE), BF16),
            pltpu.SemaphoreType.DMA((2,)),
            pltpu.SemaphoreType.DMA((2,)),
            pltpu.SemaphoreType.DMA((shards,)),
            pltpu.SemaphoreType.DMA((n,)),
            pltpu.SemaphoreType.DMA((n,)),
        ]
        + Gather.semaphores(shards),
        compiler_params=pltpu.CompilerParams(
            collective_id=2, has_side_effects=True, vmem_limit_bytes=FULL
        ),
        name="hidden",
    )(mixed_t, proj_m, proj_w, cot_all, down_w, tokens, gain[None, :])


class Plan:
    def __init__(self, shards, reps, length, width, ffn_part, q_part, kv_part):
        self.shards, self.reps, self.length, self.width = shards, reps, length, width
        self.ffn_part, self.q_part, self.kv_part = ffn_part, q_part, kv_part
        self.layers = reps // 2
        self.half = self.layers // 2
        self.rows = width // 2
        self.own = width // shards
        self.block = self.own // 2
        self.proj_half = q_part // 2
        self.proj_blocks = self.rows // self.proj_half
        self.tiles = ffn_part // TILE
        self.out_tiles = width // TILE
        per_slot = 2
        self.back_slot = self.tiles
        self.send_slot = self.back_slot + -(-self.out_tiles // per_slot) - 1
        self.rows_slot = self.send_slot + 4
        self.pass_slot = self.rows_slot + 1
        self.mixed_slot = self.rows_slot + 3
        self.unit_slot = self.mixed_slot + 1
        self.per_slot = per_slot
        self.units = (length // TILE) * (kv_part // HEAD)
        self.norm_slot = self.unit_slot + self.units // 2
        self.down_at = 2 * self.tiles
        self.ffn_end = 3 * self.tiles
        self.q_at = max(self.ffn_end, self.norm_slot)
        self.kv_at = self.q_at + q_part // TILE
        self.proj_at = self.kv_at + 1
        self.chunks = self.proj_at + width // TILE // self.proj_blocks
        self.tokens_slot = max(self.norm_slot + 7, self.chunks + 1)
        self.early_res = length <= 1024
        if self.early_res:
            self.res_slot = self.send_slot + 1
            self.res_send_slot = max(self.mixed_slot + 1, self.res_slot + self.out_tiles // 2)
            self.result_slot = max(self.res_send_slot + 5, self.norm_slot + 4)
            assert self.result_slot < self.norm_slot + 5
        else:
            self.res_slot = max(self.ffn_end + 1, self.norm_slot + 1)
            self.res_send_slot = max(self.res_slot + self.out_tiles // 2 - 1, self.tokens_slot + 1)
            self.result_slot = self.res_send_slot + 6
        self.arrive = self.layers + 2
        self.spread_slot = self.mixed_slot + 1
        self.spread_first = max(0, self.send_slot + 1 - self.arrive)
        assert self.tiles >= 3
        self.hand = 4
        self.gain_slot = self.tokens_slot + 2
        self.rep_slot = max(self.chunks + self.arrive - 1, self.gain_slot + 1)
        self.slots = max(self.chunks + self.arrive + self.hand, self.rep_slot, self.result_slot) + 1
        assert self.spread_slot + self.chunks // 2 < self.slots - self.hand
        self.mine_ring = self.half + 1
        self.sum_ring = 3


def backward_kernel(
    plan, early, x, cot_all, grad_activ, gate_w, up_w, gate_e, up_e, down_w, hidden, tokens, proj_w, qkv_m,
    normed,
    mlp_rms, mlp_gain, attn_gain, seg_col, seg_row, cos_ref, sin_ref, lse_ref, q_ref, mixed_ref,
    k_ref, kt_ref, v_ref,
    f_down, f_gate, f_up, f_proj, f_q, f_kv, result_ref, tokens_out, gains_out,
    swapped, from_outer, from_middle, totals, back_land, res_land, norm_land, norm_part,
    gate_m, up_m, activ, dgate, dup, back_part, res_part,
    left_a, left_b, right, gate_v, up_v, grad_v, back_v, tile_v, both, proj_v, qkv_v, hidden_v,
    row_sum, land_v,
    mine, theirs, swap_v, outer_v, middle_v, sums, total_v,
    grad_hidden, gh_own, g_t, back_t, dk_acc, dv_acc, activ_v,
    gain_part, gain_land, gain_sum, gain_reps,
    load_sem, right_sem, small_sem, swap_send, swap_recv, in_send, outer_recv, middle_recv,
    out_send, total_recv, total_store, cross_recv, cross_send, pass_send, pass_recv,
    back_send, back_recv, res_send, res_recv, norm_send, norm_recv,
    gather_send, gather_recv, gather_local, gain_send, gain_recv, rep_send, rep_recv,
    tile_send, tile_recv, tile_pass, tile_passed, down_sem, back_sem, tile_sem,
):
    p = plan
    shards, reps, n = p.shards, p.reps, p.shards - 1
    rep, me = place()
    core, layer = rep % 2, rep // 2
    upper = layer >= p.half
    depth = jnp.where(upper, p.layers - 1 - layer, layer)
    inward = jnp.where(upper, rep - 2, rep + 2)
    outward = jnp.where(upper, rep + 2, rep - 2)
    is_middle = depth == p.half - 1
    count = tokens.shape[0]
    ffn_end, proj_at, q_at, kv_at, end_at = p.ffn_end, p.proj_at, p.q_at, p.kv_at, p.chunks
    gh_all = both.at[:, pl.ds(0, p.width)]

    def columns(index, size=TILE):
        return pl.ds(pl.multiple_of(index * size, size), size)

    def load(src, dst, i):
        return pltpu.make_async_copy(src, dst, load_sem.at[i])

    load_cot = load(cot_all, left_a, 0)
    load_x = load(x, left_b, 1)
    load_normed = load(normed, left_a, 2)
    load_proj = load(proj_w, proj_v, 3)
    load_qkv = load(qkv_m, qkv_v, 4)
    load_hidden = load(hidden, hidden_v, 5)
    load_activ = load(activ, left_b.at[:, pl.ds(0, p.ffn_part)], 6)
    load_tokens = load(tokens, gh_own, 7)
    first_tile = early // TILE
    assert first_tile >= 2 or p.tiles < 3

    def tile_bytes(tile, sem):
        piece = gate_m.at[pl.ds(0, 2 * n * p.block), pl.ds(0, TILE)]
        return pltpu.make_async_copy(piece, piece, sem.at[tile])

    def send_tile(tile):
        rows = columns(core, p.block)
        into = pl.ds(pl.multiple_of(me * p.own + core * p.block, p.block), p.block)
        for weight, full in ((gate_w, gate_m), (up_w, up_m)):
            for i in range(n):
                peer = me ^ (i + 1)
                at = pl.ds(pl.multiple_of(peer * p.ffn_part + tile * TILE, TILE), TILE)
                pltpu.make_async_remote_copy(
                    src_ref=weight.at[rows, at], dst_ref=full.at[into, columns(tile)],
                    send_sem=tile_send.at[tile], recv_sem=tile_recv.at[tile],
                    device_id=(rep, peer), device_id_type=MESH,
                ).start()

    def pass_tile(tile):
        tile_bytes(tile, tile_recv).wait()
        for full in (gate_m, up_m):
            for i in range(n):
                peer = me ^ (i + 1)
                at = pl.ds(pl.multiple_of(peer * p.own + core * p.block, p.block), p.block)
                piece = full.at[at, columns(tile)]
                pltpu.make_async_remote_copy(
                    src_ref=piece, dst_ref=piece,
                    send_sem=tile_pass.at[tile], recv_sem=tile_passed.at[tile],
                    device_id=(rep ^ 1, me), device_id_type=MESH,
                ).start()

    def load_grad(tile):
        return pltpu.make_async_copy(grad_activ.at[:, columns(tile)], grad_v, down_sem.at[0])

    def load_tile(tile):
        @pl.when(tile >= first_tile)
        def _():
            tile_bytes(tile, tile_passed).wait()

        own_at = pl.ds(pl.multiple_of(me * p.ffn_part + tile * TILE, TILE), TILE)
        held_rows = [pl.ds(pl.multiple_of((me ^ i) * p.own, p.own), p.own) for i in range(shards)]
        for i, (weight, tiles, full, held) in enumerate(
            ((gate_w, gate_e, gate_m, gate_v), (up_w, up_e, up_m, up_v))
        ):
            sem = down_sem.at[i + 1]
            pltpu.make_async_copy(weight.at[:, own_at], held.at[held_rows[0], :], sem).start()
            for rows in held_rows[1:]:

                @pl.when(tile < first_tile)
                def _(rows=rows, tiles=tiles, held=held, sem=sem):
                    src = tiles.at[rows, columns(tile)]
                    pltpu.make_async_copy(src, held.at[rows, :], sem).start()

                @pl.when(tile >= first_tile)
                def _(rows=rows, full=full, held=held, sem=sem):
                    src = full.at[rows, columns(tile)]
                    pltpu.make_async_copy(src, held.at[rows, :], sem).start()

        load_grad(tile).start()

    def units_of(tile):
        return activ_v.at[:, columns(tile)] if p.early_res else tile_v.at[tile % 2]

    def store_tile(tile):
        dup_columns = pl.ds(pl.multiple_of(p.ffn_part + tile * TILE, TILE), TILE)
        return [
            pltpu.make_async_copy(src, dst.at[:, columns(tile)], tile_sem.at[i])
            for i, (src, dst) in enumerate(
                (
                    (units_of(tile), activ),
                    (both.at[:, columns(tile)], dgate),
                    (both.at[:, dup_columns], dup),
                )
            )
        ]

    def stored(tile):
        for copy in store_tile(tile):
            copy.wait()

    def ffn_tile(tile):
        for i, held in enumerate((gate_v, up_v)):
            pltpu.make_async_copy(held, held, down_sem.at[i + 1]).wait()
        load_grad(tile).wait()
        dup_columns = pl.ds(pl.multiple_of(p.ffn_part + tile * TILE, TILE), TILE)

        def go(i, carry):
            here = columns(i, ROWS)
            rows = left_b[here, :]
            gate = dot(rows, gate_v[...], NN)
            up = dot(rows, up_v[...], NN)
            grad = grad_v[here, :].astype(F32)
            sigm = jax.nn.sigmoid(gate)
            swish = gate * sigm
            units_of(tile)[here, :] = (swish * up).astype(BF16)
            both[here, columns(tile)] = (
                grad * up * sigm * (1.0 + gate * (1.0 - sigm))
            ).astype(BF16)
            both[here, dup_columns] = (grad * swish).astype(BF16)
            return carry

        lax.fori_loop(0, p.length // ROWS, go, 0)

        @pl.when(tile >= 3)
        def _():
            stored(tile - 1)

        for copy in store_tile(tile):
            copy.start()

        @pl.when(tile <= 1)
        def _():
            stored(tile)

        @pl.when(tile + 1 < p.tiles)
        def _():
            load_tile(tile + 1)

        @pl.when(tile + 1 == p.tiles)
        def _():
            load_back(0)

    def load_back(tile):
        slot = tile % 2
        per_shard = p.own // TILE
        for i, (weight, tiles, full) in enumerate(
            ((gate_w, gate_e, gate_m), (up_w, up_e, up_m))
        ):
            sem, at = back_sem.at[slot, i], i * p.ffn_part

            @pl.when(tile // per_shard == me)
            def _(weight=weight, sem=sem, at=at):
                src = weight.at[columns(tile - me * per_shard), columns(me, p.ffn_part)]
                pltpu.make_async_copy(src, back_v.at[slot, :, pl.ds(at, p.ffn_part)], sem).start()

            @pl.when(tile // per_shard != me)
            def _(tiles=tiles, full=full, sem=sem, at=at):
                into = back_v.at[slot, :, pl.ds(at, early)]
                pltpu.make_async_copy(tiles.at[columns(tile), :], into, sem).start()
                rest = p.ffn_part - early
                into = back_v.at[slot, :, pl.ds(at + early, rest)]
                src = full.at[columns(tile), pl.ds(early, rest)]
                pltpu.make_async_copy(src, into, sem).start()

    def wait_back(tile):
        slot = tile % 2
        for i in range(2):
            half = back_v.at[slot, :, pl.ds(i * p.ffn_part, p.ffn_part)]
            pltpu.make_async_copy(half, half, back_sem.at[slot, i]).wait()

    def back_tiles(first):
        def store(tile):
            return pltpu.make_async_copy(
                tile_v.at[tile % 2], back_part.at[:, columns(tile)], tile_sem.at[tile % 2]
            )

        @pl.when(first == 0)
        def _():
            stored(p.tiles - 1)

        def tile_go(k, carry):
            tile = first + k
            wait_back(tile)

            @pl.when(tile + 1 < p.out_tiles)
            def _():
                load_back(tile + 1)

            @pl.when(k >= 2)
            def _():
                store(tile - 2).wait()

            def go(i, c):
                here = columns(i, ROWS)
                tile_v[tile % 2, here, :] = dot(both[here, :], back_v[tile % 2], NT).astype(BF16)
                return c

            lax.fori_loop(0, p.length // ROWS, go, 0)
            store(tile).start()
            return carry

        size = jnp.minimum(p.per_slot, p.out_tiles - first)
        lax.fori_loop(0, size, tile_go, 0)
        store(first + size - 2).wait()
        store(first + size - 1).wait()

    def load_res(tile):
        def copies(action):
            for i, held in enumerate((gate_v, up_v)):

                @pl.when(tile % 2 == i)
                def _(i=i, held=held):
                    action(
                        pltpu.make_async_copy(
                            down_w.at[:, columns(tile)], held.at[pl.ds(0, p.ffn_part), :], back_sem.at[i, 0]
                        )
                    )

        return copies

    def res_tiles(first):
        hidden_units = activ_v if p.early_res else left_b

        def store(tile):
            return pltpu.make_async_copy(
                tile_v.at[tile % 2], res_part.at[:, columns(tile)], tile_sem.at[tile % 2]
            )

        for k, held in enumerate((gate_v, up_v)):
            tile = first + k
            load_res(tile)(lambda copy: copy.wait())

            @pl.when(tile + 1 < p.out_tiles)
            def _(tile=tile):
                load_res(tile + 1)(lambda copy: copy.start())

            def go(i, c, k=k, held=held):
                here = columns(i, ROWS)
                tile_v[k, here, :] = dot(
                    hidden_units[here, : p.ffn_part], held[: p.ffn_part, :], NN
                ).astype(BF16)
                return c

            lax.fori_loop(0, p.length // ROWS, go, 0)
            store(tile).start()
        store(first).wait()
        store(first + 1).wait()

    def is_chunk(j, kind):
        if kind == 0:
            return (j >= p.down_at) & (j < ffn_end)
        return (j >= 0) & (j < p.down_at) & (j % 2 == kind - 1)

    def tile_of(j):
        return jnp.where(j < p.down_at, j // 2, j - p.down_at)

    def load_right(t):
        slot = right.at[t % 2]

        def copies(action):
            for i, ref in enumerate((activ, dgate, dup)):

                @pl.when(is_chunk(t, i))
                def _(ref=ref):
                    action(
                        pltpu.make_async_copy(
                            ref.at[:, columns(tile_of(t))], slot, right_sem.at[t % 2]
                        )
                    )

        return copies

    side = p.width // 2
    left_half, right_half = pl.ds(0, side), pl.ds(side, side)

    def rows_of(shard):
        return pl.ds(pl.multiple_of(shard * count, count), count)

    class Scatter:
        def __init__(self, part, land, sends, recvs):
            self.part, self.land = part, land
            self.second = []
            if shards != 4:
                self.first = [
                    remote(split_rows(part, me ^ (i + 1), count), land.at[i], sends, recvs, i, rep, me ^ (i + 1))
                    for i in range(n)
                ]
                return
            order = (
                (3, left_half, 0, right_half, 1),
                (3, right_half, 1, right_half, 2),
                (1, left_half, 0, left_half, 1),
                (2, right_half, 1, left_half, 2),
            )
            self.first = [
                remote(
                    part.at[rows_of(me ^ block), cols], land.at[into, :, into_cols],
                    sends, recvs, i, rep, me ^ to,
                )
                for i, (block, cols, into, into_cols, to) in enumerate(order)
            ]
            self.second = [
                remote(gh_own.at[:, cols], land.at[2, :, cols], sends, recvs, 4 + i, rep, me ^ to)
                for i, (cols, to) in enumerate(((left_half, 2), (right_half, 1)))
            ]

        def start(self):
            for copy in self.first:
                copy.start()

        def hand_on(self):
            if not self.second:
                return
            for copy in self.first[:2]:
                copy.wait_recv()
            loads = [
                (self.part.at[rows_of(me ^ 2), left_half], 0, left_half),
                (self.part.at[rows_of(me ^ 1), right_half], 0, right_half),
                (self.land.at[0, :, right_half], 1, left_half),
                (self.land.at[1, :, right_half], 1, right_half),
            ]
            for src, slot, cols in loads:
                pltpu.make_async_copy(src, land_v.at[slot, :, cols], small_sem.at[slot]).start()
            for slot in range(2):
                pltpu.make_async_copy(land_v.at[slot], land_v.at[slot], small_sem.at[slot]).wait()

            def strip(here):
                gh_own[here, :] = (
                    land_v[0, here, :].astype(F32) + land_v[1, here, :].astype(F32)
                ).astype(BF16)

            strips(strip)
            for copy in self.second:
                copy.start()

        def fetch(self):
            for copy in self.first[2 if self.second else 0 :] + self.second:
                copy.wait_recv()
            for copy in self.second:
                copy.wait_send()
            pieces = [[(split_rows(self.part, me, count), pl.ds(0, p.width))]]
            if self.second:
                pieces.append(
                    [
                        (self.land.at[0, :, left_half], left_half),
                        (self.land.at[1, :, left_half], right_half),
                    ]
                )
                pieces.append([(self.land.at[2], pl.ds(0, p.width))])
            else:
                pieces += [[(self.land.at[i], pl.ds(0, p.width))] for i in range(n)]

            def load(i):
                for src, cols in pieces[i]:
                    pltpu.make_async_copy(
                        src, land_v.at[i % 2, :, cols], small_sem.at[i % 2]
                    ).start()

            load(0)
            for i in range(len(pieces)):
                if i + 1 < len(pieces):
                    load(i + 1)
                held = land_v.at[i % 2]
                pltpu.make_async_copy(held, held, small_sem.at[i % 2]).wait()

                def strip(here, i=i):
                    value = land_v[i % 2, here, :].astype(F32)
                    row_sum[here, :] = value if i == 0 else row_sum[here, :] + value

                strips(strip)

        def settle(self):
            for copy in self.first:
                copy.wait_send()

    back_rows = Scatter(back_part, back_land, back_send, back_recv)
    res_rows = Scatter(res_part, res_land, res_send, res_recv)
    norm_rows = Scatter(norm_part, norm_land, norm_send, norm_recv)

    STRIP = 32

    def strips(body):
        def go(i, carry):
            body(pl.ds(pl.multiple_of(i * STRIP, STRIP), STRIP))
            return carry

        lax.fori_loop(0, count // STRIP, go, 0)

    def norm_strip(here, values, rms, gain, row):
        grad_in = row_sum[here, :]
        weighted = grad_in * gain
        inner = jnp.mean(weighted * values, axis=-1, keepdims=True)
        gain_part[row : row + 1, :] += jnp.sum(grad_in * values * rms, axis=0, keepdims=True)
        return rms * weighted - values * (rms * rms * rms) * inner

    gather = Gather(shards, gh_own, gh_all, gather_send, gather_recv, gather_local)

    def hidden_back():
        load_hidden.wait()
        back_rows.fetch()
        gain_part[...] = jnp.zeros_like(gain_part)

        def strip(here):
            own = pl.ds(pl.multiple_of(me * count, count) + here.start, STRIP)
            grad = left_a[own, :].astype(F32) + norm_strip(
                here, hidden_v[here, :], mlp_rms[here, :], mlp_gain[...], 1
            )
            grad_hidden[here, :] = grad
            gh_own[here, :] = grad.astype(BF16)

        strips(strip)
        gather.start()

    def finish_result():
        res_rows.fetch()

        def strip(here):
            row_sum[here, :] = hidden_v[here, :] + row_sum[here, :]

        strips(strip)
        store_result = pltpu.make_async_copy(row_sum, result_ref, small_sem.at[0])
        store_result.start()
        store_result.wait()

    def mixed_back():
        gather.finish()
        load_proj.wait()

        def go(i, carry):
            here = pl.ds(pl.multiple_of(i * TILE, TILE), TILE)
            g_t[:, here] = dot(proj_v[...], both[here, : p.width], NT).astype(BF16)
            return carry

        lax.fori_loop(0, p.length // TILE, go, 0)

    blocks = p.length // TILE
    rows = GROUP * HEAD
    wide = GROUP * TILE
    mid = HEAD // 2

    def attention_unit(unit):
        g, turn = unit // blocks, unit % blocks
        block = jnp.where(turn % 2 == 0, turn // 2, blocks - 1 - turn // 2)
        query_at = pl.multiple_of(block * TILE, TILE)
        here_q = pl.ds(query_at, TILE)

        queries = side_by_side(q_ref, g, here_q)
        grads = side_by_side(g_t, g, here_q)
        mixed = side_by_side(mixed_ref, g, here_q)
        lse = jnp.concatenate([lse_ref[g, h : h + 1, here_q] for h in range(GROUP)], axis=1)
        inner = jnp.sum(grads.astype(F32) * mixed.astype(F32), axis=0, keepdims=True)

        @pl.when(turn == 0)
        def _():
            dk_acc[...] = jnp.zeros_like(dk_acc)
            dv_acc[...] = jnp.zeros_like(dv_acc)

        def step(c, acc):
            key_at = pl.multiple_of(c * TILE, TILE)
            here = pl.ds(key_at, TILE)
            scores = dot(k_ref[g, here, :], queries, NN)
            scores = scores + block_bias(seg_col, seg_row, key_at, query_at)
            probs = jnp.exp(scores - lse)
            grad_probs = dot(v_ref[g, here, :], grads, NN)
            grad_scores = (probs * (grad_probs - inner)).astype(BF16)
            dv_acc[:, here] += dot(grads, probs.astype(BF16), NT)
            dk_acc[:, here] += dot(queries, grad_scores, NT)
            key_rows = pl.ds(pl.multiple_of(g * HEAD, HEAD), HEAD)
            return acc + dot(kt_ref[key_rows, here], grad_scores, NN)

        acc = lax.fori_loop(0, block + 1, step, jnp.zeros((HEAD, wide), F32))
        cos, sin = cos_ref[:, here_q], sin_ref[:, here_q]
        for h in range(GROUP):
            grad = acc[:, h * TILE : (h + 1) * TILE] * SCALE
            first, second = grad[:mid], grad[mid:]
            at = pl.multiple_of(g * rows + h * HEAD, HEAD)
            back_t[pl.ds(at, mid), here_q] = (first * cos + second * sin).astype(BF16)
            back_t[pl.ds(at + mid, mid), here_q] = (second * cos - first * sin).astype(BF16)

        @pl.when(turn == blocks - 1)
        def _():
            cos, sin = cos_ref[...], sin_ref[...]
            first, second = dk_acc[:mid, :], dk_acc[mid:, :]
            at = pl.multiple_of(p.q_part + g * HEAD, HEAD)
            back_t[pl.ds(at, mid), :] = (first * cos + second * sin).astype(BF16)
            back_t[pl.ds(at + mid, mid), :] = (second * cos - first * sin).astype(BF16)
            at = pl.multiple_of(p.q_part + p.kv_part + g * HEAD, HEAD)
            back_t[pl.ds(at, HEAD), :] = dv_acc[...].astype(BF16)

    def normed_back():
        load_qkv.wait()

        stores = [
            pltpu.make_async_copy(
                land_v.at[i % 2], norm_part.at[pl.ds(i * count, count), :], small_sem.at[i % 2]
            )
            for i in range(shards)
        ]
        for i, store in enumerate(stores):
            if i >= 2:
                stores[i - 2].wait()
            here = pl.ds(i * count, count)
            land_v[i % 2] = dot(back_t[:, here].T, qkv_v[...], NT).astype(BF16)
            store.start()
        for store in stores[-2:]:
            store.wait()
        norm_rows.start()

    gain_cols = p.width // shards

    def gain_slice(shard):
        return pl.ds(pl.multiple_of(shard * gain_cols, gain_cols), gain_cols)

    gain_plane = [
        remote(
            gain_part.at[:, gain_slice(me ^ (i + 1))], gain_land.at[me],
            gain_send, gain_recv, i, rep, me ^ (i + 1),
        )
        for i in range(n)
    ]
    gain_all = [
        remote(gain_sum, gain_reps.at[rep], rep_send, rep_recv, i, rep ^ (i + 1), me)
        for i in range(reps - 1)
    ]

    def tokens_back():
        norm_rows.fetch()
        load_tokens.start()
        load_tokens.wait()

        def strip(here):
            values = gh_own[here, :].astype(F32)
            rms = lax.rsqrt(jnp.mean(values * values, axis=-1, keepdims=True) + epsilon)
            grad_hidden[here, :] += norm_strip(here, values, rms, attn_gain[...], 0)

        strips(strip)
        store_tokens = pltpu.make_async_copy(grad_hidden, tokens_out, small_sem.at[0])
        store_tokens.start()
        store_tokens.wait()
        gain_land[me] = gain_part[:, gain_slice(me)]
        for copy in gain_plane:
            copy.start()

    def gains_plane():
        for copy in gain_plane:
            copy.wait_recv()
        total = gain_land[0]
        for s in range(1, shards):
            total = total + gain_land[s]
        gain_sum[...] = total
        gain_reps[rep] = total
        for copy in gain_all:
            copy.start()

    def gains_reps():
        for copy in gain_all:
            copy.wait_recv()
        total = gain_reps[0]
        for r in range(1, reps):
            total = total + gain_reps[r]
        gains_out[...] = total

    def swap_copy(j):
        return pltpu.make_async_remote_copy(
            src_ref=theirs.at[j % 2], dst_ref=swapped.at[j],
            send_sem=swap_send.at[j % 2], recv_sem=swap_recv.at[j],
            device_id=(rep ^ 1, me), device_id_type=MESH,
        )

    def store_chunk(slot, other_slot, at, size, product, columns=TILE):
        here = pl.ds(pl.multiple_of(at, size), size)
        mine[slot, here, :columns] = product(core).astype(BF16)
        theirs[other_slot, here, :columns] = product(1 - core).astype(BF16)

    def make(t):
        slot, other = t % p.mine_ring, t % 2

        @pl.when(t >= 2)
        def _():
            swap_copy(t - 2).wait_send()

        @pl.when(t == 0)
        def _():
            load_right(0)(lambda copy: copy.start())

        load_right(t)(lambda copy: copy.wait())

        @pl.when(t + 1 < ffn_end)
        def _():
            load_right(t + 1)(lambda copy: copy.start())

        @pl.when(is_chunk(t, 0))
        def _():
            left = right[t % 2].T

            def product(which):
                return dot(left, left_a[:, columns(which, p.rows)], NN).astype(BF16)

            ours, others = product(core), product(1 - core)
            for at in range(0, p.rows, TILE):
                mine[slot, at : at + TILE, :] = ours[:, at : at + TILE]
                theirs[other, at : at + TILE, :] = others[:, at : at + TILE]

        def wide_chunk(left, factor, columns):
            def go(s, carry):
                def product(which):
                    at = pl.multiple_of(s * p.own + which * p.block, p.block)
                    return dot(factor, left[:, pl.ds(at, p.block)], NN).T

                store_chunk(slot, other, s * p.block, p.block, product, columns)
                return carry

            lax.fori_loop(0, shards, go, 0)

        @pl.when(t < p.down_at)
        def _():
            wide_chunk(left_b, right[t % 2].T, TILE)

        @pl.when((t >= proj_at) & (t < end_at))
        def _():
            def go(i, carry):
                at = columns((t - proj_at) * p.proj_blocks + i)

                def product(which):
                    part = columns(which, p.proj_half)
                    return dot(mixed_ref[part, :], both[:, at], NN)

                store_chunk(slot, other, i * p.proj_half, p.proj_half, product)
                return carry

            lax.fori_loop(0, p.proj_blocks, go, 0)

        @pl.when((t >= q_at) & (t < kv_at))
        def _():
            wide_chunk(left_a, back_t[columns(t - q_at), :], TILE)

        @pl.when(t == kv_at)
        def _():
            wide_chunk(left_a, back_t[p.q_part :, :], 2 * p.kv_part)

        swap_copy(t).start()

    def inward_copies(j):
        common = dict(
            src_ref=sums.at[j % p.sum_ring], send_sem=in_send.at[j % p.sum_ring],
            device_id=(inward, me), device_id_type=MESH,
        )
        to_layer = pltpu.make_async_remote_copy(
            dst_ref=from_outer.at[j], recv_sem=outer_recv.at[j], **common
        )
        to_middle = pltpu.make_async_remote_copy(
            dst_ref=from_middle.at[j], recv_sem=middle_recv.at[j], **common
        )
        return to_layer, to_middle

    def total_places(j, action):
        @pl.when(is_chunk(j, 0))
        def _():
            action(
                [
                    (
                        i * TILE, TILE, TILE,
                        f_down.at[
                            columns(tile_of(j)),
                            pl.ds(pl.multiple_of(core * p.rows + i * TILE, TILE), TILE),
                        ],
                    )
                    for i in range(p.rows // TILE)
                ]
            )

        @pl.when((j >= proj_at) & (j < end_at))
        def _():
            action(
                [
                    (
                        i * p.proj_half, p.proj_half, TILE,
                        f_proj.at[
                            columns(core, p.proj_half),
                            columns((j - proj_at) * p.proj_blocks + i),
                        ],
                    )
                    for i in range(p.proj_blocks)
                ]
            )

        for when, full, part, tile, sem, wide_by in wide_kinds(j):

            @pl.when(when)
            def _(full=full, part=part, tile=tile, wide_by=wide_by):
                blocks = []
                for i in range(shards):
                    at = pl.multiple_of((me ^ i) * p.block, p.block)
                    place_there = totals.at[j, pl.ds(at, p.block), pl.ds(0, wide_by)]
                    if i == 0:
                        place_there = window(full, me, part, tile, wide_by)
                    blocks.append((at, p.block, wide_by, place_there))
                action(blocks)

    def chunk_bytes(j, sem):
        @pl.when(j == kv_at)
        def _():
            whole = totals.at[0, :, pl.ds(0, 2 * p.kv_part)]
            pltpu.make_async_copy(whole, whole, sem).wait()

        @pl.when(j != kv_at)
        def _():
            whole = totals.at[0]
            pltpu.make_async_copy(whole, whole, sem).wait()

    def send_total(src, dst, j):
        return pltpu.make_async_remote_copy(
            src_ref=src, dst_ref=dst, send_sem=out_send.at[j % 2],
            recv_sem=total_recv.at[j], device_id=(outward, me), device_id_type=MESH,
        )

    def add_rows(body):
        def go(i, carry):
            body(pl.ds(pl.multiple_of(i * TILE, TILE), TILE))
            return carry

        lax.fori_loop(0, p.rows // TILE, go, 0)

    def load_swapped(j):
        return pltpu.make_async_copy(swapped.at[j], swap_v, small_sem.at[2])

    def load_outer(j):
        return pltpu.make_async_copy(from_outer.at[j], outer_v, small_sem.at[3])

    def load_middle(j):
        return pltpu.make_async_copy(from_middle.at[j], middle_v, small_sem.at[4])

    def valid(j):
        return (j >= 0) & (j < p.chunks)

    def take_inward(j):
        @pl.when(valid(j))
        def _():
            swap_copy(j).wait_recv()
            load_swapped(j).start()

            @pl.when(depth > 0)
            def _():
                inward_copies(j)[0].wait_recv()
                load_outer(j).start()

    def send_inward(j):
        @pl.when(valid(j))
        def _():
            @pl.when(j >= p.sum_ring)
            def _():
                inward_copies(j - p.sum_ring)[0].wait_send()

            load_swapped(j).wait()
            ours = mine.at[j % p.mine_ring]
            total = sums.at[j % p.sum_ring]

            @pl.when(depth > 0)
            def _():
                load_outer(j).wait()

                def add(here):
                    total[here, :] = (
                        ours[here, :].astype(F32)
                        + swap_v[here, :].astype(F32)
                        + outer_v[here, :].astype(F32)
                    ).astype(BF16)

                add_rows(add)

            @pl.when(depth == 0)
            def _():
                def add(here):
                    total[here, :] = (
                        ours[here, :].astype(F32) + swap_v[here, :].astype(F32)
                    ).astype(BF16)

                add_rows(add)

            to_layer, to_middle = inward_copies(j)

            @pl.when(is_middle)
            def _():
                to_middle.start()

            @pl.when(jnp.logical_not(is_middle))
            def _():
                to_layer.start()

    def take_middle(j):
        @pl.when(is_middle & valid(j))
        def _():
            inward_copies(j)[1].wait_recv()
            load_middle(j).start()

    def meet_in_middle(j):
        @pl.when(is_middle & valid(j))
        def _():
            @pl.when(j >= 1)
            def _():
                chunk_bytes(j - 1, total_store.at[0])

            if p.half > 1:

                @pl.when(j >= 2)
                def _():
                    chunk_bytes(j - 2, out_send.at[j % 2])

            load_middle(j).wait()
            out, held = total_v.at[j % 2], sums.at[j % p.sum_ring]

            def add(here):
                out[here, :] = (
                    held[here, :].astype(F32) + middle_v[here, :].astype(F32)
                ).astype(BF16)

            add_rows(add)

            def put(blocks):
                for at, size, wide_by, dst in blocks:
                    src = out.at[pl.ds(at, size), pl.ds(0, wide_by)]
                    if p.half > 1:
                        send_total(src, dst, j).start()
                    pltpu.make_async_copy(src, dst, total_store.at[0]).start()

            total_places(j, put)

    def last_store(t):
        @pl.when(is_middle & (t == p.chunks + p.arrive - 1))
        def _():
            chunk_bytes(p.chunks - 1, total_store.at[0])

    def send_outward(j):
        @pl.when(jnp.logical_not(is_middle) & valid(j))
        def _():
            chunk_bytes(j, total_recv.at[j])

            if p.half > 2:

                @pl.when(depth > 0)
                def _():
                    @pl.when(j >= 2)
                    def _():
                        chunk_bytes(j - 2, out_send.at[j % 2])

                    def put(blocks):
                        for _, _, _, dst in blocks:
                            send_total(dst, dst, j).start()

                    total_places(j, put)

    def remote_pass(src, dst, sem):
        return pltpu.make_async_remote_copy(
            src_ref=src, dst_ref=dst, send_sem=pass_send.at[sem], recv_sem=pass_recv.at[sem],
            device_id=(rep ^ 1, me), device_id_type=MESH,
        )

    def window(full, shard, part, tile, columns=TILE):
        at = pl.multiple_of(shard * part + tile * columns, columns)
        return full.at[pl.ds(pl.multiple_of(core * p.block, p.block), p.block), pl.ds(at, columns)]

    def wide_kinds(j):
        return (
            (is_chunk(j, 1), f_gate, p.ffn_part, tile_of(j), 1, TILE),
            (is_chunk(j, 2), f_up, p.ffn_part, tile_of(j), 2, TILE),
            ((j >= q_at) & (j < kv_at), f_q, p.q_part, j - q_at, 4, TILE),
            (j == kv_at, f_kv, 2 * p.kv_part, 0, 5, 2 * p.kv_part),
        )

    def spread_total(j):
        for kind, sem in ((is_chunk(j, 0), 0), ((j >= proj_at) & (j < end_at), 3)):

            @pl.when(kind)
            def _(sem=sem):
                def put(blocks):
                    for _, _, _, dst in blocks:
                        remote_pass(dst, dst, sem).start()

                total_places(j, put)

        for when, full, part, tile, sem, wide_by in wide_kinds(j):

            @pl.when(when)
            def _(full=full, part=part, tile=tile, sem=sem, wide_by=wide_by):
                place_here = window(full, me, part, tile, wide_by)
                for i in range(n):
                    at = columns(me ^ (i + 1), p.block)
                    pltpu.make_async_remote_copy(
                        src_ref=totals.at[j, at, pl.ds(0, wide_by)], dst_ref=place_here,
                        send_sem=cross_send.at[sem], recv_sem=cross_recv.at[j],
                        device_id=(rep, me ^ (i + 1)), device_id_type=MESH,
                    ).start()
                remote_pass(place_here, place_here, sem).start()

    def pass_on(j):
        for when, full, part, tile, sem, wide_by in wide_kinds(j):

            @pl.when(when)
            def _(full=full, part=part, tile=tile, sem=sem, wide_by=wide_by):
                came = totals.at[j, pl.ds(0, n * p.block), pl.ds(0, wide_by)]
                pltpu.make_async_copy(came, came, cross_recv.at[j]).wait()
                for i in range(n):
                    here = window(full, me ^ (i + 1), part, tile, wide_by)
                    remote_pass(here, here, sem).start()

    for copy in (load_x, load_cot):
        copy.start()
    load_tile(0)
    greet(plane_partners(rep, me, shards) + [(rep ^ i, me) for i in range(1, reps)])
    ahead = 3
    for tile in range(first_tile, min(first_tile + ahead, p.tiles)):
        send_tile(tile)
    for copy in (load_hidden, load_proj, load_qkv):
        copy.start()
    for copy in (load_x, load_cot):
        copy.wait()

    def slot(t, carry):
        inner = t - 1 - depth
        met = t - 1 - p.half
        take_inward(inner)
        send_inward(inner)
        send_outward(t - p.arrive + depth)

        def spread_until(u):
            ready = jnp.minimum(u - p.arrive + 1, p.chunks)
            later = p.spread_first + 2 * jnp.maximum(u - p.spread_slot + 1, 0)
            most = jnp.where(u <= p.send_slot, p.chunks, later)
            return jnp.maximum(jnp.minimum(ready, most), 0)

        def over(action, u):
            def go(j, c):
                action(j)
                return c

            lax.fori_loop(spread_until(u - 1), spread_until(u), go, 0)

        last_store(t)
        over(spread_total, t)
        over(pass_on, t - p.hand)

        @pl.when(t + first_tile + ahead < p.tiles)
        def _():
            send_tile(t + first_tile + ahead)

        @pl.when((t > 0) & (t + 1 >= first_tile) & (t + 1 < p.tiles))
        def _():
            pass_tile(t + 1)

        @pl.when(t < p.tiles)
        def _():
            ffn_tile(t)

        @pl.when((t >= p.back_slot) & (t <= p.send_slot))
        def _():
            back_tiles((t - p.back_slot) * p.per_slot)

        @pl.when(t == ffn_end)
        def _():
            load_normed.start()
            if not p.early_res:
                load_activ.start()

        @pl.when(t == q_at)
        def _():
            load_normed.wait()

        def at(when, action):
            @pl.when(t == when)
            def _():
                action()

        at(p.tokens_slot, tokens_back)
        take_middle(met)
        meet_in_middle(met)
        at(p.send_slot, back_rows.start)
        at(p.send_slot + 2, back_rows.hand_on)
        at(p.rows_slot, hidden_back)
        at(p.pass_slot, gather.hand_on)
        at(p.mixed_slot, mixed_back)

        @pl.when((t >= p.unit_slot) & (t < p.norm_slot))
        def _():
            def go(i, c):
                attention_unit((t - p.unit_slot) * 2 + i)
                return c

            lax.fori_loop(0, 2, go, 0)

        at(p.norm_slot, normed_back)
        at(p.norm_slot + 5, norm_rows.hand_on)

        @pl.when(t < p.chunks)
        def _():
            make(t)

        at(p.gain_slot, gains_plane)
        at(p.rep_slot, gains_reps)

        @pl.when((t >= p.res_slot) & (t < p.res_slot + p.out_tiles // 2))
        def _():
            @pl.when(t == p.res_slot)
            def _():
                if not p.early_res:
                    load_activ.wait()
                load_res(0)(lambda copy: copy.start())

            res_tiles((t - p.res_slot) * 2)

        at(p.res_send_slot, res_rows.start)
        at(p.res_send_slot + 3, res_rows.hand_on)
        at(p.result_slot, finish_result)
        return carry

    lax.fori_loop(0, p.slots, slot, 0)

    for j in range(max(0, p.chunks - 2), p.chunks):
        swap_copy(j).wait_send()
    for j in range(max(0, p.chunks - p.sum_ring), p.chunks):
        inward_copies(j)[0].wait_send()
    if p.half > 1:

        @pl.when(depth > 0)
        def _():
            for j in range(max(0, p.chunks - 2), p.chunks):
                chunk_bytes(j, out_send.at[j % 2])

    for rows in (back_rows, res_rows, norm_rows):
        rows.settle()
    for copies in (gain_plane, gain_all):
        for copy in copies:
            copy.wait_send()

    def settle(ref, sem):
        pltpu.make_async_copy(ref, ref, sem).wait()

    for tile in range(first_tile, p.tiles):
        tile_bytes(tile, tile_send).wait()
        tile_bytes(tile, tile_pass).wait()
    for sem, part in (
        (0, f_down.at[:, pl.ds(0, p.rows)]),
        (3, f_proj.at[pl.ds(0, p.proj_half), :]),
    ):
        settle(part, pass_send.at[sem])
        settle(part, pass_recv.at[sem])
    for _, full, part, _, sem, _ in wide_kinds(0):
        here = full.at[pl.ds(0, p.block), :]
        settle(here, pass_send.at[sem])
        settle(here, pass_recv.at[sem])
        settle(full.at[pl.ds(0, p.block), pl.ds(0, n * part)], cross_send.at[sem])


def backward(
    shards, reps, x, cot_all, grad_activ, gate_w, up_w, gate_e, up_e, down_w, hidden, tokens, proj_w,
    qkv_m, normed, mlp_rms, mlp_gain, attn_gain, seg_col, seg_row, cos_t, sin_t, lse, q_t, mixed_t,
    k, k_t, v,
):
    length, width = x.shape
    count = tokens.shape[0]
    ffn_part = down_w.shape[0]
    q_part, kv_part = q_t.shape[0], k_t.shape[0]
    n = shards - 1
    p = Plan(shards, reps, length, width, ffn_part, q_part, kv_part)
    shape = jax.ShapeDtypeStruct
    own = width // shards
    chunk = (p.rows, TILE)
    dma = pltpu.SemaphoreType.DMA
    return pl.pallas_call(
        functools.partial(backward_kernel, p, gate_e.shape[1]),
        in_specs=[ANY] * 13 + [IN_VMEM] * 13,
        out_specs=[ANY] * 8 + [IN_VMEM] + [ANY] * 15,
        out_shape=[
            shape((ffn_part, width), BF16),
            shape((own, shards * ffn_part), BF16),
            shape((own, shards * ffn_part), BF16),
            shape((q_part, width), BF16),
            shape((own, shards * q_part), BF16),
            shape((own, shards * 2 * kv_part), BF16),
            shape((count, width), F32),
            shape((count, width), F32),
            shape((8, width // shards), F32),
        ]
        + [shape((p.chunks,) + chunk, BF16)] * 4
        + [shape((n, count, width), BF16)] * 3
        + [shape((length, width), BF16)]
        + [shape((width, ffn_part), BF16)] * 2
        + [shape((length, ffn_part), BF16)] * 3
        + [shape((length, width), BF16)] * 2,
        scratch_shapes=[
            pltpu.VMEM((length, width), BF16),
            pltpu.VMEM((length, width), BF16),
            pltpu.VMEM((2, length, TILE), BF16),
            pltpu.VMEM((width, TILE), BF16),
            pltpu.VMEM((width, TILE), BF16),
            pltpu.VMEM((length, TILE), BF16),
            pltpu.VMEM((2, TILE, 2 * ffn_part), BF16),
            pltpu.VMEM((2, length, TILE), BF16),
            pltpu.VMEM((length, 2 * ffn_part), BF16),
            pltpu.VMEM(proj_w.shape, BF16),
            pltpu.VMEM(qkv_m.shape, BF16),
            pltpu.VMEM((count, width), F32),
            pltpu.VMEM((count, width), F32),
            pltpu.VMEM((2, count, width), BF16),
            pltpu.VMEM((p.mine_ring,) + chunk, BF16),
            pltpu.VMEM((2,) + chunk, BF16),
            pltpu.VMEM(chunk, BF16),
            pltpu.VMEM(chunk, BF16),
            pltpu.VMEM(chunk, BF16),
            pltpu.VMEM((p.sum_ring,) + chunk, BF16),
            pltpu.VMEM((2,) + chunk, BF16),
            pltpu.VMEM((count, width), F32),
            pltpu.VMEM((count, width), BF16),
            pltpu.VMEM((q_part, length), BF16),
            pltpu.VMEM((q_part + 2 * kv_part, length), BF16),
            pltpu.VMEM((HEAD, length), F32),
            pltpu.VMEM((HEAD, length), F32),
            pltpu.VMEM((length, ffn_part) if p.early_res else (16, 128), BF16),
            pltpu.VMEM((8, width), F32),
            pltpu.VMEM((shards, 8, own), F32),
            pltpu.VMEM((8, own), F32),
            pltpu.VMEM((reps, 8, own), F32),
            dma((12,)), dma((2,)), dma((5,)), dma((2,)), dma((p.chunks,)), dma((p.sum_ring,)),
            dma((p.chunks,)), dma((p.chunks,)), dma((2,)), dma((p.chunks,)), dma((2,)),
            dma((p.chunks,)), dma((6,)), dma((6,)), dma((6,)),
        ]
        + [dma((max(6, n),))] * 6
        + Gather.semaphores(shards)
        + [dma((n,)), dma((n,)), dma((reps - 1,)), dma((reps - 1,))]
        + [dma((p.tiles,))] * 4
        + [dma((3,)), dma((2, 2)), dma((3,))],
        compiler_params=pltpu.CompilerParams(
            collective_id=3, has_side_effects=True, vmem_limit_bytes=FULL
        ),
        name="backward",
    )(
        x, cot_all, grad_activ, gate_w, up_w, gate_e, up_e, down_w, hidden, tokens, proj_w,
        qkv_m, normed, mlp_rms, mlp_gain[None, :], attn_gain[None, :], seg_col, seg_row,
        cos_t, sin_t, lse, q_t, mixed_t, k, k_t, v,
    )[:9]


def widen_kernel(count, rows, columns, group, *refs):
    paired = 1 if group else 0
    srcs, dsts = refs[:count], refs[count : 2 * count + paired]
    narrow, wide, in_sem, out_sem = refs[2 * count + paired :]
    depth = narrow.shape[0]
    jobs = []
    for i, src in enumerate(srcs):
        width = min(columns, src.shape[1])
        for r in range(src.shape[0] // rows):
            for c in range(src.shape[1] // width):
                slot = len(jobs) % depth
                at = (pl.ds(r * rows, rows), pl.ds(c * width, width))
                own = (slice(None), pl.ds(0, width))
                pair = paired and i == 0
                direct = src.dtype == F32
                into = (wide if direct else narrow).at[slot].at[own]
                load = pltpu.make_async_copy(src.at[at], into, in_sem.at[slot])
                held = wide.at[slot].at[own]
                if pair:
                    side = width // 2
                    puts = [
                        pltpu.make_async_copy(
                            wide.at[slot, :, pl.ds(k * side, side)],
                            dsts[k].at[pl.ds(r * rows, rows), :],
                            out_sem.at[slot],
                        )
                        for k in range(2)
                    ]
                else:
                    puts = [pltpu.make_async_copy(held, dsts[i + paired].at[at], out_sem.at[slot])]
                done = pltpu.make_async_copy(held, held, out_sem.at[slot])
                jobs.append((load, puts, done, direct, pair, width))
    total = len(jobs)
    ahead = depth - 1

    def load(i):
        if jobs[i][3] and i >= depth:
            jobs[i - depth][2].wait()
        jobs[i][0].start()

    for i in range(min(ahead, total)):
        load(i)
    for i in range(total):
        slot = i % depth
        fetch, puts, _, direct, pair, width = jobs[i]
        fetch.wait()
        if not direct:
            if i >= depth:
                jobs[i - depth][2].wait()
            for strip in range(0, rows, 64):
                here = pl.ds(strip, 64)
                if pair:
                    for k in range(width // group):
                        to = (k % 2) * (width // 2) + (k // 2) * group
                        wide[slot, here, pl.ds(to, group)] = narrow[
                            slot, here, pl.ds(k * group, group)
                        ].astype(F32)
                else:
                    wide[slot, here, pl.ds(0, width)] = narrow[
                        slot, here, pl.ds(0, width)
                    ].astype(F32)
        for put in puts:
            put.start()
        if i + ahead < total:
            load(i + ahead)
    for i in range(max(0, total - depth), total):
        jobs[i][2].wait()


def widen(arrays, group):
    rows, columns, depth = 256, 2048, 4
    rows = min([rows] + [a.shape[0] for a in arrays])
    shapes = [jax.ShapeDtypeStruct(a.shape, F32) for a in arrays]
    if group:
        tall, width = arrays[0].shape
        shapes[:1] = [jax.ShapeDtypeStruct((tall, width // 2), F32)] * 2
    return pl.pallas_call(
        functools.partial(widen_kernel, len(arrays), rows, columns, group),
        in_specs=[ANY] * len(arrays),
        out_specs=[ANY] * len(shapes),
        out_shape=shapes,
        scratch_shapes=[
            pltpu.VMEM((depth, rows, columns), BF16),
            pltpu.VMEM((depth, rows, columns), F32),
            pltpu.SemaphoreType.DMA((depth,)),
            pltpu.SemaphoreType.DMA((depth,)),
        ],
        compiler_params=pltpu.CompilerParams(vmem_limit_bytes=FULL),
        name="widen",
    )(*arrays)


def local(
    tokens, segments, query_w, key_w, value_w, proj_w, attn_gain,
    gate_w, up_w, down_w, mlp_gain, cotangent,
):
    shards = lax.axis_size("shard")
    reps = lax.axis_size("rep")
    tok_count, width = tokens.shape
    kv_part = key_w.shape[1] // shards
    q_part = query_w.shape[1] // shards
    length = tok_count * shards

    if kv_part % 128:
        kv_w = jnp.concatenate(
            [
                w[:, s * kv_part : (s + 1) * kv_part]
                for s in range(shards)
                for w in (key_w, value_w)
            ],
            axis=1,
        )
        weights = (query_w, kv_w)
    else:
        weights = (query_w, key_w, value_w)
    early = min(2 * TILE, down_w.shape[0] // 2)
    (
        normed, cot_all, proj_m, gate_e, up_e, qkv_m,
        q_t, k, k_t, v, mixed_t, lse, cos_t, sin_t, seg_col, seg_row,
    ) = attend(
        tokens, segments[None, :], weights, cotangent, proj_w, gate_w, up_w, attn_gain,
        q_part, kv_part, early, shards,
    )
    hidden, mlp_rms, normed_mlp, grad_activ = hidden_layer(
        mixed_t, proj_m, proj_w, cot_all, down_w, tokens, mlp_gain, shards
    )
    down, gate, up, proj, query, kv, result, grad_tokens, gains = backward(
        shards, reps, normed_mlp, cot_all, grad_activ, gate_w, up_w, gate_e, up_e, down_w, hidden, tokens,
        proj_w, qkv_m, normed, mlp_rms, mlp_gain, attn_gain, seg_col, seg_row, cos_t, sin_t, lse,
        q_t, mixed_t, k, k_t, v,
    )

    def every_other(first):
        parts = [
            kv[:, (2 * s + first) * kv_part : (2 * s + first + 1) * kv_part] for s in range(shards)
        ]
        return jnp.concatenate(parts, axis=1).astype(F32)

    others = [gate, up, down, query, proj, result, grad_tokens]
    if kv_part % 128:
        key, value = every_other(0), every_other(1)
        gate, up, down, query, proj, result, grad_tokens = widen(others, 0)
    else:
        key, value, gate, up, down, query, proj, result, grad_tokens = widen([kv] + others, kv_part)
    return (
        result, grad_tokens, query, key, value, proj, gains[0], gate, up, down, gains[1],
    )


def solution(mesh):
    rows = P(("rep", "shard"), None)
    held = P("shard", None)
    in_specs = (
        rows, P(("rep", "shard")), held, held, held, held, P(), held, held, held, P(), rows,
    )
    out_specs = (
        rows, rows, held, held, held, held, P("shard"), held, held, held, P("shard"),
    )
    return jax.shard_map(local, mesh=mesh, in_specs=in_specs, out_specs=out_specs, check_vma=False)
```

```python
import functools
import math

import jax
import jax.numpy as jnp
from jax import lax
from jax.experimental import pallas as pl
from jax.experimental.pallas import tpu as pltpu
from jax.sharding import PartitionSpec as P

HEADS = 32
KV_HEADS = 8
HEAD = 64
GROUP = HEADS // KV_HEADS
SCALE = 1.0 / math.sqrt(HEAD)
TILE = 256
ROWS = 512
NEG = -1e30
MIB = 1024 * 1024
FULL = 63 * MIB + MIB // 2

epsilon = 1e-05
rope_base = 500000.0
F32 = jnp.float32
BF16 = jnp.bfloat16


def dot(left, right, dims):
    return lax.dot_general(left, right, (dims, ((), ())), preferred_element_type=F32)


NN = ((1,), (0,))
NT = ((1,), (1,))
TN = ((0,), (0,))
TT = ((0,), (1,))


MESH = pl.DeviceIdType.MESH


def place():
    return lax.axis_index("rep"), lax.axis_index("shard")


def remote(src, dst, sends, recvs, index, rep, shard):
    return pltpu.make_async_remote_copy(
        src_ref=src,
        dst_ref=dst,
        send_sem=sends.at[index],
        recv_sem=recvs.at[index],
        device_id=(rep, shard),
        device_id_type=MESH,
    )


def greet(partners):
    barrier = pltpu.get_barrier_semaphore()
    for partner in partners:
        pl.semaphore_signal(barrier, inc=1, device_id=partner, device_id_type=MESH)
    pl.semaphore_wait(barrier, len(partners))


def plane_partners(rep, me, shards):
    return [(rep, me ^ step) for step in range(1, shards)]


class Spread:
    def __init__(self, shards, own, full, columns, sends, recvs, held=None, held_sem=None):
        rep, me = place()
        quarter = rep % 4
        count = own.shape[0]
        part = count // 4
        own_rows = pl.ds(pl.multiple_of(quarter * part, part), part)

        def at(shard, which):
            return full.at[pl.ds(pl.multiple_of(shard * count + which * part, part), part), :]

        def piece(shard):
            return own.at[own_rows, :] if columns is None else own.at[own_rows, columns(shard)]

        self.first, self.core, self.layer, self.last = [], [], [], []
        n = shards - 1
        for i in range(n):
            peer = me ^ (i + 1)
            self.first.append(remote(piece(peer), at(me, quarter), sends, recvs, i, rep, peer))
            mine = at(peer, quarter)
            self.core.append(remote(mine, mine, sends, recvs, n + i, rep ^ 1, me))
            self.layer.append(remote(mine, mine, sends, recvs, 2 * n + i, rep ^ 2, me))
            theirs = at(peer, quarter ^ 2)
            self.last.append(remote(theirs, theirs, sends, recvs, 3 * n + i, rep ^ 1, me))
        self.take = self.keep = None
        if held is not None:
            kept = full.at[pl.ds(pl.multiple_of(me * count, count), count), :]
            self.take = pltpu.make_async_copy(own.at[:, columns(me)], held, held_sem.at[0])
            self.keep = pltpu.make_async_copy(held, kept, held_sem.at[1])

    def start(self):
        for copy in self.first:
            copy.start()
        if self.take is not None:
            self.take.start()

    def hand_on(self):
        if self.take is not None:
            self.take.wait()
            self.keep.start()
        for i, copy in enumerate(self.first):
            copy.wait_recv()
            self.layer[i].start()
            self.core[i].start()

    def hand_on_last(self):
        for i, copy in enumerate(self.layer):
            copy.wait_recv()
            self.last[i].start()

    def finish(self):
        for copy in self.core + self.last:
            copy.wait_recv()
        for copy in self.first + self.core + self.layer + self.last:
            copy.wait_send()
        if self.keep is not None:
            self.keep.wait()

    @staticmethod
    def semaphores(shards):
        n = 4 * (shards - 1)
        return [pltpu.SemaphoreType.DMA((n,)), pltpu.SemaphoreType.DMA((n,))]


class WideSpread:
    def __init__(self, shards, own, full, sends, recvs):
        rep, me = place()
        eighth = rep % 8
        count = own.shape[0]
        part = count // 8
        own_rows = pl.ds(pl.multiple_of(eighth * part, part), part)

        def at(shard, which):
            return full.at[pl.ds(pl.multiple_of(shard * count + which * part, part), part), :]

        self.first, self.near, self.layer, self.far, self.passed = [], [], [], [], []
        n = shards - 1
        for i in range(n):
            peer = me ^ (i + 1)

            def hand(which, kind, to, i=i, peer=peer):
                piece = at(peer, which)
                return remote(piece, piece, sends, recvs, kind * n + i, to, me)

            self.first.append(
                remote(own.at[own_rows, :], at(me, eighth), sends, recvs, i, rep, peer)
            )
            self.layer.append(hand(eighth, 1, rep ^ 2))
            self.far.append((hand(eighth, 2, rep ^ 4), hand(eighth ^ 2, 3, rep ^ 4)))
            self.passed.append(
                tuple(
                    hand(which, 4 + k, rep ^ 1)
                    for k, which in enumerate((eighth, eighth ^ 2, eighth ^ 4, eighth ^ 6))
                )
            )

    def start(self):
        for copy in self.first:
            copy.start()

    def hand_on(self):
        for i, copy in enumerate(self.first):
            copy.wait_recv()
            self.layer[i].start()
            self.passed[i][0].start()
        for far in self.far:
            far[0].start()

    def hand_on_next(self):
        for i, copy in enumerate(self.layer):
            copy.wait_recv()
            self.far[i][1].start()
            self.passed[i][1].start()

    def hand_on_last(self):
        for k in range(2):
            for i, far in enumerate(self.far):
                far[k].wait_recv()
                self.passed[i][2 + k].start()

    def finish(self):
        for passed in self.passed:
            for copy in passed:
                copy.wait_recv()
        for i in range(len(self.first)):
            for copy in (self.first[i], self.layer[i], *self.far[i], *self.passed[i]):
                copy.wait_send()

    @staticmethod
    def semaphores(shards):
        n = 8 * (shards - 1)
        return [pltpu.SemaphoreType.DMA((n,)), pltpu.SemaphoreType.DMA((n,))]


class Gather:
    def __init__(self, shards, own, full, sends, recvs, local_sem=None):
        rep, me = place()
        count = own.shape[0]
        half = count // 2

        def at(shard, start, size):
            return full.at[pl.ds(pl.multiple_of(shard * count + start, half), size), :]

        self.direct, self.passed, self.kept = [], [], None
        if shards == 4:
            for i, (step, start) in enumerate(((1, 0), (2, half), (1, half), (2, 0))):
                self.direct.append(
                    remote(
                        own.at[pl.ds(start, half), :], at(me, start, half),
                        sends, recvs, i, rep, me ^ step,
                    )
                )
            for i, (step, start) in enumerate(((1, 0), (2, half))):
                came = at(me ^ step, start, half)
                self.passed.append(remote(came, came, sends, recvs, 4 + i, rep, me ^ step ^ 3))
        else:
            for i in range(shards - 1):
                self.direct.append(
                    remote(own, at(me, 0, count), sends, recvs, i, rep, me ^ (i + 1))
                )
        if local_sem is not None:
            self.kept = pltpu.make_async_copy(own, at(me, 0, count), local_sem)

    def start(self):
        for copy in self.direct:
            copy.start()
        if self.kept is not None:
            self.kept.start()

    def hand_on(self):
        for i, copy in enumerate(self.passed):
            self.direct[i].wait_recv()
            copy.start()

    def finish(self):
        for copy in self.direct[len(self.passed) :] + self.passed:
            copy.wait_recv()
        for copy in self.direct + self.passed:
            copy.wait_send()
        if self.kept is not None:
            self.kept.wait()

    @staticmethod
    def semaphores(shards):
        n = max(6, shards - 1)
        return [
            pltpu.SemaphoreType.DMA((n,)),
            pltpu.SemaphoreType.DMA((n,)),
            pltpu.SemaphoreType.DMA,
        ]


def split_rows(ref, index, size):
    return ref.at[pl.ds(pl.multiple_of(index * size, size), size), :]


def column_block(part):
    return lambda shard: pl.ds(pl.multiple_of(shard * part, part), part)


def pair_partners(rep, me):
    return [(rep ^ 1, me), (rep ^ 2, me)]


ANY = pl.BlockSpec(memory_space=pl.ANY)
IN_VMEM = pl.BlockSpec(memory_space=pltpu.VMEM)


def rope_tables(seg_col, seg_row, freqs):
    length = seg_row.shape[1]
    begins = jnp.sum((seg_col < seg_row).astype(jnp.int32), axis=0, keepdims=True)
    positions = lax.broadcasted_iota(jnp.int32, (1, length), 1) - begins
    angles = freqs * positions.astype(F32)
    return (jnp.cos(angles), jnp.sin(angles))


def side_by_side(ref, group, here):
    rows = GROUP * HEAD
    return jnp.concatenate(
        [
            ref[pl.ds(pl.multiple_of(group * rows + h * HEAD, HEAD), HEAD), here]
            for h in range(GROUP)
        ],
        axis=1,
    )


def block_bias(seg_col_ref, seg_row_ref, key_at, query_at):
    same = seg_col_ref[pl.ds(key_at, TILE), :] == seg_row_ref[:, pl.ds(query_at, TILE)]
    key_index = key_at + lax.broadcasted_iota(jnp.int32, (TILE, TILE), 0)
    query_index = query_at + lax.broadcasted_iota(jnp.int32, (TILE, TILE), 1)
    bias = jnp.where(same & (key_index <= query_index), 0.0, NEG).astype(F32)
    return jnp.concatenate([bias] * GROUP, axis=1)


def attend_kernel(
    shards, ffn_part, early, parts, tokens, seg, cot, proj_w, gate_w, up_w, *refs,
):
    count = len(parts)
    weights, refs = refs[:count], refs[count:]
    (
        gain, freqs, normed_out, cot_all, proj_m, gate_m, up_m, qkv_m,
        q_ref, k_ref, kt_ref, v_ref, out_ref, lse_ref, cos_ref, sin_ref, seg_col, seg_row,
        tokens_v, normed_v, qkv_v, turned_v, vt_ref, cot_v, seg_v, store_sem, qkv_sem, own_sem,
        seg_send, seg_recv, *sems,
    ) = refs
    rep, me = place()
    length, width = tokens_v.shape
    kv_heads = k_ref.shape[0]
    q_part, kv_part = q_ref.shape[0], kt_ref.shape[0]
    blocks = length // TILE

    at, spreads, own = 0, [], []
    for i, (weight, part) in enumerate(zip(weights, parts)):
        full, rows = qkv_v.at[:, pl.ds(at, part)], weight.shape[0]
        spreads.append(
            Spread(shards, weight, full, column_block(part), *sems[2 * i : 2 * i + 2])
        )
        own.append(
            pltpu.make_async_copy(
                weight.at[:, column_block(part)(me)], split_rows(full, me, rows), own_sem.at[i]
            )
        )
        at += part
    sems = sems[2 * count :]
    rows = Gather(shards, tokens, tokens_v, *sems[:3])
    segs = [
        remote(seg, seg_v.at[me], seg_send, seg_recv, i, rep, me ^ (i + 1))
        for i in range(shards - 1)
    ]
    own.append(pltpu.make_async_copy(seg, seg_v.at[me], own_sem.at[count]))
    take = pltpu.make_async_copy(cot, cot_v, own_sem.at[count + 1])
    sems = sems[3:]

    def first_tiles(shard):
        return pl.ds(pl.multiple_of(shard * ffn_part, ffn_part), early)

    proj = WideSpread(shards, proj_w, proj_m, *sems[:2])
    gate = Spread(shards, gate_w, gate_m, first_tiles, *sems[2:4])
    up = Spread(shards, up_w, up_m, first_tiles, *sems[4:6])
    cots = Gather(shards, cot_v, cot_all, *sems[6:9])

    for copy in (*own, take):
        copy.start()
    greet(plane_partners(rep, me, shards) + pair_partners(rep, me) + [(rep ^ 4, me)])
    proj.start()
    for spread in spreads:
        spread.start()
    for copy in segs:
        copy.start()
    rows.start()
    proj.hand_on()
    for spread in spreads:
        spread.hand_on()
    rows.hand_on()
    gate.start()
    up.start()
    take.wait()
    cots.start()
    proj.hand_on_next()
    for spread in spreads:
        spread.hand_on_last()

    for copy in segs:
        copy.wait()
    for copy in own:
        copy.wait()
    seg_row[...] = jnp.concatenate([seg_v[i] for i in range(shards)], axis=1)
    tall = jnp.broadcast_to(seg_row[...], (8, length)).astype(F32).T[:, :1]
    seg_col[...] = tall.astype(jnp.int32)
    cos_ref[...], sin_ref[...] = rope_tables(seg_col[...], seg_row[...], freqs[...])
    for spread in spreads:
        spread.finish()
    keep_qkv = pltpu.make_async_copy(qkv_v, qkv_m, qkv_sem)
    keep_qkv.start()

    def block_rows(i):
        return pl.ds(pl.multiple_of(i * TILE, TILE), TILE)

    def store(i):
        return pltpu.make_async_copy(
            normed_v.at[i % 2], normed_out.at[block_rows(i), :], store_sem.at[i % 2]
        )

    def turn_weights(i, carry):
        turned_v[:, block_rows(i)] = qkv_v[block_rows(i), :].T
        return carry

    lax.fori_loop(0, width // TILE, turn_weights, 0)
    rows.finish()
    half = HEAD // 2

    def project(i, carry):
        here = block_rows(i)

        @pl.when(i >= 2)
        def _():
            store(i - 2).wait()

        values = tokens_v[here, :].astype(F32)
        rms = lax.rsqrt(jnp.mean(values * values, axis=-1, keepdims=True) + epsilon)
        normed_v[i % 2] = (values * rms * gain[...]).astype(BF16)
        store(i).start()
        heads = dot(turned_v[...], normed_v[i % 2], NT)
        cos, sin = cos_ref[:, here], sin_ref[:, here]

        def turned(at):
            first, second = heads[at : at + half], heads[at + half : at + HEAD]
            return (
                (first * cos - second * sin).astype(BF16),
                (second * cos + first * sin).astype(BF16),
            )

        for at in range(0, q_part, HEAD):
            first, second = turned(at)
            q_ref[at : at + half, here] = (first.astype(F32) * SCALE).astype(BF16)
            q_ref[at + half : at + HEAD, here] = (second.astype(F32) * SCALE).astype(BF16)
        for g in range(kv_heads):
            at = g * HEAD
            first, second = turned(q_part + at)
            kt_ref[at : at + half, here] = first
            kt_ref[at + half : at + HEAD, here] = second
            vt_ref[at : at + HEAD, here] = heads[
                q_part + kv_part + at : q_part + kv_part + at + HEAD
            ].astype(BF16)
            k_ref[g, here, :] = kt_ref[at : at + HEAD, here].T
            v_ref[g, here, :] = vt_ref[at : at + HEAD, here].T
        return carry

    lax.fori_loop(0, blocks, project, 0)
    for i in range(max(0, blocks - 2), blocks):
        store(i).wait()
    wide = GROUP * TILE

    def unit(at, carry_out):
        g, block = at // blocks, at % blocks
        query_at = pl.multiple_of(block * TILE, TILE)
        here = pl.ds(query_at, TILE)
        queries = side_by_side(q_ref, g, here)
        value_rows = pl.ds(pl.multiple_of(g * HEAD, HEAD), HEAD)

        def step(c, carry):
            top, total, acc = carry
            key_at = pl.multiple_of(c * TILE, TILE)
            keys = pl.ds(key_at, TILE)
            scores = dot(k_ref[g, keys, :], queries, NN)
            scores = scores + block_bias(seg_col, seg_row, key_at, query_at)
            new_top = jnp.maximum(top, jnp.max(scores, axis=0, keepdims=True))
            expo = jnp.exp(scores - new_top)
            fade = jnp.exp(top - new_top)
            total = total * fade + jnp.sum(expo, axis=0, keepdims=True)
            acc = acc * fade + dot(vt_ref[value_rows, keys], expo.astype(BF16), NN)
            return new_top, total, acc

        start = (
            jnp.full((1, wide), NEG, F32),
            jnp.zeros((1, wide), F32),
            jnp.zeros((HEAD, wide), F32),
        )
        top, total, acc = lax.fori_loop(0, block, step, step(block, start))
        mixed = (acc / total).astype(BF16)
        lse = top + jnp.log(total)
        for h in range(GROUP):
            at_row = pl.multiple_of(g * GROUP * HEAD + h * HEAD, HEAD)
            out_ref[pl.ds(at_row, HEAD), here] = mixed[:, h * TILE : (h + 1) * TILE]
            lse_ref[g, h : h + 1, here] = lse[:, h * TILE : (h + 1) * TILE]
        return carry_out

    units = kv_heads * blocks
    lax.fori_loop(0, units // 2, unit, 0)
    lax.fori_loop(units // 2, units, unit, 0)
    gate.hand_on()
    up.hand_on()
    cots.hand_on()
    proj.hand_on_last()
    gate.hand_on_last()
    up.hand_on_last()
    for transfer in (proj, gate, up, cots):
        transfer.finish()
    keep_qkv.wait()


def attend(
    tokens, seg, weights, cot, proj_w, gate_w, up_w, gain, q_part, kv_part, early, shards
):
    count, width = tokens.shape
    length = shards * count
    kv_heads = kv_part // HEAD
    ffn_part = gate_w.shape[1] // shards
    parts = [w.shape[1] // shards for w in weights]
    freqs = rope_base ** (-(jnp.arange(HEAD // 2, dtype=F32) * (2.0 / HEAD)))
    shape = jax.ShapeDtypeStruct
    dma = pltpu.SemaphoreType.DMA
    n = shards - 1
    return pl.pallas_call(
        functools.partial(attend_kernel, shards, ffn_part, early, parts),
        in_specs=[ANY] * (6 + len(weights)) + [IN_VMEM] * 2,
        out_specs=[ANY] * 6 + [IN_VMEM] * 10,
        out_shape=[
            shape((length, width), BF16),
            shape((length, width), BF16),
            shape((shards * proj_w.shape[0], width), BF16),
            shape((width, early), BF16),
            shape((width, early), BF16),
            shape((width, sum(parts)), BF16),
            shape((q_part, length), BF16),
            shape((kv_heads, length, HEAD), BF16),
            shape((kv_part, length), BF16),
            shape((kv_heads, length, HEAD), BF16),
            shape((q_part, length), BF16),
            shape((kv_heads, GROUP, length), F32),
            shape((HEAD // 2, length), F32),
            shape((HEAD // 2, length), F32),
            shape((length, 1), jnp.int32),
            shape((1, length), jnp.int32),
        ],
        scratch_shapes=[
            pltpu.VMEM((length, width), BF16),
            pltpu.VMEM((2, TILE, width), BF16),
            pltpu.VMEM((width, sum(parts)), BF16),
            pltpu.VMEM((sum(parts), width), BF16),
            pltpu.VMEM((kv_part, length), BF16),
            pltpu.VMEM(cot.shape, BF16),
            pltpu.VMEM((shards, 1, count), jnp.int32),
            dma((2,)), dma, dma((len(weights) + 2,)), dma((n,)), dma((n,)),
        ]
        + len(weights) * Spread.semaphores(shards)
        + Gather.semaphores(shards)
        + WideSpread.semaphores(shards)
        + 2 * Spread.semaphores(shards)
        + Gather.semaphores(shards),
        compiler_params=pltpu.CompilerParams(
            collective_id=1, has_side_effects=True, vmem_limit_bytes=FULL
        ),
        name="attend",
    )(tokens, seg, cot, proj_w, gate_w, up_w, *weights, gain[None, :], freqs[:, None])


def hidden_kernel(
    shards, mixed_t, proj_m, proj_w, cot_all, down_w, tokens, gain, hidden_ref, rms_ref, normed_all,
    grad_activ, proj_v, mixed_own, normed, cot_v, down_v, out_v, cot_sem, out_sem, proj_sem, mix_send, mix_recv, gather_send, gather_recv, local_sem,
):
    rep, me = place()
    part, _ = mixed_t.shape
    count = tokens.shape[0]
    rows = [
        pltpu.make_async_copy(
            split_rows(proj_m, me ^ i, part) if i else proj_w,
            split_rows(proj_v, me ^ i, part),
            proj_sem.at[i],
        )
        for i in range(shards)
    ]
    for copy in rows:
        copy.start()
    early = [
        pltpu.make_async_copy(cot_all, cot_v, cot_sem.at[0]),
        pltpu.make_async_copy(down_w, down_v, cot_sem.at[1]),
    ]
    for copy in early:
        copy.start()
    greet(plane_partners(rep, me, shards))

    def columns(shard):
        return mixed_t.at[:, pl.ds(pl.multiple_of(shard * count, count), count)]

    copies = [
        remote(columns(me ^ (i + 1)), mixed_own.at[i], mix_send, mix_recv, i, rep, me ^ (i + 1))
        for i in range(shards - 1)
    ]
    for copy in copies:
        copy.start()

    def product(block, i):
        rows[i].wait()
        return dot(block, split_rows(proj_v, me ^ i, part)[...], TN)

    hidden_ref[...] = tokens[...].astype(F32) + product(
        mixed_t[:, pl.ds(pl.multiple_of(me * count, count), count)], 0
    )
    for i, copy in enumerate(copies):
        copy.wait_recv()
        hidden_ref[...] += product(mixed_own[i], i + 1)
    hidden = hidden_ref[...]
    rms = lax.rsqrt(jnp.mean(hidden * hidden, axis=-1, keepdims=True) + epsilon)
    rms_ref[...] = rms
    normed[...] = (hidden * rms * gain[...]).astype(BF16)
    gather = Gather(shards, normed, normed_all, gather_send, gather_recv, local_sem)
    gather.start()
    for copy in copies:
        copy.wait_send()
    for copy in early:
        copy.wait()

    steps = down_w.shape[0] // TILE

    def store(i):
        at = pl.ds(pl.multiple_of(i * TILE, TILE), TILE)
        return pltpu.make_async_copy(out_v.at[i % 2], grad_activ.at[:, at], out_sem.at[i % 2])

    def step(i, carry):
        @pl.when(i >= 2)
        def _():
            store(i - 2).wait()

        units = down_v[pl.ds(pl.multiple_of(i * TILE, TILE), TILE), :]
        out_v[i % 2] = dot(cot_v[...], units, NT).astype(BF16)
        store(i).start()
        return carry

    lax.fori_loop(0, steps // 2, step, 0)
    gather.hand_on()
    lax.fori_loop(steps // 2, steps, step, 0)
    for i in range(max(0, steps - 2), steps):
        store(i).wait()
    gather.finish()


def hidden_layer(mixed_t, proj_m, proj_w, cot_all, down_w, tokens, gain, shards):
    part, length = mixed_t.shape
    count, width = tokens.shape
    n = shards - 1
    return pl.pallas_call(
        functools.partial(hidden_kernel, shards),
        in_specs=[IN_VMEM, ANY, ANY, ANY, ANY, IN_VMEM, IN_VMEM],
        out_specs=[IN_VMEM, IN_VMEM, ANY, ANY],
        out_shape=[
            jax.ShapeDtypeStruct((count, width), F32),
            jax.ShapeDtypeStruct((count, 1), F32),
            jax.ShapeDtypeStruct((length, width), BF16),
            jax.ShapeDtypeStruct((length, down_w.shape[0]), BF16),
        ],
        scratch_shapes=[
            pltpu.VMEM(proj_m.shape, BF16),
            pltpu.VMEM((n, part, count), BF16),
            pltpu.VMEM((count, width), BF16),
            pltpu.VMEM(cot_all.shape, BF16),
            pltpu.VMEM(down_w.shape, BF16),
            pltpu.VMEM((2, length, TILE), BF16),
            pltpu.SemaphoreType.DMA((2,)),
            pltpu.SemaphoreType.DMA((2,)),
            pltpu.SemaphoreType.DMA((shards,)),
            pltpu.SemaphoreType.DMA((n,)),
            pltpu.SemaphoreType.DMA((n,)),
        ]
        + Gather.semaphores(shards),
        compiler_params=pltpu.CompilerParams(
            collective_id=2, has_side_effects=True, vmem_limit_bytes=FULL
        ),
        name="hidden",
    )(mixed_t, proj_m, proj_w, cot_all, down_w, tokens, gain[None, :])


class Plan:
    def __init__(self, shards, reps, length, width, ffn_part, q_part, kv_part):
        self.shards, self.reps, self.length, self.width = shards, reps, length, width
        self.ffn_part, self.q_part, self.kv_part = ffn_part, q_part, kv_part
        self.layers = reps // 2
        self.half = self.layers // 2
        self.rows = width // 2
        self.own = width // shards
        self.block = self.own // 2
        self.proj_half = q_part // 2
        self.proj_blocks = self.rows // self.proj_half
        self.tiles = ffn_part // TILE
        self.out_tiles = width // TILE
        per_slot = 2
        self.back_slot = self.tiles
        self.send_slot = self.back_slot + -(-self.out_tiles // per_slot) - 1
        self.rows_slot = self.send_slot + 4
        self.pass_slot = self.rows_slot + 1
        self.mixed_slot = self.rows_slot + 3
        self.unit_slot = self.mixed_slot + 1
        self.per_slot = per_slot
        self.units = (length // TILE) * (kv_part // HEAD)
        self.norm_slot = self.unit_slot + self.units // 2
        self.down_at = 2 * self.tiles
        self.ffn_end = 3 * self.tiles
        self.q_at = max(self.ffn_end, self.norm_slot)
        self.kv_at = self.q_at + q_part // TILE
        self.proj_at = self.kv_at + 1
        self.chunks = self.proj_at + width // TILE // self.proj_blocks
        self.tokens_slot = max(self.norm_slot + 7, self.chunks + 1)
        self.early_res = length <= 1024
        if self.early_res:
            self.res_slot = self.send_slot + 1
            self.res_send_slot = max(self.mixed_slot + 1, self.res_slot + self.out_tiles // 2)
            self.result_slot = max(self.res_send_slot + 5, self.norm_slot + 4)
            assert self.result_slot < self.norm_slot + 5
        else:
            self.res_slot = max(self.ffn_end + 1, self.norm_slot + 1)
            self.res_send_slot = max(self.res_slot + self.out_tiles // 2 - 1, self.tokens_slot + 1)
            self.result_slot = self.res_send_slot + 6
        self.arrive = self.layers + 2
        self.spread_slot = self.mixed_slot + 1
        self.spread_first = max(0, self.send_slot + 1 - self.arrive)
        assert self.tiles >= 3
        self.hand = 4
        self.gain_slot = self.tokens_slot + 2
        self.rep_slot = max(self.chunks + self.arrive - 1, self.gain_slot + 1)
        self.slots = max(self.chunks + self.arrive + self.hand, self.rep_slot, self.result_slot) + 1
        assert self.spread_slot + self.chunks // 2 < self.slots - self.hand
        self.mine_ring = self.half + 1
        self.sum_ring = 3


def backward_kernel(
    plan, early, x, cot_all, grad_activ, gate_w, up_w, gate_e, up_e, down_w, hidden, tokens, proj_w, qkv_m,
    normed,
    mlp_rms, mlp_gain, attn_gain, seg_col, seg_row, cos_ref, sin_ref, lse_ref, q_ref, mixed_ref,
    k_ref, kt_ref, v_ref,
    f_down, f_gate, f_up, f_proj, f_q, f_kv, result_ref, tokens_out, gains_out,
    swapped, from_outer, from_middle, totals, back_land, res_land, norm_land, norm_part,
    gate_m, up_m, activ, dgate, dup, back_part, res_part,
    left_a, left_b, right, gate_v, up_v, grad_v, back_v, tile_v, both, proj_v, qkv_v, hidden_v,
    row_sum, land_v,
    mine, theirs, swap_v, outer_v, middle_v, sums, total_v,
    grad_hidden, gh_own, g_t, back_t, dk_acc, dv_acc, activ_v,
    gain_part, gain_land, gain_sum, gain_reps,
    load_sem, right_sem, small_sem, swap_send, swap_recv, in_send, outer_recv, middle_recv,
    out_send, total_recv, total_store, cross_recv, cross_send, pass_send, pass_recv,
    back_send, back_recv, res_send, res_recv, norm_send, norm_recv,
    gather_send, gather_recv, gather_local, gain_send, gain_recv, rep_send, rep_recv,
    tile_send, tile_recv, tile_pass, tile_passed, down_sem, back_sem, tile_sem,
):
    p = plan
    shards, reps, n = p.shards, p.reps, p.shards - 1
    rep, me = place()
    core, layer = rep % 2, rep // 2
    upper = layer >= p.half
    depth = jnp.where(upper, p.layers - 1 - layer, layer)
    inward = jnp.where(upper, rep - 2, rep + 2)
    outward = jnp.where(upper, rep + 2, rep - 2)
    is_middle = depth == p.half - 1
    count = tokens.shape[0]
    ffn_end, proj_at, q_at, kv_at, end_at = p.ffn_end, p.proj_at, p.q_at, p.kv_at, p.chunks
    gh_all = both.at[:, pl.ds(0, p.width)]

    def columns(index, size=TILE):
        return pl.ds(pl.multiple_of(index * size, size), size)

    def load(src, dst, i):
        return pltpu.make_async_copy(src, dst, load_sem.at[i])

    load_cot = load(cot_all, left_a, 0)
    load_x = load(x, left_b, 1)
    load_normed = load(normed, left_a, 2)
    load_proj = load(proj_w, proj_v, 3)
    load_qkv = load(qkv_m, qkv_v, 4)
    load_hidden = load(hidden, hidden_v, 5)
    load_activ = load(activ, left_b.at[:, pl.ds(0, p.ffn_part)], 6)
    load_tokens = load(tokens, gh_own, 7)
    first_tile = early // TILE
    assert first_tile >= 2 or p.tiles < 3

    def tile_bytes(tile, sem):
        piece = gate_m.at[pl.ds(0, 2 * n * p.block), pl.ds(0, TILE)]
        return pltpu.make_async_copy(piece, piece, sem.at[tile])

    def send_tile(tile):
        rows = columns(core, p.block)
        into = pl.ds(pl.multiple_of(me * p.own + core * p.block, p.block), p.block)
        for weight, full in ((gate_w, gate_m), (up_w, up_m)):
            for i in range(n):
                peer = me ^ (i + 1)
                at = pl.ds(pl.multiple_of(peer * p.ffn_part + tile * TILE, TILE), TILE)
                pltpu.make_async_remote_copy(
                    src_ref=weight.at[rows, at], dst_ref=full.at[into, columns(tile)],
                    send_sem=tile_send.at[tile], recv_sem=tile_recv.at[tile],
                    device_id=(rep, peer), device_id_type=MESH,
                ).start()

    def pass_tile(tile):
        tile_bytes(tile, tile_recv).wait()
        for full in (gate_m, up_m):
            for i in range(n):
                peer = me ^ (i + 1)
                at = pl.ds(pl.multiple_of(peer * p.own + core * p.block, p.block), p.block)
                piece = full.at[at, columns(tile)]
                pltpu.make_async_remote_copy(
                    src_ref=piece, dst_ref=piece,
                    send_sem=tile_pass.at[tile], recv_sem=tile_passed.at[tile],
                    device_id=(rep ^ 1, me), device_id_type=MESH,
                ).start()

    def load_grad(tile):
        return pltpu.make_async_copy(grad_activ.at[:, columns(tile)], grad_v, down_sem.at[0])

    def load_tile(tile):
        @pl.when(tile >= first_tile)
        def _():
            tile_bytes(tile, tile_passed).wait()

        own_at = pl.ds(pl.multiple_of(me * p.ffn_part + tile * TILE, TILE), TILE)
        held_rows = [pl.ds(pl.multiple_of((me ^ i) * p.own, p.own), p.own) for i in range(shards)]
        for i, (weight, tiles, full, held) in enumerate(
            ((gate_w, gate_e, gate_m, gate_v), (up_w, up_e, up_m, up_v))
        ):
            sem = down_sem.at[i + 1]
            pltpu.make_async_copy(weight.at[:, own_at], held.at[held_rows[0], :], sem).start()
            for rows in held_rows[1:]:

                @pl.when(tile < first_tile)
                def _(rows=rows, tiles=tiles, held=held, sem=sem):
                    src = tiles.at[rows, columns(tile)]
                    pltpu.make_async_copy(src, held.at[rows, :], sem).start()

                @pl.when(tile >= first_tile)
                def _(rows=rows, full=full, held=held, sem=sem):
                    src = full.at[rows, columns(tile)]
                    pltpu.make_async_copy(src, held.at[rows, :], sem).start()

        load_grad(tile).start()

    def units_of(tile):
        return activ_v.at[:, columns(tile)] if p.early_res else tile_v.at[tile % 2]

    def store_tile(tile):
        dup_columns = pl.ds(pl.multiple_of(p.ffn_part + tile * TILE, TILE), TILE)
        return [
            pltpu.make_async_copy(src, dst.at[:, columns(tile)], tile_sem.at[i])
            for i, (src, dst) in enumerate(
                (
                    (units_of(tile), activ),
                    (both.at[:, columns(tile)], dgate),
                    (both.at[:, dup_columns], dup),
                )
            )
        ]

    def stored(tile):
        for copy in store_tile(tile):
            copy.wait()

    def ffn_tile(tile):
        for i, held in enumerate((gate_v, up_v)):
            pltpu.make_async_copy(held, held, down_sem.at[i + 1]).wait()
        load_grad(tile).wait()
        dup_columns = pl.ds(pl.multiple_of(p.ffn_part + tile * TILE, TILE), TILE)

        def go(i, carry):
            here = columns(i, ROWS)
            rows = left_b[here, :]
            gate = dot(rows, gate_v[...], NN)
            up = dot(rows, up_v[...], NN)
            grad = grad_v[here, :].astype(F32)
            sigm = jax.nn.sigmoid(gate)
            swish = gate * sigm
            units_of(tile)[here, :] = (swish * up).astype(BF16)
            both[here, columns(tile)] = (
                grad * up * sigm * (1.0 + gate * (1.0 - sigm))
            ).astype(BF16)
            both[here, dup_columns] = (grad * swish).astype(BF16)
            return carry

        lax.fori_loop(0, p.length // ROWS, go, 0)

        @pl.when(tile >= 3)
        def _():
            stored(tile - 1)

        for copy in store_tile(tile):
            copy.start()

        @pl.when(tile <= 1)
        def _():
            stored(tile)

        @pl.when(tile + 1 < p.tiles)
        def _():
            load_tile(tile + 1)

        @pl.when(tile + 1 == p.tiles)
        def _():
            load_back(0)

    def load_back(tile):
        slot = tile % 2
        per_shard = p.own // TILE
        for i, (weight, tiles, full) in enumerate(
            ((gate_w, gate_e, gate_m), (up_w, up_e, up_m))
        ):
            sem, at = back_sem.at[slot, i], i * p.ffn_part

            @pl.when(tile // per_shard == me)
            def _(weight=weight, sem=sem, at=at):
                src = weight.at[columns(tile - me * per_shard), columns(me, p.ffn_part)]
                pltpu.make_async_copy(src, back_v.at[slot, :, pl.ds(at, p.ffn_part)], sem).start()

            @pl.when(tile // per_shard != me)
            def _(tiles=tiles, full=full, sem=sem, at=at):
                into = back_v.at[slot, :, pl.ds(at, early)]
                pltpu.make_async_copy(tiles.at[columns(tile), :], into, sem).start()
                rest = p.ffn_part - early
                into = back_v.at[slot, :, pl.ds(at + early, rest)]
                src = full.at[columns(tile), pl.ds(early, rest)]
                pltpu.make_async_copy(src, into, sem).start()

    def wait_back(tile):
        slot = tile % 2
        for i in range(2):
            half = back_v.at[slot, :, pl.ds(i * p.ffn_part, p.ffn_part)]
            pltpu.make_async_copy(half, half, back_sem.at[slot, i]).wait()

    def back_tiles(first):
        def store(tile):
            return pltpu.make_async_copy(
                tile_v.at[tile % 2], back_part.at[:, columns(tile)], tile_sem.at[tile % 2]
            )

        @pl.when(first == 0)
        def _():
            stored(p.tiles - 1)

        def tile_go(k, carry):
            tile = first + k
            wait_back(tile)

            @pl.when(tile + 1 < p.out_tiles)
            def _():
                load_back(tile + 1)

            @pl.when(k >= 2)
            def _():
                store(tile - 2).wait()

            def go(i, c):
                here = columns(i, ROWS)
                tile_v[tile % 2, here, :] = dot(both[here, :], back_v[tile % 2], NT).astype(BF16)
                return c

            lax.fori_loop(0, p.length // ROWS, go, 0)
            store(tile).start()
            return carry

        size = jnp.minimum(p.per_slot, p.out_tiles - first)
        lax.fori_loop(0, size, tile_go, 0)
        store(first + size - 2).wait()
        store(first + size - 1).wait()

    def load_res(tile):
        def copies(action):
            for i, held in enumerate((gate_v, up_v)):

                @pl.when(tile % 2 == i)
                def _(i=i, held=held):
                    action(
                        pltpu.make_async_copy(
                            down_w.at[:, columns(tile)], held.at[pl.ds(0, p.ffn_part), :], back_sem.at[i, 0]
                        )
                    )

        return copies

    def res_tiles(first):
        hidden_units = activ_v if p.early_res else left_b

        def store(tile):
            return pltpu.make_async_copy(
                tile_v.at[tile % 2], res_part.at[:, columns(tile)], tile_sem.at[tile % 2]
            )

        for k, held in enumerate((gate_v, up_v)):
            tile = first + k
            load_res(tile)(lambda copy: copy.wait())

            @pl.when(tile + 1 < p.out_tiles)
            def _(tile=tile):
                load_res(tile + 1)(lambda copy: copy.start())

            def go(i, c, k=k, held=held):
                here = columns(i, ROWS)
                tile_v[k, here, :] = dot(
                    hidden_units[here, : p.ffn_part], held[: p.ffn_part, :], NN
                ).astype(BF16)
                return c

            lax.fori_loop(0, p.length // ROWS, go, 0)
            store(tile).start()
        store(first).wait()
        store(first + 1).wait()

    def is_chunk(j, kind):
        if kind == 0:
            return (j >= p.down_at) & (j < ffn_end)
        return (j >= 0) & (j < p.down_at) & (j % 2 == kind - 1)

    def tile_of(j):
        return jnp.where(j < p.down_at, j // 2, j - p.down_at)

    def load_right(t):
        slot = right.at[t % 2]

        def copies(action):
            for i, ref in enumerate((activ, dgate, dup)):

                @pl.when(is_chunk(t, i))
                def _(ref=ref):
                    action(
                        pltpu.make_async_copy(
                            ref.at[:, columns(tile_of(t))], slot, right_sem.at[t % 2]
                        )
                    )

        return copies

    side = p.width // 2
    left_half, right_half = pl.ds(0, side), pl.ds(side, side)

    def rows_of(shard):
        return pl.ds(pl.multiple_of(shard * count, count), count)

    class Scatter:
        def __init__(self, part, land, sends, recvs):
            self.part, self.land = part, land
            self.second = []
            if shards != 4:
                self.first = [
                    remote(split_rows(part, me ^ (i + 1), count), land.at[i], sends, recvs, i, rep, me ^ (i + 1))
                    for i in range(n)
                ]
                return
            order = (
                (3, left_half, 0, right_half, 1),
                (3, right_half, 1, right_half, 2),
                (1, left_half, 0, left_half, 1),
                (2, right_half, 1, left_half, 2),
            )
            self.first = [
                remote(
                    part.at[rows_of(me ^ block), cols], land.at[into, :, into_cols],
                    sends, recvs, i, rep, me ^ to,
                )
                for i, (block, cols, into, into_cols, to) in enumerate(order)
            ]
            self.second = [
                remote(gh_own.at[:, cols], land.at[2, :, cols], sends, recvs, 4 + i, rep, me ^ to)
                for i, (cols, to) in enumerate(((left_half, 2), (right_half, 1)))
            ]

        def start(self):
            for copy in self.first:
                copy.start()

        def hand_on(self):
            if not self.second:
                return
            for copy in self.first[:2]:
                copy.wait_recv()
            loads = [
                (self.part.at[rows_of(me ^ 2), left_half], 0, left_half),
                (self.part.at[rows_of(me ^ 1), right_half], 0, right_half),
                (self.land.at[0, :, right_half], 1, left_half),
                (self.land.at[1, :, right_half], 1, right_half),
            ]
            for src, slot, cols in loads:
                pltpu.make_async_copy(src, land_v.at[slot, :, cols], small_sem.at[slot]).start()
            for slot in range(2):
                pltpu.make_async_copy(land_v.at[slot], land_v.at[slot], small_sem.at[slot]).wait()

            def strip(here):
                gh_own[here, :] = (
                    land_v[0, here, :].astype(F32) + land_v[1, here, :].astype(F32)
                ).astype(BF16)

            strips(strip)
            for copy in self.second:
                copy.start()

        def fetch(self):
            for copy in self.first[2 if self.second else 0 :] + self.second:
                copy.wait_recv()
            for copy in self.second:
                copy.wait_send()
            pieces = [[(split_rows(self.part, me, count), pl.ds(0, p.width))]]
            if self.second:
                pieces.append(
                    [
                        (self.land.at[0, :, left_half], left_half),
                        (self.land.at[1, :, left_half], right_half),
                    ]
                )
                pieces.append([(self.land.at[2], pl.ds(0, p.width))])
            else:
                pieces += [[(self.land.at[i], pl.ds(0, p.width))] for i in range(n)]

            def load(i):
                for src, cols in pieces[i]:
                    pltpu.make_async_copy(
                        src, land_v.at[i % 2, :, cols], small_sem.at[i % 2]
                    ).start()

            load(0)
            for i in range(len(pieces)):
                if i + 1 < len(pieces):
                    load(i + 1)
                held = land_v.at[i % 2]
                pltpu.make_async_copy(held, held, small_sem.at[i % 2]).wait()

                def strip(here, i=i):
                    value = land_v[i % 2, here, :].astype(F32)
                    row_sum[here, :] = value if i == 0 else row_sum[here, :] + value

                strips(strip)

        def settle(self):
            for copy in self.first:
                copy.wait_send()

    back_rows = Scatter(back_part, back_land, back_send, back_recv)
    res_rows = Scatter(res_part, res_land, res_send, res_recv)
    norm_rows = Scatter(norm_part, norm_land, norm_send, norm_recv)

    STRIP = 32

    def strips(body):
        def go(i, carry):
            body(pl.ds(pl.multiple_of(i * STRIP, STRIP), STRIP))
            return carry

        lax.fori_loop(0, count // STRIP, go, 0)

    def norm_strip(here, values, rms, gain, row):
        grad_in = row_sum[here, :]
        weighted = grad_in * gain
        inner = jnp.mean(weighted * values, axis=-1, keepdims=True)
        gain_part[row : row + 1, :] += jnp.sum(grad_in * values * rms, axis=0, keepdims=True)
        return rms * weighted - values * (rms * rms * rms) * inner

    gather = Gather(shards, gh_own, gh_all, gather_send, gather_recv, gather_local)

    def hidden_back():
        load_hidden.wait()
        back_rows.fetch()
        gain_part[...] = jnp.zeros_like(gain_part)

        def strip(here):
            own = pl.ds(pl.multiple_of(me * count, count) + here.start, STRIP)
            grad = left_a[own, :].astype(F32) + norm_strip(
                here, hidden_v[here, :], mlp_rms[here, :], mlp_gain[...], 1
            )
            grad_hidden[here, :] = grad
            gh_own[here, :] = grad.astype(BF16)

        strips(strip)
        gather.start()

    def finish_result():
        res_rows.fetch()

        def strip(here):
            row_sum[here, :] = hidden_v[here, :] + row_sum[here, :]

        strips(strip)
        store_result = pltpu.make_async_copy(row_sum, result_ref, small_sem.at[0])
        store_result.start()
        store_result.wait()

    def mixed_back():
        gather.finish()
        load_proj.wait()

        def go(i, carry):
            here = pl.ds(pl.multiple_of(i * TILE, TILE), TILE)
            g_t[:, here] = dot(proj_v[...], both[here, : p.width], NT).astype(BF16)
            return carry

        lax.fori_loop(0, p.length // TILE, go, 0)

    blocks = p.length // TILE
    rows = GROUP * HEAD
    wide = GROUP * TILE
    mid = HEAD // 2

    def attention_unit(unit):
        g, turn = unit // blocks, unit % blocks
        block = jnp.where(turn % 2 == 0, turn // 2, blocks - 1 - turn // 2)
        query_at = pl.multiple_of(block * TILE, TILE)
        here_q = pl.ds(query_at, TILE)

        queries = side_by_side(q_ref, g, here_q)
        grads = side_by_side(g_t, g, here_q)
        mixed = side_by_side(mixed_ref, g, here_q)
        lse = jnp.concatenate([lse_ref[g, h : h + 1, here_q] for h in range(GROUP)], axis=1)
        inner = jnp.sum(grads.astype(F32) * mixed.astype(F32), axis=0, keepdims=True)

        @pl.when(turn == 0)
        def _():
            dk_acc[...] = jnp.zeros_like(dk_acc)
            dv_acc[...] = jnp.zeros_like(dv_acc)

        def step(c, acc):
            key_at = pl.multiple_of(c * TILE, TILE)
            here = pl.ds(key_at, TILE)
            scores = dot(k_ref[g, here, :], queries, NN)
            scores = scores + block_bias(seg_col, seg_row, key_at, query_at)
            probs = jnp.exp(scores - lse)
            grad_probs = dot(v_ref[g, here, :], grads, NN)
            grad_scores = (probs * (grad_probs - inner)).astype(BF16)
            dv_acc[:, here] += dot(grads, probs.astype(BF16), NT)
            dk_acc[:, here] += dot(queries, grad_scores, NT)
            key_rows = pl.ds(pl.multiple_of(g * HEAD, HEAD), HEAD)
            return acc + dot(kt_ref[key_rows, here], grad_scores, NN)

        acc = lax.fori_loop(0, block + 1, step, jnp.zeros((HEAD, wide), F32))
        cos, sin = cos_ref[:, here_q], sin_ref[:, here_q]
        for h in range(GROUP):
            grad = acc[:, h * TILE : (h + 1) * TILE] * SCALE
            first, second = grad[:mid], grad[mid:]
            at = pl.multiple_of(g * rows + h * HEAD, HEAD)
            back_t[pl.ds(at, mid), here_q] = (first * cos + second * sin).astype(BF16)
            back_t[pl.ds(at + mid, mid), here_q] = (second * cos - first * sin).astype(BF16)

        @pl.when(turn == blocks - 1)
        def _():
            cos, sin = cos_ref[...], sin_ref[...]
            first, second = dk_acc[:mid, :], dk_acc[mid:, :]
            at = pl.multiple_of(p.q_part + g * HEAD, HEAD)
            back_t[pl.ds(at, mid), :] = (first * cos + second * sin).astype(BF16)
            back_t[pl.ds(at + mid, mid), :] = (second * cos - first * sin).astype(BF16)
            at = pl.multiple_of(p.q_part + p.kv_part + g * HEAD, HEAD)
            back_t[pl.ds(at, HEAD), :] = dv_acc[...].astype(BF16)

    def normed_back():
        load_qkv.wait()

        stores = [
            pltpu.make_async_copy(
                land_v.at[i % 2], norm_part.at[pl.ds(i * count, count), :], small_sem.at[i % 2]
            )
            for i in range(shards)
        ]
        for i, store in enumerate(stores):
            if i >= 2:
                stores[i - 2].wait()
            here = pl.ds(i * count, count)
            land_v[i % 2] = dot(back_t[:, here].T, qkv_v[...], NT).astype(BF16)
            store.start()
        for store in stores[-2:]:
            store.wait()
        norm_rows.start()

    gain_cols = p.width // shards

    def gain_slice(shard):
        return pl.ds(pl.multiple_of(shard * gain_cols, gain_cols), gain_cols)

    gain_plane = [
        remote(
            gain_part.at[:, gain_slice(me ^ (i + 1))], gain_land.at[me],
            gain_send, gain_recv, i, rep, me ^ (i + 1),
        )
        for i in range(n)
    ]
    gain_all = [
        remote(gain_sum, gain_reps.at[rep], rep_send, rep_recv, i, rep ^ (i + 1), me)
        for i in range(reps - 1)
    ]

    def tokens_back():
        norm_rows.fetch()
        load_tokens.start()
        load_tokens.wait()

        def strip(here):
            values = gh_own[here, :].astype(F32)
            rms = lax.rsqrt(jnp.mean(values * values, axis=-1, keepdims=True) + epsilon)
            grad_hidden[here, :] += norm_strip(here, values, rms, attn_gain[...], 0)

        strips(strip)
        store_tokens = pltpu.make_async_copy(grad_hidden, tokens_out, small_sem.at[0])
        store_tokens.start()
        store_tokens.wait()
        gain_land[me] = gain_part[:, gain_slice(me)]
        for copy in gain_plane:
            copy.start()

    def gains_plane():
        for copy in gain_plane:
            copy.wait_recv()
        total = gain_land[0]
        for s in range(1, shards):
            total = total + gain_land[s]
        gain_sum[...] = total
        gain_reps[rep] = total
        for copy in gain_all:
            copy.start()

    def gains_reps():
        for copy in gain_all:
            copy.wait_recv()
        total = gain_reps[0]
        for r in range(1, reps):
            total = total + gain_reps[r]
        gains_out[...] = total

    def swap_copy(j):
        return pltpu.make_async_remote_copy(
            src_ref=theirs.at[j % 2], dst_ref=swapped.at[j],
            send_sem=swap_send.at[j % 2], recv_sem=swap_recv.at[j],
            device_id=(rep ^ 1, me), device_id_type=MESH,
        )

    def store_chunk(slot, other_slot, at, size, product, columns=TILE):
        here = pl.ds(pl.multiple_of(at, size), size)
        mine[slot, here, :columns] = product(core).astype(BF16)
        theirs[other_slot, here, :columns] = product(1 - core).astype(BF16)

    def make(t):
        slot, other = t % p.mine_ring, t % 2

        @pl.when(t >= 2)
        def _():
            swap_copy(t - 2).wait_send()

        @pl.when(t == 0)
        def _():
            load_right(0)(lambda copy: copy.start())

        load_right(t)(lambda copy: copy.wait())

        @pl.when(t + 1 < ffn_end)
        def _():
            load_right(t + 1)(lambda copy: copy.start())

        @pl.when(is_chunk(t, 0))
        def _():
            left = right[t % 2].T

            def product(which):
                return dot(left, left_a[:, columns(which, p.rows)], NN).astype(BF16)

            ours, others = product(core), product(1 - core)
            for at in range(0, p.rows, TILE):
                mine[slot, at : at + TILE, :] = ours[:, at : at + TILE]
                theirs[other, at : at + TILE, :] = others[:, at : at + TILE]

        def wide_chunk(left, factor, columns):
            def go(s, carry):
                def product(which):
                    at = pl.multiple_of(s * p.own + which * p.block, p.block)
                    return dot(factor, left[:, pl.ds(at, p.block)], NN).T

                store_chunk(slot, other, s * p.block, p.block, product, columns)
                return carry

            lax.fori_loop(0, shards, go, 0)

        @pl.when(t < p.down_at)
        def _():
            wide_chunk(left_b, right[t % 2].T, TILE)

        @pl.when((t >= proj_at) & (t < end_at))
        def _():
            def go(i, carry):
                at = columns((t - proj_at) * p.proj_blocks + i)

                def product(which):
                    part = columns(which, p.proj_half)
                    return dot(mixed_ref[part, :], both[:, at], NN)

                store_chunk(slot, other, i * p.proj_half, p.proj_half, product)
                return carry

            lax.fori_loop(0, p.proj_blocks, go, 0)

        @pl.when((t >= q_at) & (t < kv_at))
        def _():
            wide_chunk(left_a, back_t[columns(t - q_at), :], TILE)

        @pl.when(t == kv_at)
        def _():
            wide_chunk(left_a, back_t[p.q_part :, :], 2 * p.kv_part)

        swap_copy(t).start()

    def inward_copies(j):
        common = dict(
            src_ref=sums.at[j % p.sum_ring], send_sem=in_send.at[j % p.sum_ring],
            device_id=(inward, me), device_id_type=MESH,
        )
        to_layer = pltpu.make_async_remote_copy(
            dst_ref=from_outer.at[j], recv_sem=outer_recv.at[j], **common
        )
        to_middle = pltpu.make_async_remote_copy(
            dst_ref=from_middle.at[j], recv_sem=middle_recv.at[j], **common
        )
        return to_layer, to_middle

    def total_places(j, action):
        @pl.when(is_chunk(j, 0))
        def _():
            action(
                [
                    (
                        i * TILE, TILE, TILE,
                        f_down.at[
                            columns(tile_of(j)),
                            pl.ds(pl.multiple_of(core * p.rows + i * TILE, TILE), TILE),
                        ],
                    )
                    for i in range(p.rows // TILE)
                ]
            )

        @pl.when((j >= proj_at) & (j < end_at))
        def _():
            action(
                [
                    (
                        i * p.proj_half, p.proj_half, TILE,
                        f_proj.at[
                            columns(core, p.proj_half),
                            columns((j - proj_at) * p.proj_blocks + i),
                        ],
                    )
                    for i in range(p.proj_blocks)
                ]
            )

        for when, full, part, tile, sem, wide_by in wide_kinds(j):

            @pl.when(when)
            def _(full=full, part=part, tile=tile, wide_by=wide_by):
                blocks = []
                for i in range(shards):
                    at = pl.multiple_of((me ^ i) * p.block, p.block)
                    place_there = totals.at[j, pl.ds(at, p.block), pl.ds(0, wide_by)]
                    if i == 0:
                        place_there = window(full, me, part, tile, wide_by)
                    blocks.append((at, p.block, wide_by, place_there))
                action(blocks)

    def chunk_bytes(j, sem):
        @pl.when(j == kv_at)
        def _():
            whole = totals.at[0, :, pl.ds(0, 2 * p.kv_part)]
            pltpu.make_async_copy(whole, whole, sem).wait()

        @pl.when(j != kv_at)
        def _():
            whole = totals.at[0]
            pltpu.make_async_copy(whole, whole, sem).wait()

    def send_total(src, dst, j):
        return pltpu.make_async_remote_copy(
            src_ref=src, dst_ref=dst, send_sem=out_send.at[j % 2],
            recv_sem=total_recv.at[j], device_id=(outward, me), device_id_type=MESH,
        )

    def add_rows(body):
        def go(i, carry):
            body(pl.ds(pl.multiple_of(i * TILE, TILE), TILE))
            return carry

        lax.fori_loop(0, p.rows // TILE, go, 0)

    def load_swapped(j):
        return pltpu.make_async_copy(swapped.at[j], swap_v, small_sem.at[2])

    def load_outer(j):
        return pltpu.make_async_copy(from_outer.at[j], outer_v, small_sem.at[3])

    def load_middle(j):
        return pltpu.make_async_copy(from_middle.at[j], middle_v, small_sem.at[4])

    def valid(j):
        return (j >= 0) & (j < p.chunks)

    def take_inward(j):
        @pl.when(valid(j))
        def _():
            swap_copy(j).wait_recv()
            load_swapped(j).start()

            @pl.when(depth > 0)
            def _():
                inward_copies(j)[0].wait_recv()
                load_outer(j).start()

    def send_inward(j):
        @pl.when(valid(j))
        def _():
            @pl.when(j >= p.sum_ring)
            def _():
                inward_copies(j - p.sum_ring)[0].wait_send()

            load_swapped(j).wait()
            ours = mine.at[j % p.mine_ring]
            total = sums.at[j % p.sum_ring]

            @pl.when(depth > 0)
            def _():
                load_outer(j).wait()

                def add(here):
                    total[here, :] = (
                        ours[here, :].astype(F32)
                        + swap_v[here, :].astype(F32)
                        + outer_v[here, :].astype(F32)
                    ).astype(BF16)

                add_rows(add)

            @pl.when(depth == 0)
            def _():
                def add(here):
                    total[here, :] = (
                        ours[here, :].astype(F32) + swap_v[here, :].astype(F32)
                    ).astype(BF16)

                add_rows(add)

            to_layer, to_middle = inward_copies(j)

            @pl.when(is_middle)
            def _():
                to_middle.start()

            @pl.when(jnp.logical_not(is_middle))
            def _():
                to_layer.start()

    def take_middle(j):
        @pl.when(is_middle & valid(j))
        def _():
            inward_copies(j)[1].wait_recv()
            load_middle(j).start()

    def meet_in_middle(j):
        @pl.when(is_middle & valid(j))
        def _():
            @pl.when(j >= 1)
            def _():
                chunk_bytes(j - 1, total_store.at[0])

            if p.half > 1:

                @pl.when(j >= 2)
                def _():
                    chunk_bytes(j - 2, out_send.at[j % 2])

            load_middle(j).wait()
            out, held = total_v.at[j % 2], sums.at[j % p.sum_ring]

            def add(here):
                out[here, :] = (
                    held[here, :].astype(F32) + middle_v[here, :].astype(F32)
                ).astype(BF16)

            add_rows(add)

            def put(blocks):
                for at, size, wide_by, dst in blocks:
                    src = out.at[pl.ds(at, size), pl.ds(0, wide_by)]
                    if p.half > 1:
                        send_total(src, dst, j).start()
                    pltpu.make_async_copy(src, dst, total_store.at[0]).start()

            total_places(j, put)

    def last_store(t):
        @pl.when(is_middle & (t == p.chunks + p.arrive - 1))
        def _():
            chunk_bytes(p.chunks - 1, total_store.at[0])

    def send_outward(j):
        @pl.when(jnp.logical_not(is_middle) & valid(j))
        def _():
            chunk_bytes(j, total_recv.at[j])

            if p.half > 2:

                @pl.when(depth > 0)
                def _():
                    @pl.when(j >= 2)
                    def _():
                        chunk_bytes(j - 2, out_send.at[j % 2])

                    def put(blocks):
                        for _, _, _, dst in blocks:
                            send_total(dst, dst, j).start()

                    total_places(j, put)

    def remote_pass(src, dst, sem):
        return pltpu.make_async_remote_copy(
            src_ref=src, dst_ref=dst, send_sem=pass_send.at[sem], recv_sem=pass_recv.at[sem],
            device_id=(rep ^ 1, me), device_id_type=MESH,
        )

    def window(full, shard, part, tile, columns=TILE):
        at = pl.multiple_of(shard * part + tile * columns, columns)
        return full.at[pl.ds(pl.multiple_of(core * p.block, p.block), p.block), pl.ds(at, columns)]

    def wide_kinds(j):
        return (
            (is_chunk(j, 1), f_gate, p.ffn_part, tile_of(j), 1, TILE),
            (is_chunk(j, 2), f_up, p.ffn_part, tile_of(j), 2, TILE),
            ((j >= q_at) & (j < kv_at), f_q, p.q_part, j - q_at, 4, TILE),
            (j == kv_at, f_kv, 2 * p.kv_part, 0, 5, 2 * p.kv_part),
        )

    def spread_total(j):
        for kind, sem in ((is_chunk(j, 0), 0), ((j >= proj_at) & (j < end_at), 3)):

            @pl.when(kind)
            def _(sem=sem):
                def put(blocks):
                    for _, _, _, dst in blocks:
                        remote_pass(dst, dst, sem).start()

                total_places(j, put)

        for when, full, part, tile, sem, wide_by in wide_kinds(j):

            @pl.when(when)
            def _(full=full, part=part, tile=tile, sem=sem, wide_by=wide_by):
                place_here = window(full, me, part, tile, wide_by)
                for i in range(n):
                    at = columns(me ^ (i + 1), p.block)
                    pltpu.make_async_remote_copy(
                        src_ref=totals.at[j, at, pl.ds(0, wide_by)], dst_ref=place_here,
                        send_sem=cross_send.at[sem], recv_sem=cross_recv.at[j],
                        device_id=(rep, me ^ (i + 1)), device_id_type=MESH,
                    ).start()
                remote_pass(place_here, place_here, sem).start()

    def pass_on(j):
        for when, full, part, tile, sem, wide_by in wide_kinds(j):

            @pl.when(when)
            def _(full=full, part=part, tile=tile, sem=sem, wide_by=wide_by):
                came = totals.at[j, pl.ds(0, n * p.block), pl.ds(0, wide_by)]
                pltpu.make_async_copy(came, came, cross_recv.at[j]).wait()
                for i in range(n):
                    here = window(full, me ^ (i + 1), part, tile, wide_by)
                    remote_pass(here, here, sem).start()

    for copy in (load_x, load_cot):
        copy.start()
    load_tile(0)
    greet(plane_partners(rep, me, shards) + [(rep ^ i, me) for i in range(1, reps)])
    ahead = 3
    for tile in range(first_tile, min(first_tile + ahead, p.tiles)):
        send_tile(tile)
    for copy in (load_hidden, load_proj, load_qkv):
        copy.start()
    load_x.wait()

    def slot(t, carry):
        inner = t - 1 - depth
        met = t - 1 - p.half
        take_inward(inner)
        send_inward(inner)
        send_outward(t - p.arrive + depth)

        def spread_until(u):
            ready = jnp.minimum(u - p.arrive + 1, p.chunks)
            later = p.spread_first + 2 * jnp.maximum(u - p.spread_slot + 1, 0)
            most = jnp.where(u <= p.send_slot, p.chunks, later)
            return jnp.maximum(jnp.minimum(ready, most), 0)

        def over(action, u):
            def go(j, c):
                action(j)
                return c

            lax.fori_loop(spread_until(u - 1), spread_until(u), go, 0)

        last_store(t)
        over(spread_total, t)
        over(pass_on, t - p.hand)

        @pl.when(t + first_tile + ahead < p.tiles)
        def _():
            send_tile(t + first_tile + ahead)

        @pl.when((t > 0) & (t + 1 >= first_tile) & (t + 1 < p.tiles))
        def _():
            pass_tile(t + 1)

        @pl.when(t < p.tiles)
        def _():
            ffn_tile(t)

        @pl.when((t >= p.back_slot) & (t <= p.send_slot))
        def _():
            back_tiles((t - p.back_slot) * p.per_slot)

        @pl.when(t == ffn_end)
        def _():
            load_normed.start()
            if not p.early_res:
                load_activ.start()

        @pl.when(t == q_at)
        def _():
            load_normed.wait()

        def at(when, action):
            @pl.when(t == when)
            def _():
                action()

        at(p.tokens_slot, tokens_back)
        take_middle(met)
        meet_in_middle(met)
        at(p.send_slot, back_rows.start)
        at(p.send_slot + 2, back_rows.hand_on)
        at(p.send_slot, load_cot.wait)
        at(p.rows_slot, hidden_back)
        at(p.pass_slot, gather.hand_on)
        at(p.mixed_slot, mixed_back)

        @pl.when((t >= p.unit_slot) & (t < p.norm_slot))
        def _():
            def go(i, c):
                attention_unit((t - p.unit_slot) * 2 + i)
                return c

            lax.fori_loop(0, 2, go, 0)

        at(p.norm_slot, normed_back)
        at(p.norm_slot + 5, norm_rows.hand_on)

        @pl.when(t < p.chunks)
        def _():
            make(t)

        at(p.gain_slot, gains_plane)
        at(p.rep_slot, gains_reps)

        @pl.when((t >= p.res_slot) & (t < p.res_slot + p.out_tiles // 2))
        def _():
            @pl.when(t == p.res_slot)
            def _():
                if not p.early_res:
                    load_activ.wait()
                load_res(0)(lambda copy: copy.start())

            res_tiles((t - p.res_slot) * 2)

        at(p.res_send_slot, res_rows.start)
        at(p.res_send_slot + 3, res_rows.hand_on)
        at(p.result_slot, finish_result)
        return carry

    lax.fori_loop(0, p.slots, slot, 0)

    for j in range(max(0, p.chunks - 2), p.chunks):
        swap_copy(j).wait_send()
    for j in range(max(0, p.chunks - p.sum_ring), p.chunks):
        inward_copies(j)[0].wait_send()
    if p.half > 1:

        @pl.when(depth > 0)
        def _():
            for j in range(max(0, p.chunks - 2), p.chunks):
                chunk_bytes(j, out_send.at[j % 2])

    for rows in (back_rows, res_rows, norm_rows):
        rows.settle()
    for copies in (gain_plane, gain_all):
        for copy in copies:
            copy.wait_send()

    def settle(ref, sem):
        pltpu.make_async_copy(ref, ref, sem).wait()

    for tile in range(first_tile, p.tiles):
        tile_bytes(tile, tile_send).wait()
        tile_bytes(tile, tile_pass).wait()
    for sem, part in (
        (0, f_down.at[:, pl.ds(0, p.rows)]),
        (3, f_proj.at[pl.ds(0, p.proj_half), :]),
    ):
        settle(part, pass_send.at[sem])
        settle(part, pass_recv.at[sem])
    for _, full, part, _, sem, _ in wide_kinds(0):
        here = full.at[pl.ds(0, p.block), :]
        settle(here, pass_send.at[sem])
        settle(here, pass_recv.at[sem])
        settle(full.at[pl.ds(0, p.block), pl.ds(0, n * part)], cross_send.at[sem])


def backward(
    shards, reps, x, cot_all, grad_activ, gate_w, up_w, gate_e, up_e, down_w, hidden, tokens, proj_w,
    qkv_m, normed, mlp_rms, mlp_gain, attn_gain, seg_col, seg_row, cos_t, sin_t, lse, q_t, mixed_t,
    k, k_t, v,
):
    length, width = x.shape
    count = tokens.shape[0]
    ffn_part = down_w.shape[0]
    q_part, kv_part = q_t.shape[0], k_t.shape[0]
    n = shards - 1
    p = Plan(shards, reps, length, width, ffn_part, q_part, kv_part)
    shape = jax.ShapeDtypeStruct
    own = width // shards
    chunk = (p.rows, TILE)
    dma = pltpu.SemaphoreType.DMA
    return pl.pallas_call(
        functools.partial(backward_kernel, p, gate_e.shape[1]),
        in_specs=[ANY] * 13 + [IN_VMEM] * 13,
        out_specs=[ANY] * 8 + [IN_VMEM] + [ANY] * 15,
        out_shape=[
            shape((ffn_part, width), BF16),
            shape((own, shards * ffn_part), BF16),
            shape((own, shards * ffn_part), BF16),
            shape((q_part, width), BF16),
            shape((own, shards * q_part), BF16),
            shape((own, shards * 2 * kv_part), BF16),
            shape((count, width), F32),
            shape((count, width), F32),
            shape((8, width // shards), F32),
        ]
        + [shape((p.chunks,) + chunk, BF16)] * 4
        + [shape((n, count, width), BF16)] * 3
        + [shape((length, width), BF16)]
        + [shape((width, ffn_part), BF16)] * 2
        + [shape((length, ffn_part), BF16)] * 3
        + [shape((length, width), BF16)] * 2,
        scratch_shapes=[
            pltpu.VMEM((length, width), BF16),
            pltpu.VMEM((length, width), BF16),
            pltpu.VMEM((2, length, TILE), BF16),
            pltpu.VMEM((width, TILE), BF16),
            pltpu.VMEM((width, TILE), BF16),
            pltpu.VMEM((length, TILE), BF16),
            pltpu.VMEM((2, TILE, 2 * ffn_part), BF16),
            pltpu.VMEM((2, length, TILE), BF16),
            pltpu.VMEM((length, 2 * ffn_part), BF16),
            pltpu.VMEM(proj_w.shape, BF16),
            pltpu.VMEM(qkv_m.shape, BF16),
            pltpu.VMEM((count, width), F32),
            pltpu.VMEM((count, width), F32),
            pltpu.VMEM((2, count, width), BF16),
            pltpu.VMEM((p.mine_ring,) + chunk, BF16),
            pltpu.VMEM((2,) + chunk, BF16),
            pltpu.VMEM(chunk, BF16),
            pltpu.VMEM(chunk, BF16),
            pltpu.VMEM(chunk, BF16),
            pltpu.VMEM((p.sum_ring,) + chunk, BF16),
            pltpu.VMEM((2,) + chunk, BF16),
            pltpu.VMEM((count, width), F32),
            pltpu.VMEM((count, width), BF16),
            pltpu.VMEM((q_part, length), BF16),
            pltpu.VMEM((q_part + 2 * kv_part, length), BF16),
            pltpu.VMEM((HEAD, length), F32),
            pltpu.VMEM((HEAD, length), F32),
            pltpu.VMEM((length, ffn_part) if p.early_res else (16, 128), BF16),
            pltpu.VMEM((8, width), F32),
            pltpu.VMEM((shards, 8, own), F32),
            pltpu.VMEM((8, own), F32),
            pltpu.VMEM((reps, 8, own), F32),
            dma((12,)), dma((2,)), dma((5,)), dma((2,)), dma((p.chunks,)), dma((p.sum_ring,)),
            dma((p.chunks,)), dma((p.chunks,)), dma((2,)), dma((p.chunks,)), dma((2,)),
            dma((p.chunks,)), dma((6,)), dma((6,)), dma((6,)),
        ]
        + [dma((max(6, n),))] * 6
        + Gather.semaphores(shards)
        + [dma((n,)), dma((n,)), dma((reps - 1,)), dma((reps - 1,))]
        + [dma((p.tiles,))] * 4
        + [dma((3,)), dma((2, 2)), dma((3,))],
        compiler_params=pltpu.CompilerParams(
            collective_id=3, has_side_effects=True, vmem_limit_bytes=FULL
        ),
        name="backward",
    )(
        x, cot_all, grad_activ, gate_w, up_w, gate_e, up_e, down_w, hidden, tokens, proj_w,
        qkv_m, normed, mlp_rms, mlp_gain[None, :], attn_gain[None, :], seg_col, seg_row,
        cos_t, sin_t, lse, q_t, mixed_t, k, k_t, v,
    )[:9]


def widen_kernel(count, rows, columns, group, *refs):
    paired = 1 if group else 0
    srcs, dsts = refs[:count], refs[count : 2 * count + paired]
    narrow, wide, in_sem, out_sem = refs[2 * count + paired :]
    depth = narrow.shape[0]
    jobs = []
    for i, src in enumerate(srcs):
        width = min(columns, src.shape[1])
        for r in range(src.shape[0] // rows):
            for c in range(src.shape[1] // width):
                slot = len(jobs) % depth
                at = (pl.ds(r * rows, rows), pl.ds(c * width, width))
                own = (slice(None), pl.ds(0, width))
                pair = paired and i == 0
                direct = src.dtype == F32
                into = (wide if direct else narrow).at[slot].at[own]
                load = pltpu.make_async_copy(src.at[at], into, in_sem.at[slot])
                held = wide.at[slot].at[own]
                if pair:
                    side = width // 2
                    puts = [
                        pltpu.make_async_copy(
                            wide.at[slot, :, pl.ds(k * side, side)],
                            dsts[k].at[pl.ds(r * rows, rows), :],
                            out_sem.at[slot],
                        )
                        for k in range(2)
                    ]
                else:
                    puts = [pltpu.make_async_copy(held, dsts[i + paired].at[at], out_sem.at[slot])]
                done = pltpu.make_async_copy(held, held, out_sem.at[slot])
                jobs.append((load, puts, done, direct, pair, width))
    total = len(jobs)
    ahead = depth - 1

    def load(i):
        if jobs[i][3] and i >= depth:
            jobs[i - depth][2].wait()
        jobs[i][0].start()

    for i in range(min(ahead, total)):
        load(i)
    for i in range(total):
        slot = i % depth
        fetch, puts, _, direct, pair, width = jobs[i]
        fetch.wait()
        if not direct:
            if i >= depth:
                jobs[i - depth][2].wait()
            for strip in range(0, rows, 64):
                here = pl.ds(strip, 64)
                if pair:
                    for k in range(width // group):
                        to = (k % 2) * (width // 2) + (k // 2) * group
                        wide[slot, here, pl.ds(to, group)] = narrow[
                            slot, here, pl.ds(k * group, group)
                        ].astype(F32)
                else:
                    wide[slot, here, pl.ds(0, width)] = narrow[
                        slot, here, pl.ds(0, width)
                    ].astype(F32)
        for put in puts:
            put.start()
        if i + ahead < total:
            load(i + ahead)
    for i in range(max(0, total - depth), total):
        jobs[i][2].wait()


def widen(arrays, group):
    rows, columns, depth = 256, 2048, 4
    rows = min([rows] + [a.shape[0] for a in arrays])
    shapes = [jax.ShapeDtypeStruct(a.shape, F32) for a in arrays]
    if group:
        tall, width = arrays[0].shape
        shapes[:1] = [jax.ShapeDtypeStruct((tall, width // 2), F32)] * 2
    return pl.pallas_call(
        functools.partial(widen_kernel, len(arrays), rows, columns, group),
        in_specs=[ANY] * len(arrays),
        out_specs=[ANY] * len(shapes),
        out_shape=shapes,
        scratch_shapes=[
            pltpu.VMEM((depth, rows, columns), BF16),
            pltpu.VMEM((depth, rows, columns), F32),
            pltpu.SemaphoreType.DMA((depth,)),
            pltpu.SemaphoreType.DMA((depth,)),
        ],
        compiler_params=pltpu.CompilerParams(vmem_limit_bytes=FULL),
        name="widen",
    )(*arrays)


def local(
    tokens, segments, query_w, key_w, value_w, proj_w, attn_gain,
    gate_w, up_w, down_w, mlp_gain, cotangent,
):
    shards = lax.axis_size("shard")
    reps = lax.axis_size("rep")
    tok_count, width = tokens.shape
    kv_part = key_w.shape[1] // shards
    q_part = query_w.shape[1] // shards
    length = tok_count * shards

    if kv_part % 128:
        kv_w = jnp.concatenate(
            [
                w[:, s * kv_part : (s + 1) * kv_part]
                for s in range(shards)
                for w in (key_w, value_w)
            ],
            axis=1,
        )
        weights = (query_w, kv_w)
    else:
        weights = (query_w, key_w, value_w)
    early = min(2 * TILE, down_w.shape[0] // 2)
    (
        normed, cot_all, proj_m, gate_e, up_e, qkv_m,
        q_t, k, k_t, v, mixed_t, lse, cos_t, sin_t, seg_col, seg_row,
    ) = attend(
        tokens, segments[None, :], weights, cotangent, proj_w, gate_w, up_w, attn_gain,
        q_part, kv_part, early, shards,
    )
    hidden, mlp_rms, normed_mlp, grad_activ = hidden_layer(
        mixed_t, proj_m, proj_w, cot_all, down_w, tokens, mlp_gain, shards
    )
    down, gate, up, proj, query, kv, result, grad_tokens, gains = backward(
        shards, reps, normed_mlp, cot_all, grad_activ, gate_w, up_w, gate_e, up_e, down_w, hidden, tokens,
        proj_w, qkv_m, normed, mlp_rms, mlp_gain, attn_gain, seg_col, seg_row, cos_t, sin_t, lse,
        q_t, mixed_t, k, k_t, v,
    )

    def every_other(first):
        parts = [
            kv[:, (2 * s + first) * kv_part : (2 * s + first + 1) * kv_part] for s in range(shards)
        ]
        return jnp.concatenate(parts, axis=1).astype(F32)

    others = [gate, up, down, query, proj, result, grad_tokens]
    if kv_part % 128:
        key, value = every_other(0), every_other(1)
        gate, up, down, query, proj, result, grad_tokens = widen(others, 0)
    else:
        key, value, gate, up, down, query, proj, result, grad_tokens = widen([kv] + others, kv_part)
    return (
        result, grad_tokens, query, key, value, proj, gains[0], gate, up, down, gains[1],
    )


def solution(mesh):
    rows = P(("rep", "shard"), None)
    held = P("shard", None)
    in_specs = (
        rows, P(("rep", "shard")), held, held, held, held, P(), held, held, held, P(), rows,
    )
    out_specs = (
        rows, rows, held, held, held, held, P("shard"), held, held, held, P("shard"),
    )
    return jax.shard_map(local, mesh=mesh, in_specs=in_specs, out_specs=out_specs, check_vma=False)
```

```python
import functools
import math

import jax
import jax.numpy as jnp
import numpy as np
from jax import lax
from jax.experimental import pallas as pl
from jax.experimental.pallas import tpu as pltpu
from jax.sharding import PartitionSpec as P

HEADS = 32
KV_HEADS = 8
HEAD = 64
GROUP = HEADS // KV_HEADS
SCALE = 1.0 / math.sqrt(HEAD)
TILE = 256
ROWS = 512
NEG = -1e30
MIB = 1024 * 1024
FULL = 63 * MIB + MIB // 2

epsilon = 1e-05
rope_base = 500000.0
F32 = jnp.float32
BF16 = jnp.bfloat16


def dot(left, right, dims):
    return lax.dot_general(left, right, (dims, ((), ())), preferred_element_type=F32)


NN = ((1,), (0,))
NT = ((1,), (1,))
TN = ((0,), (0,))
TT = ((0,), (1,))


MESH = pl.DeviceIdType.MESH


def place():
    return lax.axis_index("rep"), lax.axis_index("shard")


def remote(src, dst, sends, recvs, index, rep, shard):
    return pltpu.make_async_remote_copy(
        src_ref=src,
        dst_ref=dst,
        send_sem=sends.at[index],
        recv_sem=recvs.at[index],
        device_id=(rep, shard),
        device_id_type=MESH,
    )


def greet(partners):
    barrier = pltpu.get_barrier_semaphore()
    for partner in partners:
        pl.semaphore_signal(barrier, inc=1, device_id=partner, device_id_type=MESH)
    pl.semaphore_wait(barrier, len(partners))


def plane_partners(rep, me, shards):
    return [(rep, me ^ step) for step in range(1, shards)]


class Spread:
    def __init__(self, shards, own, full, columns, sends, recvs, held=None, held_sem=None):
        rep, me = place()
        quarter = rep % 4
        count = own.shape[0]
        part = count // 4
        own_rows = pl.ds(pl.multiple_of(quarter * part, part), part)

        def at(shard, which):
            return full.at[pl.ds(pl.multiple_of(shard * count + which * part, part), part), :]

        def piece(shard):
            return own.at[own_rows, :] if columns is None else own.at[own_rows, columns(shard)]

        self.first, self.core, self.layer, self.last = [], [], [], []
        n = shards - 1
        for i in range(n):
            peer = me ^ (i + 1)
            self.first.append(remote(piece(peer), at(me, quarter), sends, recvs, i, rep, peer))
            mine = at(peer, quarter)
            self.core.append(remote(mine, mine, sends, recvs, n + i, rep ^ 1, me))
            self.layer.append(remote(mine, mine, sends, recvs, 2 * n + i, rep ^ 2, me))
            theirs = at(peer, quarter ^ 2)
            self.last.append(remote(theirs, theirs, sends, recvs, 3 * n + i, rep ^ 1, me))
        self.take = self.keep = None
        if held is not None:
            kept = full.at[pl.ds(pl.multiple_of(me * count, count), count), :]
            self.take = pltpu.make_async_copy(own.at[:, columns(me)], held, held_sem.at[0])
            self.keep = pltpu.make_async_copy(held, kept, held_sem.at[1])

    def start(self):
        for copy in self.first:
            copy.start()
        if self.take is not None:
            self.take.start()

    def hand_on(self):
        if self.take is not None:
            self.take.wait()
            self.keep.start()
        for i, copy in enumerate(self.first):
            copy.wait_recv()
            self.layer[i].start()
            self.core[i].start()

    def hand_on_last(self):
        for i, copy in enumerate(self.layer):
            copy.wait_recv()
            self.last[i].start()

    def finish(self):
        for copy in self.core + self.last:
            copy.wait_recv()
        for copy in self.first + self.core + self.layer + self.last:
            copy.wait_send()
        if self.keep is not None:
            self.keep.wait()

    @staticmethod
    def semaphores(shards):
        n = 4 * (shards - 1)
        return [pltpu.SemaphoreType.DMA((n,)), pltpu.SemaphoreType.DMA((n,))]


class WideSpread:
    def __init__(self, shards, own, full, sends, recvs):
        rep, me = place()
        eighth = rep % 8
        count = own.shape[0]
        part = count // 8
        own_rows = pl.ds(pl.multiple_of(eighth * part, part), part)

        def at(shard, which):
            return full.at[pl.ds(pl.multiple_of(shard * count + which * part, part), part), :]

        self.first, self.near, self.layer, self.far, self.passed = [], [], [], [], []
        n = shards - 1
        for i in range(n):
            peer = me ^ (i + 1)

            def hand(which, kind, to, i=i, peer=peer):
                piece = at(peer, which)
                return remote(piece, piece, sends, recvs, kind * n + i, to, me)

            self.first.append(
                remote(own.at[own_rows, :], at(me, eighth), sends, recvs, i, rep, peer)
            )
            self.layer.append(hand(eighth, 1, rep ^ 2))
            self.far.append((hand(eighth, 2, rep ^ 4), hand(eighth ^ 2, 3, rep ^ 4)))
            self.passed.append(
                tuple(
                    hand(which, 4 + k, rep ^ 1)
                    for k, which in enumerate((eighth, eighth ^ 2, eighth ^ 4, eighth ^ 6))
                )
            )

    def start(self):
        for copy in self.first:
            copy.start()

    def hand_on(self):
        for i, copy in enumerate(self.first):
            copy.wait_recv()
            self.layer[i].start()
            self.passed[i][0].start()
        for far in self.far:
            far[0].start()

    def hand_on_next(self):
        for i, copy in enumerate(self.layer):
            copy.wait_recv()
            self.far[i][1].start()
            self.passed[i][1].start()

    def hand_on_last(self):
        for k in range(2):
            for i, far in enumerate(self.far):
                far[k].wait_recv()
                self.passed[i][2 + k].start()

    def finish(self):
        for passed in self.passed:
            for copy in passed:
                copy.wait_recv()
        for i in range(len(self.first)):
            for copy in (self.first[i], self.layer[i], *self.far[i], *self.passed[i]):
                copy.wait_send()

    @staticmethod
    def semaphores(shards):
        n = 8 * (shards - 1)
        return [pltpu.SemaphoreType.DMA((n,)), pltpu.SemaphoreType.DMA((n,))]


class Gather:
    def __init__(self, shards, own, full, sends, recvs, local_sem=None):
        rep, me = place()
        count = own.shape[0]
        half = count // 2

        def at(shard, start, size):
            return full.at[pl.ds(pl.multiple_of(shard * count + start, half), size), :]

        self.direct, self.passed, self.kept = [], [], None
        if shards == 4:
            for i, (step, start) in enumerate(((1, 0), (2, half), (1, half), (2, 0))):
                self.direct.append(
                    remote(
                        own.at[pl.ds(start, half), :], at(me, start, half),
                        sends, recvs, i, rep, me ^ step,
                    )
                )
            for i, (step, start) in enumerate(((1, 0), (2, half))):
                came = at(me ^ step, start, half)
                self.passed.append(remote(came, came, sends, recvs, 4 + i, rep, me ^ step ^ 3))
        else:
            for i in range(shards - 1):
                self.direct.append(
                    remote(own, at(me, 0, count), sends, recvs, i, rep, me ^ (i + 1))
                )
        if local_sem is not None:
            self.kept = pltpu.make_async_copy(own, at(me, 0, count), local_sem)

    def start(self):
        for copy in self.direct:
            copy.start()
        if self.kept is not None:
            self.kept.start()

    def hand_on(self):
        for i, copy in enumerate(self.passed):
            self.direct[i].wait_recv()
            copy.start()

    def finish(self):
        for copy in self.direct[len(self.passed) :] + self.passed:
            copy.wait_recv()
        for copy in self.direct + self.passed:
            copy.wait_send()
        if self.kept is not None:
            self.kept.wait()

    @staticmethod
    def semaphores(shards):
        n = max(6, shards - 1)
        return [
            pltpu.SemaphoreType.DMA((n,)),
            pltpu.SemaphoreType.DMA((n,)),
            pltpu.SemaphoreType.DMA,
        ]


def split_rows(ref, index, size):
    return ref.at[pl.ds(pl.multiple_of(index * size, size), size), :]


def column_block(part):
    return lambda shard: pl.ds(pl.multiple_of(shard * part, part), part)


def pair_partners(rep, me):
    return [(rep ^ 1, me), (rep ^ 2, me)]


ANY = pl.BlockSpec(memory_space=pl.ANY)
IN_VMEM = pl.BlockSpec(memory_space=pltpu.VMEM)


def rope_tables(seg_col, seg_row, freqs):
    length = seg_row.shape[1]
    begins = jnp.sum((seg_col < seg_row).astype(jnp.int32), axis=0, keepdims=True)
    positions = lax.broadcasted_iota(jnp.int32, (1, length), 1) - begins
    angles = freqs * positions.astype(F32)
    return (jnp.cos(angles), jnp.sin(angles))


def side_by_side(ref, group, here):
    rows = GROUP * HEAD
    return jnp.concatenate(
        [
            ref[pl.ds(pl.multiple_of(group * rows + h * HEAD, HEAD), HEAD), here]
            for h in range(GROUP)
        ],
        axis=1,
    )


def block_bias(seg_col_ref, seg_row_ref, key_at, query_at):
    same = seg_col_ref[pl.ds(key_at, TILE), :] == seg_row_ref[:, pl.ds(query_at, TILE)]
    key_index = key_at + lax.broadcasted_iota(jnp.int32, (TILE, TILE), 0)
    query_index = query_at + lax.broadcasted_iota(jnp.int32, (TILE, TILE), 1)
    bias = jnp.where(same & (key_index <= query_index), 0.0, NEG).astype(F32)
    return jnp.concatenate([bias] * GROUP, axis=1)


def attend_kernel(
    shards, ffn_part, early, parts, tokens, seg, cot, proj_w, gate_w, up_w, *refs,
):
    count = len(parts)
    weights, refs = refs[:count], refs[count:]
    (
        gain, freqs, normed_out, cot_all, proj_m, gate_m, up_m, qkv_m,
        q_ref, k_ref, kt_ref, v_ref, out_ref, lse_ref, cos_ref, sin_ref, seg_col, seg_row,
        tokens_v, normed_v, qkv_v, turned_v, vt_ref, cot_v, seg_v, store_sem, qkv_sem, own_sem,
        seg_send, seg_recv, *sems,
    ) = refs
    rep, me = place()
    length, width = tokens_v.shape
    kv_heads = k_ref.shape[0]
    q_part, kv_part = q_ref.shape[0], kt_ref.shape[0]
    blocks = length // TILE

    at, spreads, own = 0, [], []
    for i, (weight, part) in enumerate(zip(weights, parts)):
        full, rows = qkv_v.at[:, pl.ds(at, part)], weight.shape[0]
        spreads.append(
            Spread(shards, weight, full, column_block(part), *sems[2 * i : 2 * i + 2])
        )
        own.append(
            pltpu.make_async_copy(
                weight.at[:, column_block(part)(me)], split_rows(full, me, rows), own_sem.at[i]
            )
        )
        at += part
    sems = sems[2 * count :]
    rows = Gather(shards, tokens, tokens_v, *sems[:3])
    segs = [
        remote(seg, seg_v.at[me], seg_send, seg_recv, i, rep, me ^ (i + 1))
        for i in range(shards - 1)
    ]
    own.append(pltpu.make_async_copy(seg, seg_v.at[me], own_sem.at[count]))
    take = pltpu.make_async_copy(cot, cot_v, own_sem.at[count + 1])
    sems = sems[3:]

    def first_tiles(shard):
        return pl.ds(pl.multiple_of(shard * ffn_part, ffn_part), early)

    proj = WideSpread(shards, proj_w, proj_m, *sems[:2])
    gate = Spread(shards, gate_w, gate_m, first_tiles, *sems[2:4])
    up = Spread(shards, up_w, up_m, first_tiles, *sems[4:6])
    cots = Gather(shards, cot_v, cot_all, *sems[6:9])

    for copy in (*own, take):
        copy.start()
    greet(plane_partners(rep, me, shards) + pair_partners(rep, me) + [(rep ^ 4, me)])
    proj.start()
    for spread in spreads:
        spread.start()
    for copy in segs:
        copy.start()
    rows.start()
    proj.hand_on()
    for spread in spreads:
        spread.hand_on()
    rows.hand_on()
    gate.start()
    up.start()
    take.wait()
    cots.start()
    proj.hand_on_next()
    for spread in spreads:
        spread.hand_on_last()

    for copy in segs:
        copy.wait()
    for copy in own:
        copy.wait()
    seg_row[...] = jnp.concatenate([seg_v[i] for i in range(shards)], axis=1)
    tall = jnp.broadcast_to(seg_row[...], (8, length)).astype(F32).T[:, :1]
    seg_col[...] = tall.astype(jnp.int32)
    cos_ref[...], sin_ref[...] = rope_tables(seg_col[...], seg_row[...], freqs[...])
    for spread in spreads:
        spread.finish()
    keep_qkv = pltpu.make_async_copy(qkv_v, qkv_m, qkv_sem)
    keep_qkv.start()

    def block_rows(i):
        return pl.ds(pl.multiple_of(i * TILE, TILE), TILE)

    def store(i):
        return pltpu.make_async_copy(
            normed_v.at[i % 2], normed_out.at[block_rows(i), :], store_sem.at[i % 2]
        )

    def turn_weights(i, carry):
        turned_v[:, block_rows(i)] = qkv_v[block_rows(i), :].T
        return carry

    lax.fori_loop(0, width // TILE, turn_weights, 0)
    rows.finish()
    half = HEAD // 2

    def project(i, carry):
        here = block_rows(i)

        @pl.when(i >= 2)
        def _():
            store(i - 2).wait()

        values = tokens_v[here, :].astype(F32)
        rms = lax.rsqrt(jnp.mean(values * values, axis=-1, keepdims=True) + epsilon)
        normed_v[i % 2] = (values * rms * gain[...]).astype(BF16)
        store(i).start()
        heads = dot(turned_v[...], normed_v[i % 2], NT)
        cos, sin = cos_ref[:, here], sin_ref[:, here]

        def turned(at):
            first, second = heads[at : at + half], heads[at + half : at + HEAD]
            return (
                (first * cos - second * sin).astype(BF16),
                (second * cos + first * sin).astype(BF16),
            )

        for at in range(0, q_part, HEAD):
            first, second = turned(at)
            q_ref[at : at + half, here] = (first.astype(F32) * SCALE).astype(BF16)
            q_ref[at + half : at + HEAD, here] = (second.astype(F32) * SCALE).astype(BF16)
        for g in range(kv_heads):
            at = g * HEAD
            first, second = turned(q_part + at)
            kt_ref[at : at + half, here] = first
            kt_ref[at + half : at + HEAD, here] = second
            vt_ref[at : at + HEAD, here] = heads[
                q_part + kv_part + at : q_part + kv_part + at + HEAD
            ].astype(BF16)
            k_ref[g, here, :] = kt_ref[at : at + HEAD, here].T
            v_ref[g, here, :] = vt_ref[at : at + HEAD, here].T
        return carry

    lax.fori_loop(0, blocks, project, 0)
    for i in range(max(0, blocks - 2), blocks):
        store(i).wait()
    wide = GROUP * TILE

    def unit(at, carry_out):
        g, block = at // blocks, at % blocks
        query_at = pl.multiple_of(block * TILE, TILE)
        here = pl.ds(query_at, TILE)
        queries = side_by_side(q_ref, g, here)
        value_rows = pl.ds(pl.multiple_of(g * HEAD, HEAD), HEAD)

        def step(c, carry):
            top, total, acc = carry
            key_at = pl.multiple_of(c * TILE, TILE)
            keys = pl.ds(key_at, TILE)
            scores = dot(k_ref[g, keys, :], queries, NN)
            scores = scores + block_bias(seg_col, seg_row, key_at, query_at)
            new_top = jnp.maximum(top, jnp.max(scores, axis=0, keepdims=True))
            expo = jnp.exp(scores - new_top)
            fade = jnp.exp(top - new_top)
            total = total * fade + jnp.sum(expo, axis=0, keepdims=True)
            acc = acc * fade + dot(vt_ref[value_rows, keys], expo.astype(BF16), NN)
            return new_top, total, acc

        start = (
            jnp.full((1, wide), NEG, F32),
            jnp.zeros((1, wide), F32),
            jnp.zeros((HEAD, wide), F32),
        )
        top, total, acc = lax.fori_loop(0, block, step, step(block, start))
        mixed = (acc / total).astype(BF16)
        lse = top + jnp.log(total)
        for h in range(GROUP):
            at_row = pl.multiple_of(g * GROUP * HEAD + h * HEAD, HEAD)
            out_ref[pl.ds(at_row, HEAD), here] = mixed[:, h * TILE : (h + 1) * TILE]
            lse_ref[g, h : h + 1, here] = lse[:, h * TILE : (h + 1) * TILE]
        return carry_out

    units = kv_heads * blocks
    lax.fori_loop(0, units // 2, unit, 0)
    lax.fori_loop(units // 2, units, unit, 0)
    gate.hand_on()
    up.hand_on()
    cots.hand_on()
    proj.hand_on_last()
    gate.hand_on_last()
    up.hand_on_last()
    for transfer in (proj, gate, up, cots):
        transfer.finish()
    keep_qkv.wait()


def attend(
    tokens, seg, weights, cot, proj_w, gate_w, up_w, gain, q_part, kv_part, early, shards
):
    count, width = tokens.shape
    length = shards * count
    kv_heads = kv_part // HEAD
    ffn_part = gate_w.shape[1] // shards
    parts = [w.shape[1] // shards for w in weights]
    freqs = np.asarray(rope_base ** (-(np.arange(HEAD // 2) * (2.0 / HEAD))), np.float32)
    shape = jax.ShapeDtypeStruct
    dma = pltpu.SemaphoreType.DMA
    n = shards - 1
    return pl.pallas_call(
        functools.partial(attend_kernel, shards, ffn_part, early, parts),
        in_specs=[ANY] * (6 + len(weights)) + [IN_VMEM] * 2,
        out_specs=[ANY] * 6 + [IN_VMEM] * 10,
        out_shape=[
            shape((length, width), BF16),
            shape((length, width), BF16),
            shape((shards * proj_w.shape[0], width), BF16),
            shape((width, early), BF16),
            shape((width, early), BF16),
            shape((width, sum(parts)), BF16),
            shape((q_part, length), BF16),
            shape((kv_heads, length, HEAD), BF16),
            shape((kv_part, length), BF16),
            shape((kv_heads, length, HEAD), BF16),
            shape((q_part, length), BF16),
            shape((kv_heads, GROUP, length), F32),
            shape((HEAD // 2, length), F32),
            shape((HEAD // 2, length), F32),
            shape((length, 1), jnp.int32),
            shape((1, length), jnp.int32),
        ],
        scratch_shapes=[
            pltpu.VMEM((length, width), BF16),
            pltpu.VMEM((2, TILE, width), BF16),
            pltpu.VMEM((width, sum(parts)), BF16),
            pltpu.VMEM((sum(parts), width), BF16),
            pltpu.VMEM((kv_part, length), BF16),
            pltpu.VMEM(cot.shape, BF16),
            pltpu.VMEM((shards, 1, count), jnp.int32),
            dma((2,)), dma, dma((len(weights) + 2,)), dma((n,)), dma((n,)),
        ]
        + len(weights) * Spread.semaphores(shards)
        + Gather.semaphores(shards)
        + WideSpread.semaphores(shards)
        + 2 * Spread.semaphores(shards)
        + Gather.semaphores(shards),
        compiler_params=pltpu.CompilerParams(
            collective_id=1, has_side_effects=True, vmem_limit_bytes=FULL
        ),
        name="attend",
    )(tokens, seg, cot, proj_w, gate_w, up_w, *weights, gain[None, :], jnp.asarray(freqs[:, None]))


def hidden_kernel(
    shards, mixed_t, proj_m, proj_w, cot_all, down_w, tokens, gain, hidden_ref, rms_ref, normed_all,
    grad_activ, proj_v, mixed_own, normed, cot_v, down_v, out_v, cot_sem, out_sem, proj_sem, mix_send, mix_recv, gather_send, gather_recv, local_sem,
):
    rep, me = place()
    part, _ = mixed_t.shape
    count = tokens.shape[0]
    rows = [
        pltpu.make_async_copy(
            split_rows(proj_m, me ^ i, part) if i else proj_w,
            split_rows(proj_v, me ^ i, part),
            proj_sem.at[i],
        )
        for i in range(shards)
    ]
    for copy in rows:
        copy.start()
    early = [
        pltpu.make_async_copy(cot_all, cot_v, cot_sem.at[0]),
        pltpu.make_async_copy(down_w, down_v, cot_sem.at[1]),
    ]
    for copy in early:
        copy.start()
    greet(plane_partners(rep, me, shards))

    def columns(shard):
        return mixed_t.at[:, pl.ds(pl.multiple_of(shard * count, count), count)]

    copies = [
        remote(columns(me ^ (i + 1)), mixed_own.at[i], mix_send, mix_recv, i, rep, me ^ (i + 1))
        for i in range(shards - 1)
    ]
    for copy in copies:
        copy.start()

    def product(block, i):
        rows[i].wait()
        return dot(block, split_rows(proj_v, me ^ i, part)[...], TN)

    hidden_ref[...] = tokens[...].astype(F32) + product(
        mixed_t[:, pl.ds(pl.multiple_of(me * count, count), count)], 0
    )
    for i, copy in enumerate(copies):
        copy.wait_recv()
        hidden_ref[...] += product(mixed_own[i], i + 1)
    hidden = hidden_ref[...]
    rms = lax.rsqrt(jnp.mean(hidden * hidden, axis=-1, keepdims=True) + epsilon)
    rms_ref[...] = rms
    normed[...] = (hidden * rms * gain[...]).astype(BF16)
    gather = Gather(shards, normed, normed_all, gather_send, gather_recv, local_sem)
    gather.start()
    for copy in copies:
        copy.wait_send()
    for copy in early:
        copy.wait()

    steps = down_w.shape[0] // TILE

    def store(i):
        at = pl.ds(pl.multiple_of(i * TILE, TILE), TILE)
        return pltpu.make_async_copy(out_v.at[i % 2], grad_activ.at[:, at], out_sem.at[i % 2])

    def step(i, carry):
        @pl.when(i >= 2)
        def _():
            store(i - 2).wait()

        units = down_v[pl.ds(pl.multiple_of(i * TILE, TILE), TILE), :]
        out_v[i % 2] = dot(cot_v[...], units, NT).astype(BF16)
        store(i).start()
        return carry

    lax.fori_loop(0, steps // 2, step, 0)
    gather.hand_on()
    lax.fori_loop(steps // 2, steps, step, 0)
    for i in range(max(0, steps - 2), steps):
        store(i).wait()
    gather.finish()


def hidden_layer(mixed_t, proj_m, proj_w, cot_all, down_w, tokens, gain, shards):
    part, length = mixed_t.shape
    count, width = tokens.shape
    n = shards - 1
    return pl.pallas_call(
        functools.partial(hidden_kernel, shards),
        in_specs=[IN_VMEM, ANY, ANY, ANY, ANY, IN_VMEM, IN_VMEM],
        out_specs=[IN_VMEM, IN_VMEM, ANY, ANY],
        out_shape=[
            jax.ShapeDtypeStruct((count, width), F32),
            jax.ShapeDtypeStruct((count, 1), F32),
            jax.ShapeDtypeStruct((length, width), BF16),
            jax.ShapeDtypeStruct((length, down_w.shape[0]), BF16),
        ],
        scratch_shapes=[
            pltpu.VMEM(proj_m.shape, BF16),
            pltpu.VMEM((n, part, count), BF16),
            pltpu.VMEM((count, width), BF16),
            pltpu.VMEM(cot_all.shape, BF16),
            pltpu.VMEM(down_w.shape, BF16),
            pltpu.VMEM((2, length, TILE), BF16),
            pltpu.SemaphoreType.DMA((2,)),
            pltpu.SemaphoreType.DMA((2,)),
            pltpu.SemaphoreType.DMA((shards,)),
            pltpu.SemaphoreType.DMA((n,)),
            pltpu.SemaphoreType.DMA((n,)),
        ]
        + Gather.semaphores(shards),
        compiler_params=pltpu.CompilerParams(
            collective_id=2, has_side_effects=True, vmem_limit_bytes=FULL
        ),
        name="hidden",
    )(mixed_t, proj_m, proj_w, cot_all, down_w, tokens, gain[None, :])


class Plan:
    def __init__(self, shards, reps, length, width, ffn_part, q_part, kv_part):
        self.shards, self.reps, self.length, self.width = shards, reps, length, width
        self.ffn_part, self.q_part, self.kv_part = ffn_part, q_part, kv_part
        self.layers = reps // 2
        self.half = self.layers // 2
        self.rows = width // 2
        self.own = width // shards
        self.block = self.own // 2
        self.proj_half = q_part // 2
        self.proj_blocks = self.rows // self.proj_half
        self.tiles = ffn_part // TILE
        self.out_tiles = width // TILE
        per_slot = 2
        self.back_slot = self.tiles
        self.send_slot = self.back_slot + -(-self.out_tiles // per_slot) - 1
        self.rows_slot = self.send_slot + 4
        self.pass_slot = self.rows_slot + 1
        self.mixed_slot = self.rows_slot + 3
        self.unit_slot = self.mixed_slot + 1
        self.per_slot = per_slot
        self.units = (length // TILE) * (kv_part // HEAD)
        self.norm_slot = self.unit_slot + self.units // 2
        self.down_at = 2 * self.tiles
        self.ffn_end = 3 * self.tiles
        self.q_at = max(self.ffn_end, self.norm_slot)
        self.kv_at = self.q_at + q_part // TILE
        self.proj_at = self.kv_at + 1
        self.chunks = self.proj_at + width // TILE // self.proj_blocks
        self.tokens_slot = max(self.norm_slot + 7, self.chunks + 1)
        self.early_res = length <= 1024
        if self.early_res:
            self.res_slot = self.send_slot + 1
            self.res_send_slot = max(self.mixed_slot + 1, self.res_slot + self.out_tiles // 2)
            self.result_slot = max(self.res_send_slot + 5, self.norm_slot + 4)
            assert self.result_slot < self.norm_slot + 5
        else:
            self.res_slot = max(self.ffn_end + 1, self.norm_slot + 1)
            self.res_send_slot = max(self.res_slot + self.out_tiles // 2 - 1, self.tokens_slot + 1)
            self.result_slot = self.res_send_slot + 6
        self.arrive = self.layers + 2
        self.spread_slot = self.mixed_slot + 1
        self.spread_first = max(0, self.send_slot + 1 - self.arrive)
        assert self.tiles >= 3
        self.hand = 3
        self.gain_slot = self.tokens_slot + 2
        self.rep_slot = max(self.chunks + self.arrive - 1, self.gain_slot + 1)
        self.slots = max(self.chunks + self.arrive + self.hand, self.rep_slot, self.result_slot) + 1
        assert self.spread_slot + self.chunks // 2 < self.slots - self.hand
        self.mine_ring = self.half + 1
        self.sum_ring = 3


def backward_kernel(
    plan, early, x, cot_all, grad_activ, gate_w, up_w, gate_e, up_e, down_w, hidden, tokens, proj_w, qkv_m,
    normed,
    mlp_rms, mlp_gain, attn_gain, seg_col, seg_row, cos_ref, sin_ref, lse_ref, q_ref, mixed_ref,
    k_ref, kt_ref, v_ref,
    f_down, f_gate, f_up, f_proj, f_q, f_kv, result_ref, tokens_out, gains_out,
    swapped, from_outer, from_middle, totals, back_land, res_land, norm_land, norm_part,
    gate_m, up_m, activ, dgate, dup, back_part, res_part,
    left_a, left_b, right, gate_v, up_v, grad_v, back_v, tile_v, both, proj_v, qkv_v, hidden_v,
    row_sum, land_v,
    mine, theirs, swap_v, outer_v, middle_v, sums, total_v,
    grad_hidden, gh_own, g_t, back_t, dk_acc, dv_acc, activ_v,
    gain_part, gain_land, gain_sum, gain_reps,
    load_sem, right_sem, small_sem, swap_send, swap_recv, in_send, outer_recv, middle_recv,
    out_send, total_recv, total_store, cross_recv, cross_send, pass_send, pass_recv,
    back_send, back_recv, res_send, res_recv, norm_send, norm_recv,
    gather_send, gather_recv, gather_local, gain_send, gain_recv, rep_send, rep_recv,
    tile_send, tile_recv, tile_pass, tile_passed, down_sem, back_sem, tile_sem,
):
    p = plan
    shards, reps, n = p.shards, p.reps, p.shards - 1
    rep, me = place()
    core, layer = rep % 2, rep // 2
    upper = layer >= p.half
    depth = jnp.where(upper, p.layers - 1 - layer, layer)
    inward = jnp.where(upper, rep - 2, rep + 2)
    outward = jnp.where(upper, rep + 2, rep - 2)
    is_middle = depth == p.half - 1
    count = tokens.shape[0]
    ffn_end, proj_at, q_at, kv_at, end_at = p.ffn_end, p.proj_at, p.q_at, p.kv_at, p.chunks
    gh_all = both.at[:, pl.ds(0, p.width)]

    def columns(index, size=TILE):
        return pl.ds(pl.multiple_of(index * size, size), size)

    def load(src, dst, i):
        return pltpu.make_async_copy(src, dst, load_sem.at[i])

    load_cot = load(cot_all, left_a, 0)
    load_x = load(x, left_b, 1)
    load_normed = load(normed, left_a, 2)
    load_proj = load(proj_w, proj_v, 3)
    load_qkv = load(qkv_m, qkv_v, 4)
    load_hidden = load(hidden, hidden_v, 5)
    load_activ = load(activ, left_b.at[:, pl.ds(0, p.ffn_part)], 6)
    load_tokens = load(tokens, gh_own, 7)
    first_tile = early // TILE
    assert first_tile >= 2 or p.tiles < 3

    def tile_bytes(tile, sem):
        piece = gate_m.at[pl.ds(0, 2 * n * p.block), pl.ds(0, TILE)]
        return pltpu.make_async_copy(piece, piece, sem.at[tile])

    def send_tile(tile):
        rows = columns(core, p.block)
        into = pl.ds(pl.multiple_of(me * p.own + core * p.block, p.block), p.block)
        for weight, full in ((gate_w, gate_m), (up_w, up_m)):
            for i in range(n):
                peer = me ^ (i + 1)
                at = pl.ds(pl.multiple_of(peer * p.ffn_part + tile * TILE, TILE), TILE)
                pltpu.make_async_remote_copy(
                    src_ref=weight.at[rows, at], dst_ref=full.at[into, columns(tile)],
                    send_sem=tile_send.at[tile], recv_sem=tile_recv.at[tile],
                    device_id=(rep, peer), device_id_type=MESH,
                ).start()

    def pass_tile(tile):
        tile_bytes(tile, tile_recv).wait()
        for full in (gate_m, up_m):
            for i in range(n):
                peer = me ^ (i + 1)
                at = pl.ds(pl.multiple_of(peer * p.own + core * p.block, p.block), p.block)
                piece = full.at[at, columns(tile)]
                pltpu.make_async_remote_copy(
                    src_ref=piece, dst_ref=piece,
                    send_sem=tile_pass.at[tile], recv_sem=tile_passed.at[tile],
                    device_id=(rep ^ 1, me), device_id_type=MESH,
                ).start()

    def load_grad(tile):
        return pltpu.make_async_copy(grad_activ.at[:, columns(tile)], grad_v, down_sem.at[0])

    def load_tile(tile):
        @pl.when(tile >= first_tile)
        def _():
            tile_bytes(tile, tile_passed).wait()

        own_at = pl.ds(pl.multiple_of(me * p.ffn_part + tile * TILE, TILE), TILE)
        held_rows = [pl.ds(pl.multiple_of((me ^ i) * p.own, p.own), p.own) for i in range(shards)]
        for i, (weight, tiles, full, held) in enumerate(
            ((gate_w, gate_e, gate_m, gate_v), (up_w, up_e, up_m, up_v))
        ):
            sem = down_sem.at[i + 1]
            pltpu.make_async_copy(weight.at[:, own_at], held.at[held_rows[0], :], sem).start()
            for rows in held_rows[1:]:

                @pl.when(tile < first_tile)
                def _(rows=rows, tiles=tiles, held=held, sem=sem):
                    src = tiles.at[rows, columns(tile)]
                    pltpu.make_async_copy(src, held.at[rows, :], sem).start()

                @pl.when(tile >= first_tile)
                def _(rows=rows, full=full, held=held, sem=sem):
                    src = full.at[rows, columns(tile)]
                    pltpu.make_async_copy(src, held.at[rows, :], sem).start()

        load_grad(tile).start()

    def units_of(tile):
        return activ_v.at[:, columns(tile)] if p.early_res else tile_v.at[tile % 2]

    def store_tile(tile):
        dup_columns = pl.ds(pl.multiple_of(p.ffn_part + tile * TILE, TILE), TILE)
        return [
            pltpu.make_async_copy(src, dst.at[:, columns(tile)], tile_sem.at[i])
            for i, (src, dst) in enumerate(
                (
                    (units_of(tile), activ),
                    (both.at[:, columns(tile)], dgate),
                    (both.at[:, dup_columns], dup),
                )
            )
        ]

    def stored(tile):
        for copy in store_tile(tile):
            copy.wait()

    def ffn_tile(tile):
        for i, held in enumerate((gate_v, up_v)):
            pltpu.make_async_copy(held, held, down_sem.at[i + 1]).wait()
        load_grad(tile).wait()
        dup_columns = pl.ds(pl.multiple_of(p.ffn_part + tile * TILE, TILE), TILE)

        def go(i, carry):
            here = columns(i, ROWS)
            rows = left_b[here, :]
            gate = dot(rows, gate_v[...], NN)
            up = dot(rows, up_v[...], NN)
            grad = grad_v[here, :].astype(F32)
            sigm = jax.nn.sigmoid(gate)
            swish = gate * sigm
            units_of(tile)[here, :] = (swish * up).astype(BF16)
            both[here, columns(tile)] = (
                grad * up * sigm * (1.0 + gate * (1.0 - sigm))
            ).astype(BF16)
            both[here, dup_columns] = (grad * swish).astype(BF16)
            return carry

        lax.fori_loop(0, p.length // ROWS, go, 0)

        @pl.when(tile >= 3)
        def _():
            stored(tile - 1)

        for copy in store_tile(tile):
            copy.start()

        @pl.when(tile <= 1)
        def _():
            stored(tile)

        @pl.when(tile + 1 < p.tiles)
        def _():
            load_tile(tile + 1)

        @pl.when(tile + 1 == p.tiles)
        def _():
            load_back(0)

    def load_back(tile):
        slot = tile % 2
        per_shard = p.own // TILE
        for i, (weight, tiles, full) in enumerate(
            ((gate_w, gate_e, gate_m), (up_w, up_e, up_m))
        ):
            sem, at = back_sem.at[slot, i], i * p.ffn_part

            @pl.when(tile // per_shard == me)
            def _(weight=weight, sem=sem, at=at):
                src = weight.at[columns(tile - me * per_shard), columns(me, p.ffn_part)]
                pltpu.make_async_copy(src, back_v.at[slot, :, pl.ds(at, p.ffn_part)], sem).start()

            @pl.when(tile // per_shard != me)
            def _(tiles=tiles, full=full, sem=sem, at=at):
                into = back_v.at[slot, :, pl.ds(at, early)]
                pltpu.make_async_copy(tiles.at[columns(tile), :], into, sem).start()
                rest = p.ffn_part - early
                into = back_v.at[slot, :, pl.ds(at + early, rest)]
                src = full.at[columns(tile), pl.ds(early, rest)]
                pltpu.make_async_copy(src, into, sem).start()

    def wait_back(tile):
        slot = tile % 2
        for i in range(2):
            half = back_v.at[slot, :, pl.ds(i * p.ffn_part, p.ffn_part)]
            pltpu.make_async_copy(half, half, back_sem.at[slot, i]).wait()

    def back_tiles(first):
        def store(tile):
            return pltpu.make_async_copy(
                tile_v.at[tile % 2], back_part.at[:, columns(tile)], tile_sem.at[tile % 2]
            )

        @pl.when(first == 0)
        def _():
            stored(p.tiles - 1)

        def tile_go(k, carry):
            tile = first + k
            wait_back(tile)

            @pl.when(tile + 1 < p.out_tiles)
            def _():
                load_back(tile + 1)

            @pl.when(k >= 2)
            def _():
                store(tile - 2).wait()

            def go(i, c):
                here = columns(i, ROWS)
                tile_v[tile % 2, here, :] = dot(both[here, :], back_v[tile % 2], NT).astype(BF16)
                return c

            lax.fori_loop(0, p.length // ROWS, go, 0)
            store(tile).start()
            return carry

        size = jnp.minimum(p.per_slot, p.out_tiles - first)
        lax.fori_loop(0, size, tile_go, 0)
        store(first + size - 2).wait()
        store(first + size - 1).wait()

    def load_res(tile):
        def copies(action):
            for i, held in enumerate((gate_v, up_v)):

                @pl.when(tile % 2 == i)
                def _(i=i, held=held):
                    action(
                        pltpu.make_async_copy(
                            down_w.at[:, columns(tile)], held.at[pl.ds(0, p.ffn_part), :], back_sem.at[i, 0]
                        )
                    )

        return copies

    def res_tiles(first):
        hidden_units = activ_v if p.early_res else left_b

        def store(tile):
            return pltpu.make_async_copy(
                tile_v.at[tile % 2], res_part.at[:, columns(tile)], tile_sem.at[tile % 2]
            )

        for k, held in enumerate((gate_v, up_v)):
            tile = first + k
            load_res(tile)(lambda copy: copy.wait())

            @pl.when(tile + 1 < p.out_tiles)
            def _(tile=tile):
                load_res(tile + 1)(lambda copy: copy.start())

            def go(i, c, k=k, held=held):
                here = columns(i, ROWS)
                tile_v[k, here, :] = dot(
                    hidden_units[here, : p.ffn_part], held[: p.ffn_part, :], NN
                ).astype(BF16)
                return c

            lax.fori_loop(0, p.length // ROWS, go, 0)
            store(tile).start()
        store(first).wait()
        store(first + 1).wait()

    def is_chunk(j, kind):
        if kind == 0:
            return (j >= p.down_at) & (j < ffn_end)
        return (j >= 0) & (j < p.down_at) & (j % 2 == kind - 1)

    def tile_of(j):
        return jnp.where(j < p.down_at, j // 2, j - p.down_at)

    def load_right(t):
        slot = right.at[t % 2]

        def copies(action):
            for i, ref in enumerate((activ, dgate, dup)):

                @pl.when(is_chunk(t, i))
                def _(ref=ref):
                    action(
                        pltpu.make_async_copy(
                            ref.at[:, columns(tile_of(t))], slot, right_sem.at[t % 2]
                        )
                    )

        return copies

    side = p.width // 2
    left_half, right_half = pl.ds(0, side), pl.ds(side, side)

    def rows_of(shard):
        return pl.ds(pl.multiple_of(shard * count, count), count)

    class Scatter:
        def __init__(self, part, land, sends, recvs):
            self.part, self.land = part, land
            self.second = []
            if shards != 4:
                self.first = [
                    remote(split_rows(part, me ^ (i + 1), count), land.at[i], sends, recvs, i, rep, me ^ (i + 1))
                    for i in range(n)
                ]
                return
            order = (
                (3, left_half, 0, right_half, 1),
                (3, right_half, 1, right_half, 2),
                (1, left_half, 0, left_half, 1),
                (2, right_half, 1, left_half, 2),
            )
            self.first = [
                remote(
                    part.at[rows_of(me ^ block), cols], land.at[into, :, into_cols],
                    sends, recvs, i, rep, me ^ to,
                )
                for i, (block, cols, into, into_cols, to) in enumerate(order)
            ]
            self.second = [
                remote(gh_own.at[:, cols], land.at[2, :, cols], sends, recvs, 4 + i, rep, me ^ to)
                for i, (cols, to) in enumerate(((left_half, 2), (right_half, 1)))
            ]

        def start(self):
            for copy in self.first:
                copy.start()

        def hand_on(self):
            if not self.second:
                return
            for copy in self.first[:2]:
                copy.wait_recv()
            loads = [
                (self.part.at[rows_of(me ^ 2), left_half], 0, left_half),
                (self.part.at[rows_of(me ^ 1), right_half], 0, right_half),
                (self.land.at[0, :, right_half], 1, left_half),
                (self.land.at[1, :, right_half], 1, right_half),
            ]
            for src, slot, cols in loads:
                pltpu.make_async_copy(src, land_v.at[slot, :, cols], small_sem.at[slot]).start()
            for slot in range(2):
                pltpu.make_async_copy(land_v.at[slot], land_v.at[slot], small_sem.at[slot]).wait()

            def strip(here):
                gh_own[here, :] = (
                    land_v[0, here, :].astype(F32) + land_v[1, here, :].astype(F32)
                ).astype(BF16)

            strips(strip)
            for copy in self.second:
                copy.start()

        def fetch(self):
            for copy in self.first[2 if self.second else 0 :] + self.second:
                copy.wait_recv()
            for copy in self.second:
                copy.wait_send()
            pieces = [[(split_rows(self.part, me, count), pl.ds(0, p.width))]]
            if self.second:
                pieces.append(
                    [
                        (self.land.at[0, :, left_half], left_half),
                        (self.land.at[1, :, left_half], right_half),
                    ]
                )
                pieces.append([(self.land.at[2], pl.ds(0, p.width))])
            else:
                pieces += [[(self.land.at[i], pl.ds(0, p.width))] for i in range(n)]

            def load(i):
                for src, cols in pieces[i]:
                    pltpu.make_async_copy(
                        src, land_v.at[i % 2, :, cols], small_sem.at[i % 2]
                    ).start()

            load(0)
            for i in range(len(pieces)):
                if i + 1 < len(pieces):
                    load(i + 1)
                held = land_v.at[i % 2]
                pltpu.make_async_copy(held, held, small_sem.at[i % 2]).wait()

                def strip(here, i=i):
                    value = land_v[i % 2, here, :].astype(F32)
                    row_sum[here, :] = value if i == 0 else row_sum[here, :] + value

                strips(strip)

        def settle(self):
            for copy in self.first:
                copy.wait_send()

    back_rows = Scatter(back_part, back_land, back_send, back_recv)
    res_rows = Scatter(res_part, res_land, res_send, res_recv)
    norm_rows = Scatter(norm_part, norm_land, norm_send, norm_recv)

    STRIP = 32

    def strips(body):
        def go(i, carry):
            body(pl.ds(pl.multiple_of(i * STRIP, STRIP), STRIP))
            return carry

        lax.fori_loop(0, count // STRIP, go, 0)

    def norm_strip(here, values, rms, gain, row):
        grad_in = row_sum[here, :]
        weighted = grad_in * gain
        inner = jnp.mean(weighted * values, axis=-1, keepdims=True)
        gain_part[row : row + 1, :] += jnp.sum(grad_in * values * rms, axis=0, keepdims=True)
        return rms * weighted - values * (rms * rms * rms) * inner

    gather = Gather(shards, gh_own, gh_all, gather_send, gather_recv, gather_local)

    def hidden_back():
        load_hidden.wait()
        back_rows.fetch()
        gain_part[...] = jnp.zeros_like(gain_part)

        def strip(here):
            own = pl.ds(pl.multiple_of(me * count, count) + here.start, STRIP)
            grad = left_a[own, :].astype(F32) + norm_strip(
                here, hidden_v[here, :], mlp_rms[here, :], mlp_gain[...], 1
            )
            grad_hidden[here, :] = grad
            gh_own[here, :] = grad.astype(BF16)

        strips(strip)
        gather.start()

    def finish_result():
        res_rows.fetch()

        def strip(here):
            row_sum[here, :] = hidden_v[here, :] + row_sum[here, :]

        strips(strip)
        store_result = pltpu.make_async_copy(row_sum, result_ref, small_sem.at[0])
        store_result.start()
        store_result.wait()

    def mixed_back():
        gather.finish()
        load_proj.wait()

        def go(i, carry):
            here = pl.ds(pl.multiple_of(i * TILE, TILE), TILE)
            g_t[:, here] = dot(proj_v[...], both[here, : p.width], NT).astype(BF16)
            return carry

        lax.fori_loop(0, p.length // TILE, go, 0)

    blocks = p.length // TILE
    rows = GROUP * HEAD
    wide = GROUP * TILE
    mid = HEAD // 2

    def attention_unit(unit):
        g, turn = unit // blocks, unit % blocks
        block = jnp.where(turn % 2 == 0, turn // 2, blocks - 1 - turn // 2)
        query_at = pl.multiple_of(block * TILE, TILE)
        here_q = pl.ds(query_at, TILE)

        queries = side_by_side(q_ref, g, here_q)
        grads = side_by_side(g_t, g, here_q)
        mixed = side_by_side(mixed_ref, g, here_q)
        lse = jnp.concatenate([lse_ref[g, h : h + 1, here_q] for h in range(GROUP)], axis=1)
        inner = jnp.sum(grads.astype(F32) * mixed.astype(F32), axis=0, keepdims=True)

        @pl.when(turn == 0)
        def _():
            dk_acc[...] = jnp.zeros_like(dk_acc)
            dv_acc[...] = jnp.zeros_like(dv_acc)

        def step(c, acc):
            key_at = pl.multiple_of(c * TILE, TILE)
            here = pl.ds(key_at, TILE)
            scores = dot(k_ref[g, here, :], queries, NN)
            scores = scores + block_bias(seg_col, seg_row, key_at, query_at)
            probs = jnp.exp(scores - lse)
            grad_probs = dot(v_ref[g, here, :], grads, NN)
            grad_scores = (probs * (grad_probs - inner)).astype(BF16)
            dv_acc[:, here] += dot(grads, probs.astype(BF16), NT)
            dk_acc[:, here] += dot(queries, grad_scores, NT)
            key_rows = pl.ds(pl.multiple_of(g * HEAD, HEAD), HEAD)
            return acc + dot(kt_ref[key_rows, here], grad_scores, NN)

        acc = lax.fori_loop(0, block + 1, step, jnp.zeros((HEAD, wide), F32))
        cos, sin = cos_ref[:, here_q], sin_ref[:, here_q]
        for h in range(GROUP):
            grad = acc[:, h * TILE : (h + 1) * TILE] * SCALE
            first, second = grad[:mid], grad[mid:]
            at = pl.multiple_of(g * rows + h * HEAD, HEAD)
            back_t[pl.ds(at, mid), here_q] = (first * cos + second * sin).astype(BF16)
            back_t[pl.ds(at + mid, mid), here_q] = (second * cos - first * sin).astype(BF16)

        @pl.when(turn == blocks - 1)
        def _():
            cos, sin = cos_ref[...], sin_ref[...]
            first, second = dk_acc[:mid, :], dk_acc[mid:, :]
            at = pl.multiple_of(p.q_part + g * HEAD, HEAD)
            back_t[pl.ds(at, mid), :] = (first * cos + second * sin).astype(BF16)
            back_t[pl.ds(at + mid, mid), :] = (second * cos - first * sin).astype(BF16)
            at = pl.multiple_of(p.q_part + p.kv_part + g * HEAD, HEAD)
            back_t[pl.ds(at, HEAD), :] = dv_acc[...].astype(BF16)

    def normed_back():
        load_qkv.wait()

        stores = [
            pltpu.make_async_copy(
                land_v.at[i % 2], norm_part.at[pl.ds(i * count, count), :], small_sem.at[i % 2]
            )
            for i in range(shards)
        ]
        for i, store in enumerate(stores):
            if i >= 2:
                stores[i - 2].wait()
            here = pl.ds(i * count, count)
            land_v[i % 2] = dot(back_t[:, here].T, qkv_v[...], NT).astype(BF16)
            store.start()
        for store in stores[-2:]:
            store.wait()
        norm_rows.start()

    gain_cols = p.width // shards

    def gain_slice(shard):
        return pl.ds(pl.multiple_of(shard * gain_cols, gain_cols), gain_cols)

    gain_plane = [
        remote(
            gain_part.at[:, gain_slice(me ^ (i + 1))], gain_land.at[me],
            gain_send, gain_recv, i, rep, me ^ (i + 1),
        )
        for i in range(n)
    ]
    gain_all = [
        remote(gain_sum, gain_reps.at[rep], rep_send, rep_recv, i, rep ^ (i + 1), me)
        for i in range(reps - 1)
    ]

    def tokens_back():
        norm_rows.fetch()
        load_tokens.start()
        load_tokens.wait()

        def strip(here):
            values = gh_own[here, :].astype(F32)
            rms = lax.rsqrt(jnp.mean(values * values, axis=-1, keepdims=True) + epsilon)
            grad_hidden[here, :] += norm_strip(here, values, rms, attn_gain[...], 0)

        strips(strip)
        store_tokens = pltpu.make_async_copy(grad_hidden, tokens_out, small_sem.at[0])
        store_tokens.start()
        store_tokens.wait()
        gain_land[me] = gain_part[:, gain_slice(me)]
        for copy in gain_plane:
            copy.start()

    def gains_plane():
        for copy in gain_plane:
            copy.wait_recv()
        total = gain_land[0]
        for s in range(1, shards):
            total = total + gain_land[s]
        gain_sum[...] = total
        gain_reps[rep] = total
        for copy in gain_all:
            copy.start()

    def gains_reps():
        for copy in gain_all:
            copy.wait_recv()
        total = gain_reps[0]
        for r in range(1, reps):
            total = total + gain_reps[r]
        gains_out[...] = total

    def swap_copy(j):
        return pltpu.make_async_remote_copy(
            src_ref=theirs.at[j % 2], dst_ref=swapped.at[j],
            send_sem=swap_send.at[j % 2], recv_sem=swap_recv.at[j],
            device_id=(rep ^ 1, me), device_id_type=MESH,
        )

    def store_chunk(slot, other_slot, at, size, product, columns=TILE):
        here = pl.ds(pl.multiple_of(at, size), size)
        mine[slot, here, :columns] = product(core).astype(BF16)
        theirs[other_slot, here, :columns] = product(1 - core).astype(BF16)

    def make(t):
        slot, other = t % p.mine_ring, t % 2

        @pl.when(t >= 2)
        def _():
            swap_copy(t - 2).wait_send()

        @pl.when(t == 0)
        def _():
            load_right(0)(lambda copy: copy.start())

        load_right(t)(lambda copy: copy.wait())

        @pl.when(t + 1 < ffn_end)
        def _():
            load_right(t + 1)(lambda copy: copy.start())

        @pl.when(is_chunk(t, 0))
        def _():
            left = right[t % 2].T

            def product(which):
                return dot(left, left_a[:, columns(which, p.rows)], NN).astype(BF16)

            ours, others = product(core), product(1 - core)
            for at in range(0, p.rows, TILE):
                mine[slot, at : at + TILE, :] = ours[:, at : at + TILE]
                theirs[other, at : at + TILE, :] = others[:, at : at + TILE]

        def wide_chunk(left, factor, columns):
            def go(s, carry):
                def product(which):
                    at = pl.multiple_of(s * p.own + which * p.block, p.block)
                    return dot(factor, left[:, pl.ds(at, p.block)], NN).T

                store_chunk(slot, other, s * p.block, p.block, product, columns)
                return carry

            lax.fori_loop(0, shards, go, 0)

        @pl.when(t < p.down_at)
        def _():
            wide_chunk(left_b, right[t % 2].T, TILE)

        @pl.when((t >= proj_at) & (t < end_at))
        def _():
            def go(i, carry):
                at = columns((t - proj_at) * p.proj_blocks + i)

                def product(which):
                    part = columns(which, p.proj_half)
                    return dot(mixed_ref[part, :], both[:, at], NN)

                store_chunk(slot, other, i * p.proj_half, p.proj_half, product)
                return carry

            lax.fori_loop(0, p.proj_blocks, go, 0)

        @pl.when((t >= q_at) & (t < kv_at))
        def _():
            wide_chunk(left_a, back_t[columns(t - q_at), :], TILE)

        @pl.when(t == kv_at)
        def _():
            wide_chunk(left_a, back_t[p.q_part :, :], 2 * p.kv_part)

        swap_copy(t).start()

    def inward_copies(j):
        common = dict(
            src_ref=sums.at[j % p.sum_ring], send_sem=in_send.at[j % p.sum_ring],
            device_id=(inward, me), device_id_type=MESH,
        )
        to_layer = pltpu.make_async_remote_copy(
            dst_ref=from_outer.at[j], recv_sem=outer_recv.at[j], **common
        )
        to_middle = pltpu.make_async_remote_copy(
            dst_ref=from_middle.at[j], recv_sem=middle_recv.at[j], **common
        )
        return to_layer, to_middle

    def total_places(j, action):
        @pl.when(is_chunk(j, 0))
        def _():
            action(
                [
                    (
                        i * TILE, TILE, TILE,
                        f_down.at[
                            columns(tile_of(j)),
                            pl.ds(pl.multiple_of(core * p.rows + i * TILE, TILE), TILE),
                        ],
                    )
                    for i in range(p.rows // TILE)
                ]
            )

        @pl.when((j >= proj_at) & (j < end_at))
        def _():
            action(
                [
                    (
                        i * p.proj_half, p.proj_half, TILE,
                        f_proj.at[
                            columns(core, p.proj_half),
                            columns((j - proj_at) * p.proj_blocks + i),
                        ],
                    )
                    for i in range(p.proj_blocks)
                ]
            )

        for when, full, part, tile, sem, wide_by in wide_kinds(j):

            @pl.when(when)
            def _(full=full, part=part, tile=tile, wide_by=wide_by):
                blocks = []
                for i in range(shards):
                    at = pl.multiple_of((me ^ i) * p.block, p.block)
                    place_there = totals.at[j, pl.ds(at, p.block), pl.ds(0, wide_by)]
                    if i == 0:
                        place_there = window(full, me, part, tile, wide_by)
                    blocks.append((at, p.block, wide_by, place_there))
                action(blocks)

    def chunk_bytes(j, sem):
        @pl.when(j == kv_at)
        def _():
            whole = totals.at[0, :, pl.ds(0, 2 * p.kv_part)]
            pltpu.make_async_copy(whole, whole, sem).wait()

        @pl.when(j != kv_at)
        def _():
            whole = totals.at[0]
            pltpu.make_async_copy(whole, whole, sem).wait()

    def send_total(src, dst, j):
        return pltpu.make_async_remote_copy(
            src_ref=src, dst_ref=dst, send_sem=out_send.at[j % 2],
            recv_sem=total_recv.at[j], device_id=(outward, me), device_id_type=MESH,
        )

    def add_rows(body):
        def go(i, carry):
            body(pl.ds(pl.multiple_of(i * TILE, TILE), TILE))
            return carry

        lax.fori_loop(0, p.rows // TILE, go, 0)

    def load_swapped(j):
        return pltpu.make_async_copy(swapped.at[j], swap_v, small_sem.at[2])

    def load_outer(j):
        return pltpu.make_async_copy(from_outer.at[j], outer_v, small_sem.at[3])

    def load_middle(j):
        return pltpu.make_async_copy(from_middle.at[j], middle_v, small_sem.at[4])

    def valid(j):
        return (j >= 0) & (j < p.chunks)

    def take_inward(j):
        @pl.when(valid(j))
        def _():
            swap_copy(j).wait_recv()
            load_swapped(j).start()

            @pl.when(depth > 0)
            def _():
                inward_copies(j)[0].wait_recv()
                load_outer(j).start()

    def send_inward(j):
        @pl.when(valid(j))
        def _():
            @pl.when(j >= p.sum_ring)
            def _():
                inward_copies(j - p.sum_ring)[0].wait_send()

            load_swapped(j).wait()
            ours = mine.at[j % p.mine_ring]
            total = sums.at[j % p.sum_ring]

            @pl.when(depth > 0)
            def _():
                load_outer(j).wait()

                def add(here):
                    total[here, :] = (
                        ours[here, :].astype(F32)
                        + swap_v[here, :].astype(F32)
                        + outer_v[here, :].astype(F32)
                    ).astype(BF16)

                add_rows(add)

            @pl.when(depth == 0)
            def _():
                def add(here):
                    total[here, :] = (
                        ours[here, :].astype(F32) + swap_v[here, :].astype(F32)
                    ).astype(BF16)

                add_rows(add)

            to_layer, to_middle = inward_copies(j)

            @pl.when(is_middle)
            def _():
                to_middle.start()

            @pl.when(jnp.logical_not(is_middle))
            def _():
                to_layer.start()

    def take_middle(j):
        @pl.when(is_middle & valid(j))
        def _():
            inward_copies(j)[1].wait_recv()
            load_middle(j).start()

    def meet_in_middle(j):
        @pl.when(is_middle & valid(j))
        def _():
            @pl.when(j >= 1)
            def _():
                chunk_bytes(j - 1, total_store.at[0])

            if p.half > 1:

                @pl.when(j >= 2)
                def _():
                    chunk_bytes(j - 2, out_send.at[j % 2])

            load_middle(j).wait()
            out, held = total_v.at[j % 2], sums.at[j % p.sum_ring]

            def add(here):
                out[here, :] = (
                    held[here, :].astype(F32) + middle_v[here, :].astype(F32)
                ).astype(BF16)

            add_rows(add)

            def put(blocks):
                for at, size, wide_by, dst in blocks:
                    src = out.at[pl.ds(at, size), pl.ds(0, wide_by)]
                    if p.half > 1:
                        send_total(src, dst, j).start()
                    pltpu.make_async_copy(src, dst, total_store.at[0]).start()

            total_places(j, put)

    def last_store(t):
        @pl.when(is_middle & (t == p.chunks + p.arrive - 1))
        def _():
            chunk_bytes(p.chunks - 1, total_store.at[0])

    def send_outward(j):
        @pl.when(jnp.logical_not(is_middle) & valid(j))
        def _():
            chunk_bytes(j, total_recv.at[j])

            if p.half > 2:

                @pl.when(depth > 0)
                def _():
                    @pl.when(j >= 2)
                    def _():
                        chunk_bytes(j - 2, out_send.at[j % 2])

                    def put(blocks):
                        for _, _, _, dst in blocks:
                            send_total(dst, dst, j).start()

                    total_places(j, put)

    def remote_pass(src, dst, sem):
        return pltpu.make_async_remote_copy(
            src_ref=src, dst_ref=dst, send_sem=pass_send.at[sem], recv_sem=pass_recv.at[sem],
            device_id=(rep ^ 1, me), device_id_type=MESH,
        )

    def window(full, shard, part, tile, columns=TILE):
        at = pl.multiple_of(shard * part + tile * columns, columns)
        return full.at[pl.ds(pl.multiple_of(core * p.block, p.block), p.block), pl.ds(at, columns)]

    def wide_kinds(j):
        return (
            (is_chunk(j, 1), f_gate, p.ffn_part, tile_of(j), 1, TILE),
            (is_chunk(j, 2), f_up, p.ffn_part, tile_of(j), 2, TILE),
            ((j >= q_at) & (j < kv_at), f_q, p.q_part, j - q_at, 4, TILE),
            (j == kv_at, f_kv, 2 * p.kv_part, 0, 5, 2 * p.kv_part),
        )

    def spread_total(j):
        for kind, sem in ((is_chunk(j, 0), 0), ((j >= proj_at) & (j < end_at), 3)):

            @pl.when(kind)
            def _(sem=sem):
                def put(blocks):
                    for _, _, _, dst in blocks:
                        remote_pass(dst, dst, sem).start()

                total_places(j, put)

        for when, full, part, tile, sem, wide_by in wide_kinds(j):

            @pl.when(when)
            def _(full=full, part=part, tile=tile, sem=sem, wide_by=wide_by):
                place_here = window(full, me, part, tile, wide_by)
                for i in range(n):
                    at = columns(me ^ (i + 1), p.block)
                    pltpu.make_async_remote_copy(
                        src_ref=totals.at[j, at, pl.ds(0, wide_by)], dst_ref=place_here,
                        send_sem=cross_send.at[sem], recv_sem=cross_recv.at[j],
                        device_id=(rep, me ^ (i + 1)), device_id_type=MESH,
                    ).start()
                remote_pass(place_here, place_here, sem).start()

    def pass_on(j):
        for when, full, part, tile, sem, wide_by in wide_kinds(j):

            @pl.when(when)
            def _(full=full, part=part, tile=tile, sem=sem, wide_by=wide_by):
                came = totals.at[j, pl.ds(0, n * p.block), pl.ds(0, wide_by)]
                pltpu.make_async_copy(came, came, cross_recv.at[j]).wait()
                for i in range(n):
                    here = window(full, me ^ (i + 1), part, tile, wide_by)
                    remote_pass(here, here, sem).start()

    for copy in (load_x, load_cot):
        copy.start()
    load_tile(0)
    greet(plane_partners(rep, me, shards) + [(rep ^ i, me) for i in range(1, reps)])
    ahead = 3
    for tile in range(first_tile, min(first_tile + ahead, p.tiles)):
        send_tile(tile)
    for copy in (load_hidden, load_proj, load_qkv):
        copy.start()
    load_x.wait()

    def slot(t, carry):
        inner = t - 1 - depth
        met = t - 1 - p.half
        take_inward(inner)
        send_inward(inner)
        send_outward(t - p.arrive + depth)

        def spread_until(u):
            ready = jnp.minimum(u - p.arrive + 1, p.chunks)
            later = p.spread_first + 2 * jnp.maximum(u - p.spread_slot + 1, 0)
            most = jnp.where(u <= p.send_slot, p.chunks, later)
            return jnp.maximum(jnp.minimum(ready, most), 0)

        def over(action, u):
            def go(j, c):
                action(j)
                return c

            lax.fori_loop(spread_until(u - 1), spread_until(u), go, 0)

        last_store(t)
        over(spread_total, t)
        over(pass_on, t - p.hand)

        @pl.when(t + first_tile + ahead < p.tiles)
        def _():
            send_tile(t + first_tile + ahead)

        @pl.when((t > 0) & (t + 1 >= first_tile) & (t + 1 < p.tiles))
        def _():
            pass_tile(t + 1)

        @pl.when(t < p.tiles)
        def _():
            ffn_tile(t)

        @pl.when((t >= p.back_slot) & (t <= p.send_slot))
        def _():
            back_tiles((t - p.back_slot) * p.per_slot)

        @pl.when(t == ffn_end)
        def _():
            load_normed.start()
            if not p.early_res:
                load_activ.start()

        @pl.when(t == q_at)
        def _():
            load_normed.wait()

        def at(when, action):
            @pl.when(t == when)
            def _():
                action()

        at(p.tokens_slot, tokens_back)
        take_middle(met)
        meet_in_middle(met)
        at(p.send_slot, back_rows.start)
        at(p.send_slot + 2, back_rows.hand_on)
        at(p.send_slot, load_cot.wait)
        at(p.rows_slot, hidden_back)
        at(p.pass_slot, gather.hand_on)
        at(p.mixed_slot, mixed_back)

        @pl.when((t >= p.unit_slot) & (t < p.norm_slot))
        def _():
            def go(i, c):
                attention_unit((t - p.unit_slot) * 2 + i)
                return c

            lax.fori_loop(0, 2, go, 0)

        at(p.norm_slot, normed_back)
        at(p.norm_slot + 5, norm_rows.hand_on)

        @pl.when(t < p.chunks)
        def _():
            make(t)

        at(p.gain_slot, gains_plane)
        at(p.rep_slot, gains_reps)

        @pl.when((t >= p.res_slot) & (t < p.res_slot + p.out_tiles // 2))
        def _():
            @pl.when(t == p.res_slot)
            def _():
                if not p.early_res:
                    load_activ.wait()
                load_res(0)(lambda copy: copy.start())

            res_tiles((t - p.res_slot) * 2)

        at(p.res_send_slot, res_rows.start)
        at(p.res_send_slot + 3, res_rows.hand_on)
        at(p.result_slot, finish_result)
        return carry

    lax.fori_loop(0, p.slots, slot, 0)

    for j in range(max(0, p.chunks - 2), p.chunks):
        swap_copy(j).wait_send()
    for j in range(max(0, p.chunks - p.sum_ring), p.chunks):
        inward_copies(j)[0].wait_send()
    if p.half > 1:

        @pl.when(depth > 0)
        def _():
            for j in range(max(0, p.chunks - 2), p.chunks):
                chunk_bytes(j, out_send.at[j % 2])

    for rows in (back_rows, res_rows, norm_rows):
        rows.settle()
    for copies in (gain_plane, gain_all):
        for copy in copies:
            copy.wait_send()

    def settle(ref, sem):
        pltpu.make_async_copy(ref, ref, sem).wait()

    for tile in range(first_tile, p.tiles):
        tile_bytes(tile, tile_send).wait()
        tile_bytes(tile, tile_pass).wait()
    for sem, part in (
        (0, f_down.at[:, pl.ds(0, p.rows)]),
        (3, f_proj.at[pl.ds(0, p.proj_half), :]),
    ):
        settle(part, pass_send.at[sem])
        settle(part, pass_recv.at[sem])
    for _, full, part, _, sem, _ in wide_kinds(0):
        here = full.at[pl.ds(0, p.block), :]
        settle(here, pass_send.at[sem])
        settle(here, pass_recv.at[sem])
        settle(full.at[pl.ds(0, p.block), pl.ds(0, n * part)], cross_send.at[sem])


def backward(
    shards, reps, x, cot_all, grad_activ, gate_w, up_w, gate_e, up_e, down_w, hidden, tokens, proj_w,
    qkv_m, normed, mlp_rms, mlp_gain, attn_gain, seg_col, seg_row, cos_t, sin_t, lse, q_t, mixed_t,
    k, k_t, v,
):
    length, width = x.shape
    count = tokens.shape[0]
    ffn_part = down_w.shape[0]
    q_part, kv_part = q_t.shape[0], k_t.shape[0]
    n = shards - 1
    p = Plan(shards, reps, length, width, ffn_part, q_part, kv_part)
    shape = jax.ShapeDtypeStruct
    own = width // shards
    chunk = (p.rows, TILE)
    dma = pltpu.SemaphoreType.DMA
    return pl.pallas_call(
        functools.partial(backward_kernel, p, gate_e.shape[1]),
        in_specs=[ANY] * 13 + [IN_VMEM] * 13,
        out_specs=[ANY] * 8 + [IN_VMEM] + [ANY] * 15,
        out_shape=[
            shape((ffn_part, width), BF16),
            shape((own, shards * ffn_part), BF16),
            shape((own, shards * ffn_part), BF16),
            shape((q_part, width), BF16),
            shape((own, shards * q_part), BF16),
            shape((own, shards * 2 * kv_part), BF16),
            shape((count, width), F32),
            shape((count, width), F32),
            shape((8, width // shards), F32),
        ]
        + [shape((p.chunks,) + chunk, BF16)] * 4
        + [shape((n, count, width), BF16)] * 3
        + [shape((length, width), BF16)]
        + [shape((width, ffn_part), BF16)] * 2
        + [shape((length, ffn_part), BF16)] * 3
        + [shape((length, width), BF16)] * 2,
        scratch_shapes=[
            pltpu.VMEM((length, width), BF16),
            pltpu.VMEM((length, width), BF16),
            pltpu.VMEM((2, length, TILE), BF16),
            pltpu.VMEM((width, TILE), BF16),
            pltpu.VMEM((width, TILE), BF16),
            pltpu.VMEM((length, TILE), BF16),
            pltpu.VMEM((2, TILE, 2 * ffn_part), BF16),
            pltpu.VMEM((2, length, TILE), BF16),
            pltpu.VMEM((length, 2 * ffn_part), BF16),
            pltpu.VMEM(proj_w.shape, BF16),
            pltpu.VMEM(qkv_m.shape, BF16),
            pltpu.VMEM((count, width), F32),
            pltpu.VMEM((count, width), F32),
            pltpu.VMEM((2, count, width), BF16),
            pltpu.VMEM((p.mine_ring,) + chunk, BF16),
            pltpu.VMEM((2,) + chunk, BF16),
            pltpu.VMEM(chunk, BF16),
            pltpu.VMEM(chunk, BF16),
            pltpu.VMEM(chunk, BF16),
            pltpu.VMEM((p.sum_ring,) + chunk, BF16),
            pltpu.VMEM((2,) + chunk, BF16),
            pltpu.VMEM((count, width), F32),
            pltpu.VMEM((count, width), BF16),
            pltpu.VMEM((q_part, length), BF16),
            pltpu.VMEM((q_part + 2 * kv_part, length), BF16),
            pltpu.VMEM((HEAD, length), F32),
            pltpu.VMEM((HEAD, length), F32),
            pltpu.VMEM((length, ffn_part) if p.early_res else (16, 128), BF16),
            pltpu.VMEM((8, width), F32),
            pltpu.VMEM((shards, 8, own), F32),
            pltpu.VMEM((8, own), F32),
            pltpu.VMEM((reps, 8, own), F32),
            dma((12,)), dma((2,)), dma((5,)), dma((2,)), dma((p.chunks,)), dma((p.sum_ring,)),
            dma((p.chunks,)), dma((p.chunks,)), dma((2,)), dma((p.chunks,)), dma((2,)),
            dma((p.chunks,)), dma((6,)), dma((6,)), dma((6,)),
        ]
        + [dma((max(6, n),))] * 6
        + Gather.semaphores(shards)
        + [dma((n,)), dma((n,)), dma((reps - 1,)), dma((reps - 1,))]
        + [dma((p.tiles,))] * 4
        + [dma((3,)), dma((2, 2)), dma((3,))],
        compiler_params=pltpu.CompilerParams(
            collective_id=3, has_side_effects=True, vmem_limit_bytes=FULL
        ),
        name="backward",
    )(
        x, cot_all, grad_activ, gate_w, up_w, gate_e, up_e, down_w, hidden, tokens, proj_w,
        qkv_m, normed, mlp_rms, mlp_gain[None, :], attn_gain[None, :], seg_col, seg_row,
        cos_t, sin_t, lse, q_t, mixed_t, k, k_t, v,
    )[:9]


def widen_kernel(count, rows, columns, group, *refs):
    paired = 1 if group else 0
    srcs, dsts = refs[:count], refs[count : 2 * count + paired]
    narrow, wide, in_sem, out_sem = refs[2 * count + paired :]
    depth = narrow.shape[0]
    jobs = []
    for i, src in enumerate(srcs):
        width = min(columns, src.shape[1])
        for r in range(src.shape[0] // rows):
            for c in range(src.shape[1] // width):
                slot = len(jobs) % depth
                at = (pl.ds(r * rows, rows), pl.ds(c * width, width))
                own = (slice(None), pl.ds(0, width))
                pair = paired and i == 0
                direct = src.dtype == F32
                into = (wide if direct else narrow).at[slot].at[own]
                load = pltpu.make_async_copy(src.at[at], into, in_sem.at[slot])
                held = wide.at[slot].at[own]
                if pair:
                    side = width // 2
                    puts = [
                        pltpu.make_async_copy(
                            wide.at[slot, :, pl.ds(k * side, side)],
                            dsts[k].at[pl.ds(r * rows, rows), :],
                            out_sem.at[slot],
                        )
                        for k in range(2)
                    ]
                else:
                    puts = [pltpu.make_async_copy(held, dsts[i + paired].at[at], out_sem.at[slot])]
                done = pltpu.make_async_copy(held, held, out_sem.at[slot])
                jobs.append((load, puts, done, direct, pair, width))
    total = len(jobs)
    ahead = depth - 1

    def load(i):
        if jobs[i][3] and i >= depth:
            jobs[i - depth][2].wait()
        jobs[i][0].start()

    for i in range(min(ahead, total)):
        load(i)
    for i in range(total):
        slot = i % depth
        fetch, puts, _, direct, pair, width = jobs[i]
        fetch.wait()
        if not direct:
            if i >= depth:
                jobs[i - depth][2].wait()
            for strip in range(0, rows, 64):
                here = pl.ds(strip, 64)
                if pair:
                    for k in range(width // group):
                        to = (k % 2) * (width // 2) + (k // 2) * group
                        wide[slot, here, pl.ds(to, group)] = narrow[
                            slot, here, pl.ds(k * group, group)
                        ].astype(F32)
                else:
                    wide[slot, here, pl.ds(0, width)] = narrow[
                        slot, here, pl.ds(0, width)
                    ].astype(F32)
        for put in puts:
            put.start()
        if i + ahead < total:
            load(i + ahead)
    for i in range(max(0, total - depth), total):
        jobs[i][2].wait()


def widen(arrays, group):
    rows, columns, depth = 64, 2048, 12
    rows = min([rows] + [a.shape[0] for a in arrays])
    shapes = [jax.ShapeDtypeStruct(a.shape, F32) for a in arrays]
    if group:
        tall, width = arrays[0].shape
        shapes[:1] = [jax.ShapeDtypeStruct((tall, width // 2), F32)] * 2
    return pl.pallas_call(
        functools.partial(widen_kernel, len(arrays), rows, columns, group),
        in_specs=[ANY] * len(arrays),
        out_specs=[ANY] * len(shapes),
        out_shape=shapes,
        scratch_shapes=[
            pltpu.VMEM((depth, rows, columns), BF16),
            pltpu.VMEM((depth, rows, columns), F32),
            pltpu.SemaphoreType.DMA((depth,)),
            pltpu.SemaphoreType.DMA((depth,)),
        ],
        compiler_params=pltpu.CompilerParams(vmem_limit_bytes=FULL),
        name="widen",
    )(*arrays)


def local(
    tokens, segments, query_w, key_w, value_w, proj_w, attn_gain,
    gate_w, up_w, down_w, mlp_gain, cotangent,
):
    shards = lax.axis_size("shard")
    reps = lax.axis_size("rep")
    tok_count, width = tokens.shape
    kv_part = key_w.shape[1] // shards
    q_part = query_w.shape[1] // shards
    length = tok_count * shards

    if kv_part % 128:
        kv_w = jnp.concatenate(
            [
                w[:, s * kv_part : (s + 1) * kv_part]
                for s in range(shards)
                for w in (key_w, value_w)
            ],
            axis=1,
        )
        weights = (query_w, kv_w)
    else:
        weights = (query_w, key_w, value_w)
    early = min(2 * TILE, down_w.shape[0] // 2)
    (
        normed, cot_all, proj_m, gate_e, up_e, qkv_m,
        q_t, k, k_t, v, mixed_t, lse, cos_t, sin_t, seg_col, seg_row,
    ) = attend(
        tokens, segments[None, :], weights, cotangent, proj_w, gate_w, up_w, attn_gain,
        q_part, kv_part, early, shards,
    )
    hidden, mlp_rms, normed_mlp, grad_activ = hidden_layer(
        mixed_t, proj_m, proj_w, cot_all, down_w, tokens, mlp_gain, shards
    )
    down, gate, up, proj, query, kv, result, grad_tokens, gains = backward(
        shards, reps, normed_mlp, cot_all, grad_activ, gate_w, up_w, gate_e, up_e, down_w, hidden, tokens,
        proj_w, qkv_m, normed, mlp_rms, mlp_gain, attn_gain, seg_col, seg_row, cos_t, sin_t, lse,
        q_t, mixed_t, k, k_t, v,
    )

    def every_other(first):
        parts = [
            kv[:, (2 * s + first) * kv_part : (2 * s + first + 1) * kv_part] for s in range(shards)
        ]
        return jnp.concatenate(parts, axis=1).astype(F32)

    others = [gate, up, down, query, proj, result, grad_tokens]
    if kv_part % 128:
        key, value = every_other(0), every_other(1)
        gate, up, down, query, proj, result, grad_tokens = widen(others, 0)
    else:
        key, value, gate, up, down, query, proj, result, grad_tokens = widen([kv] + others, kv_part)
    return (
        result, grad_tokens, query, key, value, proj, gains[0], gate, up, down, gains[1],
    )


def solution(mesh):
    rows = P(("rep", "shard"), None)
    held = P("shard", None)
    in_specs = (
        rows, P(("rep", "shard")), held, held, held, held, P(), held, held, held, P(), rows,
    )
    out_specs = (
        rows, rows, held, held, held, held, P("shard"), held, held, held, P("shard"),
    )
    return jax.shard_map(local, mesh=mesh, in_specs=in_specs, out_specs=out_specs, check_vma=False)
```
